32 devices in a mesh: dp: 16 (over z, y, x), tensor: 2 (over core).
Axes of the slice: x: 2, y: 2, z: 4, core: 2. Of those that a mesh axis runs over, the one named last changes fastest.
Arguments:
- source_tokens: bfloat16 [16384, 768], P('dp'), may hold values from -6 to 6
- target_tokens: bfloat16 [8192, 768], P('dp'), may hold values from -6 to 6
- target_cotangent: bfloat16 [8192, 768], P('dp'), may hold values from -6 to 6
- retrieved: int32 [16, 1024], P('dp'), may hold values from 0 to 8191, as said below
- kept_mask: int32 [16384], P('dp'), may hold values from 0 to 1, as said below
- owner_slots: int32 [504], replicated, may hold values from 0 to 511, as said below
- master: float32 [2, 512, 128, 128], P('tensor', 'dp'), may hold values from -1.299038 to 1.299038
- first_moment: float32 [2, 512, 128, 128], P('tensor', 'dp'), may hold values from -80 to 80
- second_moment: float32 [2, 512, 128, 128], P('tensor', 'dp'), may hold values from 819.2 to 3276.8
- left_stats: float32 [2, 512, 128, 128], P('tensor', 'dp'), may hold values from -491.52 to 419430.4, as said below
- right_stats: float32 [2, 512, 128, 128], P('tensor', 'dp'), may hold values from -491.52 to 419430.4, as said below
- left_basis: float32 [2, 512, 128, 128], P('tensor', 'dp'), may hold values from -1.001 to 1.001, as said below
- right_basis: float32 [2, 512, 128, 128], P('tensor', 'dp'), may hold values from -1.001 to 1.001, as said below
- shared_vectors: float32 [15, 768], P(None, 'dp'), may hold values from -1.8 to 1.8
- shared_first: float32 [15, 768], P(None, 'dp'), may hold values from -80 to 80
- shared_second: float32 [15, 768], P(None, 'dp'), may hold values from 819.2 to 3276.8
- split_vectors: float32 [2, 7, 768], P('tensor', None, 'dp'), may hold values from -4 to 4
- split_first: float32 [2, 7, 768], P('tensor', None, 'dp'), may hold values from -80 to 80
- split_second: float32 [2, 7, 768], P('tensor', None, 'dp'), may hold values from 819.2 to 3276.8
Outputs:
- encoder_states: float32 [16384, 768], P('dp')
- decoder_states: float32 [8192, 768], P('dp')
- source_grad: float32 [16384, 768], P('dp')
- target_grad: float32 [8192, 768], P('dp')
- new_master: float32 [2, 512, 128, 128], P('tensor', 'dp')
- new_first: float32 [2, 512, 128, 128], P('tensor', 'dp')
- new_second: float32 [2, 512, 128, 128], P('tensor', 'dp')
- new_left_stats: float32 [2, 512, 128, 128], P('tensor', 'dp')
- new_right_stats: float32 [2, 512, 128, 128], P('tensor', 'dp')
- new_left_basis: float32 [2, 512, 128, 128], P('tensor', 'dp')
- new_right_basis: float32 [2, 512, 128, 128], P('tensor', 'dp')
- shared_new_first: float32 [15, 768], P(None, 'dp')
- shared_new_second: float32 [15, 768], P(None, 'dp')
- shared_updated: float32 [15, 768], P(None, 'dp')
- split_new_first: float32 [2, 7, 768], P('tensor', None, 'dp')
- split_new_second: float32 [2, 7, 768], P('tensor', None, 'dp')
- split_updated: float32 [2, 7, 768], P('tensor', None, 'dp')
The draws below stay inside these ranges and needn't reach their ends.
Inputs may be any that keep to these rules, and one draw needn't show every extreme that they name: `retrieved`: in each row, entries j * 64 to (j + 1) * 64 - 1 are distinct datastore rows of j * 512 to (j + 1) * 512 - 1, j from 0. `kept_mask`: in each group the ones form one run of exactly 512 positions; in the first group it starts at the group's start, in the last it ends at the group's end. `owner_slots`: distinct slots. `left_stats`: each block is symmetric positive definite. `right_stats`: each block is symmetric positive definite. `left_basis`: each block is orthogonal up to rounding. `right_basis`: each block is orthogonal up to rounding.
All inputs are finite; a program needn't handle non-finite values.
Results may differ from the reference program's by a relative error of at most 0.035.
Values may be sent and summed in bfloat16 or wider, within the bound.
A program may use at most 384 MiB of HBM per device.

```python
import math
from functools import partial
import jax
import jax.numpy as jnp
import numpy as np
from jax import lax

D = 768
HD = 64
FF = 3072
GROUP = 1024
KEEP = 512
TGT_DEV = 512
QROWS = 512
R = 1024
BLK = 128
SLOTS = 512
VS = 15
STEP = 10
CAP = 64
QB_DEV = 1
NQB = 16
ENC_TOK = 16384
DEC_TOK = 8192
STORE = 8192
NBLK = 504
VT = 7
N_DP = 16
N_TENSOR = 2


def owner_permutation(key):
    return jax.random.permutation(jax.random.fold_in(key, 17), SLOTS)[:NBLK].astype(jnp.int32)


def block_scales():
    half_width = D // N_TENSOR
    hidden_half = FF // N_TENSOR
    drawn = D ** (-0.5)
    outward = 6.0 * D ** (-0.5)
    downward = FF ** (-0.5)
    plan = [(D, 3 * half_width, drawn), (half_width, D, outward), (D, hidden_half, drawn), (hidden_half, D, downward), (D, 3 * half_width, drawn), (half_width, D, outward), (D, half_width, drawn), (D, 2 * half_width, drawn), (half_width, D, outward), (D, hidden_half, drawn), (hidden_half, D, downward)]
    scales = []
    for height, breadth, factor in plan:
        scales.extend([factor] * (height // BLK * (breadth // BLK)))
    return np.asarray(scales, np.float32)


def draw_owner_slots(key, part):
    return owner_permutation(key)


def draw_master(key, part):
    slots = owner_permutation(key)
    scales = jnp.full((SLOTS,), D ** (-0.5), jnp.float32).at[slots].set(jnp.asarray(block_scales()))
    values = jnp.clip(jax.random.normal(jax.random.fold_in(key, 23), (N_TENSOR, SLOTS, BLK, BLK), jnp.float32), -6.0, 6.0)
    return values * scales[None, :, None, None]


def draw_retrieved(key, part):
    keys_all = jax.random.split(jax.random.fold_in(key, 31), NQB * N_DP)

    def choose(one_key):
        return jax.random.permutation(one_key, KEEP)[:CAP]
    picks = jax.vmap(choose)(keys_all).reshape(NQB, N_DP, CAP).astype(jnp.int32)
    offsets = (jnp.arange(N_DP, dtype=jnp.int32) * KEEP)[None, :, None]
    return (picks + offsets).reshape(NQB, N_DP * CAP)


def draw_kept_mask(key, part):
    jitter = (GROUP - KEEP) // 8
    centre = (GROUP - KEEP) // 2
    starts = jax.random.randint(jax.random.fold_in(key, 37), (N_DP,), centre - jitter, centre + jitter + 1)
    starts = starts.at[0].set(0).at[N_DP - 1].set(GROUP - KEEP)
    positions = jnp.arange(GROUP, dtype=jnp.int32)[None, :]
    inside = (positions >= starts[:, None]) & (positions < starts[:, None] + KEEP)
    return inside.astype(jnp.int32).reshape(-1)


def statistics(key):
    scale = 0.05 * BLK * N_DP * GROUP
    diagonal = jnp.exp(jax.random.uniform(jax.random.fold_in(key, 1), (N_TENSOR, SLOTS, BLK), jnp.float32, 0.0, math.log(4.0))) * scale
    spread = jax.random.uniform(jax.random.fold_in(key, 2), (N_TENSOR, SLOTS, BLK, BLK), jnp.float32, -1.0, 1.0)
    symmetric = (spread + jnp.swapaxes(spread, -1, -2)) * (0.3 * scale / BLK)
    identity = jnp.eye(BLK, dtype=jnp.float32)
    return symmetric * (1.0 - identity) + diagonal[..., None] * identity


def draw_left_stats(key, part):
    return statistics(jax.random.fold_in(key, 41))


def draw_right_stats(key, part):
    return statistics(jax.random.fold_in(key, 43))


def basis(key):
    half_count = BLK // 2
    angles = jax.random.uniform(jax.random.fold_in(key, 1), (N_TENSOR, SLOTS, half_count), jnp.float32, -math.pi, math.pi)
    cosine = jnp.cos(angles)
    sine = jnp.sin(angles)
    flips = jax.random.randint(jax.random.fold_in(key, 2), (N_TENSOR, SLOTS, BLK), 0, 2).astype(jnp.float32)
    vector = (2.0 * flips - 1.0) * BLK ** (-0.5)
    even_part = vector[..., 0::2]
    odd_part = vector[..., 1::2]
    turned_even = cosine * even_part + sine * odd_part
    turned_odd = cosine * odd_part - sine * even_part
    turned = jnp.stack([turned_even, turned_odd], -1).reshape(N_TENSOR, SLOTS, BLK)
    rows = jnp.arange(BLK, dtype=jnp.int32)[:, None]
    cols = jnp.arange(BLK, dtype=jnp.int32)[None, :]
    same_pair = (rows // 2 == cols // 2).astype(jnp.float32)
    diagonal_mask = (rows == cols).astype(jnp.float32)
    row_even = (rows % 2 == 0).astype(jnp.float32)
    cos_rows = jnp.repeat(cosine, 2, axis=-1)[..., :, None]
    sin_rows = jnp.repeat(sine, 2, axis=-1)[..., :, None]
    off_value = sin_rows * (1.0 - 2.0 * row_even)
    rotation = same_pair * (diagonal_mask * cos_rows + (1.0 - diagonal_mask) * off_value)
    return rotation - 2.0 * vector[..., :, None] * turned[..., None, :]


def draw_left_basis(key, part):
    return basis(jax.random.fold_in(key, 47))


def draw_right_basis(key, part):
    return basis(jax.random.fold_in(key, 53))


def draw_shared_vectors(key, part):
    gain_rows = np.zeros((VS,), np.bool_)
    gain_rows[[1, 4, 7, 10, 13]] = True
    gains = jnp.exp(jax.random.uniform(jax.random.fold_in(key, 59), (VS, D), jnp.float32, math.log(0.6), math.log(1.6)))
    shifts = 0.3 * jnp.clip(jax.random.normal(jax.random.fold_in(key, 61), (VS, D), jnp.float32), -6.0, 6.0)
    return jnp.where(jnp.asarray(gain_rows)[:, None], gains, shifts)


def levels(stream_key, extent, cuts, smallest, largest):
    loudness = 1.0
    for dim, parts in cuts:
        draws = jax.random.uniform(jax.random.fold_in(jax.random.fold_in(stream_key, 6), dim), (parts,), jnp.float32, smallest / len(cuts), largest / len(cuts))
        loudness = loudness * jnp.repeat(jnp.exp(draws), extent[dim] // parts).reshape((-1,) + (1,) * (len(extent) - 1 - dim))
    return loudness


def bell_draw(rng, shape, width, reach, cuts=(), kind=jnp.bfloat16):
    values = jax.random.normal(rng, shape, jnp.float32) * width
    if len(cuts) > 0:
        values = levels(rng, shape, cuts, -0.22, 0.18) * values
    return jnp.clip(values, min=-reach, max=reach).astype(kind)


def setup_inputs(seed: int = 0) -> dict:
    key_list = jax.random.split(jax.random.key(seed), 20)
    return {
        "source_tokens": bell_draw(key_list[0], (ENC_TOK, D), 1.0, 6.0, ((0, 16),)),
        "target_tokens": bell_draw(key_list[1], (DEC_TOK, D), 1.0, 6.0, ((0, 16),)),
        "target_cotangent": bell_draw(key_list[2], (DEC_TOK, D), 1.0, 6.0, ((0, 16),)),
        "retrieved": draw_retrieved(jax.random.fold_in(key_list[19], 71), 0),
        "kept_mask": draw_kept_mask(jax.random.fold_in(key_list[19], 71), 0),
        "owner_slots": draw_owner_slots(jax.random.fold_in(key_list[19], 71), 0),
        "master": draw_master(jax.random.fold_in(key_list[19], 71), 0),
        "first_moment": bell_draw(key_list[7], (N_TENSOR, SLOTS, BLK, BLK), (0.1 * (N_DP * GROUP) ** 0.5), 80.0, ((0, 2), (1, 16)), jnp.float32),
        "second_moment": jnp.clip(jnp.exp(math.log(3276.8) - 1.3862944 * jax.random.uniform(key_list[8], (N_TENSOR, SLOTS, BLK, BLK), jnp.float32) ** levels(key_list[8], (N_TENSOR, SLOTS, BLK, BLK), ((0, 2), (1, 16)), -0.2, 0.2)), 819.2, 3276.8),
        "left_stats": draw_left_stats(jax.random.fold_in(key_list[19], 71), 0),
        "right_stats": draw_right_stats(jax.random.fold_in(key_list[19], 71), 0),
        "left_basis": draw_left_basis(jax.random.fold_in(key_list[19], 71), 0),
        "right_basis": draw_right_basis(jax.random.fold_in(key_list[19], 71), 0),
        "shared_vectors": draw_shared_vectors(jax.random.fold_in(key_list[19], 71), 0),
        "shared_first": bell_draw(key_list[14], (VS, D), (0.1 * (N_DP * GROUP) ** 0.5), 80.0, ((1, 16),), jnp.float32),
        "shared_second": jnp.clip(jnp.exp(math.log(3276.8) - 1.3862944 * jax.random.uniform(key_list[15], (VS, D), jnp.float32) ** levels(key_list[15], (VS, D), ((1, 16),), -0.2, 0.2)), 819.2, 3276.8),
        "split_vectors": bell_draw(key_list[16], (N_TENSOR, VT, D), 0.3, 4.0, ((0, 2), (2, 16)), jnp.float32),
        "split_first": bell_draw(key_list[17], (N_TENSOR, VT, D), (0.1 * (N_DP * GROUP) ** 0.5), 80.0, ((0, 2), (2, 16)), jnp.float32),
        "split_second": jnp.clip(jnp.exp(math.log(3276.8) - 1.3862944 * jax.random.uniform(key_list[18], (N_TENSOR, VT, D), jnp.float32) ** levels(key_list[18], (N_TENSOR, VT, D), ((0, 2), (2, 16)), -0.2, 0.2)), 819.2, 3276.8),
    }


MATMUL_ACCURACY = lax.Precision.HIGHEST
BETA_ONE = 0.9
BETA_TWO = 0.95
ADAM_EPSILON = 1e-08
MATRIX_RATE = 0.1
VECTOR_RATE = 0.5
WEIGHT_DECAY = 0.01
NORM_EPSILON = 1e-05

@jax.custom_vjp
def reduced_precision(v):
    return lax.optimization_barrier(v.astype(jnp.bfloat16)).astype(jnp.float32)

@jax.custom_vjp
def reduced_backward(v):
    return v

def low_keep(v):
    return (reduced_precision(v), None)

def low_pass(kept, grad):
    return (grad,)

def back_keep(v):
    return (v, None)

def back_low(kept, grad):
    return (reduced_precision(grad),)
reduced_precision.defvjp(low_keep, low_pass)
reduced_backward.defvjp(back_keep, back_low)

def matrix_list(model_width, hidden_width, tensor_count):
    half_width = model_width // tensor_count
    hidden_half = hidden_width // tensor_count
    return [('enc_qkv', model_width, 3 * half_width), ('enc_out', half_width, model_width), ('enc_up', model_width, hidden_half), ('enc_down', hidden_half, model_width), ('dec_qkv', model_width, 3 * half_width), ('dec_out', half_width, model_width), ('crs_q', model_width, half_width), ('crs_kv', model_width, 2 * half_width), ('crs_out', half_width, model_width), ('dec_up', model_width, hidden_half), ('dec_down', hidden_half, model_width)]

def unpack(blocks, model_width, hidden_width, tensor_count):
    tile_size = blocks.shape[-1]
    matrices = {}
    offset = 0
    for matrix_name, height, breadth in matrix_list(model_width, hidden_width, tensor_count):
        block_count = height // tile_size * (breadth // tile_size)
        pieces = blocks[offset:offset + block_count].reshape(height // tile_size, breadth // tile_size, tile_size, tile_size)
        matrices[matrix_name] = pieces.transpose(0, 2, 1, 3).reshape(height, breadth)
        offset = offset + block_count
    return matrices

def pack(matrices, model_width, hidden_width, tensor_count, tile_size):
    pieces = []
    for matrix_name, height, breadth in matrix_list(model_width, hidden_width, tensor_count):
        shaped = matrices[matrix_name].reshape(height // tile_size, tile_size, breadth // tile_size, tile_size)
        pieces.append(shaped.transpose(0, 2, 1, 3).reshape(-1, tile_size, tile_size))
    return jnp.concatenate(pieces, 0)

def split_biases(flat_vector, half_width, hidden_half):
    layout = [('enc_q', half_width), ('enc_v', half_width), ('enc_up', hidden_half), ('dec_q', half_width), ('dec_v', half_width), ('crs_q', half_width), ('crs_v', half_width), ('dec_up', hidden_half)]
    result = {}
    offset = 0
    for label_name, length in layout:
        result[label_name] = flat_vector[offset:offset + length]
        offset = offset + length
    return result

def layer_norm(values, gain, shift):
    center = values - lax.optimization_barrier(jnp.mean(values, -1, keepdims=True))
    spread = lax.optimization_barrier(jnp.mean(center * center, -1, keepdims=True))
    return center * lax.rsqrt(spread + NORM_EPSILON) * gain + shift

def attend(query_rows, keys, values, causal):
    scale = query_rows.shape[-1] ** (-0.5)
    scores = jnp.einsum('bqhe,bkhe->bhqk', query_rows, keys, precision=MATMUL_ACCURACY) * scale
    if causal:
        query_pos = lax.broadcasted_iota(jnp.int32, scores.shape, 2)
        key_pos = lax.broadcasted_iota(jnp.int32, scores.shape, 3)
        scores = jnp.where(key_pos <= query_pos, scores, -1000000000.0)
    scores = reduced_backward(scores)
    weights = reduced_precision(jax.nn.softmax(scores, axis=-1))
    return jnp.einsum('bhqk,bkhe->bqhe', weights, values, precision=MATMUL_ACCURACY)

def self_part(inputs, weight_qkv, bias_qkv, output_weight, causal):
    part_width = weight_qkv.shape[1] // 3
    blended_output = reduced_backward(reduced_precision(jnp.einsum('bsd,df->bsf', inputs, weight_qkv, precision=MATMUL_ACCURACY) + bias_qkv))
    head_shape = inputs.shape[:2] + (part_width // HD, HD)
    query_rows = blended_output[..., :part_width].reshape(head_shape)
    keys = blended_output[..., part_width:2 * part_width].reshape(head_shape)
    values = blended_output[..., 2 * part_width:].reshape(head_shape)
    attended = attend(query_rows, keys, values, causal)
    combined_heads = reduced_backward(reduced_precision(attended.reshape(inputs.shape[:2] + (part_width,))))
    return jnp.einsum('bsf,fd->bsd', combined_heads, output_weight, precision=MATMUL_ACCURACY)

def ffn_part(hidden_low, weight_up, bias_up, weight_down):
    upward = reduced_backward(jnp.einsum('bsd,df->bsf', hidden_low, weight_up, precision=MATMUL_ACCURACY) + bias_up)
    active = reduced_precision(jax.nn.gelu(upward, approximate=False))
    return jnp.einsum('bsf,fd->bsd', active, weight_down, precision=MATMUL_ACCURACY)

def cross_part(query_inputs, retrieved_entries, query_weight, query_bias_vector, key_value_weight, bias_v, output_weight):
    part_width = query_weight.shape[1]
    blocks, qrow_count = (query_inputs.shape[0], query_inputs.shape[1])
    query_rows = reduced_backward(reduced_precision(jnp.einsum('kpl,le->kpe', query_inputs, query_weight, precision=MATMUL_ACCURACY) + query_bias_vector))
    query_rows = query_rows.reshape(blocks, qrow_count, part_width // HD, HD)
    key_value_bias = jnp.concatenate([jnp.zeros((part_width,), jnp.float32), bias_v])
    blended_output = reduced_backward(reduced_precision(jnp.einsum('uwo,ot->uwt', retrieved_entries, key_value_weight, precision=MATMUL_ACCURACY) + key_value_bias))
    keys = blended_output[..., :part_width].reshape(blocks, -1, part_width // HD, HD)
    values = blended_output[..., part_width:].reshape(blocks, -1, part_width // HD, HD)
    attended = attend(query_rows, keys, values, False)
    combined_heads = reduced_backward(reduced_precision(attended.reshape(blocks, qrow_count, part_width)))
    return jnp.einsum('tia,ax->tix', combined_heads, output_weight, precision=MATMUL_ACCURACY)

def encode_group(params, group_rows):
    rank_mats, shared, splits = params
    half_width = D // N_TENSOR
    hidden_half = FF // N_TENSOR
    inputs = group_rows[None]
    zero_half = jnp.zeros((half_width,), jnp.float32)
    attention = jnp.zeros_like(inputs)
    for tensor_rank in range(N_TENSOR):
        biases = split_biases(splits[tensor_rank], half_width, hidden_half)
        bias_qkv = jnp.concatenate([biases['enc_q'], zero_half, biases['enc_v']])
        attention = attention + self_part(inputs, rank_mats[tensor_rank]['enc_qkv'], bias_qkv, rank_mats[tensor_rank]['enc_out'], False)
    attention = reduced_backward(attention)
    hidden = layer_norm(inputs + attention + shared[0], shared[1], shared[2])
    hidden_low = reduced_precision(hidden)
    feed = jnp.zeros_like(inputs)
    for tensor_rank in range(N_TENSOR):
        biases = split_biases(splits[tensor_rank], half_width, hidden_half)
        feed = feed + ffn_part(hidden_low, rank_mats[tensor_rank]['enc_up'], biases['enc_up'], rank_mats[tensor_rank]['enc_down'])
    feed = reduced_backward(feed)
    return layer_norm(hidden + feed + shared[3], shared[4], shared[5])[0]

def decode_seq(params, store, inputs):
    rank_mats, shared, splits = params
    target_rows, index_rows = inputs
    half_width = D // N_TENSOR
    hidden_half = FF // N_TENSOR
    seq_rows = target_rows[None]
    zero_half = jnp.zeros((half_width,), jnp.float32)
    attention = jnp.zeros_like(seq_rows)
    for tensor_rank in range(N_TENSOR):
        biases = split_biases(splits[tensor_rank], half_width, hidden_half)
        bias_qkv = jnp.concatenate([biases['dec_q'], zero_half, biases['dec_v']])
        attention = attention + self_part(seq_rows, rank_mats[tensor_rank]['dec_qkv'], bias_qkv, rank_mats[tensor_rank]['dec_out'], True)
    attention = reduced_backward(attention)
    first = layer_norm(seq_rows + attention + shared[6], shared[7], shared[8])
    retrieved_entries = reduced_backward(store[index_rows])
    first_low = reduced_precision(first).reshape(QB_DEV, QROWS, D)
    cross = jnp.zeros((QB_DEV, QROWS, D), jnp.float32)
    for tensor_rank in range(N_TENSOR):
        biases = split_biases(splits[tensor_rank], half_width, hidden_half)
        mats = rank_mats[tensor_rank]
        cross = cross + cross_part(first_low, retrieved_entries, mats['crs_q'], biases['crs_q'], mats['crs_kv'], biases['crs_v'], mats['crs_out'])
    cross = reduced_backward(cross).reshape(1, TGT_DEV, D)
    second = layer_norm(first + cross + shared[9], shared[10], shared[11])
    second_low = reduced_precision(second)
    feed = jnp.zeros_like(seq_rows)
    for tensor_rank in range(N_TENSOR):
        biases = split_biases(splits[tensor_rank], half_width, hidden_half)
        feed = feed + ffn_part(second_low, rank_mats[tensor_rank]['dec_up'], biases['dec_up'], rank_mats[tensor_rank]['dec_down'])
    feed = reduced_backward(feed)
    return layer_norm(second + feed + shared[12], shared[13], shared[14])[0]

def take_kept(group_states, start_row):
    return lax.dynamic_slice_in_dim(group_states, start_row, KEEP, 0)

def orthonormal(matrix):
    gram = jnp.matmul(matrix.T, matrix, precision=MATMUL_ACCURACY)
    factor = jnp.linalg.cholesky(gram)
    return jax.scipy.linalg.solve_triangular(factor, matrix.T, lower=True).T

def soap_update(grad_block, weight_block, first_block, second_block, left_block, right_block, left_turn, right_turn):
    product = partial(jnp.matmul, precision=MATMUL_ACCURACY)
    rotated = product(product(left_turn.T, grad_block), right_turn)
    new_first = BETA_ONE * first_block + (1.0 - BETA_ONE) * grad_block
    new_second = BETA_TWO * second_block + (1.0 - BETA_TWO) * rotated * rotated
    first_rotated = product(product(left_turn.T, new_first), right_turn)
    correct_one = 1.0 - BETA_ONE ** STEP
    correct_two = 1.0 - BETA_TWO ** STEP
    normed = first_rotated / correct_one / (jnp.sqrt(new_second / correct_two) + ADAM_EPSILON)
    new_weight = weight_block - MATRIX_RATE * product(product(left_turn, normed), right_turn.T) - MATRIX_RATE * WEIGHT_DECAY * weight_block
    new_left = BETA_TWO * left_block + (1.0 - BETA_TWO) * product(grad_block, grad_block.T)
    new_right = BETA_TWO * right_block + (1.0 - BETA_TWO) * product(grad_block.T, grad_block)
    return (new_first, new_second, new_weight, new_left, new_right, orthonormal(product(new_left, left_turn)), orthonormal(product(new_right, right_turn)))

def adam_vector(grad_value, value, first, second):
    new_first = BETA_ONE * first + (1.0 - BETA_ONE) * grad_value
    new_second = BETA_TWO * second + (1.0 - BETA_TWO) * grad_value * grad_value
    correct_one = 1.0 - BETA_ONE ** STEP
    correct_two = 1.0 - BETA_TWO ** STEP
    updated = value - VECTOR_RATE * (new_first / correct_one) / (jnp.sqrt(new_second / correct_two) + ADAM_EPSILON)
    return (new_first, new_second, updated)

def reference(source_tokens, target_tokens, target_cotangent, retrieved, kept_mask, owner_slots, master, first_moment, second_moment, left_stats, right_stats, left_basis, right_basis, shared_vectors, shared_first, shared_second, split_vectors, split_first, split_second):
    rounded_master = lax.optimization_barrier(master.astype(jnp.bfloat16)).astype(jnp.float32)
    rank_mats = [unpack(rounded_master[tensor_rank][owner_slots], D, FF, N_TENSOR) for tensor_rank in range(N_TENSOR)]
    shared = lax.optimization_barrier(shared_vectors.astype(jnp.bfloat16)).astype(jnp.float32)
    splits = lax.optimization_barrier(split_vectors.astype(jnp.bfloat16)).astype(jnp.float32).reshape(N_TENSOR, -1)
    starts = jnp.argmax(kept_mask.reshape(N_DP, GROUP), axis=1).astype(jnp.int32)

    def forward(source, target, mats, shared_in, splits_in):
        params = (mats, shared_in, splits_in)
        states = lax.map(partial(jax.checkpoint(encode_group), params), source.reshape(N_DP, GROUP, D))
        store = jax.vmap(take_kept)(reduced_precision(states), starts).reshape(STORE, D)
        decoded = lax.map(partial(jax.checkpoint(decode_seq), params, store), (target.reshape(N_DP, TGT_DEV, D), retrieved.reshape(N_DP, QB_DEV, R)))
        return (states.reshape(ENC_TOK, D), decoded.reshape(DEC_TOK, D))
    outputs, pullback = jax.vjp(forward, source_tokens.astype(jnp.float32), target_tokens.astype(jnp.float32), rank_mats, shared, splits)
    encoder_states, decoder_states = outputs
    source_grad, target_grad, mat_grads, shared_grad, split_grad = pullback((jnp.zeros_like(encoder_states), target_cotangent.astype(jnp.float32)))
    slot_list = []
    for tensor_rank in range(N_TENSOR):
        packed = pack(mat_grads[tensor_rank], D, FF, N_TENSOR, BLK)
        slot_list.append(jnp.zeros((SLOTS, BLK, BLK), jnp.float32).at[owner_slots].set(packed))
    slot_grads = jnp.stack(slot_list).reshape(-1, BLK, BLK)
    flat_shape = (N_TENSOR * SLOTS, BLK, BLK)
    results = jax.vmap(soap_update)(slot_grads, master.reshape(flat_shape), first_moment.reshape(flat_shape), second_moment.reshape(flat_shape), left_stats.reshape(flat_shape), right_stats.reshape(flat_shape), left_basis.reshape(flat_shape), right_basis.reshape(flat_shape))
    full_shape = (N_TENSOR, SLOTS, BLK, BLK)
    new_first, new_second, new_master, new_left, new_right, new_lbasis, new_rbasis = [item.reshape(full_shape) for item in results]
    shared_new_first, shared_new_second, shared_updated = adam_vector(shared_grad, shared_vectors, shared_first, shared_second)
    split_new_first, split_new_second, split_updated = adam_vector(split_grad.reshape(N_TENSOR, VT, D), split_vectors, split_first, split_second)
    return (encoder_states, decoder_states, source_grad, target_grad, new_master, new_first, new_second, new_left, new_right, new_lbasis, new_rbasis, shared_new_first, shared_new_second, shared_updated, split_new_first, split_new_second, split_updated)
```

```python
import functools
from functools import partial

import jax
import jax.numpy as jnp
from jax import lax
from jax.experimental import pallas as pl
from jax.experimental.pallas import tpu as pltpu
from jax.sharding import PartitionSpec as P

HD = 64
KEEP = 512
STEP = 10


BETA_ONE = 0.9
BETA_TWO = 0.95
ADAM_EPSILON = 1e-08
MATRIX_RATE = 0.1
VECTOR_RATE = 0.5
WEIGHT_DECAY = 0.01
NORM_EPSILON = 1e-05
TILE = 128
PANEL = 32


def for_sending(x):

    def short(part):
        return part.astype(jnp.bfloat16) if part.dtype == jnp.float32 else part

    return jax.tree.map(short, x)


def matrix_list(model_width, hidden_width, tensor_count):
    half_width = model_width // tensor_count
    hidden_half = hidden_width // tensor_count
    return [
        ("enc_qkv", model_width, 3 * half_width),
        ("enc_out", half_width, model_width),
        ("enc_up", model_width, hidden_half),
        ("enc_down", hidden_half, model_width),
        ("dec_qkv", model_width, 3 * half_width),
        ("dec_out", half_width, model_width),
        ("crs_q", model_width, half_width),
        ("crs_kv", model_width, 2 * half_width),
        ("crs_out", half_width, model_width),
        ("dec_up", model_width, hidden_half),
        ("dec_down", hidden_half, model_width),
    ]


def split_biases(flat_vector, half_width, hidden_half):
    layout = [
        ("enc_q", half_width),
        ("enc_v", half_width),
        ("enc_up", hidden_half),
        ("dec_q", half_width),
        ("dec_v", half_width),
        ("crs_q", half_width),
        ("crs_v", half_width),
        ("dec_up", hidden_half),
    ]
    result = {}
    offset = 0
    for label_name, length in layout:
        result[label_name] = flat_vector[offset : offset + length]
        offset = offset + length
    return result


def layer_norm(values, gain, shift):
    center = values - jnp.mean(values, -1, keepdims=True)
    spread = jnp.mean(center * center, -1, keepdims=True)
    return center * lax.rsqrt(spread + NORM_EPSILON) * gain + shift


def project(left, right):
    return jnp.dot(left, right, preferred_element_type=jnp.float32)


def inner_rows(left, right):
    return jnp.einsum("sa,sb->ab", left, right, preferred_element_type=jnp.float32)


def times_transposed(left, right):
    return jnp.einsum("sa,ba->sb", left, right, preferred_element_type=jnp.float32)


def tensor_sum(values):
    return lax.psum(values.astype(jnp.bfloat16), "tensor").astype(jnp.float32)


def tensor_back(values):
    return jax.tree.map(
        lambda part: part.astype(jnp.float32), lax.psum(for_sending(values), "tensor")
    )


def raw_scores(query_rows, keys, causal):
    scale = query_rows.shape[-1] ** (-0.5)
    scores = (
        jnp.einsum("bqhe,bkhe->bhqk", query_rows, keys, preferred_element_type=jnp.float32) * scale
    )
    if causal:
        query_pos = lax.broadcasted_iota(jnp.int32, scores.shape, 2)
        key_pos = lax.broadcasted_iota(jnp.int32, scores.shape, 3)
        scores = jnp.where(key_pos <= query_pos, scores, -1000000000.0)
    return scores


def attend_forward(query_rows, keys, values, causal):
    scores = raw_scores(query_rows, keys, causal)
    totals = jax.nn.logsumexp(scores, axis=-1, keepdims=True)
    probs = jnp.exp(scores - totals)
    attended = jnp.einsum(
        "bhqk,bkhe->bqhe", probs.astype(jnp.bfloat16), values, preferred_element_type=jnp.float32
    )
    return (attended.astype(jnp.bfloat16), totals)


def attend_backward(query_rows, keys, values, totals, grad_out, causal):
    scale = query_rows.shape[-1] ** (-0.5)
    probs = jnp.exp(raw_scores(query_rows, keys, causal) - totals)
    grad_values = jnp.einsum(
        "bhqk,bqhe->bkhe", probs.astype(jnp.bfloat16), grad_out, preferred_element_type=jnp.float32
    )
    grad_probs = jnp.einsum("bqhe,bkhe->bhqk", grad_out, values, preferred_element_type=jnp.float32)
    grad_scores = (probs * (grad_probs - jnp.sum(grad_probs * probs, -1, keepdims=True))).astype(
        jnp.bfloat16
    )
    grad_queries = (
        jnp.einsum("bhqk,bkhe->bqhe", grad_scores, keys, preferred_element_type=jnp.float32) * scale
    )
    grad_keys = (
        jnp.einsum("bhqk,bqhe->bkhe", grad_scores, query_rows, preferred_element_type=jnp.float32)
        * scale
    )
    return (grad_queries, grad_keys, grad_values)


def self_forward(inputs_low, weight_qkv, bias_qkv, output_weight, causal):
    length = inputs_low.shape[0]
    part_width = weight_qkv.shape[1] // 3
    blended_output = (project(inputs_low, weight_qkv) + bias_qkv).astype(jnp.bfloat16)
    head_shape = (1, length, part_width // HD, HD)
    query_rows = blended_output[:, :part_width].reshape(head_shape)
    keys = blended_output[:, part_width : 2 * part_width].reshape(head_shape)
    values = blended_output[:, 2 * part_width :].reshape(head_shape)
    attended, totals = attend_forward(query_rows, keys, values, causal)
    combined_heads = attended.reshape(length, part_width)
    return (
        project(combined_heads, output_weight),
        (query_rows, keys, values, totals, combined_heads),
    )


def self_backward(grad_pre, inputs_low, saved, weight_qkv, output_weight, causal):
    query_rows, keys, values, totals, combined_heads = saved
    length = inputs_low.shape[0]
    part_width = combined_heads.shape[1]
    grad_branch = grad_pre.astype(jnp.bfloat16)
    grad_wout = inner_rows(combined_heads, grad_branch)
    grad_merged = (
        times_transposed(grad_branch, output_weight).astype(jnp.bfloat16).reshape(query_rows.shape)
    )
    grad_q, grad_k, grad_v = attend_backward(query_rows, keys, values, totals, grad_merged, causal)
    grad_mixed = jnp.concatenate(
        [
            grad_q.reshape(length, part_width),
            grad_k.reshape(length, part_width),
            grad_v.reshape(length, part_width),
        ],
        1,
    ).astype(jnp.bfloat16)
    grad_wqkv = inner_rows(inputs_low, grad_mixed)
    bias_sums = jnp.sum(grad_mixed.astype(jnp.float32), 0)
    part_input = times_transposed(grad_mixed, weight_qkv)
    return (grad_wqkv, bias_sums[:part_width], bias_sums[2 * part_width :], grad_wout, part_input)


def ffn_forward(hidden_low, weight_up, bias_up, weight_down):
    upward = project(hidden_low, weight_up) + bias_up
    active = jax.nn.gelu(upward, approximate=False).astype(jnp.bfloat16)
    return (project(active, weight_down), (upward, active))


def ffn_backward(grad_pre, hidden_low, saved, weight_up, weight_down):
    upward, active = saved
    grad_down = grad_pre.astype(jnp.bfloat16)
    grad_wdown = inner_rows(active, grad_down)
    grad_active = times_transposed(grad_down, weight_down)
    gelu_back = jax.vjp(partial(jax.nn.gelu, approximate=False), upward)[1]
    grad_up = gelu_back(grad_active)[0].astype(jnp.bfloat16)
    grad_wup = inner_rows(hidden_low, grad_up)
    grad_bias = jnp.sum(grad_up.astype(jnp.float32), 0)
    return (grad_wup, grad_bias, grad_wdown, times_transposed(grad_up, weight_up))


def cross_forward(
    query_inputs,
    retrieved_entries,
    query_weight,
    query_bias_vector,
    key_value_weight,
    bias_v,
    output_weight,
):
    blocks, qrow_count, model_width = query_inputs.shape
    part_width = query_weight.shape[1]
    query_rows = (
        jnp.einsum("kpl,le->kpe", query_inputs, query_weight, preferred_element_type=jnp.float32)
        + query_bias_vector
    )
    query_rows = query_rows.astype(jnp.bfloat16).reshape(blocks, qrow_count, part_width // HD, HD)
    key_value_bias = jnp.concatenate([jnp.zeros((part_width,), jnp.float32), bias_v])
    blended_output = (
        jnp.einsum(
            "uwo,ot->uwt", retrieved_entries, key_value_weight, preferred_element_type=jnp.float32
        )
        + key_value_bias
    ).astype(jnp.bfloat16)
    keys = blended_output[..., :part_width].reshape(blocks, -1, part_width // HD, HD)
    values = blended_output[..., part_width:].reshape(blocks, -1, part_width // HD, HD)
    attended, totals = attend_forward(query_rows, keys, values, False)
    combined_heads = attended.reshape(blocks * qrow_count, part_width)
    return (
        project(combined_heads, output_weight),
        (query_rows, keys, values, totals, combined_heads),
    )


def cross_backward(
    grad_pre, first_low, retrieved_entries, saved, query_weight, key_value_weight, output_weight
):
    query_rows, keys, values, totals, combined_heads = saved
    part_width = combined_heads.shape[1]
    grad_branch = grad_pre.astype(jnp.bfloat16)
    grad_wout = inner_rows(combined_heads, grad_branch)
    grad_merged = (
        times_transposed(grad_branch, output_weight).astype(jnp.bfloat16).reshape(query_rows.shape)
    )
    grad_q, grad_k, grad_v = attend_backward(query_rows, keys, values, totals, grad_merged, False)
    grad_query = grad_q.reshape(-1, part_width).astype(jnp.bfloat16)
    grad_wq = inner_rows(first_low, grad_query)
    grad_bq = jnp.sum(grad_query.astype(jnp.float32), 0)
    grad_kv = jnp.concatenate(
        [grad_k.reshape(-1, part_width), grad_v.reshape(-1, part_width)], 1
    ).astype(jnp.bfloat16)
    fetched_rows = retrieved_entries.reshape(-1, retrieved_entries.shape[-1])
    grad_wkv = inner_rows(fetched_rows, grad_kv)
    grad_bv = jnp.sum(grad_kv[:, part_width:].astype(jnp.float32), 0)
    part_first = times_transposed(grad_query, query_weight)
    part_fetched = times_transposed(grad_kv, key_value_weight).reshape(retrieved_entries.shape)
    return (grad_wq, grad_bq, grad_wkv, grad_bv, grad_wout, part_first, part_fetched)


def halves(x):
    hi = x.astype(jnp.bfloat16)
    return hi, (x - hi.astype(jnp.float32)).astype(jnp.bfloat16)

def mm(a, b, dims=((1,), (0,)), passes=3):
    dot = functools.partial(lax.dot_general, dimension_numbers=(dims, ((), ())), preferred_element_type=jnp.float32)
    if passes == 6:
        return dot(a, b, precision=lax.Precision.HIGHEST)
    if passes == 1:
        return dot(a.astype(jnp.bfloat16), b.astype(jnp.bfloat16))
    ah, al = halves(a); bh, bl = halves(b)
    return dot(ah, bh) + (dot(ah, bl) + dot(al, bh))

NN=((1,),(0,)); NT=((1,),(1,)); TN=((0,),(0,))

def soap_kernel(passes, used_ref, g_ref, w_ref, m_ref, v_ref, l_ref, r_ref, ql_ref, qr_ref,
                nw_ref, nm_ref, nv_ref, nl_ref, nr_ref, nql_ref, nqr_ref, sa_ref):
    nb = g_ref.shape[0]
    p_rot, p_orth, p_chol = passes
    c1 = 1.0 - BETA_ONE**STEP
    c2 = 1.0 - BETA_TWO**STEP

    def one(i, carry):
        used = used_ref[pl.program_id(0) * nb + i] > 0
        g = jnp.where(used, g_ref[i], 0.0)
        ql = ql_ref[i]
        qr = qr_ref[i]
        gt = g.T
        nm = BETA_ONE * m_ref[i] + (1.0 - BETA_ONE) * g
        nm_ref[i] = nm
        qlt = ql.T
        side = mm(jnp.concatenate([g, nm], 0), qr, NN, p_rot)
        both = mm(qlt, jnp.concatenate([side[:TILE], side[TILE:]], 1), NN, p_rot)
        rotated, first = both[:, :TILE], both[:, TILE:]
        nv = BETA_TWO * v_ref[i] + (1.0 - BETA_TWO) * rotated * rotated
        nv_ref[i] = nv
        normed = first / c1 / (jnp.sqrt(nv / c2) + ADAM_EPSILON)
        step = mm(mm(ql, normed, NN, p_rot), qr, NT, p_rot)
        w = w_ref[i]
        nw_ref[i] = w - MATRIX_RATE * step - MATRIX_RATE * WEIGHT_DECAY * w
        nl = BETA_TWO * l_ref[i] + (1.0 - BETA_TWO) * mm(g, gt, NN, p_rot)
        nr = BETA_TWO * r_ref[i] + (1.0 - BETA_TWO) * mm(gt, g, NN, p_rot)
        nl_ref[i] = nl
        nr_ref[i] = nr
        for k, (stat, turn) in enumerate(((nl, ql), (nr, qr))):
            a = mm(stat, turn, NN, p_orth)
            at = a.T
            sa_ref[2 * i + k, :, :TILE] = mm(at, a, NN, p_orth)
            sa_ref[2 * i + k, :, TILE:] = at
        return carry

    lax.fori_loop(0, nb, one, 0, unroll=2)

    count = 2 * nb
    per = TILE // (2 * PANEL)
    rows = count // per * PANEL
    lane = lax.broadcasted_iota(jnp.int32, (rows, TILE), 1)
    start = lane // (2 * PANEL) * (2 * PANEL)
    sub = lax.broadcasted_iota(jnp.int32, (count // per, PANEL, TILE), 1)
    lane1 = lax.broadcasted_iota(jnp.int32, (PANEL, 2 * PANEL), 1)
    sub1 = lax.broadcasted_iota(jnp.int32, (PANEL, 2 * PANEL), 0)
    eye = (lane1[:, :PANEL] == sub1[:, :PANEL]).astype(jnp.float32)
    for p in range(TILE // PANEL):
        r0 = p * PANEL
        packs = []
        for q in range(count // per):
            pieces = []
            for k in range(per):
                pieces += [sa_ref[q * per + k, r0:r0 + PANEL, r0:r0 + PANEL], eye]
            packs.append(jnp.concatenate(pieces, 1)[None])
        x = jnp.concatenate(packs, 0)
        piv = jnp.ones_like(x)
        for j in range(PANEL):
            col = jnp.take_along_axis(x.reshape(rows, TILE), start + j, axis=1).reshape(x.shape)
            row = x[:, j:j + 1, :]
            pivot = col[:, j:j + 1, :]
            piv = jnp.where(sub == j, pivot, piv)
            if j < PANEL - 1:
                x = x - jnp.where(sub > j, col, 0.0) * (row * (1.0 / pivot))
        x = x * lax.rsqrt(piv)
        for q in range(count // per):
            for k in range(per):
                i = q * per + k
                wmat = x[q, :, 2 * PANEL * k + PANEL:2 * PANEL * (k + 1)]
                u = mm(wmat, sa_ref[i, r0:r0 + PANEL, :], NN, p_chol)
                sa_ref[i, r0:r0 + PANEL, TILE:] = u[:, TILE:]
                if p < TILE // PANEL - 1:
                    ut = u[:, :TILE].T
                    sa_ref[i, r0 + PANEL:, :] -= mm(ut[r0 + PANEL:, :], u, NN, p_chol)
    def fin(i, carry):
        nql_ref[i] = sa_ref[2 * i, :, TILE:].T
        nqr_ref[i] = sa_ref[2 * i + 1, :, TILE:].T
        return carry
    lax.fori_loop(0, nb, fin, 0)

def soap_all(used, g, w, m, v, l, r, ql, qr, nb=16, passes=(3, 3, 3)):
    s = g.shape[0]
    nb = min(nb, s)
    spec = pl.BlockSpec((nb, TILE, TILE), lambda i: (i, 0, 0))
    return pl.pallas_call(
        functools.partial(soap_kernel, passes),
        grid=(s // nb,),
        out_shape=[jax.ShapeDtypeStruct(g.shape, jnp.float32)] * 7,
        in_specs=[pl.BlockSpec(memory_space=pltpu.SMEM)] + [spec] * 8,
        out_specs=[spec] * 7,
        scratch_shapes=[pltpu.VMEM((2 * nb, TILE, 2 * TILE), jnp.float32)],
        compiler_params=pltpu.CompilerParams(vmem_limit_bytes=48 << 20),
        name="soap",
    )(used, g, w, m, v, l, r, ql, qr)


MESH = pl.DeviceIdType.MESH
ANY = pl.BlockSpec(memory_space=pl.ANY)


def chip_grid(device_count):
    if device_count == 16:
        return 4, 2, 2
    side = round(device_count ** (1 / 3))
    if side**3 == device_count:
        return side, side, side
    return 1, 1, device_count


def place(grid):
    zs, ys, xs = grid
    me = lax.axis_index("dp")
    return me // (ys * xs), lax.rem(me // xs, ys), lax.rem(me, xs)


def peers(grid):
    zs, ys, xs = grid
    z, y, x = place(grid)

    def device(zz, yy, xx):
        return {"dp": (zz * ys + yy) * xs + xx}

    return (
        lambda k: device(lax.rem(z + k, zs), y, x),
        lambda k: device(z, lax.rem(y + k, ys), x),
        lambda k: device(z, y, lax.rem(x + k, xs)),
    )


def greet(grid):
    barrier = pltpu.get_barrier_semaphore()
    count = 0
    for size, peer in zip(grid, peers(grid)):
        for k in range(1, size):
            pl.semaphore_signal(barrier, inc=1, device_id=peer(k), device_id_type=MESH)
            count += 1
    pl.semaphore_wait(barrier, count)


def remote(src, dst, send, recv, device):
    return pltpu.make_async_remote_copy(
        src_ref=src, dst_ref=dst, send_sem=send, recv_sem=recv, device_id=device, device_id_type=MESH
    )


def chunking(slots):
    half = slots // 2
    chunks = min(16, half)
    return half, chunks, half // chunks


def rs_kernel(grid, *refs):
    zs, ys, xs = grid
    n = 0
    in_ref, small_ref, out_ref, small_out_ref = refs[:4]
    (own0, own1, ra0, ra1, rb0, rb1, rc0, rc1, total, rs_z, rs_y, rs_x, load_sem,
     as0, as1, ar0, ar1, bs0, bs1, br0, br1, cs0, cs1, cr0, cr1,
     ssz, ssy, ssx, srz, sry, srx) = refs[4:]
    own, rec_a, rec_b, rec_c = (own0, own1), (ra0, ra1), (rb0, rb1), (rc0, rc1)
    a_send, a_recv, b_send, b_recv, c_send, c_recv = (as0, as1), (ar0, ar1), (bs0, bs1), (br0, br1), (cs0, cs1), (cr0, cr1)
    rec_s, s_send, s_recv = (rs_z, rs_y, rs_x), (ssz, ssy, ssx), (srz, sry, srx)

    z, y, x = place(grid)
    tos = peers(grid)
    to_z, to_y, to_x = tos
    slots = out_ref.shape[0]
    half, chunks, size = chunking(slots)
    first = ((xs, x, to_x), (ys, y, to_y))
    second = ((ys, y, to_y), (xs, x, to_x))

    def source(g, c, other):
        span = pl.ds(g * half + c * size, size)
        return in_ref.at[:, :, other, span] if g == 0 else in_ref.at[:, other, :, span]

    def load(g, c):
        return pltpu.make_async_copy(source(g, c, first[g][1]), own[g].at[c], load_sem.at[g, c])

    def send_a(g, c, k):
        count, mine, to = first[g]
        return remote(source(g, c, lax.rem(mine + k, count)), rec_a[g].at[c, k - 1],
                      a_send[g].at[c, k - 1], a_recv[g].at[c, k - 1], to(k))

    def send_b(g, c, k):
        count, mine, to = second[g]
        return remote(own[g].at[c, :, lax.rem(mine + k, count)], rec_b[g].at[c, k - 1],
                      b_send[g].at[c, k - 1], b_recv[g].at[c, k - 1], to(k))

    def send_c(g, c, k):
        return remote(own[g].at[c, lax.rem(z + k, zs), second[g][1]], rec_c[g].at[c, k - 1],
                      c_send[g].at[c, k - 1], c_recv[g].at[c, k - 1], to_z(k))

    def start_a(c):
        for g in range(2):
            for k in range(1, first[g][0]):
                send_a(g, c, k).start()

    def send_s(axis, k):
        return remote(total.at[2 - axis], rec_s[axis].at[k - 1],
                      s_send[axis].at[k - 1], s_recv[axis].at[k - 1], tos[axis](k))

    def small_start(axis):
        for k in range(1, grid[axis]):
            send_s(axis, k).start()

    def small_add(axis):
        value = total[2 - axis]
        for k in range(1, grid[axis]):
            send_s(axis, k).wait_recv()
            value += rec_s[axis][k - 1]
        return value

    for c in range(chunks):
        for g in range(2):
            load(g, c).start()
    total[0] = small_ref[...]
    greet(grid)
    small_start(2)
    start_a(0)
    if chunks > 1:
        start_a(1)
    total[1] = small_add(2)
    small_start(1)
    total[2] = small_add(1)
    small_start(0)

    def step_a(c):
        for g in range(2):
            load(g, c).wait()
            for k in range(1, first[g][0]):
                send_a(g, c, k).wait_recv()
        if c + 2 < chunks:
            start_a(c + 2)
        for g in range(2):
            n2 = second[g][0]

            def add(e, carry):
                a, b = e // n2, lax.rem(e, n2)
                value = own[g][c, a, b].astype(jnp.float32)
                for k in range(1, first[g][0]):
                    value += rec_a[g][c, k - 1, a, b].astype(jnp.float32)
                own[g][c, a, b] = value.astype(jnp.bfloat16)
                return carry

            lax.fori_loop(0, zs * n2, add, 0)
            for k in range(1, n2):
                send_b(g, c, k).start()

    def step_b(c):
        for g in range(2):
            n2, mine = second[g][0], second[g][1]
            for k in range(1, n2):
                send_b(g, c, k).wait_recv()

            def add(a, carry):
                value = own[g][c, a, mine].astype(jnp.float32)
                for k in range(1, n2):
                    value += rec_b[g][c, k - 1, a].astype(jnp.float32)
                own[g][c, a, mine] = value.astype(jnp.bfloat16)
                return carry

            lax.fori_loop(0, zs, add, 0)
            for k in range(1, zs):
                send_c(g, c, k).start()

    def step_c(c):
        for g in range(2):
            for k in range(1, zs):
                send_c(g, c, k).wait_recv()
            mine = second[g][1]

            def add(e, carry):
                value = own[g][c, z, mine, e].astype(jnp.float32)
                for k in range(1, zs):
                    value += rec_c[g][c, k - 1, e].astype(jnp.float32)
                out_ref[g * half + c * size + e] = value
                return carry

            lax.fori_loop(0, size, add, 0)

    for t in range(chunks + 2):
        if t < chunks:
            step_a(t)
        if 1 <= t <= chunks:
            step_b(t - 1)
        if t >= 2:
            step_c(t - 2)
    small_out_ref[...] = small_add(0)
    for axis in range(3):
        for k in range(1, grid[axis]):
            send_s(axis, k).wait_send()
    for c in range(chunks):
        for g in range(2):
            for k in range(1, first[g][0]):
                send_a(g, c, k).wait_send()
            for k in range(1, second[g][0]):
                send_b(g, c, k).wait_send()
            for k in range(1, zs):
                send_c(g, c, k).wait_send()


def some(shape):
    return tuple(max(1, s) for s in shape)


def reduce_to_owners(slot_grads, small, device_count):
    grid = chip_grid(device_count)
    zs, ys, xs = grid
    slots = slot_grads.shape[0] // device_count
    half, chunks, size = chunking(slots)
    block = (size, TILE, TILE)
    bf = jnp.bfloat16
    dma = pltpu.SemaphoreType.DMA
    firsts, seconds = (xs, ys), (ys, xs)
    scratch = (
        [pltpu.VMEM((chunks, zs, seconds[g]) + block, bf) for g in range(2)]
        + [pltpu.VMEM(some((chunks, firsts[g] - 1, zs, seconds[g])) + block, bf) for g in range(2)]
        + [pltpu.VMEM(some((chunks, seconds[g] - 1, zs)) + block, bf) for g in range(2)]
        + [pltpu.VMEM(some((chunks, zs - 1)) + block, bf) for g in range(2)]
        + [pltpu.VMEM((3,) + small.shape, jnp.float32)]
        + [pltpu.VMEM((max(1, n - 1),) + small.shape, jnp.float32) for n in grid]
        + [dma((2, chunks))]
        + [dma(some((chunks, firsts[g] - 1))) for g in range(2)] * 2
        + [dma(some((chunks, seconds[g] - 1))) for g in range(2)] * 2
        + [dma(some((chunks, zs - 1))) for g in range(2)] * 2
        + [dma((max(1, n - 1),)) for n in grid] * 2
    )
    return pl.pallas_call(
        functools.partial(rs_kernel, grid),
        out_shape=[jax.ShapeDtypeStruct((slots, TILE, TILE), jnp.float32), jax.ShapeDtypeStruct(small.shape, jnp.float32)],
        in_specs=[ANY, pl.BlockSpec(memory_space=pltpu.VMEM)],
        out_specs=[pl.BlockSpec(memory_space=pltpu.VMEM)] * 2,
        scratch_shapes=scratch,
        compiler_params=pltpu.CompilerParams(collective_id=1, has_side_effects=True, vmem_limit_bytes=48 << 20),
        name="reduce_to_owners",
    )(slot_grads.reshape(zs, ys, xs, slots, TILE, TILE), small)


def ag_kernel(grid, own_ref, small_ref, out_ref, small_out_ref,
              load_sem, z_send, z_recv, b_send0, b_send1, b_recv0, b_recv1, a_send0, a_send1, a_recv0, a_recv1,
              s_load, ssz, ssy, ssx, srz, sry, srx):
    zs, ys, xs = grid
    z, y, x = place(grid)
    tos = peers(grid)
    to_z, to_y, to_x = tos
    slots = own_ref.shape[0]
    half, chunks, size = chunking(slots)
    first = ((xs, to_x), (ys, to_y))
    second = ((ys, to_y), (xs, to_x))
    b_send, b_recv, a_send, a_recv = (b_send0, b_send1), (b_recv0, b_recv1), (a_send0, a_send1), (a_recv0, a_recv1)
    s_send, s_recv = (ssz, ssy, ssx), (srz, sry, srx)

    def span(g, c):
        return pl.ds(g * half + c * size, size)

    def send_z(g, c, k):
        return remote(own_ref.at[span(g, c)], out_ref.at[z, y, x, span(g, c)],
                      z_send.at[g, c, k - 1], z_recv.at[g, c, k - 1], to_z(k))

    def send_b(g, c, k):
        part = out_ref.at[:, y, x, span(g, c)]
        return remote(part, part, b_send[g].at[c, k - 1], b_recv[g].at[c, k - 1], second[g][1](k))

    def send_a(g, c, k):
        part = out_ref.at[:, :, x, span(g, c)] if g == 0 else out_ref.at[:, y, :, span(g, c)]
        return remote(part, part, a_send[g].at[c, k - 1], a_recv[g].at[c, k - 1], first[g][1](k))

    def send_s(axis, k):
        if axis == 0:
            source, target = small_ref, small_out_ref.at[z, y, x]
        else:
            source = target = small_out_ref.at[:, y, x] if axis == 1 else small_out_ref.at[:, :, x]
        return remote(source, target, s_send[axis].at[k - 1], s_recv[axis].at[k - 1], tos[axis](k))

    keep = pltpu.make_async_copy(own_ref, out_ref.at[z, y, x], load_sem)
    keep_small = pltpu.make_async_copy(small_ref, small_out_ref.at[z, y, x], s_load)
    keep.start()
    keep_small.start()
    greet(grid)

    for k in range(1, grid[0]):
        send_s(0, k).start()
    def start_z(c):
        for g in range(2):
            for k in range(1, zs):
                send_z(g, c, k).start()

    def small_wait(axis):
        for k in range(1, grid[axis]):
            send_s(axis, k).wait_recv()

    def small_start(axis):
        for k in range(1, grid[axis]):
            send_s(axis, k).start()

    start_z(0)
    for t in range(chunks + 1):
        if t < chunks:
            for g in range(2):
                for k in range(1, zs):
                    send_z(g, t, k).wait_recv()
            if t == 0:
                keep.wait()
                keep_small.wait()
                small_wait(0)
                small_start(1)
            if t + 1 < chunks:
                start_z(t + 1)
            for g in range(2):
                for k in range(1, second[g][0]):
                    send_b(g, t, k).start()
        if t >= 1:
            for g in range(2):
                for k in range(1, second[g][0]):
                    send_b(g, t - 1, k).wait_recv()
                for k in range(1, first[g][0]):
                    send_a(g, t - 1, k).start()
        if t == 1:
            small_wait(1)
            small_start(2)
    small_wait(2)
    for c in range(chunks):
        for g in range(2):
            for k in range(1, first[g][0]):
                send_a(g, c, k).wait_recv()
    for axis in range(3):
        for k in range(1, grid[axis]):
            send_s(axis, k).wait_send()
    for c in range(chunks):
        for g in range(2):
            for k in range(1, zs):
                send_z(g, c, k).wait_send()
            for k in range(1, second[g][0]):
                send_b(g, c, k).wait_send()
            for k in range(1, first[g][0]):
                send_a(g, c, k).wait_send()


def gather_all(own, small, device_count):
    grid = chip_grid(device_count)
    zs, ys, xs = grid
    slots = own.shape[0]
    half, chunks, size = chunking(slots)
    dma = pltpu.SemaphoreType.DMA
    firsts, seconds = (xs, ys), (ys, xs)
    scratch = (
        [dma, dma(some((2, chunks, zs - 1))), dma(some((2, chunks, zs - 1)))]
        + [dma(some((chunks, seconds[g] - 1))) for g in range(2)] * 2
        + [dma(some((chunks, firsts[g] - 1))) for g in range(2)] * 2
        + [dma]
        + [dma((max(1, n - 1),)) for n in grid] * 2
    )
    blocks, smalls = pl.pallas_call(
        functools.partial(ag_kernel, grid),
        out_shape=[jax.ShapeDtypeStruct(grid + own.shape, own.dtype), jax.ShapeDtypeStruct(grid + small.shape, small.dtype)],
        in_specs=[pl.BlockSpec(memory_space=pltpu.VMEM)] * 2,
        out_specs=[ANY, ANY],
        scratch_shapes=scratch,
        compiler_params=pltpu.CompilerParams(collective_id=2, has_side_effects=True),
        name="gather_all",
    )(own, small)
    return blocks.reshape((-1,) + own.shape[1:]), smalls.reshape((-1,) + small.shape)


def move_tiles_kernel(shapes, unpacking, slots_ref, *refs):
    count = len(shapes)
    if unpacking:
        packed, mats, held, sems = refs[0], refs[1:1 + count], refs[1 + count:-1], refs[-1]
    else:
        mats, packed, held, sems = refs[:count], refs[count], refs[count + 1:-1], refs[-1]

    def whole(index):
        if unpacking:
            return pltpu.make_async_copy(held[index], mats[index], sems.at[1, index])
        return pltpu.make_async_copy(mats[index], held[index], sems.at[0, index])

    def tiles(index, offset):
        height, breadth = shapes[index]
        down, across = height // TILE, breadth // TILE
        stage = 0 if unpacking else 1

        def start(i, carry):
            for j in range(across):
                tile = held[index].at[pl.ds(pl.multiple_of(i * TILE, TILE), TILE), j * TILE:(j + 1) * TILE]
                slot = packed.at[slots_ref[offset + i * across + j]]
                ends = (slot, tile) if unpacking else (tile, slot)
                pltpu.make_async_copy(*ends, sems.at[stage, index]).start()
            return carry

        lax.fori_loop(0, down, start, 0)
        return offset + down * across

    def wait_tiles(index):
        stage = 0 if unpacking else 1
        pltpu.make_async_copy(held[index], held[index], sems.at[stage, index]).wait()

    offset = 0
    if unpacking:
        for index in range(count):
            offset = tiles(index, offset)
        for index in range(count):
            wait_tiles(index)
            whole(index).start()
        for index in range(count):
            whole(index).wait()
    else:
        for index in range(count):
            whole(index).start()
        for index in range(count):
            whole(index).wait()
            offset = tiles(index, offset)
        for index in range(count):
            wait_tiles(index)


def unpack_tiles(packed, slots, shapes):
    return pl.pallas_call(
        functools.partial(move_tiles_kernel, shapes, True),
        out_shape=[jax.ShapeDtypeStruct(s, packed.dtype) for s in shapes],
        in_specs=[pl.BlockSpec(memory_space=pltpu.SMEM), ANY],
        out_specs=[ANY] * len(shapes),
        scratch_shapes=[pltpu.VMEM(s, packed.dtype) for s in shapes] + [pltpu.SemaphoreType.DMA((2, len(shapes)))],
        compiler_params=pltpu.CompilerParams(vmem_limit_bytes=24 << 20),
        name="unpack_tiles",
    )(slots, packed)


def pack_tiles(mats, slots, slot_count):
    return pl.pallas_call(
        functools.partial(move_tiles_kernel, [m.shape for m in mats], False),
        out_shape=jax.ShapeDtypeStruct((slot_count, TILE, TILE), mats[0].dtype),
        in_specs=[pl.BlockSpec(memory_space=pltpu.SMEM)] + [ANY] * len(mats),
        out_specs=ANY,
        scratch_shapes=[pltpu.VMEM(m.shape, m.dtype) for m in mats] + [pltpu.SemaphoreType.DMA((2, len(mats)))],
        compiler_params=pltpu.CompilerParams(vmem_limit_bytes=24 << 20),
        name="pack_tiles",
    )(slots, *mats)


def adam_vector(grad_value, value, first, second):
    new_first = BETA_ONE * first + (1.0 - BETA_ONE) * grad_value
    new_second = BETA_TWO * second + (1.0 - BETA_TWO) * grad_value * grad_value
    correct_one = 1.0 - BETA_ONE**STEP
    correct_two = 1.0 - BETA_TWO**STEP
    updated = value - VECTOR_RATE * (new_first / correct_one) / (
        jnp.sqrt(new_second / correct_two) + ADAM_EPSILON
    )
    return (new_first, new_second, updated)


def local(
    source_tokens,
    target_tokens,
    target_cotangent,
    retrieved,
    kept_mask,
    owner_slots,
    master,
    first_moment,
    second_moment,
    left_stats,
    right_stats,
    left_basis,
    right_basis,
    shared_vectors,
    shared_first,
    shared_second,
    split_vectors,
    split_first,
    split_second,
):
    tensor_count = lax.axis_size("tensor")
    device_count = lax.axis_size("dp")
    model_width = source_tokens.shape[1]
    tile_size = master.shape[2]
    hidden_width = (split_vectors.shape[1] - 3) * model_width
    half_width = model_width // tensor_count
    hidden_half = hidden_width // tensor_count
    qblocks = retrieved.shape[0]
    per_owner = retrieved.shape[1] // device_count
    me = lax.axis_index("dp")
    vectors = jnp.concatenate([shared_vectors, split_vectors[0]], 0)
    vector_count, vector_width = vectors.shape
    padded = -(-vector_count // 8) * 8
    small = jnp.concatenate(
        [
            jnp.pad(vectors, ((0, padded - vector_count), (0, TILE - vector_width))),
            retrieved.astype(jnp.float32).reshape(-1, TILE),
        ],
        0,
    )
    gathered, smalls = gather_all(master[0].astype(jnp.bfloat16), small, device_count)
    whole = (
        smalls[:, :vector_count, :vector_width]
        .transpose(1, 0, 2)
        .reshape(vector_count, model_width)
        .astype(jnp.bfloat16)
    )
    shared_count = shared_vectors.shape[0]
    shared_whole, split_whole = whole[:shared_count], whole[shared_count:]
    shapes = [s[1:] for s in matrix_list(model_width, hidden_width, tensor_count)]
    names = [s[0] for s in matrix_list(model_width, hidden_width, tensor_count)]
    weights = dict(zip(names, unpack_tiles(gathered, owner_slots, shapes)))
    shared = shared_whole.astype(jnp.float32)
    biases = split_biases(split_whole.astype(jnp.float32).reshape(-1), half_width, hidden_half)
    zero_half = jnp.zeros((half_width,), jnp.float32)
    source_float = source_tokens.astype(jnp.float32)
    enc_bias = jnp.concatenate([biases["enc_q"], zero_half, biases["enc_v"]])
    enc_branch, enc_saved = self_forward(
        source_tokens, weights["enc_qkv"], enc_bias, weights["enc_out"], False
    )
    pre_one = source_float + tensor_sum(enc_branch) + shared[0]
    hidden_one, norm_one_back = jax.vjp(layer_norm, pre_one, shared[1], shared[2])
    hidden_low = hidden_one.astype(jnp.bfloat16)
    enc_feed, enc_feed_saved = ffn_forward(
        hidden_low, weights["enc_up"], biases["enc_up"], weights["enc_down"]
    )
    pre_two = hidden_one + tensor_sum(enc_feed) + shared[3]
    encoder_states, norm_two_back = jax.vjp(layer_norm, pre_two, shared[4], shared[5])
    start_row = jnp.argmax(kept_mask)
    stored = lax.dynamic_slice_in_dim(encoder_states.astype(jnp.bfloat16), start_row, KEEP, 0)
    wanted = (
        smalls[:, padded:].reshape(device_count, qblocks, device_count, per_owner)[:, :, me]
        .transpose(1, 0, 2)
        .astype(jnp.int32)
        - KEEP * me
    )
    served = jnp.take(stored, wanted, axis=0)
    retrieved_entries = lax.all_to_all(
        served, "dp", split_axis=1, concat_axis=1, tiled=True
    ).reshape(qblocks, -1, model_width)
    target_float = target_tokens.astype(jnp.float32)
    dec_bias = jnp.concatenate([biases["dec_q"], zero_half, biases["dec_v"]])
    dec_branch, dec_saved = self_forward(
        target_tokens, weights["dec_qkv"], dec_bias, weights["dec_out"], True
    )
    pre_three = target_float + tensor_sum(dec_branch) + shared[6]
    first_dec, norm_three_back = jax.vjp(layer_norm, pre_three, shared[7], shared[8])
    first_low = first_dec.astype(jnp.bfloat16)
    cross_branch, cross_saved = cross_forward(
        first_low.reshape(qblocks, -1, model_width),
        retrieved_entries,
        weights["crs_q"],
        biases["crs_q"],
        weights["crs_kv"],
        biases["crs_v"],
        weights["crs_out"],
    )
    pre_four = first_dec + tensor_sum(cross_branch) + shared[9]
    second_dec, norm_four_back = jax.vjp(layer_norm, pre_four, shared[10], shared[11])
    second_low = second_dec.astype(jnp.bfloat16)
    dec_feed, dec_feed_saved = ffn_forward(
        second_low, weights["dec_up"], biases["dec_up"], weights["dec_down"]
    )
    pre_five = second_dec + tensor_sum(dec_feed) + shared[12]
    decoder_states, norm_five_back = jax.vjp(layer_norm, pre_five, shared[13], shared[14])
    grad_five, grad_gain_five, grad_shift_five = norm_five_back(
        target_cotangent.astype(jnp.float32)
    )
    grad_dec_up, grad_dec_upb, grad_dec_down, part_second = ffn_backward(
        grad_five, second_low, dec_feed_saved, weights["dec_up"], weights["dec_down"]
    )
    grad_second = grad_five + tensor_back(part_second)
    grad_four, grad_gain_four, grad_shift_four = norm_four_back(grad_second)
    grad_crs_q, grad_crs_qb, grad_crs_kv, grad_crs_vb, grad_crs_out, part_first, part_fetched = (
        cross_backward(
            grad_four,
            first_low,
            retrieved_entries,
            cross_saved,
            weights["crs_q"],
            weights["crs_kv"],
            weights["crs_out"],
        )
    )
    summed_first, summed_fetched = tensor_back((part_first, part_fetched))
    grad_first = grad_four + summed_first
    grad_three, grad_gain_three, grad_shift_three = norm_three_back(grad_first)
    grad_dec_qkv, grad_dec_qb, grad_dec_vb, grad_dec_out, part_target = self_backward(
        grad_three, target_tokens, dec_saved, weights["dec_qkv"], weights["dec_out"], True
    )
    target_grad = grad_three + tensor_back(part_target)
    fetched_low = summed_fetched.astype(jnp.bfloat16)
    returned = lax.all_to_all(
        fetched_low.reshape(qblocks, device_count, per_owner, model_width),
        "dp",
        split_axis=1,
        concat_axis=1,
        tiled=True,
    )
    matches = (wanted.reshape(1, -1) == lax.broadcasted_iota(jnp.int32, (KEEP, 1), 0)).astype(
        jnp.bfloat16
    )
    stored_grad = project(matches, returned.reshape(-1, model_width))
    grad_states = lax.dynamic_update_slice_in_dim(
        jnp.zeros_like(encoder_states), stored_grad, start_row, 0
    )
    grad_two, grad_gain_two, grad_shift_two = norm_two_back(grad_states)
    grad_enc_up, grad_enc_upb, grad_enc_down, part_hidden = ffn_backward(
        grad_two, hidden_low, enc_feed_saved, weights["enc_up"], weights["enc_down"]
    )
    grad_hidden = grad_two + tensor_back(part_hidden)
    grad_one, grad_gain_one, grad_shift_one = norm_one_back(grad_hidden)
    grad_enc_qkv, grad_enc_qb, grad_enc_vb, grad_enc_out, part_source = self_backward(
        grad_one, source_tokens, enc_saved, weights["enc_qkv"], weights["enc_out"], False
    )
    source_grad = grad_one + tensor_back(part_source)
    shared_grad = jnp.stack(
        [
            jnp.sum(grad_one, 0),
            grad_gain_one,
            grad_shift_one,
            jnp.sum(grad_two, 0),
            grad_gain_two,
            grad_shift_two,
            jnp.sum(grad_three, 0),
            grad_gain_three,
            grad_shift_three,
            jnp.sum(grad_four, 0),
            grad_gain_four,
            grad_shift_four,
            jnp.sum(grad_five, 0),
            grad_gain_five,
            grad_shift_five,
        ]
    )
    split_grad = jnp.concatenate(
        [
            grad_enc_qb,
            grad_enc_vb,
            grad_enc_upb,
            grad_dec_qb,
            grad_dec_vb,
            grad_crs_qb,
            grad_crs_vb,
            grad_dec_upb,
        ]
    ).reshape(-1, model_width)
    matrix_grads = {
        "enc_qkv": grad_enc_qkv,
        "enc_out": grad_enc_out,
        "enc_up": grad_enc_up,
        "enc_down": grad_enc_down,
        "dec_qkv": grad_dec_qkv,
        "dec_out": grad_dec_out,
        "crs_q": grad_crs_q,
        "crs_kv": grad_crs_kv,
        "crs_out": grad_crs_out,
        "dec_up": grad_dec_up,
        "dec_down": grad_dec_down,
    }
    slot_grads = pack_tiles(
        [matrix_grads[name].astype(jnp.bfloat16) for name in names], owner_slots, gathered.shape[0]
    )
    vector_grads = jnp.pad(
        jnp.concatenate([shared_grad, split_grad], 0), ((0, padded - vector_count), (0, 0))
    )
    owned_grads, vector_sums = reduce_to_owners(slot_grads, vector_grads, device_count)
    vector_owned = lax.dynamic_slice_in_dim(vector_sums, me * vector_width, vector_width, 1)
    shared_owned = vector_owned[:shared_count]
    split_owned = vector_owned[shared_count:vector_count]
    owned_slots = me * owned_grads.shape[0] + lax.broadcasted_iota(
        jnp.int32, (owned_grads.shape[0], 1), 0
    )
    used = jnp.any(owned_slots == owner_slots[None, :], 1).astype(jnp.int32)
    results = soap_all(
        used,
        owned_grads,
        master[0],
        first_moment[0],
        second_moment[0],
        left_stats[0],
        right_stats[0],
        left_basis[0],
        right_basis[0],
    )
    new_master, new_first, new_second, new_left, new_right, new_lbasis, new_rbasis = results
    shared_new_first, shared_new_second, shared_updated = adam_vector(
        shared_owned, shared_vectors, shared_first, shared_second
    )
    split_new_first, split_new_second, split_updated = adam_vector(
        split_owned, split_vectors[0], split_first[0], split_second[0]
    )
    return (
        encoder_states,
        decoder_states,
        source_grad,
        target_grad,
        new_master[None],
        new_first[None],
        new_second[None],
        new_left[None],
        new_right[None],
        new_lbasis[None],
        new_rbasis[None],
        shared_new_first,
        shared_new_second,
        shared_updated,
        split_new_first[None],
        split_new_second[None],
        split_updated[None],
    )


def solution(mesh):
    placed = (
        P("dp", None),
        P("dp", None),
        P("dp", None),
        P("dp", None),
        P("dp"),
        P(),
        P("tensor", "dp", None, None),
        P("tensor", "dp", None, None),
        P("tensor", "dp", None, None),
        P("tensor", "dp", None, None),
        P("tensor", "dp", None, None),
        P("tensor", "dp", None, None),
        P("tensor", "dp", None, None),
        P(None, "dp"),
        P(None, "dp"),
        P(None, "dp"),
        P("tensor", None, "dp"),
        P("tensor", None, "dp"),
        P("tensor", None, "dp"),
    )
    return jax.shard_map(
        local,
        mesh=mesh,
        in_specs=placed,
        out_specs=(
            P("dp", None),
            P("dp", None),
            P("dp", None),
            P("dp", None),
            P("tensor", "dp", None, None),
            P("tensor", "dp", None, None),
            P("tensor", "dp", None, None),
            P("tensor", "dp", None, None),
            P("tensor", "dp", None, None),
            P("tensor", "dp", None, None),
            P("tensor", "dp", None, None),
            P(None, "dp"),
            P(None, "dp"),
            P(None, "dp"),
            P("tensor", None, "dp"),
            P("tensor", None, "dp"),
            P("tensor", None, "dp"),
        ),
        check_vma=False,
    )
```

```python
import functools
from functools import partial

import jax
import jax.numpy as jnp
from jax import lax
from jax.experimental import pallas as pl
from jax.experimental.pallas import tpu as pltpu
from jax.sharding import PartitionSpec as P

HD = 64
KEEP = 512
STEP = 10


BETA_ONE = 0.9
BETA_TWO = 0.95
ADAM_EPSILON = 1e-08
MATRIX_RATE = 0.1
VECTOR_RATE = 0.5
WEIGHT_DECAY = 0.01
NORM_EPSILON = 1e-05
TILE = 128
PANEL = 32
ROWS = 256
KEYS = 256
PAIR = 2 * HD
NN = ((1,), (0,))
NT = ((1,), (1,))
F32 = jnp.float32
BF16 = jnp.bfloat16
MESH = pl.DeviceIdType.MESH
ANY = pl.BlockSpec(memory_space=pl.ANY)


def matrix_list(model_width, hidden_width, tensor_count):
    half_width = model_width // tensor_count
    hidden_half = hidden_width // tensor_count
    return [
        ("enc_qkv", model_width, 3 * half_width),
        ("enc_out", half_width, model_width),
        ("enc_up", model_width, hidden_half),
        ("enc_down", hidden_half, model_width),
        ("dec_qkv", model_width, 3 * half_width),
        ("dec_out", half_width, model_width),
        ("crs_q", model_width, half_width),
        ("crs_kv", model_width, 2 * half_width),
        ("crs_out", half_width, model_width),
        ("dec_up", model_width, hidden_half),
        ("dec_down", hidden_half, model_width),
    ]


def halves(x):
    high = x.astype(BF16)
    return high, (x - high.astype(F32)).astype(BF16)


def mm(a, b, dims=NN):
    ah, al = halves(a)
    bh, bl = halves(b)
    return times(jnp.concatenate([ah, ah, al], 1), jnp.concatenate([bh, bl, bh], dims[1][0]), dims)


def chip_grid(device_count):
    if device_count == 16:
        return 4, 2, 2
    side = round(device_count ** (1 / 3))
    if side**3 == device_count:
        return side, side, side
    return 1, 1, device_count


def place(grid):
    zs, ys, xs = grid
    me = lax.axis_index("dp")
    return me // (ys * xs), lax.rem(me // xs, ys), lax.rem(me, xs)


def peers(grid):
    zs, ys, xs = grid
    z, y, x = place(grid)

    def device(zz, yy, xx):
        return {"dp": (zz * ys + yy) * xs + xx}

    return (
        lambda k: device(lax.rem(z + k, zs), y, x),
        lambda k: device(z, lax.rem(y + k, ys), x),
        lambda k: device(z, y, lax.rem(x + k, xs)),
    )


def greet(grid):
    barrier = pltpu.get_barrier_semaphore()
    count = 0
    for size, peer in zip(grid, peers(grid)):
        for k in range(1, size):
            pl.semaphore_signal(barrier, inc=1, device_id=peer(k), device_id_type=MESH)
            count += 1
    pl.semaphore_wait(barrier, count)


def remote(src, dst, send, recv, device):
    return pltpu.make_async_remote_copy(
        src_ref=src, dst_ref=dst, send_sem=send, recv_sem=recv, device_id=device, device_id_type=MESH
    )


def chunking(slots):
    half = slots // 2
    chunks = min(16, half)
    return half, chunks, half // chunks


def owner_kernel(grid, *refs):
    zs, ys, xs = grid
    used_ref, in_ref, small_ref = refs[:3]
    state_in, state_out, small_out_ref, work_out_ref = refs[3:10], refs[10:17], refs[17], refs[18]
    state, rest = refs[19:26], refs[26:]
    (own0, own1, ra0, ra1, rb0, rb1, rc0, rc1, total, rs_z, rs_y, rs_x, work, load_sem,
     as0, as1, ar0, ar1, bs0, bs1, br0, br1, cs0, cs1, cr0, cr1,
     ssz, ssy, ssx, srz, sry, srx, state_sem) = rest
    own, rec_a, rec_b, rec_c = (own0, own1), (ra0, ra1), (rb0, rb1), (rc0, rc1)
    a_send, a_recv, b_send, b_recv, c_send, c_recv = (as0, as1), (ar0, ar1), (bs0, bs1), (br0, br1), (cs0, cs1), (cr0, cr1)
    rec_s, s_send, s_recv = (rs_z, rs_y, rs_x), (ssz, ssy, ssx), (srz, sry, srx)

    z, y, x = place(grid)
    tos = peers(grid)
    to_z, to_y, to_x = tos
    slots = state[0].shape[0]
    half = slots // 2
    first = ((xs, x, to_x), (ys, y, to_y))
    second = ((ys, y, to_y), (xs, x, to_x))

    def source(g, c, other):
        slot = g * half + c
        return in_ref.at[:, :, other, slot] if g == 0 else in_ref.at[:, other, :, slot]

    def load(g, c):
        return pltpu.make_async_copy(source(g, c, first[g][1]), own[g].at[c], load_sem.at[g, c])

    def send_a(g, c, k):
        count, mine, to = first[g]
        return remote(source(g, c, lax.rem(mine + k, count)), rec_a[g].at[c, k - 1],
                      a_send[g].at[c, k - 1], a_recv[g].at[c, k - 1], to(k))

    def send_b(g, c, k):
        count, mine, to = second[g]
        return remote(own[g].at[c, :, lax.rem(mine + k, count)], rec_b[g].at[c, k - 1],
                      b_send[g].at[c, k - 1], b_recv[g].at[c, k - 1], to(k))

    def send_c(g, c, k):
        return remote(own[g].at[c, lax.rem(z + k, zs), second[g][1]], rec_c[g].at[c, k - 1],
                      c_send[g].at[c, k - 1], c_recv[g].at[c, k - 1], to_z(k))

    def start_a(c):
        for g in range(2):
            for k in range(1, first[g][0]):
                send_a(g, c, k).start()

    def send_s(axis, k):
        return remote(total.at[2 - axis], rec_s[axis].at[k - 1],
                      s_send[axis].at[k - 1], s_recv[axis].at[k - 1], tos[axis](k))

    def small_start(axis):
        for k in range(1, grid[axis]):
            send_s(axis, k).start()

    def small_add(axis):
        value = total[2 - axis]
        for k in range(1, grid[axis]):
            send_s(axis, k).wait_recv()
            value += rec_s[axis][k - 1]
        return value

    def each(count, action):
        def go(c, carry):
            action(c)
            return carry

        lax.fori_loop(0, count, go, 0)

    def load_all(c):
        for g in range(2):
            load(g, c).start()

    each(half, load_all)
    for i in range(7):
        pltpu.make_async_copy(state_in[i], state[i], state_sem.at[0, i]).start()
    total[0] = small_ref[...]
    greet(grid)
    small_start(2)
    start_a(0)
    total[1] = small_add(2)
    small_start(1)
    total[2] = small_add(1)
    small_start(0)
    for i in range(7):
        pltpu.make_async_copy(state_in[i], state[i], state_sem.at[0, i]).wait()

    def step_a(c):
        for g in range(2):
            load(g, c).wait()
            for k in range(1, first[g][0]):
                send_a(g, c, k).wait_recv()

        @pl.when(c + 1 < half)
        def _():
            start_a(c + 1)

        for g in range(2):
            n2 = second[g][0]

            def add(e, carry, g=g, n2=n2):
                a, b = e // n2, lax.rem(e, n2)
                value = own[g][c, a, b].astype(F32)
                for k in range(1, first[g][0]):
                    value += rec_a[g][c, k - 1, a, b].astype(F32)
                own[g][c, a, b] = value.astype(BF16)
                return carry

            lax.fori_loop(0, zs * n2, add, 0)
            for k in range(1, n2):
                send_b(g, c, k).start()

    def step_b(c):
        for g in range(2):
            n2, mine = second[g][0], second[g][1]
            for k in range(1, n2):
                send_b(g, c, k).wait_recv()

            def add(a, carry, g=g, n2=n2, mine=mine):
                value = own[g][c, a, mine].astype(F32)
                for k in range(1, n2):
                    value += rec_b[g][c, k - 1, a].astype(F32)
                own[g][c, a, mine] = value.astype(BF16)
                return carry

            lax.fori_loop(0, zs, add, 0)
            for k in range(1, zs):
                send_c(g, c, k).start()

    def step_c(c):
        batch = lax.rem(c // 4, 2)
        for g in range(2):
            for k in range(1, zs):
                send_c(g, c, k).wait_recv()
        for g in range(2):
            value = own[g][c, z, second[g][1]].astype(F32)
            for k in range(1, zs):
                value += rec_c[g][c, k - 1].astype(F32)
            slot = g * half + c
            value = jnp.where(used_ref[slot] > 0, value, 0.0)
            soap_products(value, slot, state, work, batch, 2 * (4 * g + lax.rem(c, 4)))

    def finish(b):
        batch = lax.rem(b, 2)
        place_bases(work, batch, state[5], state[6], 4 * b)
        emit(b)

    def emit(b):
        for g in range(2):
            span = pl.ds(g * half + 4 * b, 4)
            for i in range(7):
                pltpu.make_async_copy(state[i].at[span], state_out[i].at[span], state_sem.at[1, i]).start()

    def round_of(r, carry):
        for s in range(4):
            t = 4 * r + s

            @pl.when(t < half)
            def _(t=t):
                step_a(t)

            @pl.when((t >= 1) & (t <= half))
            def _(t=t):
                step_b(t - 1)

            @pl.when((t >= 2) & (t < half + 2))
            def _(t=t):
                step_c(t - 2)

            if s >= 1:

                @pl.when((r >= 1) & (r < half // 4))
                def _(s=s):
                    b = r - 1
                    for p in ((0,), (1,), (2, 3))[s - 1]:
                        panel_step(work, lax.rem(b, 2), p)
                    if s == 3:
                        finish(b)

        return carry

    lax.fori_loop(0, half // 4 + 1, round_of, 0)
    emit(half // 4 - 1)
    work_out_ref[...] = work[(half // 4 - 1) % 2]
    small_out_ref[...] = small_add(0)
    for axis in range(3):
        for k in range(1, grid[axis]):
            send_s(axis, k).wait_send()

    def end(c):
        for g in range(2):
            for k in range(1, first[g][0]):
                send_a(g, c, k).wait_send()
            for k in range(1, second[g][0]):
                send_b(g, c, k).wait_send()
            for k in range(1, zs):
                send_c(g, c, k).wait_send()

    each(half, end)
    for i in range(7):
        pltpu.make_async_copy(state[i], state_out[i], state_sem.at[1, i]).wait()


def place_bases(work, batch, left_ref, right_ref, at):
    half = left_ref.shape[0] // 2
    for g in range(2):
        for e in range(4):
            left_ref[g * half + at + e] = work[batch, 2 * (4 * g + e), :, TILE:].T
            right_ref[g * half + at + e] = work[batch, 2 * (4 * g + e) + 1, :, TILE:].T


def last_bases_kernel(work_ref, *refs):
    state_in, state_out, state, work, sems = refs[:7], refs[7:14], refs[14:21], refs[21], refs[22]
    half = state[0].shape[0] // 2

    def copy_in(i):
        return pltpu.make_async_copy(state_in[i], state[i], sems.at[0, i])

    def copy_out(i):
        return pltpu.make_async_copy(state[i], state_out[i], sems.at[1, i])

    for i in range(7):
        copy_in(i).start()
    work[0] = work_ref[...]
    panel_step(work, 0, 0)
    for i in range(7):
        copy_in(i).wait()
        if i < 5:
            copy_out(i).start()
    for p in range(1, TILE // PANEL):
        panel_step(work, 0, p)
    place_bases(work, 0, state[5], state[6], half - 4)
    for i in range(5, 7):
        copy_out(i).start()
    for i in range(7):
        copy_out(i).wait()


def last_bases(work, state):
    whole = state[0].shape
    return pl.pallas_call(
        last_bases_kernel,
        out_shape=[jax.ShapeDtypeStruct(whole, F32)] * 7,
        in_specs=[pl.BlockSpec(memory_space=pltpu.VMEM)] + [ANY] * 7,
        out_specs=[ANY] * 7,
        scratch_shapes=[pltpu.VMEM(whole, F32)] * 7
        + [pltpu.VMEM((1,) + work.shape, F32), pltpu.SemaphoreType.DMA((2, 7))],
        compiler_params=pltpu.CompilerParams(vmem_limit_bytes=56 << 20),
        name="last_bases",
    )(work, *state)


def soap_products(g, i, state, work, batch, at):
    w_ref, m_ref, v_ref, l_ref, r_ref, ql_ref, qr_ref = state
    c1 = 1.0 - BETA_ONE**STEP
    c2 = 1.0 - BETA_TWO**STEP
    ql = ql_ref[i]
    qr = qr_ref[i]
    gt = g.T
    nm = BETA_ONE * m_ref[i] + (1.0 - BETA_ONE) * g
    m_ref[i] = nm
    side = mm(jnp.concatenate([g, nm], 0), qr)
    both = mm(ql.T, jnp.concatenate([side[:TILE], side[TILE:]], 1))
    rotated, rotated_first = both[:, :TILE], both[:, TILE:]
    nv = BETA_TWO * v_ref[i] + (1.0 - BETA_TWO) * rotated * rotated
    v_ref[i] = nv
    normed = rotated_first / c1 / (jnp.sqrt(nv / c2) + ADAM_EPSILON)
    step = mm(mm(ql, normed), qr, NT)
    w = w_ref[i]
    w_ref[i] = w - MATRIX_RATE * step - MATRIX_RATE * WEIGHT_DECAY * w
    for k, (ref, turn, left, right) in enumerate(((l_ref, ql, g, gt), (r_ref, qr, gt, g))):
        stat = BETA_TWO * ref[i] + (1.0 - BETA_TWO) * mm(left, right)
        ref[i] = stat
        a = mm(stat, turn)
        at_turned = a.T
        work[batch, at + k, :, :TILE] = mm(at_turned, a)
        work[batch, at + k, :, TILE:] = at_turned


def panel_step(work, batch, p):
    count = work.shape[1]
    per = TILE // (2 * PANEL)
    r0 = p * PANEL
    rows = count // per * 8
    lane = lax.broadcasted_iota(jnp.int32, (rows, TILE), 1)
    start = lane // (2 * PANEL) * (2 * PANEL)
    row = lax.rem(lax.broadcasted_iota(jnp.int32, (rows, TILE), 0), 8)
    sub = lax.broadcasted_iota(jnp.int32, (count // per, 8, TILE), 1)
    eye = (
        lax.broadcasted_iota(jnp.int32, (PANEL, PANEL), 0) == lax.broadcasted_iota(jnp.int32, (PANEL, PANEL), 1)
    ).astype(F32)
    packs = []
    for q in range(count // per):
        pieces = []
        for k in range(per):
            pieces += [work[batch, q * per + k, r0:r0 + PANEL, r0:r0 + PANEL], eye]
        packs.append(jnp.concatenate(pieces, 1)[None])
    x = jnp.concatenate(packs, 0)
    strips = [x[:, 8 * e:8 * e + 8, :] for e in range(PANEL // 8)]

    def segment(strip, index):
        return jnp.take_along_axis(strip.reshape(-1, TILE), index, axis=1).reshape(strip.shape)

    for j in range(0, PANEL, 2):
        e0, here = j // 8, j % 8
        one = [segment(strip, start + j) for strip in strips[e0:]]
        two = [segment(strip, start + j + 1) for strip in strips[e0:]]
        corner = one[0][:, here:here + 1, :]
        side = one[0][:, here + 1:here + 2, :]
        inverse = 1.0 / corner
        inverse_two = corner * (1.0 / (corner * two[0][:, here + 1:here + 2, :] - side * side))
        shift = side * inverse
        ratio = strips[e0][:, here:here + 1, :] * inverse
        next_off = side * ratio
        ratio_two = (strips[e0][:, here + 1:here + 2, :] - next_off) * inverse_two
        ratio_one = ratio - shift * ratio_two
        for e in range(e0, PANEL // 8):
            change = one[e - e0] * ratio_one + two[e - e0] * ratio_two
            if e == e0:
                change = jnp.where(sub > here + 1, change, jnp.where(sub == here + 1, next_off, 0.0))
            strips[e] = strips[e] - change
    for e in range(PANEL // 8):
        strips[e] = strips[e] * lax.rsqrt(segment(strips[e], start + 8 * e + row))
    x = jnp.concatenate(strips, 1)
    for q in range(count // per):
        for k in range(per):
            i = q * per + k
            inverse = x[q, :, 2 * PANEL * k + PANEL:2 * PANEL * (k + 1)]
            u = mm(inverse, work[batch, i, r0:r0 + PANEL, :])
            work[batch, i, r0:r0 + PANEL, TILE:] = u[:, TILE:]
            if r0 + PANEL < TILE:
                high, low = halves(u)
                left = jnp.concatenate([u[:, :TILE], u[:, :TILE], low[:, :TILE].astype(F32)], 0).T
                work[batch, i, r0 + PANEL:, :] -= times(
                    left[r0 + PANEL:, :].astype(BF16), jnp.concatenate([high, low, high], 0)
                )


def some(shape):
    return tuple(max(1, s) for s in shape)


def owner_update(used, slot_grads, small, state, device_count):
    grid = chip_grid(device_count)
    zs, ys, xs = grid
    slots = slot_grads.shape[0] // device_count
    half = slots // 2
    block = (TILE, TILE)
    dma = pltpu.SemaphoreType.DMA
    firsts, seconds = (xs, ys), (ys, xs)
    whole = (slots,) + block
    scratch = (
        [pltpu.VMEM(whole, F32)] * 7
        + [pltpu.VMEM((half, zs, seconds[g]) + block, BF16) for g in range(2)]
        + [pltpu.VMEM(some((half, firsts[g] - 1, zs, seconds[g])) + block, BF16) for g in range(2)]
        + [pltpu.VMEM(some((half, seconds[g] - 1, zs)) + block, BF16) for g in range(2)]
        + [pltpu.VMEM(some((half, zs - 1)) + block, BF16) for g in range(2)]
        + [pltpu.VMEM((3,) + small.shape, F32)]
        + [pltpu.VMEM((max(1, n - 1),) + small.shape, F32) for n in grid]
        + [pltpu.VMEM((2, 16, TILE, 2 * TILE), F32)]
        + [dma((2, half))]
        + [dma(some((half, firsts[g] - 1))) for g in range(2)] * 2
        + [dma(some((half, seconds[g] - 1))) for g in range(2)] * 2
        + [dma(some((half, zs - 1))) for g in range(2)] * 2
        + [dma((max(1, n - 1),)) for n in grid] * 2
        + [dma((2, 7))]
    )
    results = pl.pallas_call(
        functools.partial(owner_kernel, grid),
        out_shape=[jax.ShapeDtypeStruct(whole, F32)] * 7
        + [jax.ShapeDtypeStruct(small.shape, F32), jax.ShapeDtypeStruct((16, TILE, 2 * TILE), F32)],
        in_specs=[pl.BlockSpec(memory_space=pltpu.SMEM), ANY, pl.BlockSpec(memory_space=pltpu.VMEM)] + [ANY] * 7,
        out_specs=[ANY] * 7 + [pl.BlockSpec(memory_space=pltpu.VMEM)] * 2,
        scratch_shapes=scratch,
        compiler_params=pltpu.CompilerParams(collective_id=1, has_side_effects=True, vmem_limit_bytes=56 << 20),
        name="owner_update",
    )(used, slot_grads.reshape(zs, ys, xs, slots, TILE, TILE), small, *state)
    return last_bases(results[8], results[:7]), results[7]


def ag_kernel(grid, own_ref, small_ref, out_ref, small_out_ref,
              load_sem, z_send, z_recv, b_send0, b_send1, b_recv0, b_recv1, a_send0, a_send1, a_recv0, a_recv1,
              s_load, ssz, ssy, ssx, srz, sry, srx):
    zs, ys, xs = grid
    z, y, x = place(grid)
    tos = peers(grid)
    to_z, to_y, to_x = tos
    slots = own_ref.shape[0]
    half, chunks, size = chunking(slots)
    first = ((xs, to_x), (ys, to_y))
    second = ((ys, to_y), (xs, to_x))
    b_send, b_recv, a_send, a_recv = (b_send0, b_send1), (b_recv0, b_recv1), (a_send0, a_send1), (a_recv0, a_recv1)
    s_send, s_recv = (ssz, ssy, ssx), (srz, sry, srx)

    def span(g, c):
        return pl.ds(g * half + c * size, size)

    def send_z(g, c, k):
        return remote(own_ref.at[span(g, c)], out_ref.at[z, y, x, span(g, c)],
                      z_send.at[g, c, k - 1], z_recv.at[g, c, k - 1], to_z(k))

    def send_b(g, c, k):
        part = out_ref.at[:, y, x, span(g, c)]
        return remote(part, part, b_send[g].at[c, k - 1], b_recv[g].at[c, k - 1], second[g][1](k))

    def send_a(g, c, k):
        part = out_ref.at[:, :, x, span(g, c)] if g == 0 else out_ref.at[:, y, :, span(g, c)]
        return remote(part, part, a_send[g].at[c, k - 1], a_recv[g].at[c, k - 1], first[g][1](k))

    def send_s(axis, k):
        if axis == 0:
            source, target = small_ref, small_out_ref.at[z, y, x]
        else:
            source = target = small_out_ref.at[:, y, x] if axis == 1 else small_out_ref.at[:, :, x]
        return remote(source, target, s_send[axis].at[k - 1], s_recv[axis].at[k - 1], tos[axis](k))

    keep = pltpu.make_async_copy(own_ref, out_ref.at[z, y, x], load_sem)
    keep_small = pltpu.make_async_copy(small_ref, small_out_ref.at[z, y, x], s_load)
    keep.start()
    keep_small.start()
    greet(grid)

    for k in range(1, grid[0]):
        send_s(0, k).start()
    def start_z(c):
        for g in range(2):
            for k in range(1, zs):
                send_z(g, c, k).start()

    def small_wait(axis):
        for k in range(1, grid[axis]):
            send_s(axis, k).wait_recv()

    def small_start(axis):
        for k in range(1, grid[axis]):
            send_s(axis, k).start()

    start_z(0)
    for t in range(chunks + 1):
        if t < chunks:
            for g in range(2):
                for k in range(1, zs):
                    send_z(g, t, k).wait_recv()
            if t == 0:
                keep.wait()
                keep_small.wait()
                small_wait(0)
                small_start(1)
            if t + 1 < chunks:
                start_z(t + 1)
            for g in range(2):
                for k in range(1, second[g][0]):
                    send_b(g, t, k).start()
        if t >= 1:
            for g in range(2):
                for k in range(1, second[g][0]):
                    send_b(g, t - 1, k).wait_recv()
                for k in range(1, first[g][0]):
                    send_a(g, t - 1, k).start()
        if t == 1:
            small_wait(1)
            small_start(2)
    small_wait(2)
    for c in range(chunks):
        for g in range(2):
            for k in range(1, first[g][0]):
                send_a(g, c, k).wait_recv()
    for axis in range(3):
        for k in range(1, grid[axis]):
            send_s(axis, k).wait_send()
    for c in range(chunks):
        for g in range(2):
            for k in range(1, zs):
                send_z(g, c, k).wait_send()
            for k in range(1, second[g][0]):
                send_b(g, c, k).wait_send()
            for k in range(1, first[g][0]):
                send_a(g, c, k).wait_send()


def gather_all(own, small, device_count):
    grid = chip_grid(device_count)
    zs, ys, xs = grid
    slots = own.shape[0]
    half, chunks, size = chunking(slots)
    dma = pltpu.SemaphoreType.DMA
    firsts, seconds = (xs, ys), (ys, xs)
    scratch = (
        [dma, dma(some((2, chunks, zs - 1))), dma(some((2, chunks, zs - 1)))]
        + [dma(some((chunks, seconds[g] - 1))) for g in range(2)] * 2
        + [dma(some((chunks, firsts[g] - 1))) for g in range(2)] * 2
        + [dma]
        + [dma((max(1, n - 1),)) for n in grid] * 2
    )
    blocks, smalls = pl.pallas_call(
        functools.partial(ag_kernel, grid),
        out_shape=[jax.ShapeDtypeStruct(grid + own.shape, own.dtype), jax.ShapeDtypeStruct(grid + small.shape, small.dtype)],
        in_specs=[pl.BlockSpec(memory_space=pltpu.VMEM)] * 2,
        out_specs=[ANY, ANY],
        scratch_shapes=scratch,
        compiler_params=pltpu.CompilerParams(collective_id=2, has_side_effects=True),
        name="gather_all",
    )(own, small)
    return blocks.reshape((-1,) + own.shape[1:]), smalls.reshape((-1,) + small.shape)


def unpack_kernel(shapes, slots_ref, packed, *refs):
    count = len(shapes)
    mats, held, sems = refs[:count], refs[count:-1], refs[-1]

    def whole(index):
        return pltpu.make_async_copy(held[index], mats[index], sems.at[1, index])

    offset = 0
    for index, (height, breadth) in enumerate(shapes):
        down, across = height // TILE, breadth // TILE

        def start(i, carry, index=index, offset=offset, across=across):
            for j in range(across):
                tile = held[index].at[pl.ds(pl.multiple_of(i * TILE, TILE), TILE), j * TILE:(j + 1) * TILE]
                slot = packed.at[slots_ref[offset + i * across + j]]
                pltpu.make_async_copy(slot, tile, sems.at[0, index]).start()
            return carry

        lax.fori_loop(0, down, start, 0)
        offset += down * across
    for index in range(count):
        pltpu.make_async_copy(held[index], held[index], sems.at[0, index]).wait()
        whole(index).start()
    for index in range(count):
        whole(index).wait()


def unpack_tiles(packed, slots, shapes):
    return pl.pallas_call(
        functools.partial(unpack_kernel, shapes),
        out_shape=[jax.ShapeDtypeStruct(s, packed.dtype) for s in shapes],
        in_specs=[pl.BlockSpec(memory_space=pltpu.SMEM), ANY],
        out_specs=[ANY] * len(shapes),
        scratch_shapes=[pltpu.VMEM(s, packed.dtype) for s in shapes] + [pltpu.SemaphoreType.DMA((2, len(shapes)))],
        compiler_params=pltpu.CompilerParams(vmem_limit_bytes=56 << 20),
        name="unpack_tiles",
    )(slots, packed)


def weight_grads_kernel(plan, used, vectors, passed, slots_ref, *refs):
    arrays, refs = refs[:used], refs[used:]
    given, refs = refs[:len(vectors)], refs[len(vectors):]
    refs = refs[passed:]
    packed, refs = refs[0], refs[1:]
    if vectors:
        rows_ref, refs = refs[0], refs[1:]
    held, refs = refs[:used], refs[used:]
    turned, refs = refs[0], refs[1:]
    results, sems = refs[:len(plan)], refs[len(plan):]
    load_sem, store_sem = sems

    def load(i):
        return pltpu.make_async_copy(arrays[i], held[i], load_sem.at[i])

    order = []
    for left, tokens, right, *rest in plan:
        for i in (left, right):
            if i not in order:
                order.append(i)
    for i in order:
        load(i).start()
    if vectors:
        width = rows_ref.shape[1]
        rows_ref[...] = jnp.zeros_like(rows_ref)
        for source, (at, pieces) in zip(given, vectors):
            if pieces is None:
                rows_ref[at:at + 3, :] = source[0:3, :]
                continue
            for begin, end in pieces:
                while begin < end:
                    lane = at % width
                    size = min(end - begin, width - lane)
                    rows_ref[at // width:at // width + 1, lane:lane + size] = source[:, begin:begin + size]
                    begin, at = begin + size, at + size
    ready = set()
    last = None
    for index, (left, tokens, right, offset, stride, down, across) in enumerate(plan):
        for i in (left, right):
            if i not in ready:
                ready.add(i)
                load(i).wait()
        height = down * TILE
        if last != (left, tokens):
            for j in range(down):
                turned[j * TILE:(j + 1) * TILE, :tokens] = (
                    held[left][:tokens, j * TILE:(j + 1) * TILE].astype(F32).T.astype(BF16)
                )
            last = (left, tokens)
        result = results[index]
        group = 3 if across % 3 == 0 else 1

        def columns(n, carry, right=right, tokens=tokens, height=height, result=result, offset=offset,
                    stride=stride, down=down, group=group, index=index):
            lanes = pl.ds(pl.multiple_of(n * group * TILE, TILE), group * TILE)
            result[:, lanes] = times(turned[:height, :tokens], held[right][:tokens, lanes]).astype(BF16)

            def send(i, carry):
                for j in range(group):
                    tile = result.at[
                        pl.ds(pl.multiple_of(i * TILE, TILE), TILE),
                        pl.ds(pl.multiple_of((n * group + j) * TILE, TILE), TILE),
                    ]
                    slot = packed.at[slots_ref[offset + i * stride + n * group + j]]
                    pltpu.make_async_copy(tile, slot, store_sem.at[index]).start()
                return carry

            lax.fori_loop(0, down, send, 0)
            return carry

        lax.fori_loop(0, across // group, columns, 0)
    for index in range(len(plan)):
        pltpu.make_async_copy(results[index], results[index], store_sem.at[index]).wait()


def weight_grads(matrices, slots, slot_count, packed=None, vectors=None):
    arrays, plan, results = [], [], []

    def index_of(array):
        for i, other in enumerate(arrays):
            if other is array:
                return i
        arrays.append(array)
        return len(arrays) - 1

    for offset, parts in matrices:
        height = parts[0][0].shape[1]
        stride = sum(right.shape[1] for left, right in parts) // TILE
        for left, right in parts:
            across = right.shape[1] // TILE
            plan.append((index_of(left), right.shape[0], index_of(right), offset, stride, height // TILE, across))
            results.append(pltpu.VMEM((height, right.shape[1]), BF16))
            offset += across
    tall = max(entry[5] for entry in plan) * TILE
    long = max(entry[1] for entry in plan)
    out_shape = [jax.ShapeDtypeStruct((slot_count, TILE, TILE), BF16)]
    given, layout = [], []
    if vectors:
        rows, width, items = vectors
        out_shape.append(jax.ShapeDtypeStruct((rows, width), F32))
        given = [item[0] for item in items]
        layout = [item[1:] for item in items]
    passed = [] if packed is None else [packed]
    return pl.pallas_call(
        functools.partial(weight_grads_kernel, plan, len(arrays), layout, len(passed)),
        out_shape=out_shape,
        in_specs=[pl.BlockSpec(memory_space=pltpu.SMEM)] + [ANY] * len(arrays)
        + [pl.BlockSpec(memory_space=pltpu.VMEM)] * len(given) + [ANY] * len(passed),
        out_specs=[ANY] + [pl.BlockSpec(memory_space=pltpu.VMEM)] * (len(out_shape) - 1),
        scratch_shapes=[pltpu.VMEM(a.shape, a.dtype) for a in arrays] + [pltpu.VMEM((tall, long), BF16)] + results
        + [pltpu.SemaphoreType.DMA((len(arrays),)), pltpu.SemaphoreType.DMA((len(plan),))],
        input_output_aliases={} if packed is None else {1 + len(arrays) + len(given): 0},
        compiler_params=pltpu.CompilerParams(vmem_limit_bytes=56 << 20),
        name="weight_grads",
    )(slots, *arrays, *given, *passed)


VM = pl.BlockSpec(memory_space=pltpu.VMEM)


def times(left, right, dims=NN):
    return lax.dot_general(left, right, (dims, ((), ())), preferred_element_type=F32)


def rows_of(t, size=ROWS):
    return pl.ds(pl.multiple_of(t * size, size), size)


class Swap:
    def __init__(self, out, into, send_sem, recv_sem):
        self.out, self.into, self.send_sem, self.recv_sem = out, into, send_sem, recv_sem

    @staticmethod
    def scratch(tiles, width):
        dma = pltpu.SemaphoreType.DMA((tiles,))
        held = pltpu.VMEM((tiles, ROWS, width), BF16)
        return [held, held, dma, dma]

    @staticmethod
    def greet():
        barrier = pltpu.get_barrier_semaphore()
        other = {"tensor": 1 - lax.axis_index("tensor")}
        pl.semaphore_signal(barrier, inc=1, device_id=other, device_id_type=MESH)
        pl.semaphore_wait(barrier, 1)

    def copy(self, t):
        return pltpu.make_async_remote_copy(
            src_ref=self.out.at[t],
            dst_ref=self.into.at[t],
            send_sem=self.send_sem.at[t],
            recv_sem=self.recv_sem.at[t],
            device_id={"tensor": 1 - lax.axis_index("tensor")},
            device_id_type=MESH,
        )

    def give(self, t, value):
        self.out[t] = value.astype(BF16)
        self.copy(t).start()

    def take(self, t):
        self.copy(t).wait()
        return self.out[t].astype(F32) + self.into[t].astype(F32)


class Rows:
    def __init__(self, ref, rows):
        self.ref, self.rows = ref, rows

    def __getitem__(self, index):
        at = self.rows[index[0].start]
        return self.ref[at:at + 1, :]


def bias_places(half, hidden_half):
    places, at = {}, 0
    for name, length in (
        ("enc_q", half), ("enc_v", half), ("enc_up", hidden_half), ("dec_q", half), ("dec_v", half),
        ("crs_q", half), ("crs_v", half), ("dec_up", hidden_half),
    ):
        places[name] = slice(at, at + length)
        at += length
    return places


def bias_row(split_ref, places, names, half):
    zero = jnp.zeros((1, half), F32)
    return jnp.concatenate([zero if name is None else split_ref[:, places[name]] for name in names], 1)


def standardize(values):
    center = values - jnp.mean(values, -1, keepdims=True)
    scale = lax.rsqrt(jnp.mean(center * center, -1, keepdims=True) + NORM_EPSILON)
    return center * scale, scale


def norm_back(grad, unit, scale, gain):
    inner = grad * gain
    return scale * (
        inner - jnp.mean(inner, -1, keepdims=True) - unit * jnp.mean(inner * unit, -1, keepdims=True)
    )


def add_sums(sums_ref, grad_in, grad_out, unit):
    sums_ref[0:1, :] += jnp.sum(grad_in, 0, keepdims=True)
    sums_ref[1:2, :] += jnp.sum(grad_out * unit, 0, keepdims=True)
    sums_ref[2:3, :] += jnp.sum(grad_out, 0, keepdims=True)


def head_mask(shape):
    return lax.broadcasted_iota(jnp.int32, shape, 1) < HD


def attend(query_ref, key_ref, value_ref, attended_ref, totals_ref, score_ref, turned_ref, causal, span):
    queries, keys = query_ref.shape[0], key_ref.shape[0]
    pairs = query_ref.shape[1] // PAIR
    chunks = keys // KEYS
    for j in range(pairs):
        turned_ref[j * PAIR:(j + 1) * PAIR, :] = (
            value_ref[:, j * PAIR:(j + 1) * PAIR].astype(F32).T.astype(BF16)
        )
    for i in range(queries // span):
        mine = slice(i * span, (i + 1) * span)

        def pair(j, carry, i=i, mine=mine):
            lanes = pl.ds(pl.multiple_of(j * PAIR, PAIR), PAIR)
            query = query_ref[mine, lanes] * jnp.asarray(HD**-0.5, BF16)
            first = head_mask(query.shape)
            parts = []
            for h in range(2):
                masked = jnp.where(first if h == 0 else ~first, query, jnp.zeros_like(query))
                top = jnp.full((1, span), -jnp.inf, F32)
                for c in range(chunks):
                    if causal and c * KEYS >= (i + 1) * span:
                        continue
                    scores = times(key_ref[c * KEYS:(c + 1) * KEYS, lanes], masked, NT)
                    if causal and (c + 1) * KEYS > i * span:
                        key_at = c * KEYS + lax.broadcasted_iota(jnp.int32, scores.shape, 0)
                        query_at = i * span + lax.broadcasted_iota(jnp.int32, scores.shape, 1)
                        scores = jnp.where(key_at <= query_at, scores, -1000000000.0)
                    score_ref[h, c * KEYS:(c + 1) * KEYS, :] = scores
                    top = jnp.maximum(top, jnp.max(scores, 0, keepdims=True))
                total = jnp.zeros((1, span), F32)
                mixed = jnp.zeros((HD, span), F32)
                value_rows = pl.ds(pl.multiple_of(j * PAIR + h * HD, HD), HD)
                for c in range(chunks):
                    if causal and c * KEYS >= (i + 1) * span:
                        continue
                    probs = jnp.exp(score_ref[h, c * KEYS:(c + 1) * KEYS, :] - top)
                    total += jnp.sum(probs, 0, keepdims=True)
                    mixed += times(turned_ref[value_rows, c * KEYS:(c + 1) * KEYS], probs.astype(BF16))
                parts.append(mixed * (1.0 / total))
                totals_ref[pl.ds(2 * j + h, 1), mine] = top + jnp.log(total)
            attended_ref[mine, lanes] = jnp.concatenate(parts, 0).T.astype(BF16)
            return carry

        lax.fori_loop(0, pairs, pair, 0)


def attend_back(
    query_ref, key_ref, value_ref, attended_ref, totals_ref, grad_ref,
    grad_query_ref, grad_key_ref, grad_value_ref, turned_ref, causal,
):
    queries, keys = grad_ref.shape[0], key_ref.shape[0]
    pairs = query_ref.shape[1] // PAIR
    chunks = keys // KEYS
    scale = HD**-0.5
    for j in range(pairs):
        turned_ref[j * PAIR:(j + 1) * PAIR, :] = (
            key_ref[:, j * PAIR:(j + 1) * PAIR].astype(F32).T.astype(BF16)
        )

    def pair(j, carry):
        lanes = pl.ds(pl.multiple_of(j * PAIR, PAIR), PAIR)
        query = query_ref[:queries, lanes] * jnp.asarray(scale, BF16)
        grad = grad_ref[:, lanes]
        first = head_mask(query.shape)
        meet = (grad.astype(F32) * attended_ref[:queries, lanes].astype(F32)).T
        masked, grads, deltas, totals = [], [], [], []
        for h in range(2):
            keep = first if h == 0 else ~first
            masked.append(jnp.where(keep, query, jnp.zeros_like(query)))
            grads.append(jnp.where(keep, grad, jnp.zeros_like(grad)))
            deltas.append(jnp.sum(meet[h * HD:(h + 1) * HD], 0, keepdims=True))
            totals.append(totals_ref[pl.ds(2 * j + h, 1), :queries])
        grad_query = [jnp.zeros((HD, queries), F32) for h in range(2)]
        for c in range(chunks):
            some = slice(c * KEYS, (c + 1) * KEYS)
            low = c * KEYS if causal else 0
            grad_key = grad_value = jnp.zeros((KEYS, PAIR), F32)
            for h in range(2):
                scores = times(key_ref[some, lanes], masked[h][low:], NT)
                if causal:
                    key_at = lax.broadcasted_iota(jnp.int32, scores.shape, 0)
                    query_at = lax.broadcasted_iota(jnp.int32, scores.shape, 1)
                    scores = jnp.where(key_at <= query_at, scores, -1000000000.0)
                probs = jnp.exp(scores - totals[h][:, low:])
                grad_probs = times(value_ref[some, lanes], grads[h][low:], NT)
                grad_scores = (probs * (grad_probs - deltas[h][:, low:])).astype(BF16)
                grad_value += times(probs.astype(BF16), grads[h][low:])
                grad_key += times(grad_scores, masked[h][low:])
                key_rows = pl.ds(pl.multiple_of(j * PAIR + h * HD, HD), HD)
                part = times(turned_ref[key_rows, some], grad_scores)
                if low:
                    part = jnp.concatenate([jnp.zeros((HD, low), F32), part], 1)
                grad_query[h] += part
            grad_key_ref[some, lanes] = grad_key.astype(BF16)
            grad_value_ref[some, lanes] = grad_value.astype(BF16)
        grad_query_ref[:, lanes] = (jnp.concatenate(grad_query, 0) * scale).T.astype(BF16)
        return carry

    lax.fori_loop(0, pairs, pair, 0)


def self_forward_kernel(
    causal, span, x_ref, wide_ref, out_weight_ref, bias_ref, vec_ref,
    mixed_ref, attended_ref, totals_ref, unit_ref, scale_ref,
    score_ref, turned_ref, *swap_refs,
):
    swap = Swap(*swap_refs)
    length, width = x_ref.shape
    half = out_weight_ref.shape[0]
    tiles = length // ROWS
    totals_ref[...] = jnp.zeros_like(totals_ref)

    def mix(t, carry):
        mixed_ref[rows_of(t), :] = (times(x_ref[rows_of(t), :], wide_ref[...]) + bias_ref[...]).astype(BF16)
        return carry

    lax.fori_loop(0, tiles, mix, 0)
    attend(
        mixed_ref.at[:, :half], mixed_ref.at[:, half:2 * half], mixed_ref.at[:, 2 * half:],
        attended_ref, totals_ref, score_ref, turned_ref, causal, span,
    )

    def give(t, carry):
        swap.give(t, times(attended_ref[rows_of(t), :], out_weight_ref[...]))
        return carry

    lax.fori_loop(0, tiles, give, 0)

    def take(t, carry):
        rows = rows_of(t)
        unit, scale = standardize(x_ref[rows, :].astype(F32) + swap.take(t) + vec_ref[0:1, :])
        unit_ref[rows, :] = unit
        scale_ref[rows, :] = scale
        return carry

    lax.fori_loop(0, tiles, take, 0)


def shape(*dims, dtype=F32):
    return jax.ShapeDtypeStruct(dims, dtype)


def params(ident, mib=56):
    return pltpu.CompilerParams(collective_id=ident, has_side_effects=True, vmem_limit_bytes=mib << 20)


def cross_forward_kernel(
    span, unit_ref, fetched_ref, query_weight_ref, wide_ref, out_weight_ref, query_bias_ref, bias_ref, vec_ref,
    low_ref, query_ref, mixed_ref, attended_ref, totals_ref, unit_out_ref, scale_ref,
    score_ref, turned_ref, *swap_refs,
):
    swap = Swap(*swap_refs)
    length, width = unit_ref.shape
    half = out_weight_ref.shape[0]
    tiles = length // ROWS
    totals_ref[...] = jnp.zeros_like(totals_ref)

    def ask(t, carry):
        rows = rows_of(t)
        low = (unit_ref[rows, :] * vec_ref[0:1, :] + vec_ref[1:2, :]).astype(BF16)
        low_ref[rows, :] = low
        query_ref[rows, :] = (times(low, query_weight_ref[...]) + query_bias_ref[...]).astype(BF16)
        return carry

    lax.fori_loop(0, tiles, ask, 0)

    def mix(t, carry):
        mixed_ref[rows_of(t), :] = (
            times(fetched_ref[rows_of(t), :], wide_ref[...]) + bias_ref[...]
        ).astype(BF16)
        return carry

    lax.fori_loop(0, fetched_ref.shape[0] // ROWS, mix, 0)
    attend(
        query_ref, mixed_ref.at[:, :half], mixed_ref.at[:, half:],
        attended_ref, totals_ref, score_ref, turned_ref, False, span,
    )

    def give(t, carry):
        swap.give(t, times(attended_ref[rows_of(t), :], out_weight_ref[...]))
        return carry

    lax.fori_loop(0, tiles, give, 0)

    def take(t, carry):
        rows = rows_of(t)
        hidden = unit_ref[rows, :] * vec_ref[0:1, :] + vec_ref[1:2, :]
        unit, scale = standardize(hidden + swap.take(t) + vec_ref[2:3, :])
        unit_out_ref[rows, :] = unit
        scale_ref[rows, :] = scale
        return carry

    lax.fori_loop(0, tiles, take, 0)


def feed_forward_kernel(
    kept, unit_ref, up_ref, down_ref, bias_ref, vec_ref,
    states_ref, states_low_ref, low_ref, active_ref, slope_ref, unit_out_ref, scale_ref, *swap_refs,
):
    swap = Swap(*swap_refs)
    length, width = unit_ref.shape
    hidden_half = up_ref.shape[1]
    tiles, kept_tiles = length // ROWS, kept // ROWS
    step = 512

    def feed(t, carry, keep):
        rows = rows_of(t)
        low = (unit_ref[rows, :] * vec_ref[0:1, :] + vec_ref[1:2, :]).astype(BF16)
        if keep:
            low_ref[rows, :] = low
        total = jnp.zeros((ROWS, width), F32)
        for c in range(0, hidden_half, step):
            upward = times(low, up_ref[:, c:c + step]) + bias_ref[:, c:c + step]
            below = 0.5 * lax.erf(upward * (0.5**0.5)) + 0.5
            active = (upward * below).astype(BF16)
            if keep:
                active_ref[rows, c:c + step] = active
                bell = jnp.exp(-0.5 * upward * upward) * (0.5 / jnp.pi) ** 0.5
                slope_ref[rows, c:c + step] = (below + upward * bell).astype(BF16)
            total += times(active, down_ref[c:c + step, :])
        swap.give(t, total)
        return carry

    lax.fori_loop(0, kept_tiles, functools.partial(feed, keep=True), 0)
    if kept_tiles < tiles:
        lax.fori_loop(kept_tiles, tiles, functools.partial(feed, keep=False), 0)

    def take(t, carry, keep):
        rows = rows_of(t)
        hidden = unit_ref[rows, :] * vec_ref[0:1, :] + vec_ref[1:2, :]
        unit, scale = standardize(hidden + swap.take(t) + vec_ref[2:3, :])
        states = unit * vec_ref[3:4, :] + vec_ref[4:5, :]
        states_ref[rows, :] = states
        if keep:
            states_low_ref[rows, :] = states.astype(BF16)
            unit_out_ref[rows, :] = unit
            scale_ref[rows, :] = scale
        return carry

    lax.fori_loop(0, kept_tiles, functools.partial(take, keep=True), 0)
    if kept_tiles < tiles:
        lax.fori_loop(kept_tiles, tiles, functools.partial(take, keep=False), 0)


def feed_backward_kernel(
    grad_ref, unit_after_ref, scale_after_ref, active_ref, slope_ref, up_ref, down_ref,
    unit_before_ref, scale_before_ref, vec_ref,
    low_ref, grad_up_ref, bias_ref, grad_out_ref, sums_after_ref, sums_before_ref,
    held_ref, *swap_refs,
):
    swap = Swap(*swap_refs)
    length, width = grad_ref.shape
    hidden_half = up_ref.shape[1]
    tiles = length // ROWS
    step = 512
    sums_after_ref[...] = jnp.zeros_like(sums_after_ref)
    sums_before_ref[...] = jnp.zeros_like(sums_before_ref)
    bias_ref[...] = jnp.zeros_like(bias_ref)

    def give(t, carry):
        rows = rows_of(t)
        grad = grad_ref[rows, :].astype(F32)
        unit = unit_after_ref[rows, :]
        inner = norm_back(grad, unit, scale_after_ref[rows, :], vec_ref[0:1, :])
        add_sums(sums_after_ref, inner, grad, unit)
        held_ref[rows, :] = inner
        low = inner.astype(BF16)
        low_ref[rows, :] = low
        total = jnp.zeros((ROWS, width), F32)
        for c in range(0, hidden_half, step):
            grad_active = times(low, down_ref[c:c + step, :], NT)
            grad_up = (grad_active * slope_ref[rows, c:c + step].astype(F32)).astype(BF16)
            grad_up_ref[rows, c:c + step] = grad_up
            bias_ref[:, c:c + step] += jnp.sum(grad_up.astype(F32), 0, keepdims=True)
            total += times(grad_up, up_ref[:, c:c + step], NT)
        swap.give(t, total)
        return carry

    lax.fori_loop(0, tiles, give, 0)

    def take(t, carry):
        rows = rows_of(t)
        grad = held_ref[rows, :] + swap.take(t)
        unit = unit_before_ref[rows, :]
        inner = norm_back(grad, unit, scale_before_ref[rows, :], vec_ref[1:2, :])
        add_sums(sums_before_ref, inner, grad, unit)
        grad_out_ref[rows, :] = inner
        return carry

    lax.fori_loop(0, tiles, take, 0)


def spread(grad_pre_ref, out_weight_ref, low_ref, grad_ref):
    def one(t, carry):
        rows = rows_of(t)
        low = grad_pre_ref[rows, :].astype(BF16)
        low_ref[rows, :] = low
        grad_ref[rows, :] = times(low, out_weight_ref[...], NT).astype(BF16)
        return carry

    lax.fori_loop(0, grad_pre_ref.shape[0] // ROWS, one, 0)


def self_backward_kernel(
    causal, grad_pre_ref, mixed_ref, attended_ref, totals_ref, wide_ref, out_weight_ref,
    low_ref, grad_query_ref, grad_pair_ref, grad_x_ref, sums_ref,
    grad_ref, turned_ref, *swap_refs,
):
    swap = Swap(*swap_refs)
    queries, width = grad_pre_ref.shape
    half = out_weight_ref.shape[0]
    length = mixed_ref.shape[0]
    spread(grad_pre_ref, out_weight_ref, low_ref, grad_ref)
    attend_back(
        mixed_ref.at[:, :half], mixed_ref.at[:, half:2 * half], mixed_ref.at[:, 2 * half:],
        attended_ref, totals_ref, grad_ref,
        grad_query_ref, grad_pair_ref.at[:, :half], grad_pair_ref.at[:, half:], turned_ref, causal,
    )
    sums_ref[...] = jnp.zeros_like(sums_ref)
    first = queries // ROWS

    def give(t, carry, asked):
        rows = rows_of(t)
        pair = grad_pair_ref[rows, :]
        sums_ref[:, half:] += jnp.sum(pair.astype(F32), 0, keepdims=True)
        total = times(pair, wide_ref[:, half:], NT)
        if asked:
            query = grad_query_ref[rows, :]
            sums_ref[:, :half] += jnp.sum(query.astype(F32), 0, keepdims=True)
            total += times(query, wide_ref[:, :half], NT)
        swap.give(t, total)
        return carry

    lax.fori_loop(0, first, functools.partial(give, asked=True), 0)
    if first < length // ROWS:
        lax.fori_loop(first, length // ROWS, functools.partial(give, asked=False), 0)

    def take(t, carry, asked):
        rows = rows_of(t)
        total = swap.take(t)
        grad_x_ref[rows, :] = grad_pre_ref[rows, :] + total if asked else total
        return carry

    lax.fori_loop(0, first, functools.partial(take, asked=True), 0)
    if first < length // ROWS:
        lax.fori_loop(first, length // ROWS, functools.partial(take, asked=False), 0)


def cross_backward_kernel(
    grad_pre_ref, query_ref, mixed_ref, attended_ref, totals_ref, query_weight_ref, wide_ref, out_weight_ref,
    unit_ref, scale_ref, vec_ref,
    low_ref, grad_query_ref, grad_pair_ref, fetched_ref, grad_out_ref, sums_ref, vec_sums_ref,
    grad_ref, turned_ref, *swap_refs,
):
    near, far = Swap(*swap_refs[:4]), Swap(*swap_refs[4:])
    queries, width = grad_pre_ref.shape
    half = out_weight_ref.shape[0]
    keys = mixed_ref.shape[0]
    spread(grad_pre_ref, out_weight_ref, low_ref, grad_ref)
    attend_back(
        query_ref, mixed_ref.at[:, :half], mixed_ref.at[:, half:],
        attended_ref, totals_ref, grad_ref,
        grad_query_ref, grad_pair_ref.at[:, :half], grad_pair_ref.at[:, half:], turned_ref, False,
    )
    sums_ref[...] = jnp.zeros_like(sums_ref)
    vec_sums_ref[...] = jnp.zeros_like(vec_sums_ref)

    def give_far(t, carry):
        pair = grad_pair_ref[rows_of(t), :]
        sums_ref[:, half:] += jnp.sum(pair.astype(F32), 0, keepdims=True)
        far.give(t, times(pair, wide_ref[...], NT))
        return carry

    lax.fori_loop(0, keys // ROWS, give_far, 0)

    def give_near(t, carry):
        query = grad_query_ref[rows_of(t), :]
        sums_ref[:, :half] += jnp.sum(query.astype(F32), 0, keepdims=True)
        near.give(t, times(query, query_weight_ref[...], NT))
        return carry

    lax.fori_loop(0, queries // ROWS, give_near, 0)

    def take_far(t, carry):
        fetched_ref[rows_of(t), :] = far.take(t).astype(BF16)
        return carry

    lax.fori_loop(0, keys // ROWS, take_far, 0)

    def take_near(t, carry):
        rows = rows_of(t)
        grad = grad_pre_ref[rows, :] + near.take(t)
        unit = unit_ref[rows, :]
        inner = norm_back(grad, unit, scale_ref[rows, :], vec_ref[0:1, :])
        add_sums(vec_sums_ref, inner, grad, unit)
        grad_out_ref[rows, :] = inner
        return carry

    lax.fori_loop(0, queries // ROWS, take_near, 0)


def call(name, ident, body, inputs, outputs, scratch):
    return pl.pallas_call(
        body,
        out_shape=outputs,
        in_specs=[VM] * len(inputs),
        out_specs=[VM] * len(outputs),
        scratch_shapes=scratch,
        compiler_params=params(ident),
        name=name,
    )(*inputs)


def held(*dims, dtype=F32):
    return pltpu.VMEM(dims, dtype)


def encoder_forward(ident, x, wide, out_weight, up, down, shared, split, kept):
    length, width = x.shape
    half, hidden_half = out_weight.shape[0], up.shape[1]
    tiles, span = length // ROWS, min(length, 512)
    places = bias_places(half, hidden_half)

    def body(x_ref, wide_ref, out_weight_ref, up_ref, down_ref, shared_ref, split_ref, *refs):
        saved, fed, rest = refs[:5], refs[5:12], refs[12:]
        Swap.greet()
        self_forward_kernel(
            False, span, x_ref, wide_ref, out_weight_ref,
            bias_row(split_ref, places, ("enc_q", None, "enc_v"), half), Rows(shared_ref, (0,)),
            *saved, *rest[:6],
        )
        feed_forward_kernel(
            kept, saved[3], up_ref, down_ref, split_ref.at[:, places["enc_up"]],
            Rows(shared_ref, (1, 2, 3, 4, 5)), *fed, *rest[6:],
        )

    return call(
        "encoder_forward", ident, body, [x, wide, out_weight, up, down, shared, split],
        [
            shape(length, 3 * half, dtype=BF16), shape(length, half, dtype=BF16), shape(8, length),
            shape(length, width), shape(length, 1),
            shape(length, width), shape(kept, width, dtype=BF16), shape(kept, width, dtype=BF16),
            shape(kept, hidden_half, dtype=BF16), shape(kept, hidden_half, dtype=BF16),
            shape(kept, width), shape(kept, 1),
        ],
        [held(2, length, span), held(half, length, dtype=BF16)] + Swap.scratch(tiles, width) * 2,
    )


def decoder_self_forward(ident, x, wide, out_weight, shared, split, hidden_half):
    length, width = x.shape
    half = out_weight.shape[0]
    span = min(length, 512)
    places = bias_places(half, hidden_half)

    def body(x_ref, wide_ref, out_weight_ref, shared_ref, split_ref, *refs):
        Swap.greet()
        self_forward_kernel(
            True, span, x_ref, wide_ref, out_weight_ref,
            bias_row(split_ref, places, ("dec_q", None, "dec_v"), half), Rows(shared_ref, (6,)), *refs,
        )

    return call(
        "decoder_self_forward", ident, body, [x, wide, out_weight, shared, split],
        [
            shape(length, 3 * half, dtype=BF16), shape(length, half, dtype=BF16), shape(8, length),
            shape(length, width), shape(length, 1),
        ],
        [held(2, length, span), held(half, length, dtype=BF16)] + Swap.scratch(length // ROWS, width),
    )


def decoder_core(
    ident, unit, scale, fetched, cotangent, query_weight, wide, out_weight, up, down, shared, split
):
    length, width = unit.shape
    keys = fetched.shape[0]
    half, hidden_half = out_weight.shape[0], up.shape[1]
    tiles, span = length // ROWS, min(length, 512)
    places = bias_places(half, hidden_half)

    def body(
        unit_ref, scale_ref, fetched_ref, cotangent_ref, query_weight_ref, wide_ref, out_weight_ref,
        up_ref, down_ref, shared_ref, split_ref,
        states_ref, low_ref, attended_ref, second_low_ref, active_ref,
        feed_low_ref, grad_up_ref, up_bias_ref, sums_after_ref, sums_before_ref,
        cross_low_ref, grad_query_ref, grad_pair_ref, returned_ref, grad_out_ref, cross_sums_ref, vec_sums_ref,
        query_ref, mixed_ref, totals_ref, unit_four_ref, scale_four_ref, states_low_ref, slope_ref,
        unit_five_ref, scale_five_ref, grad_four_ref, inner_ref, score_ref, turned_ref, grad_ref, *swaps,
    ):
        Swap.greet()
        cross_forward_kernel(
            span, unit_ref, fetched_ref, query_weight_ref, wide_ref, out_weight_ref,
            split_ref.at[:, places["crs_q"]], bias_row(split_ref, places, (None, "crs_v"), half),
            Rows(shared_ref, (7, 8, 9)),
            low_ref, query_ref, mixed_ref, attended_ref, totals_ref, unit_four_ref, scale_four_ref,
            score_ref, turned_ref, *swaps[:4],
        )
        feed_forward_kernel(
            length, unit_four_ref, up_ref, down_ref, split_ref.at[:, places["dec_up"]],
            Rows(shared_ref, (10, 11, 12, 13, 14)),
            states_ref, states_low_ref, second_low_ref, active_ref, slope_ref, unit_five_ref, scale_five_ref,
            *swaps[4:8],
        )
        feed_backward_kernel(
            cotangent_ref, unit_five_ref, scale_five_ref, active_ref, slope_ref, up_ref, down_ref,
            unit_four_ref, scale_four_ref, Rows(shared_ref, (13, 10)),
            feed_low_ref, grad_up_ref, up_bias_ref, grad_four_ref, sums_after_ref, sums_before_ref,
            inner_ref, *swaps[8:12],
        )
        cross_backward_kernel(
            grad_four_ref, query_ref, mixed_ref, attended_ref, totals_ref, query_weight_ref, wide_ref,
            out_weight_ref, unit_ref, scale_ref, Rows(shared_ref, (7,)),
            cross_low_ref, grad_query_ref, grad_pair_ref, returned_ref, grad_out_ref, cross_sums_ref, vec_sums_ref,
            grad_ref, turned_ref, *swaps[12:],
        )

    return call(
        "decoder_core", ident, body,
        [unit, scale, fetched, cotangent, query_weight, wide, out_weight, up, down, shared, split],
        [
            shape(length, width), shape(length, width, dtype=BF16), shape(length, half, dtype=BF16),
            shape(length, width, dtype=BF16), shape(length, hidden_half, dtype=BF16),
            shape(length, width, dtype=BF16), shape(length, hidden_half, dtype=BF16), shape(1, hidden_half),
            shape(8, width), shape(8, width),
            shape(length, width, dtype=BF16), shape(length, half, dtype=BF16), shape(keys, 2 * half, dtype=BF16),
            shape(keys, width, dtype=BF16), shape(length, width), shape(1, 3 * half), shape(8, width),
        ],
        [
            held(length, half, dtype=BF16), held(keys, 2 * half, dtype=BF16), held(8, length),
            held(length, width), held(length, 1), held(length, width, dtype=BF16),
            held(length, hidden_half, dtype=BF16), held(length, width), held(length, 1),
            held(length, width), held(length, width), held(2, keys, span), held(half, keys, dtype=BF16),
            held(length, half, dtype=BF16),
        ]
        + Swap.scratch(tiles, width) * 4 + Swap.scratch(keys // ROWS, width),
    )


def decoder_self_backward(ident, grad_pre, mixed, attended, totals, wide, out_weight):
    queries, width = grad_pre.shape
    length, half = mixed.shape[0], out_weight.shape[0]

    def body(*refs):
        Swap.greet()
        self_backward_kernel(True, *refs)

    return call(
        "decoder_self_backward", ident, body, [grad_pre, mixed, attended, totals, wide, out_weight],
        [
            shape(queries, width, dtype=BF16), shape(queries, half, dtype=BF16), shape(length, 2 * half, dtype=BF16),
            shape(length, width), shape(1, 3 * half),
        ],
        [held(queries, half, dtype=BF16), held(half, length, dtype=BF16)] + Swap.scratch(length // ROWS, width),
    )


def encoder_backward(
    ident, grad, unit_two, scale_two, active, slope, up, down, unit_one, scale_one,
    mixed, attended, totals, wide, out_weight, shared,
):
    queries, width = grad.shape
    length, half, hidden_half = mixed.shape[0], out_weight.shape[0], up.shape[1]

    def body(
        grad_ref, unit_two_ref, scale_two_ref, active_ref, slope_ref, up_ref, down_ref, unit_one_ref, scale_one_ref,
        mixed_ref, attended_ref, totals_ref, wide_ref, out_weight_ref, shared_ref,
        feed_low_ref, grad_up_ref, up_bias_ref, sums_after_ref, sums_before_ref,
        low_ref, grad_query_ref, grad_pair_ref, grad_x_ref, sums_ref,
        grad_one_ref, inner_ref, grad_out_ref, turned_ref, *swaps,
    ):
        Swap.greet()
        feed_backward_kernel(
            grad_ref, unit_two_ref, scale_two_ref, active_ref, slope_ref, up_ref, down_ref,
            unit_one_ref, scale_one_ref, Rows(shared_ref, (4, 1)),
            feed_low_ref, grad_up_ref, up_bias_ref, grad_one_ref, sums_after_ref, sums_before_ref,
            inner_ref, *swaps[:4],
        )
        self_backward_kernel(
            False, grad_one_ref, mixed_ref, attended_ref, totals_ref, wide_ref, out_weight_ref,
            low_ref, grad_query_ref, grad_pair_ref, grad_x_ref, sums_ref, grad_out_ref, turned_ref, *swaps[4:],
        )

    return call(
        "encoder_backward", ident, body,
        [
            grad, unit_two, scale_two, active, slope, up, down, unit_one, scale_one,
            mixed, attended, totals, wide, out_weight, shared,
        ],
        [
            shape(queries, width, dtype=BF16), shape(queries, hidden_half, dtype=BF16), shape(1, hidden_half),
            shape(8, width), shape(8, width),
            shape(queries, width, dtype=BF16), shape(queries, half, dtype=BF16), shape(length, 2 * half, dtype=BF16),
            shape(length, width), shape(1, 3 * half),
        ],
        [
            held(queries, width), held(queries, width), held(queries, half, dtype=BF16),
            held(half, length, dtype=BF16),
        ]
        + Swap.scratch(queries // ROWS, width) + Swap.scratch(length // ROWS, width),
    )


def adam_vector(grad_value, value, first, second):
    new_first = BETA_ONE * first + (1.0 - BETA_ONE) * grad_value
    new_second = BETA_TWO * second + (1.0 - BETA_TWO) * grad_value * grad_value
    correct_one = 1.0 - BETA_ONE**STEP
    correct_two = 1.0 - BETA_TWO**STEP
    updated = value - VECTOR_RATE * (new_first / correct_one) / (
        jnp.sqrt(new_second / correct_two) + ADAM_EPSILON
    )
    return (new_first, new_second, updated)


def local(
    source_tokens,
    target_tokens,
    target_cotangent,
    retrieved,
    kept_mask,
    owner_slots,
    master,
    first_moment,
    second_moment,
    left_stats,
    right_stats,
    left_basis,
    right_basis,
    shared_vectors,
    shared_first,
    shared_second,
    split_vectors,
    split_first,
    split_second,
):
    tensor_count = lax.axis_size("tensor")
    device_count = lax.axis_size("dp")
    model_width = source_tokens.shape[1]
    tile_size = master.shape[2]
    hidden_width = (split_vectors.shape[1] - 3) * model_width
    half_width = model_width // tensor_count
    hidden_half = hidden_width // tensor_count
    qblocks = retrieved.shape[0]
    per_owner = retrieved.shape[1] // device_count
    me = lax.axis_index("dp")
    vectors = jnp.concatenate([shared_vectors, split_vectors[0]], 0)
    vector_count, vector_width = vectors.shape
    padded = -(-vector_count // 8) * 8
    small = jnp.concatenate(
        [
            jnp.pad(vectors, ((0, padded - vector_count), (0, TILE - vector_width))),
            retrieved.astype(jnp.float32).reshape(-1, TILE),
        ],
        0,
    )
    gathered, smalls = gather_all(master[0].astype(jnp.bfloat16), small, device_count)
    whole = (
        smalls[:, :vector_count, :vector_width]
        .transpose(1, 0, 2)
        .reshape(vector_count, model_width)
        .astype(jnp.bfloat16)
    )
    shared_count = shared_vectors.shape[0]
    shared_whole, split_whole = whole[:shared_count], whole[shared_count:]
    shapes = [s[1:] for s in matrix_list(model_width, hidden_width, tensor_count)]
    names = [s[0] for s in matrix_list(model_width, hidden_width, tensor_count)]
    weights = dict(zip(names, unpack_tiles(gathered, owner_slots, shapes)))
    shared = jnp.pad(shared_whole.astype(F32), ((0, 16 - shared_count), (0, 0)))
    split = split_whole.astype(F32).reshape(1, -1)
    start_row = jnp.argmax(kept_mask)
    turned = jnp.roll(source_tokens, -start_row, 0)

    (enc_mixed, enc_attended, enc_totals, unit_one, scale_one,
     states, stored, hidden_low, enc_active, enc_slope, unit_two, scale_two) = encoder_forward(
        10, turned, weights["enc_qkv"], weights["enc_out"], weights["enc_up"], weights["enc_down"],
        shared, split, KEEP,
    )
    encoder_states = jnp.roll(states, start_row, 0)

    wanted = (
        smalls[:, padded:].reshape(device_count, qblocks, device_count, per_owner)[:, :, me]
        .transpose(1, 0, 2)
        .astype(jnp.int32)
        - KEEP * me
    ).reshape(1, -1)
    matches = (wanted == lax.broadcasted_iota(jnp.int32, (KEEP, 1), 0)).astype(BF16)
    served = jnp.einsum("ka,kb->ab", matches, stored, preferred_element_type=F32).astype(BF16)
    fetched = lax.all_to_all(
        served.reshape(qblocks, device_count, per_owner, model_width),
        "dp", split_axis=1, concat_axis=1, tiled=True,
    ).reshape(-1, model_width)

    dec_mixed, dec_attended, dec_totals, unit_three, scale_three = decoder_self_forward(
        12, target_tokens, weights["dec_qkv"], weights["dec_out"], shared, split, hidden_half
    )
    (decoder_states, first_low, crs_attended, second_low, dec_active,
     dec_feed_low, dec_grad_up, dec_up_bias, sums_five, sums_four,
     crs_low, crs_grad_query, crs_grad_pair, fetched_low, grad_three, crs_sums, sums_three) = decoder_core(
        13, unit_three, scale_three, fetched, target_cotangent,
        weights["crs_q"], weights["crs_kv"], weights["crs_out"], weights["dec_up"], weights["dec_down"],
        shared, split,
    )
    returned = lax.all_to_all(
        fetched_low.reshape(qblocks, device_count, per_owner, model_width),
        "dp", split_axis=1, concat_axis=1, tiled=True,
    )
    dec_low, dec_grad_query, dec_grad_pair, target_grad, dec_sums = decoder_self_backward(
        17, grad_three, dec_mixed, dec_attended, dec_totals, weights["dec_qkv"], weights["dec_out"]
    )
    stored_grad = jnp.einsum(
        "ka,ab->kb", matches, returned.reshape(-1, model_width), preferred_element_type=F32
    )
    (enc_feed_low, enc_grad_up, enc_up_bias, sums_two, sums_one,
     enc_low, enc_grad_query, enc_grad_pair, grad_turned, enc_sums) = encoder_backward(
        18, stored_grad, unit_two, scale_two, enc_active, enc_slope, weights["enc_up"], weights["enc_down"],
        unit_one, scale_one, enc_mixed, enc_attended, enc_totals, weights["enc_qkv"], weights["enc_out"], shared,
    )
    source_grad = jnp.roll(grad_turned, start_row, 0)

    first_block, total_blocks = {}, 0
    for name, height, breadth in matrix_list(model_width, hidden_width, tensor_count):
        first_block[name] = total_blocks
        total_blocks += height // TILE * (breadth // TILE)
    three = 3 * half_width
    outer = ((0, half_width), (2 * half_width, three))
    everything = ((0, hidden_half),)
    items = [
        (sums, 3 * i, None) for i, sums in enumerate((sums_one, sums_two, sums_three, sums_four, sums_five))
    ]
    at = shared_count * model_width
    for array, pieces in (
        (enc_sums, outer), (enc_up_bias, everything), (dec_sums, outer), (crs_sums, outer), (dec_up_bias, everything)
    ):
        items.append((array, at, pieces))
        at += sum(end - begin for begin, end in pieces)
    (slot_grads,) = weight_grads(
        [
            (first_block["dec_down"], [(dec_active, dec_feed_low)]),
            (first_block["dec_up"], [(second_low, dec_grad_up)]),
            (first_block["crs_out"], [(crs_attended, crs_low)]),
            (first_block["crs_q"], [(first_low, crs_grad_query)]),
            (first_block["crs_kv"], [(fetched, crs_grad_pair)]),
            (first_block["dec_out"], [(dec_attended, dec_low)]),
            (first_block["dec_qkv"], [(target_tokens, dec_grad_query), (target_tokens, dec_grad_pair)]),
        ],
        owner_slots,
        gathered.shape[0],
    )
    slot_grads, vector_grads = weight_grads(
        [
            (first_block["enc_down"], [(enc_active, enc_feed_low)]),
            (first_block["enc_up"], [(hidden_low, enc_grad_up)]),
            (first_block["enc_out"], [(enc_attended, enc_low)]),
            (first_block["enc_qkv"], [(turned, enc_grad_query), (turned, enc_grad_pair)]),
        ],
        owner_slots,
        gathered.shape[0],
        slot_grads,
        (padded, model_width, items),
    )
    slots = master.shape[1]
    owned_slots = me * slots + lax.broadcasted_iota(jnp.int32, (slots, 1), 0)
    used = jnp.any(owned_slots == owner_slots[None, :], 1).astype(jnp.int32)
    results, vector_sums = owner_update(
        used,
        slot_grads,
        vector_grads,
        [
            array[0]
            for array in (
                master, first_moment, second_moment, left_stats, right_stats, left_basis, right_basis
            )
        ],
        device_count,
    )
    vector_owned = lax.dynamic_slice_in_dim(vector_sums, me * vector_width, vector_width, 1)
    shared_owned = vector_owned[:shared_count]
    split_owned = vector_owned[shared_count:vector_count]
    new_master, new_first, new_second, new_left, new_right, new_lbasis, new_rbasis = results
    shared_new_first, shared_new_second, shared_updated = adam_vector(
        shared_owned, shared_vectors, shared_first, shared_second
    )
    split_new_first, split_new_second, split_updated = adam_vector(
        split_owned, split_vectors[0], split_first[0], split_second[0]
    )
    return (
        encoder_states,
        decoder_states,
        source_grad,
        target_grad,
        new_master[None],
        new_first[None],
        new_second[None],
        new_left[None],
        new_right[None],
        new_lbasis[None],
        new_rbasis[None],
        shared_new_first,
        shared_new_second,
        shared_updated,
        split_new_first[None],
        split_new_second[None],
        split_updated[None],
    )


def solution(mesh):
    placed = (
        P("dp", None),
        P("dp", None),
        P("dp", None),
        P("dp", None),
        P("dp"),
        P(),
        P("tensor", "dp", None, None),
        P("tensor", "dp", None, None),
        P("tensor", "dp", None, None),
        P("tensor", "dp", None, None),
        P("tensor", "dp", None, None),
        P("tensor", "dp", None, None),
        P("tensor", "dp", None, None),
        P(None, "dp"),
        P(None, "dp"),
        P(None, "dp"),
        P("tensor", None, "dp"),
        P("tensor", None, "dp"),
        P("tensor", None, "dp"),
    )
    return jax.shard_map(
        local,
        mesh=mesh,
        in_specs=placed,
        out_specs=(
            P("dp", None),
            P("dp", None),
            P("dp", None),
            P("dp", None),
            P("tensor", "dp", None, None),
            P("tensor", "dp", None, None),
            P("tensor", "dp", None, None),
            P("tensor", "dp", None, None),
            P("tensor", "dp", None, None),
            P("tensor", "dp", None, None),
            P("tensor", "dp", None, None),
            P(None, "dp"),
            P(None, "dp"),
            P(None, "dp"),
            P("tensor", None, "dp"),
            P("tensor", None, "dp"),
            P("tensor", None, "dp"),
        ),
        check_vma=False,
    )
```

```python
import functools
from functools import partial

import jax
import jax.numpy as jnp
from jax import lax
from jax.experimental import pallas as pl
from jax.experimental.pallas import tpu as pltpu
from jax.sharding import PartitionSpec as P

HD = 64
KEEP = 512
STEP = 10


BETA_ONE = 0.9
BETA_TWO = 0.95
ADAM_EPSILON = 1e-08
MATRIX_RATE = 0.1
VECTOR_RATE = 0.5
WEIGHT_DECAY = 0.01
NORM_EPSILON = 1e-05
TILE = 128
PANEL = 32
ROWS = 256
KEYS = 256
PAIR = 2 * HD
NN = ((1,), (0,))
NT = ((1,), (1,))
F32 = jnp.float32
BF16 = jnp.bfloat16
MESH = pl.DeviceIdType.MESH
ANY = pl.BlockSpec(memory_space=pl.ANY)


def matrix_list(model_width, hidden_width, tensor_count):
    half_width = model_width // tensor_count
    hidden_half = hidden_width // tensor_count
    return [
        ("enc_qkv", model_width, 3 * half_width),
        ("enc_out", half_width, model_width),
        ("enc_up", model_width, hidden_half),
        ("enc_down", hidden_half, model_width),
        ("dec_qkv", model_width, 3 * half_width),
        ("dec_out", half_width, model_width),
        ("crs_q", model_width, half_width),
        ("crs_kv", model_width, 2 * half_width),
        ("crs_out", half_width, model_width),
        ("dec_up", model_width, hidden_half),
        ("dec_down", hidden_half, model_width),
    ]


def halves(x):
    high = x.astype(BF16)
    return high, (x - high.astype(F32)).astype(BF16)


def mm(a, b, dims=NN):
    ah, al = halves(a)
    bh, bl = halves(b)
    return times(jnp.concatenate([ah, ah, al], 1), jnp.concatenate([bh, bl, bh], dims[1][0]), dims)


def chip_grid(device_count):
    if device_count == 16:
        return 4, 2, 2
    side = round(device_count ** (1 / 3))
    if side**3 == device_count:
        return side, side, side
    return 1, 1, device_count


def place(grid):
    zs, ys, xs = grid
    me = lax.axis_index("dp")
    return me // (ys * xs), lax.rem(me // xs, ys), lax.rem(me, xs)


def peers(grid):
    zs, ys, xs = grid
    z, y, x = place(grid)

    def device(zz, yy, xx):
        return {"dp": (zz * ys + yy) * xs + xx}

    return (
        lambda k: device(lax.rem(z + k, zs), y, x),
        lambda k: device(z, lax.rem(y + k, ys), x),
        lambda k: device(z, y, lax.rem(x + k, xs)),
    )


def greet(grid):
    barrier = pltpu.get_barrier_semaphore()
    count = 0
    for size, peer in zip(grid, peers(grid)):
        for k in range(1, size):
            pl.semaphore_signal(barrier, inc=1, device_id=peer(k), device_id_type=MESH)
            count += 1
    pl.semaphore_wait(barrier, count)


def remote(src, dst, send, recv, device):
    return pltpu.make_async_remote_copy(
        src_ref=src, dst_ref=dst, send_sem=send, recv_sem=recv, device_id=device, device_id_type=MESH
    )


def chunking(slots):
    half = slots // 2
    chunks = min(16, half)
    return half, chunks, half // chunks


def owner_kernel(grid, *refs):
    zs, ys, xs = grid
    used_ref, in_ref, small_ref = refs[:3]
    state_in, state_out, small_out_ref, work_out_ref = refs[3:10], refs[10:17], refs[17], refs[18]
    state, rest = refs[19:26], refs[26:]
    (own0, own1, ra0, ra1, rb0, rb1, rc0, rc1, total, rs_z, rs_y, rs_x, work, load_sem,
     as0, as1, ar0, ar1, bs0, bs1, br0, br1, cs0, cs1, cr0, cr1,
     ssz, ssy, ssx, srz, sry, srx, state_sem) = rest
    own, rec_a, rec_b, rec_c = (own0, own1), (ra0, ra1), (rb0, rb1), (rc0, rc1)
    a_send, a_recv, b_send, b_recv, c_send, c_recv = (as0, as1), (ar0, ar1), (bs0, bs1), (br0, br1), (cs0, cs1), (cr0, cr1)
    rec_s, s_send, s_recv = (rs_z, rs_y, rs_x), (ssz, ssy, ssx), (srz, sry, srx)

    z, y, x = place(grid)
    tos = peers(grid)
    to_z, to_y, to_x = tos
    slots = state[0].shape[0]
    half = slots // 2
    first = ((xs, x, to_x), (ys, y, to_y))
    second = ((ys, y, to_y), (xs, x, to_x))

    def source(g, c, other):
        slot = g * half + c
        return in_ref.at[:, :, other, slot] if g == 0 else in_ref.at[:, other, :, slot]

    def load(g, c):
        return pltpu.make_async_copy(source(g, c, first[g][1]), own[g].at[c], load_sem.at[g, c])

    def send_a(g, c, k):
        count, mine, to = first[g]
        return remote(source(g, c, lax.rem(mine + k, count)), rec_a[g].at[c, k - 1],
                      a_send[g].at[c, k - 1], a_recv[g].at[c, k - 1], to(k))

    def send_b(g, c, k):
        count, mine, to = second[g]
        return remote(own[g].at[c, :, lax.rem(mine + k, count)], rec_b[g].at[c, k - 1],
                      b_send[g].at[c, k - 1], b_recv[g].at[c, k - 1], to(k))

    def send_c(g, c, k):
        return remote(own[g].at[c, lax.rem(z + k, zs), second[g][1]], rec_c[g].at[c, k - 1],
                      c_send[g].at[c, k - 1], c_recv[g].at[c, k - 1], to_z(k))

    def start_a(c):
        for g in range(2):
            for k in range(1, first[g][0]):
                send_a(g, c, k).start()

    def send_s(axis, k):
        return remote(total.at[2 - axis], rec_s[axis].at[k - 1],
                      s_send[axis].at[k - 1], s_recv[axis].at[k - 1], tos[axis](k))

    def small_start(axis):
        for k in range(1, grid[axis]):
            send_s(axis, k).start()

    def small_add(axis):
        value = total[2 - axis]
        for k in range(1, grid[axis]):
            send_s(axis, k).wait_recv()
            value += rec_s[axis][k - 1]
        return value

    def each(count, action):
        def go(c, carry):
            action(c)
            return carry

        lax.fori_loop(0, count, go, 0)

    def load_all(c):
        for g in range(2):
            load(g, c).start()

    each(half, load_all)
    for i in range(7):
        pltpu.make_async_copy(state_in[i], state[i], state_sem.at[0, i]).start()
    total[0] = small_ref[...]
    greet(grid)
    small_start(2)
    start_a(0)
    total[1] = small_add(2)
    small_start(1)
    total[2] = small_add(1)
    small_start(0)
    for i in range(7):
        pltpu.make_async_copy(state_in[i], state[i], state_sem.at[0, i]).wait()

    def step_a(c):
        for g in range(2):
            load(g, c).wait()
            for k in range(1, first[g][0]):
                send_a(g, c, k).wait_recv()

        @pl.when(c + 1 < half)
        def _():
            start_a(c + 1)

        for g in range(2):
            n2 = second[g][0]

            def add(e, carry, g=g, n2=n2):
                a, b = e // n2, lax.rem(e, n2)
                value = own[g][c, a, b].astype(F32)
                for k in range(1, first[g][0]):
                    value += rec_a[g][c, k - 1, a, b].astype(F32)
                own[g][c, a, b] = value.astype(BF16)
                return carry

            lax.fori_loop(0, zs * n2, add, 0)
            for k in range(1, n2):
                send_b(g, c, k).start()

    def step_b(c):
        for g in range(2):
            n2, mine = second[g][0], second[g][1]
            for k in range(1, n2):
                send_b(g, c, k).wait_recv()

            def add(a, carry, g=g, n2=n2, mine=mine):
                value = own[g][c, a, mine].astype(F32)
                for k in range(1, n2):
                    value += rec_b[g][c, k - 1, a].astype(F32)
                own[g][c, a, mine] = value.astype(BF16)
                return carry

            lax.fori_loop(0, zs, add, 0)
            for k in range(1, zs):
                send_c(g, c, k).start()

    def step_c(c):
        batch = lax.rem(c // 4, 2)
        for g in range(2):
            for k in range(1, zs):
                send_c(g, c, k).wait_recv()
        for g in range(2):
            value = own[g][c, z, second[g][1]].astype(F32)
            for k in range(1, zs):
                value += rec_c[g][c, k - 1].astype(F32)
            slot = g * half + c
            value = jnp.where(used_ref[slot] > 0, value, 0.0)
            soap_products(value, slot, state, work, batch, 2 * (4 * g + lax.rem(c, 4)))

    def finish(b):
        batch = lax.rem(b, 2)
        place_bases(work, batch, state[5], state[6], 4 * b)
        emit(b)

    def emit(b):
        for g in range(2):
            span = pl.ds(g * half + 4 * b, 4)
            for i in range(7):
                pltpu.make_async_copy(state[i].at[span], state_out[i].at[span], state_sem.at[1, i]).start()

    def round_of(r, carry):
        for s in range(4):
            t = 4 * r + s

            @pl.when(t < half)
            def _(t=t):
                step_a(t)

            @pl.when((t >= 1) & (t <= half))
            def _(t=t):
                step_b(t - 1)

            @pl.when((t >= 2) & (t < half + 2))
            def _(t=t):
                step_c(t - 2)

            if s >= 1:

                @pl.when((r >= 1) & (r < half // 4))
                def _(s=s):
                    b = r - 1
                    for p in ((0,), (1,), (2, 3))[s - 1]:
                        panel_step(work, lax.rem(b, 2), p)
                    if s == 3:
                        finish(b)

        return carry

    lax.fori_loop(0, half // 4 + 1, round_of, 0)
    emit(half // 4 - 1)
    work_out_ref[...] = work[(half // 4 - 1) % 2]
    small_out_ref[...] = small_add(0)
    for axis in range(3):
        for k in range(1, grid[axis]):
            send_s(axis, k).wait_send()

    def end(c):
        for g in range(2):
            for k in range(1, first[g][0]):
                send_a(g, c, k).wait_send()
            for k in range(1, second[g][0]):
                send_b(g, c, k).wait_send()
            for k in range(1, zs):
                send_c(g, c, k).wait_send()

    each(half, end)
    for i in range(7):
        pltpu.make_async_copy(state[i], state_out[i], state_sem.at[1, i]).wait()


def place_bases(work, batch, left_ref, right_ref, at):
    half = left_ref.shape[0] // 2
    for g in range(2):
        for e in range(4):
            left_ref[g * half + at + e] = work[batch, 2 * (4 * g + e), :, TILE:].T
            right_ref[g * half + at + e] = work[batch, 2 * (4 * g + e) + 1, :, TILE:].T


def last_bases_kernel(work_ref, *refs):
    state_in, state_out, state, work, sems = refs[:7], refs[7:14], refs[14:21], refs[21], refs[22]
    half = state[0].shape[0] // 2

    def copy_in(i):
        return pltpu.make_async_copy(state_in[i], state[i], sems.at[0, i])

    def copy_out(i):
        return pltpu.make_async_copy(state[i], state_out[i], sems.at[1, i])

    for i in range(7):
        copy_in(i).start()
    work[0] = work_ref[...]
    panel_step(work, 0, 0)
    for i in range(7):
        copy_in(i).wait()
        if i < 5:
            copy_out(i).start()
    for p in range(1, TILE // PANEL):
        panel_step(work, 0, p)
    place_bases(work, 0, state[5], state[6], half - 4)
    for i in range(5, 7):
        copy_out(i).start()
    for i in range(7):
        copy_out(i).wait()


def last_bases(work, state):
    whole = state[0].shape
    return pl.pallas_call(
        last_bases_kernel,
        out_shape=[jax.ShapeDtypeStruct(whole, F32)] * 7,
        in_specs=[pl.BlockSpec(memory_space=pltpu.VMEM)] + [ANY] * 7,
        out_specs=[ANY] * 7,
        scratch_shapes=[pltpu.VMEM(whole, F32)] * 7
        + [pltpu.VMEM((1,) + work.shape, F32), pltpu.SemaphoreType.DMA((2, 7))],
        compiler_params=pltpu.CompilerParams(vmem_limit_bytes=56 << 20),
        name="last_bases",
    )(work, *state)


def soap_products(g, i, state, work, batch, at):
    w_ref, m_ref, v_ref, l_ref, r_ref, ql_ref, qr_ref = state
    c1 = 1.0 - BETA_ONE**STEP
    c2 = 1.0 - BETA_TWO**STEP
    ql = ql_ref[i]
    qr = qr_ref[i]
    gt = g.T
    nm = BETA_ONE * m_ref[i] + (1.0 - BETA_ONE) * g
    m_ref[i] = nm
    side = mm(jnp.concatenate([g, nm], 0), qr)
    both = mm(ql.T, jnp.concatenate([side[:TILE], side[TILE:]], 1))
    rotated, rotated_first = both[:, :TILE], both[:, TILE:]
    nv = BETA_TWO * v_ref[i] + (1.0 - BETA_TWO) * rotated * rotated
    v_ref[i] = nv
    normed = rotated_first / c1 / (jnp.sqrt(nv / c2) + ADAM_EPSILON)
    step = mm(mm(ql, normed), qr, NT)
    w = w_ref[i]
    w_ref[i] = w - MATRIX_RATE * step - MATRIX_RATE * WEIGHT_DECAY * w
    for k, (ref, turn, left, right) in enumerate(((l_ref, ql, g, gt), (r_ref, qr, gt, g))):
        stat = BETA_TWO * ref[i] + (1.0 - BETA_TWO) * mm(left, right)
        ref[i] = stat
        a = mm(stat, turn)
        at_turned = a.T
        work[batch, at + k, :, :TILE] = mm(at_turned, a)
        work[batch, at + k, :, TILE:] = at_turned


def panel_step(work, batch, p):
    count = work.shape[1]
    per = TILE // (2 * PANEL)
    r0 = p * PANEL
    rows = count // per * 8
    lane = lax.broadcasted_iota(jnp.int32, (rows, TILE), 1)
    start = lane // (2 * PANEL) * (2 * PANEL)
    row = lax.rem(lax.broadcasted_iota(jnp.int32, (rows, TILE), 0), 8)
    sub = lax.broadcasted_iota(jnp.int32, (count // per, 8, TILE), 1)
    eye = (
        lax.broadcasted_iota(jnp.int32, (PANEL, PANEL), 0) == lax.broadcasted_iota(jnp.int32, (PANEL, PANEL), 1)
    ).astype(F32)
    packs = []
    for q in range(count // per):
        pieces = []
        for k in range(per):
            pieces += [work[batch, q * per + k, r0:r0 + PANEL, r0:r0 + PANEL], eye]
        packs.append(jnp.concatenate(pieces, 1)[None])
    x = jnp.concatenate(packs, 0)
    strips = [x[:, 8 * e:8 * e + 8, :] for e in range(PANEL // 8)]

    def segment(strip, index):
        return jnp.take_along_axis(strip.reshape(-1, TILE), index, axis=1).reshape(strip.shape)

    for j in range(0, PANEL, 2):
        e0, here = j // 8, j % 8
        one = [segment(strip, start + j) for strip in strips[e0:]]
        two = [segment(strip, start + j + 1) for strip in strips[e0:]]
        corner = one[0][:, here:here + 1, :]
        side = one[0][:, here + 1:here + 2, :]
        inverse = 1.0 / corner
        inverse_two = corner * (1.0 / (corner * two[0][:, here + 1:here + 2, :] - side * side))
        shift = side * inverse
        ratio = strips[e0][:, here:here + 1, :] * inverse
        next_off = side * ratio
        ratio_two = (strips[e0][:, here + 1:here + 2, :] - next_off) * inverse_two
        ratio_one = ratio - shift * ratio_two
        for e in range(e0, PANEL // 8):
            change = one[e - e0] * ratio_one + two[e - e0] * ratio_two
            if e == e0:
                change = jnp.where(sub > here + 1, change, jnp.where(sub == here + 1, next_off, 0.0))
            strips[e] = strips[e] - change
    for e in range(PANEL // 8):
        strips[e] = strips[e] * lax.rsqrt(segment(strips[e], start + 8 * e + row))
    x = jnp.concatenate(strips, 1)
    for q in range(count // per):
        for k in range(per):
            i = q * per + k
            inverse = x[q, :, 2 * PANEL * k + PANEL:2 * PANEL * (k + 1)]
            u = mm(inverse, work[batch, i, r0:r0 + PANEL, :])
            work[batch, i, r0:r0 + PANEL, TILE:] = u[:, TILE:]
            if r0 + PANEL < TILE:
                high, low = halves(u)
                left = jnp.concatenate([u[:, :TILE], u[:, :TILE], low[:, :TILE].astype(F32)], 0).T
                work[batch, i, r0 + PANEL:, :] -= times(
                    left[r0 + PANEL:, :].astype(BF16), jnp.concatenate([high, low, high], 0)
                )


def some(shape):
    return tuple(max(1, s) for s in shape)


def owner_update(used, slot_grads, small, state, device_count):
    grid = chip_grid(device_count)
    zs, ys, xs = grid
    slots = slot_grads.shape[0] // device_count
    half = slots // 2
    block = (TILE, TILE)
    dma = pltpu.SemaphoreType.DMA
    firsts, seconds = (xs, ys), (ys, xs)
    whole = (slots,) + block
    scratch = (
        [pltpu.VMEM(whole, F32)] * 7
        + [pltpu.VMEM((half, zs, seconds[g]) + block, BF16) for g in range(2)]
        + [pltpu.VMEM(some((half, firsts[g] - 1, zs, seconds[g])) + block, BF16) for g in range(2)]
        + [pltpu.VMEM(some((half, seconds[g] - 1, zs)) + block, BF16) for g in range(2)]
        + [pltpu.VMEM(some((half, zs - 1)) + block, BF16) for g in range(2)]
        + [pltpu.VMEM((3,) + small.shape, F32)]
        + [pltpu.VMEM((max(1, n - 1),) + small.shape, F32) for n in grid]
        + [pltpu.VMEM((2, 16, TILE, 2 * TILE), F32)]
        + [dma((2, half))]
        + [dma(some((half, firsts[g] - 1))) for g in range(2)] * 2
        + [dma(some((half, seconds[g] - 1))) for g in range(2)] * 2
        + [dma(some((half, zs - 1))) for g in range(2)] * 2
        + [dma((max(1, n - 1),)) for n in grid] * 2
        + [dma((2, 7))]
    )
    results = pl.pallas_call(
        functools.partial(owner_kernel, grid),
        out_shape=[jax.ShapeDtypeStruct(whole, F32)] * 7
        + [jax.ShapeDtypeStruct(small.shape, F32), jax.ShapeDtypeStruct((16, TILE, 2 * TILE), F32)],
        in_specs=[pl.BlockSpec(memory_space=pltpu.SMEM), ANY, pl.BlockSpec(memory_space=pltpu.VMEM)] + [ANY] * 7,
        out_specs=[ANY] * 7 + [pl.BlockSpec(memory_space=pltpu.VMEM)] * 2,
        scratch_shapes=scratch,
        compiler_params=pltpu.CompilerParams(collective_id=1, has_side_effects=True, vmem_limit_bytes=56 << 20),
        name="owner_update",
    )(used, slot_grads.reshape(zs, ys, xs, slots, TILE, TILE), small, *state)
    return last_bases(results[8], results[:7]), results[7]


def ag_kernel(grid, own_ref, small_ref, out_ref, small_out_ref,
              load_sem, z_send, z_recv, b_send0, b_send1, b_recv0, b_recv1, a_send0, a_send1, a_recv0, a_recv1,
              s_load, ssz, ssy, ssx, srz, sry, srx):
    zs, ys, xs = grid
    z, y, x = place(grid)
    tos = peers(grid)
    to_z, to_y, to_x = tos
    slots = own_ref.shape[0]
    half, chunks, size = chunking(slots)
    first = ((xs, to_x), (ys, to_y))
    second = ((ys, to_y), (xs, to_x))
    b_send, b_recv, a_send, a_recv = (b_send0, b_send1), (b_recv0, b_recv1), (a_send0, a_send1), (a_recv0, a_recv1)
    s_send, s_recv = (ssz, ssy, ssx), (srz, sry, srx)

    def span(g, c):
        return pl.ds(g * half + c * size, size)

    def send_z(g, c, k):
        return remote(own_ref.at[span(g, c)], out_ref.at[z, y, x, span(g, c)],
                      z_send.at[g, c, k - 1], z_recv.at[g, c, k - 1], to_z(k))

    def send_b(g, c, k):
        part = out_ref.at[:, y, x, span(g, c)]
        return remote(part, part, b_send[g].at[c, k - 1], b_recv[g].at[c, k - 1], second[g][1](k))

    def send_a(g, c, k):
        part = out_ref.at[:, :, x, span(g, c)] if g == 0 else out_ref.at[:, y, :, span(g, c)]
        return remote(part, part, a_send[g].at[c, k - 1], a_recv[g].at[c, k - 1], first[g][1](k))

    def send_s(axis, k):
        if axis == 0:
            source, target = small_ref, small_out_ref.at[z, y, x]
        else:
            source = target = small_out_ref.at[:, y, x] if axis == 1 else small_out_ref.at[:, :, x]
        return remote(source, target, s_send[axis].at[k - 1], s_recv[axis].at[k - 1], tos[axis](k))

    keep = pltpu.make_async_copy(own_ref, out_ref.at[z, y, x], load_sem)
    keep_small = pltpu.make_async_copy(small_ref, small_out_ref.at[z, y, x], s_load)
    keep.start()
    keep_small.start()
    greet(grid)

    for k in range(1, grid[0]):
        send_s(0, k).start()
    def start_z(c):
        for g in range(2):
            for k in range(1, zs):
                send_z(g, c, k).start()

    def small_wait(axis):
        for k in range(1, grid[axis]):
            send_s(axis, k).wait_recv()

    def small_start(axis):
        for k in range(1, grid[axis]):
            send_s(axis, k).start()

    start_z(0)
    for t in range(chunks + 1):
        if t < chunks:
            for g in range(2):
                for k in range(1, zs):
                    send_z(g, t, k).wait_recv()
            if t == 0:
                keep.wait()
                keep_small.wait()
                small_wait(0)
                small_start(1)
            if t + 1 < chunks:
                start_z(t + 1)
            for g in range(2):
                for k in range(1, second[g][0]):
                    send_b(g, t, k).start()
        if t >= 1:
            for g in range(2):
                for k in range(1, second[g][0]):
                    send_b(g, t - 1, k).wait_recv()
                for k in range(1, first[g][0]):
                    send_a(g, t - 1, k).start()
        if t == 1:
            small_wait(1)
            small_start(2)
    small_wait(2)
    for c in range(chunks):
        for g in range(2):
            for k in range(1, first[g][0]):
                send_a(g, c, k).wait_recv()
    for axis in range(3):
        for k in range(1, grid[axis]):
            send_s(axis, k).wait_send()
    for c in range(chunks):
        for g in range(2):
            for k in range(1, zs):
                send_z(g, c, k).wait_send()
            for k in range(1, second[g][0]):
                send_b(g, c, k).wait_send()
            for k in range(1, first[g][0]):
                send_a(g, c, k).wait_send()


def gather_all(own, small, device_count):
    grid = chip_grid(device_count)
    zs, ys, xs = grid
    slots = own.shape[0]
    half, chunks, size = chunking(slots)
    dma = pltpu.SemaphoreType.DMA
    firsts, seconds = (xs, ys), (ys, xs)
    scratch = (
        [dma, dma(some((2, chunks, zs - 1))), dma(some((2, chunks, zs - 1)))]
        + [dma(some((chunks, seconds[g] - 1))) for g in range(2)] * 2
        + [dma(some((chunks, firsts[g] - 1))) for g in range(2)] * 2
        + [dma]
        + [dma((max(1, n - 1),)) for n in grid] * 2
    )
    blocks, smalls = pl.pallas_call(
        functools.partial(ag_kernel, grid),
        out_shape=[jax.ShapeDtypeStruct(grid + own.shape, own.dtype), jax.ShapeDtypeStruct(grid + small.shape, small.dtype)],
        in_specs=[pl.BlockSpec(memory_space=pltpu.VMEM)] * 2,
        out_specs=[ANY, ANY],
        scratch_shapes=scratch,
        compiler_params=pltpu.CompilerParams(collective_id=2, has_side_effects=True),
        name="gather_all",
    )(own, small)
    return blocks.reshape((-1,) + own.shape[1:]), smalls.reshape((-1,) + small.shape)


def unpack_kernel(shapes, slots_ref, packed, *refs):
    count = len(shapes)
    mats, held, sems = refs[:count], refs[count:-1], refs[-1]

    def whole(index):
        return pltpu.make_async_copy(held[index], mats[index], sems.at[1, index])

    offset = 0
    for index, (height, breadth) in enumerate(shapes):
        down, across = height // TILE, breadth // TILE

        def start(i, carry, index=index, offset=offset, across=across):
            for j in range(across):
                tile = held[index].at[pl.ds(pl.multiple_of(i * TILE, TILE), TILE), j * TILE:(j + 1) * TILE]
                slot = packed.at[slots_ref[offset + i * across + j]]
                pltpu.make_async_copy(slot, tile, sems.at[0, index]).start()
            return carry

        lax.fori_loop(0, down, start, 0)
        offset += down * across
    for index in range(count):
        pltpu.make_async_copy(held[index], held[index], sems.at[0, index]).wait()
        whole(index).start()
    for index in range(count):
        whole(index).wait()


def unpack_tiles(packed, slots, shapes):
    return pl.pallas_call(
        functools.partial(unpack_kernel, shapes),
        out_shape=[jax.ShapeDtypeStruct(s, packed.dtype) for s in shapes],
        in_specs=[pl.BlockSpec(memory_space=pltpu.SMEM), ANY],
        out_specs=[ANY] * len(shapes),
        scratch_shapes=[pltpu.VMEM(s, packed.dtype) for s in shapes] + [pltpu.SemaphoreType.DMA((2, len(shapes)))],
        compiler_params=pltpu.CompilerParams(vmem_limit_bytes=56 << 20),
        name="unpack_tiles",
    )(slots, packed)


def weight_grads_kernel(plan, used, vectors, passed, slots_ref, *refs):
    arrays, refs = refs[:used], refs[used:]
    given, refs = refs[:len(vectors)], refs[len(vectors):]
    refs = refs[passed:]
    packed, refs = refs[0], refs[1:]
    if vectors:
        rows_ref, refs = refs[0], refs[1:]
    held, refs = refs[:used], refs[used:]
    turned, refs = refs[0], refs[1:]
    results, sems = refs[:len(plan)], refs[len(plan):]
    load_sem, store_sem = sems

    def load(i):
        return pltpu.make_async_copy(arrays[i], held[i], load_sem.at[i])

    order = []
    for left, tokens, right, *rest in plan:
        for i in (left, right):
            if i not in order:
                order.append(i)
    for i in order:
        load(i).start()
    if vectors:
        width = rows_ref.shape[1]
        rows_ref[...] = jnp.zeros_like(rows_ref)
        for source, (at, pieces) in zip(given, vectors):
            if pieces is None:
                rows_ref[at:at + 3, :] = source[0:3, :]
                continue
            for begin, end in pieces:
                while begin < end:
                    lane = at % width
                    size = min(end - begin, width - lane)
                    rows_ref[at // width:at // width + 1, lane:lane + size] = source[:, begin:begin + size]
                    begin, at = begin + size, at + size
    ready = set()
    last = None
    for index, (left, tokens, right, offset, stride, down, across) in enumerate(plan):
        for i in (left, right):
            if i not in ready:
                ready.add(i)
                load(i).wait()
        height = down * TILE
        if last != (left, tokens):
            for j in range(down):
                turned[j * TILE:(j + 1) * TILE, :tokens] = (
                    held[left][:tokens, j * TILE:(j + 1) * TILE].astype(F32).T.astype(BF16)
                )
            last = (left, tokens)
        result = results[index]
        group = 3 if across % 3 == 0 else 1

        def columns(n, carry, right=right, tokens=tokens, height=height, result=result, offset=offset,
                    stride=stride, down=down, group=group, index=index):
            lanes = pl.ds(pl.multiple_of(n * group * TILE, TILE), group * TILE)
            result[:, lanes] = times(turned[:height, :tokens], held[right][:tokens, lanes]).astype(BF16)

            def send(i, carry):
                for j in range(group):
                    tile = result.at[
                        pl.ds(pl.multiple_of(i * TILE, TILE), TILE),
                        pl.ds(pl.multiple_of((n * group + j) * TILE, TILE), TILE),
                    ]
                    slot = packed.at[slots_ref[offset + i * stride + n * group + j]]
                    pltpu.make_async_copy(tile, slot, store_sem.at[index]).start()
                return carry

            lax.fori_loop(0, down, send, 0)
            return carry

        lax.fori_loop(0, across // group, columns, 0)
    for index in range(len(plan)):
        pltpu.make_async_copy(results[index], results[index], store_sem.at[index]).wait()


def weight_grads(matrices, slots, slot_count, packed=None, vectors=None):
    arrays, plan, results = [], [], []

    def index_of(array):
        for i, other in enumerate(arrays):
            if other is array:
                return i
        arrays.append(array)
        return len(arrays) - 1

    for offset, parts in matrices:
        height = parts[0][0].shape[1]
        stride = sum(right.shape[1] for left, right in parts) // TILE
        for left, right in parts:
            across = right.shape[1] // TILE
            plan.append((index_of(left), right.shape[0], index_of(right), offset, stride, height // TILE, across))
            results.append(pltpu.VMEM((height, right.shape[1]), BF16))
            offset += across
    tall = max(entry[5] for entry in plan) * TILE
    long = max(entry[1] for entry in plan)
    out_shape = [jax.ShapeDtypeStruct((slot_count, TILE, TILE), BF16)]
    given, layout = [], []
    if vectors:
        rows, width, items = vectors
        out_shape.append(jax.ShapeDtypeStruct((rows, width), F32))
        given = [item[0] for item in items]
        layout = [item[1:] for item in items]
    passed = [] if packed is None else [packed]
    return pl.pallas_call(
        functools.partial(weight_grads_kernel, plan, len(arrays), layout, len(passed)),
        out_shape=out_shape,
        in_specs=[pl.BlockSpec(memory_space=pltpu.SMEM)] + [ANY] * len(arrays)
        + [pl.BlockSpec(memory_space=pltpu.VMEM)] * len(given) + [ANY] * len(passed),
        out_specs=[ANY] + [pl.BlockSpec(memory_space=pltpu.VMEM)] * (len(out_shape) - 1),
        scratch_shapes=[pltpu.VMEM(a.shape, a.dtype) for a in arrays] + [pltpu.VMEM((tall, long), BF16)] + results
        + [pltpu.SemaphoreType.DMA((len(arrays),)), pltpu.SemaphoreType.DMA((len(plan),))],
        input_output_aliases={} if packed is None else {1 + len(arrays) + len(given): 0},
        compiler_params=pltpu.CompilerParams(vmem_limit_bytes=56 << 20),
        name="weight_grads",
    )(slots, *arrays, *given, *passed)


VM = pl.BlockSpec(memory_space=pltpu.VMEM)


def times(left, right, dims=NN):
    return lax.dot_general(left, right, (dims, ((), ())), preferred_element_type=F32)


def rows_of(t, size=ROWS):
    return pl.ds(pl.multiple_of(t * size, size), size)


class Swap:
    def __init__(self, out, into, send_sem, recv_sem):
        self.out, self.into, self.send_sem, self.recv_sem = out, into, send_sem, recv_sem

    @staticmethod
    def scratch(tiles, width):
        dma = pltpu.SemaphoreType.DMA((tiles,))
        held = pltpu.VMEM((tiles, ROWS, width), BF16)
        return [held, held, dma, dma]

    @staticmethod
    def greet():
        barrier = pltpu.get_barrier_semaphore()
        other = {"tensor": 1 - lax.axis_index("tensor")}
        pl.semaphore_signal(barrier, inc=1, device_id=other, device_id_type=MESH)
        pl.semaphore_wait(barrier, 1)

    def copy(self, t):
        return pltpu.make_async_remote_copy(
            src_ref=self.out.at[t],
            dst_ref=self.into.at[t],
            send_sem=self.send_sem.at[t],
            recv_sem=self.recv_sem.at[t],
            device_id={"tensor": 1 - lax.axis_index("tensor")},
            device_id_type=MESH,
        )

    def give(self, t, value):
        self.out[t] = value.astype(BF16)
        self.copy(t).start()

    def take(self, t):
        self.copy(t).wait()
        return self.out[t].astype(F32) + self.into[t].astype(F32)


class Rows:
    def __init__(self, ref, rows):
        self.ref, self.rows = ref, rows

    def __getitem__(self, index):
        at = self.rows[index[0].start]
        return self.ref[at:at + 1, :]


def bias_places(half, hidden_half):
    places, at = {}, 0
    for name, length in (
        ("enc_q", half), ("enc_v", half), ("enc_up", hidden_half), ("dec_q", half), ("dec_v", half),
        ("crs_q", half), ("crs_v", half), ("dec_up", hidden_half),
    ):
        places[name] = slice(at, at + length)
        at += length
    return places


def bias_row(split_ref, places, names, half):
    zero = jnp.zeros((1, half), F32)
    return jnp.concatenate([zero if name is None else split_ref[:, places[name]] for name in names], 1)


def standardize(values):
    center = values - jnp.mean(values, -1, keepdims=True)
    scale = lax.rsqrt(jnp.mean(center * center, -1, keepdims=True) + NORM_EPSILON)
    return center * scale, scale


def norm_back(grad, unit, scale, gain):
    inner = grad * gain
    return scale * (
        inner - jnp.mean(inner, -1, keepdims=True) - unit * jnp.mean(inner * unit, -1, keepdims=True)
    )


def add_sums(sums_ref, grad_in, grad_out, unit):
    sums_ref[0:1, :] += jnp.sum(grad_in, 0, keepdims=True)
    sums_ref[1:2, :] += jnp.sum(grad_out * unit, 0, keepdims=True)
    sums_ref[2:3, :] += jnp.sum(grad_out, 0, keepdims=True)


def head_mask(shape):
    return lax.broadcasted_iota(jnp.int32, shape, 1) < HD


def attend(query_ref, key_ref, value_ref, attended_ref, totals_ref, score_ref, turned_ref, causal, span):
    queries, keys = query_ref.shape[0], key_ref.shape[0]
    pairs = query_ref.shape[1] // PAIR
    chunks = keys // KEYS
    for j in range(pairs):
        turned_ref[j * PAIR:(j + 1) * PAIR, :] = (
            value_ref[:, j * PAIR:(j + 1) * PAIR].astype(F32).T.astype(BF16)
        )
    for i in range(queries // span):
        mine = slice(i * span, (i + 1) * span)

        def pair(j, carry, i=i, mine=mine):
            lanes = pl.ds(pl.multiple_of(j * PAIR, PAIR), PAIR)
            query = query_ref[mine, lanes] * jnp.asarray(HD**-0.5, BF16)
            first = head_mask(query.shape)
            parts = []
            for h in range(2):
                masked = jnp.where(first if h == 0 else ~first, query, jnp.zeros_like(query))
                top = jnp.full((1, span), -jnp.inf, F32)
                for c in range(chunks):
                    if causal and c * KEYS >= (i + 1) * span:
                        continue
                    scores = times(key_ref[c * KEYS:(c + 1) * KEYS, lanes], masked, NT)
                    if causal and (c + 1) * KEYS > i * span:
                        key_at = c * KEYS + lax.broadcasted_iota(jnp.int32, scores.shape, 0)
                        query_at = i * span + lax.broadcasted_iota(jnp.int32, scores.shape, 1)
                        scores = jnp.where(key_at <= query_at, scores, -1000000000.0)
                    score_ref[h, c * KEYS:(c + 1) * KEYS, :] = scores
                    top = jnp.maximum(top, jnp.max(scores, 0, keepdims=True))
                total = jnp.zeros((1, span), F32)
                mixed = jnp.zeros((HD, span), F32)
                value_rows = pl.ds(pl.multiple_of(j * PAIR + h * HD, HD), HD)
                for c in range(chunks):
                    if causal and c * KEYS >= (i + 1) * span:
                        continue
                    probs = jnp.exp(score_ref[h, c * KEYS:(c + 1) * KEYS, :] - top)
                    total += jnp.sum(probs, 0, keepdims=True)
                    mixed += times(turned_ref[value_rows, c * KEYS:(c + 1) * KEYS], probs.astype(BF16))
                parts.append(mixed * (1.0 / total))
                totals_ref[pl.ds(2 * j + h, 1), mine] = top + jnp.log(total)
            attended_ref[mine, lanes] = jnp.concatenate(parts, 0).T.astype(BF16)
            return carry

        lax.fori_loop(0, pairs, pair, 0)


def attend_back(
    query_ref, key_ref, value_ref, attended_ref, totals_ref, grad_ref,
    grad_query_ref, grad_key_ref, grad_value_ref, turned_ref, causal,
):
    queries, keys = grad_ref.shape[0], key_ref.shape[0]
    pairs = query_ref.shape[1] // PAIR
    chunks = keys // KEYS
    scale = HD**-0.5
    for j in range(pairs):
        turned_ref[j * PAIR:(j + 1) * PAIR, :] = (
            key_ref[:, j * PAIR:(j + 1) * PAIR].astype(F32).T.astype(BF16)
        )

    def pair(j, carry):
        lanes = pl.ds(pl.multiple_of(j * PAIR, PAIR), PAIR)
        query = query_ref[:queries, lanes] * jnp.asarray(scale, BF16)
        grad = grad_ref[:, lanes]
        first = head_mask(query.shape)
        meet = (grad.astype(F32) * attended_ref[:queries, lanes].astype(F32)).T
        masked, grads, deltas, totals = [], [], [], []
        for h in range(2):
            keep = first if h == 0 else ~first
            masked.append(jnp.where(keep, query, jnp.zeros_like(query)))
            grads.append(jnp.where(keep, grad, jnp.zeros_like(grad)))
            deltas.append(jnp.sum(meet[h * HD:(h + 1) * HD], 0, keepdims=True))
            totals.append(totals_ref[pl.ds(2 * j + h, 1), :queries])
        grad_query = [jnp.zeros((HD, queries), F32) for h in range(2)]
        for c in range(chunks):
            some = slice(c * KEYS, (c + 1) * KEYS)
            low = c * KEYS if causal else 0
            grad_key = grad_value = jnp.zeros((KEYS, PAIR), F32)
            for h in range(2):
                scores = times(key_ref[some, lanes], masked[h][low:], NT)
                if causal:
                    key_at = lax.broadcasted_iota(jnp.int32, scores.shape, 0)
                    query_at = lax.broadcasted_iota(jnp.int32, scores.shape, 1)
                    scores = jnp.where(key_at <= query_at, scores, -1000000000.0)
                probs = jnp.exp(scores - totals[h][:, low:])
                grad_probs = times(value_ref[some, lanes], grads[h][low:], NT)
                grad_scores = (probs * (grad_probs - deltas[h][:, low:])).astype(BF16)
                grad_value += times(probs.astype(BF16), grads[h][low:])
                grad_key += times(grad_scores, masked[h][low:])
                key_rows = pl.ds(pl.multiple_of(j * PAIR + h * HD, HD), HD)
                part = times(turned_ref[key_rows, some], grad_scores)
                if low:
                    part = jnp.concatenate([jnp.zeros((HD, low), F32), part], 1)
                grad_query[h] += part
            grad_key_ref[some, lanes] = grad_key.astype(BF16)
            grad_value_ref[some, lanes] = grad_value.astype(BF16)
        grad_query_ref[:, lanes] = (jnp.concatenate(grad_query, 0) * scale).T.astype(BF16)
        return carry

    lax.fori_loop(0, pairs, pair, 0)


def self_forward_kernel(
    causal, span, x_ref, wide_ref, out_weight_ref, bias_ref, vec_ref,
    mixed_ref, attended_ref, totals_ref, unit_ref, scale_ref,
    score_ref, turned_ref, *swap_refs,
):
    swap = Swap(*swap_refs)
    length, width = x_ref.shape
    half = out_weight_ref.shape[0]
    tiles = length // ROWS
    totals_ref[...] = jnp.zeros_like(totals_ref)

    def mix(t, carry):
        mixed_ref[rows_of(t), :] = (times(x_ref[rows_of(t), :], wide_ref[...]) + bias_ref[...]).astype(BF16)
        return carry

    lax.fori_loop(0, tiles, mix, 0)
    attend(
        mixed_ref.at[:, :half], mixed_ref.at[:, half:2 * half], mixed_ref.at[:, 2 * half:],
        attended_ref, totals_ref, score_ref, turned_ref, causal, span,
    )

    def give(t, carry):
        swap.give(t, times(attended_ref[rows_of(t), :], out_weight_ref[...]))
        return carry

    lax.fori_loop(0, tiles, give, 0)

    def take(t, carry):
        rows = rows_of(t)
        unit, scale = standardize(x_ref[rows, :].astype(F32) + swap.take(t) + vec_ref[0:1, :])
        unit_ref[rows, :] = unit
        scale_ref[rows, :] = scale
        return carry

    lax.fori_loop(0, tiles, take, 0)


def shape(*dims, dtype=F32):
    return jax.ShapeDtypeStruct(dims, dtype)


def params(ident, mib=56):
    return pltpu.CompilerParams(collective_id=ident, has_side_effects=True, vmem_limit_bytes=mib << 20)


def cross_forward_kernel(
    span, unit_ref, fetched_ref, query_weight_ref, wide_ref, out_weight_ref, query_bias_ref, bias_ref, vec_ref,
    low_ref, query_ref, mixed_ref, attended_ref, totals_ref, unit_out_ref, scale_ref,
    score_ref, turned_ref, *swap_refs,
):
    swap = Swap(*swap_refs)
    length, width = unit_ref.shape
    half = out_weight_ref.shape[0]
    tiles = length // ROWS
    totals_ref[...] = jnp.zeros_like(totals_ref)

    def ask(t, carry):
        rows = rows_of(t)
        low = (unit_ref[rows, :] * vec_ref[0:1, :] + vec_ref[1:2, :]).astype(BF16)
        low_ref[rows, :] = low
        query_ref[rows, :] = (times(low, query_weight_ref[...]) + query_bias_ref[...]).astype(BF16)
        return carry

    lax.fori_loop(0, tiles, ask, 0)

    def mix(t, carry):
        mixed_ref[rows_of(t), :] = (
            times(fetched_ref[rows_of(t), :], wide_ref[...]) + bias_ref[...]
        ).astype(BF16)
        return carry

    lax.fori_loop(0, fetched_ref.shape[0] // ROWS, mix, 0)
    attend(
        query_ref, mixed_ref.at[:, :half], mixed_ref.at[:, half:],
        attended_ref, totals_ref, score_ref, turned_ref, False, span,
    )

    def give(t, carry):
        swap.give(t, times(attended_ref[rows_of(t), :], out_weight_ref[...]))
        return carry

    lax.fori_loop(0, tiles, give, 0)

    def take(t, carry):
        rows = rows_of(t)
        hidden = unit_ref[rows, :] * vec_ref[0:1, :] + vec_ref[1:2, :]
        unit, scale = standardize(hidden + swap.take(t) + vec_ref[2:3, :])
        unit_out_ref[rows, :] = unit
        scale_ref[rows, :] = scale
        return carry

    lax.fori_loop(0, tiles, take, 0)


def feed_forward_kernel(
    kept, unit_ref, up_ref, down_ref, bias_ref, vec_ref,
    states_ref, states_low_ref, low_ref, active_ref, slope_ref, unit_out_ref, scale_ref, *swap_refs,
):
    swap = Swap(*swap_refs)
    length, width = unit_ref.shape
    hidden_half = up_ref.shape[1]
    tiles, kept_tiles = length // ROWS, kept // ROWS
    step = 512

    def feed(t, carry, keep):
        rows = rows_of(t)
        low = (unit_ref[rows, :] * vec_ref[0:1, :] + vec_ref[1:2, :]).astype(BF16)
        if keep:
            low_ref[rows, :] = low
        total = jnp.zeros((ROWS, width), F32)
        for c in range(0, hidden_half, step):
            upward = times(low, up_ref[:, c:c + step]) + bias_ref[:, c:c + step]
            below = 0.5 * lax.erf(upward * (0.5**0.5)) + 0.5
            active = (upward * below).astype(BF16)
            if keep:
                active_ref[rows, c:c + step] = active
                bell = jnp.exp(-0.5 * upward * upward) * (0.5 / jnp.pi) ** 0.5
                slope_ref[rows, c:c + step] = (below + upward * bell).astype(BF16)
            total += times(active, down_ref[c:c + step, :])
        swap.give(t, total)
        return carry

    lax.fori_loop(0, kept_tiles, functools.partial(feed, keep=True), 0)
    if kept_tiles < tiles:
        lax.fori_loop(kept_tiles, tiles, functools.partial(feed, keep=False), 0)

    def take(t, carry, keep):
        rows = rows_of(t)
        hidden = unit_ref[rows, :] * vec_ref[0:1, :] + vec_ref[1:2, :]
        unit, scale = standardize(hidden + swap.take(t) + vec_ref[2:3, :])
        states = unit * vec_ref[3:4, :] + vec_ref[4:5, :]
        states_ref[rows, :] = states
        if keep:
            states_low_ref[rows, :] = states.astype(BF16)
            unit_out_ref[rows, :] = unit
            scale_ref[rows, :] = scale
        return carry

    lax.fori_loop(0, kept_tiles, functools.partial(take, keep=True), 0)
    if kept_tiles < tiles:
        lax.fori_loop(kept_tiles, tiles, functools.partial(take, keep=False), 0)


def feed_backward_kernel(
    grad_ref, unit_after_ref, scale_after_ref, active_ref, slope_ref, up_ref, down_ref,
    unit_before_ref, scale_before_ref, vec_ref,
    low_ref, grad_up_ref, bias_ref, grad_out_ref, sums_after_ref, sums_before_ref,
    held_ref, *swap_refs,
):
    swap = Swap(*swap_refs)
    length, width = grad_ref.shape
    hidden_half = up_ref.shape[1]
    tiles = length // ROWS
    step = 512
    sums_after_ref[...] = jnp.zeros_like(sums_after_ref)
    sums_before_ref[...] = jnp.zeros_like(sums_before_ref)
    bias_ref[...] = jnp.zeros_like(bias_ref)

    def give(t, carry):
        rows = rows_of(t)
        grad = grad_ref[rows, :].astype(F32)
        unit = unit_after_ref[rows, :]
        inner = norm_back(grad, unit, scale_after_ref[rows, :], vec_ref[0:1, :])
        add_sums(sums_after_ref, inner, grad, unit)
        held_ref[rows, :] = inner
        low = inner.astype(BF16)
        low_ref[rows, :] = low
        total = jnp.zeros((ROWS, width), F32)
        for c in range(0, hidden_half, step):
            grad_active = times(low, down_ref[c:c + step, :], NT)
            grad_up = (grad_active * slope_ref[rows, c:c + step].astype(F32)).astype(BF16)
            grad_up_ref[rows, c:c + step] = grad_up
            bias_ref[:, c:c + step] += jnp.sum(grad_up.astype(F32), 0, keepdims=True)
            total += times(grad_up, up_ref[:, c:c + step], NT)
        swap.give(t, total)
        return carry

    lax.fori_loop(0, tiles, give, 0)

    def take(t, carry):
        rows = rows_of(t)
        grad = held_ref[rows, :] + swap.take(t)
        unit = unit_before_ref[rows, :]
        inner = norm_back(grad, unit, scale_before_ref[rows, :], vec_ref[1:2, :])
        add_sums(sums_before_ref, inner, grad, unit)
        grad_out_ref[rows, :] = inner
        return carry

    lax.fori_loop(0, tiles, take, 0)


def spread(grad_pre_ref, out_weight_ref, low_ref, grad_ref):
    def one(t, carry):
        rows = rows_of(t)
        low = grad_pre_ref[rows, :].astype(BF16)
        low_ref[rows, :] = low
        grad_ref[rows, :] = times(low, out_weight_ref[...], NT).astype(BF16)
        return carry

    lax.fori_loop(0, grad_pre_ref.shape[0] // ROWS, one, 0)


def self_backward_kernel(
    causal, grad_pre_ref, mixed_ref, attended_ref, totals_ref, wide_ref, out_weight_ref,
    low_ref, grad_query_ref, grad_pair_ref, grad_x_ref, sums_ref,
    grad_ref, turned_ref, *swap_refs,
):
    swap = Swap(*swap_refs)
    queries, width = grad_pre_ref.shape
    half = out_weight_ref.shape[0]
    length = mixed_ref.shape[0]
    spread(grad_pre_ref, out_weight_ref, low_ref, grad_ref)
    attend_back(
        mixed_ref.at[:, :half], mixed_ref.at[:, half:2 * half], mixed_ref.at[:, 2 * half:],
        attended_ref, totals_ref, grad_ref,
        grad_query_ref, grad_pair_ref.at[:, :half], grad_pair_ref.at[:, half:], turned_ref, causal,
    )
    sums_ref[...] = jnp.zeros_like(sums_ref)
    first = queries // ROWS

    def give(t, carry, asked):
        rows = rows_of(t)
        pair = grad_pair_ref[rows, :]
        sums_ref[:, half:] += jnp.sum(pair.astype(F32), 0, keepdims=True)
        total = times(pair, wide_ref[:, half:], NT)
        if asked:
            query = grad_query_ref[rows, :]
            sums_ref[:, :half] += jnp.sum(query.astype(F32), 0, keepdims=True)
            total += times(query, wide_ref[:, :half], NT)
        swap.give(t, total)
        return carry

    lax.fori_loop(0, first, functools.partial(give, asked=True), 0)
    if first < length // ROWS:
        lax.fori_loop(first, length // ROWS, functools.partial(give, asked=False), 0)

    def take(t, carry, asked):
        rows = rows_of(t)
        total = swap.take(t)
        grad_x_ref[rows, :] = grad_pre_ref[rows, :] + total if asked else total
        return carry

    lax.fori_loop(0, first, functools.partial(take, asked=True), 0)
    if first < length // ROWS:
        lax.fori_loop(first, length // ROWS, functools.partial(take, asked=False), 0)


def cross_backward_kernel(
    grad_pre_ref, query_ref, mixed_ref, attended_ref, totals_ref, query_weight_ref, wide_ref, out_weight_ref,
    unit_ref, scale_ref, vec_ref,
    low_ref, grad_query_ref, grad_pair_ref, fetched_ref, grad_out_ref, sums_ref, vec_sums_ref,
    grad_ref, turned_ref, *swap_refs,
):
    near, far = Swap(*swap_refs[:4]), Swap(*swap_refs[4:])
    queries, width = grad_pre_ref.shape
    half = out_weight_ref.shape[0]
    keys = mixed_ref.shape[0]
    spread(grad_pre_ref, out_weight_ref, low_ref, grad_ref)
    attend_back(
        query_ref, mixed_ref.at[:, :half], mixed_ref.at[:, half:],
        attended_ref, totals_ref, grad_ref,
        grad_query_ref, grad_pair_ref.at[:, :half], grad_pair_ref.at[:, half:], turned_ref, False,
    )
    sums_ref[...] = jnp.zeros_like(sums_ref)
    vec_sums_ref[...] = jnp.zeros_like(vec_sums_ref)

    def give_far(t, carry):
        pair = grad_pair_ref[rows_of(t), :]
        sums_ref[:, half:] += jnp.sum(pair.astype(F32), 0, keepdims=True)
        far.give(t, times(pair, wide_ref[...], NT))
        return carry

    lax.fori_loop(0, keys // ROWS, give_far, 0)

    def give_near(t, carry):
        query = grad_query_ref[rows_of(t), :]
        sums_ref[:, :half] += jnp.sum(query.astype(F32), 0, keepdims=True)
        near.give(t, times(query, query_weight_ref[...], NT))
        return carry

    lax.fori_loop(0, queries // ROWS, give_near, 0)

    def take_far(t, carry):
        fetched_ref[rows_of(t), :] = far.take(t).astype(BF16)
        return carry

    lax.fori_loop(0, keys // ROWS, take_far, 0)

    def take_near(t, carry):
        rows = rows_of(t)
        grad = grad_pre_ref[rows, :] + near.take(t)
        unit = unit_ref[rows, :]
        inner = norm_back(grad, unit, scale_ref[rows, :], vec_ref[0:1, :])
        add_sums(vec_sums_ref, inner, grad, unit)
        grad_out_ref[rows, :] = inner
        return carry

    lax.fori_loop(0, queries // ROWS, take_near, 0)


def held(*dims, dtype=F32):
    return pltpu.VMEM(dims, dtype)


def streams(array):
    rows, width = array.shape
    return rows % 16 == 0 and width % TILE == 0 and rows * width * array.dtype.itemsize >= 1 << 18


def call(name, ident, body, inputs, outputs, scratch):
    ins = [i for i, array in enumerate(inputs) if streams(array)]
    outs = [i for i, array in enumerate(outputs) if streams(array)]
    count_in, count_out = len(inputs), len(outputs)

    def kernel(*refs):
        in_refs, out_refs, rest = refs[:count_in], refs[count_in:count_in + count_out], refs[count_in + count_out:]
        near_in, near_out = list(in_refs), list(out_refs)
        for place, ref in zip(ins, rest[:len(ins)]):
            near_in[place] = ref
        rest = rest[len(ins):]
        for place, ref in zip(outs, rest[:len(outs)]):
            near_out[place] = ref
        rest = rest[len(outs):]
        in_sem, out_sem, rest = rest[0], rest[1], rest[2:]

        def load(place):
            return pltpu.make_async_copy(in_refs[place], near_in[place], in_sem.at[place])

        def store(place):
            return pltpu.make_async_copy(near_out[place], out_refs[place], out_sem.at[place])

        def need(*places):
            for place in places:
                if place in ins:
                    load(place).wait()

        def done(*places):
            for place in places:
                if place in outs:
                    store(place).start()

        for place in ins:
            load(place).start()
        body(need, done, *near_in, *near_out, *rest)
        for place in outs:
            store(place).wait()

    return pl.pallas_call(
        kernel,
        out_shape=outputs,
        in_specs=[ANY if i in ins else VM for i in range(count_in)],
        out_specs=[ANY if i in outs else VM for i in range(count_out)],
        scratch_shapes=[pltpu.VMEM(inputs[i].shape, inputs[i].dtype) for i in ins]
        + [pltpu.VMEM(outputs[i].shape, outputs[i].dtype) for i in outs]
        + [pltpu.SemaphoreType.DMA((count_in,)), pltpu.SemaphoreType.DMA((count_out,))]
        + scratch,
        compiler_params=params(ident),
        name=name,
    )(*inputs)


def encoder_forward(ident, x, wide, out_weight, up, down, shared, split, kept):
    length, width = x.shape
    half, hidden_half = out_weight.shape[0], up.shape[1]
    tiles, span = length // ROWS, min(length, 512)
    places = bias_places(half, hidden_half)

    def body(need, done, x_ref, wide_ref, out_weight_ref, up_ref, down_ref, shared_ref, split_ref, *refs):
        saved, fed, rest = refs[:5], refs[5:12], refs[12:]
        need(0, 1, 2)
        Swap.greet()
        self_forward_kernel(
            False, span, x_ref, wide_ref, out_weight_ref,
            bias_row(split_ref, places, ("enc_q", None, "enc_v"), half), Rows(shared_ref, (0,)),
            *saved, *rest[:6],
        )
        done(0, 1, 2, 3, 4)
        need(3, 4, 5, 6)
        feed_forward_kernel(
            kept, saved[3], up_ref, down_ref, split_ref.at[:, places["enc_up"]],
            Rows(shared_ref, (1, 2, 3, 4, 5)), *fed, *rest[6:],
        )
        done(*range(5, 12))

    return call(
        "encoder_forward", ident, body, [x, wide, out_weight, up, down, shared, split],
        [
            shape(length, 3 * half, dtype=BF16), shape(length, half, dtype=BF16), shape(8, length),
            shape(length, width), shape(length, 1),
            shape(length, width), shape(kept, width, dtype=BF16), shape(kept, width, dtype=BF16),
            shape(kept, hidden_half, dtype=BF16), shape(kept, hidden_half, dtype=BF16),
            shape(kept, width), shape(kept, 1),
        ],
        [held(2, length, span), held(half, length, dtype=BF16)] + Swap.scratch(tiles, width) * 2,
    )


class Trade:
    def __init__(self, count, into, send_sem, recv_sem, give_sem, take_sem):
        self.count, self.into = count, into
        self.send_sem, self.recv_sem, self.give_sem, self.take_sem = send_sem, recv_sem, give_sem, take_sem
        self.me, self.core = lax.axis_index("dp"), lax.axis_index("tensor")
        self.rows, self.half = into.shape[0] // count, into.shape[1] // 2

    @staticmethod
    def scratch(count):
        return [pltpu.SemaphoreType.DMA((count,))] * 4

    def greet(self):
        barrier = pltpu.get_barrier_semaphore()

        def signal(k, carry):
            other = {"dp": lax.rem(self.me + k, self.count)}
            pl.semaphore_signal(barrier, inc=1, device_id=other, device_id_type=MESH)
            return carry

        lax.fori_loop(1, self.count, signal, 0)
        pl.semaphore_signal(barrier, inc=1, device_id={"tensor": 1 - self.core}, device_id_type=MESH)
        pl.semaphore_wait(barrier, self.count)

    def rows_of(self, device):
        return pl.ds(pl.multiple_of(device * self.rows, self.rows), self.rows)

    def mine(self):
        return pl.ds(pl.multiple_of(self.core * self.half, self.half), self.half)

    def send(self, source, k):
        other = lax.rem(self.me + k, self.count)
        return pltpu.make_async_remote_copy(
            src_ref=source.at[self.rows_of(other), :],
            dst_ref=self.into.at[self.rows_of(self.me), self.mine()],
            send_sem=self.send_sem.at[k],
            recv_sem=self.recv_sem.at[k],
            device_id={"dp": other},
            device_id_type=MESH,
        )

    def pass_on(self, k):
        part = self.into.at[self.rows_of(lax.rem(self.me - k + self.count, self.count)), self.mine()]
        return pltpu.make_async_remote_copy(
            src_ref=part,
            dst_ref=part,
            send_sem=self.give_sem.at[k],
            recv_sem=self.take_sem.at[k],
            device_id={"tensor": 1 - self.core},
            device_id_type=MESH,
        )

    def start(self, source):
        def go(k, carry):
            self.send(source, k).start()
            return carry

        lax.fori_loop(1, self.count, go, 0)
        self.into[self.rows_of(self.me), self.mine()] = source[self.rows_of(self.me), :]
        self.pass_on(0).start()

    def finish(self, source):
        def meet(k, carry):
            self.send(source, k).wait_recv()
            self.pass_on(k).start()
            return carry

        lax.fori_loop(1, self.count, meet, 0)

        def end(k, carry):
            self.pass_on(k).wait()
            return carry

        lax.fori_loop(0, self.count, end, 0)

        def sent(k, carry):
            self.send(source, k).wait_send()
            return carry

        lax.fori_loop(1, self.count, sent, 0)


def fetch_and_self_forward(ident, stored, wanted, x, wide, out_weight, shared, split, hidden_half, count):
    length, width = x.shape
    half = out_weight.shape[0]
    span = min(length, 512)
    fetched_rows = wanted.shape[0]
    places = bias_places(half, hidden_half)

    def body(
        need, done, stored_ref, wanted_ref, x_ref, wide_ref, out_weight_ref, shared_ref, split_ref,
        mixed_ref, attended_ref, totals_ref, unit_ref, scale_ref, fetched_ref,
        served_ref, landed_ref, send_sem, recv_sem, give_sem, take_sem, *rest,
    ):
        trade = Trade(count, landed_ref, send_sem, recv_sem, give_sem, take_sem)
        need(0, 1)

        def serve(t, carry):
            want = wanted_ref[rows_of(t), :]
            match = want == lax.broadcasted_iota(jnp.int32, (ROWS, stored_ref.shape[0]), 1)
            pick = jnp.where(match, 1.0, 0.0).astype(BF16)
            served_ref[rows_of(t), :] = times(pick, stored_ref[:, trade.mine()]).astype(BF16)
            return carry

        lax.fori_loop(0, fetched_rows // ROWS, serve, 0)
        trade.greet()
        trade.start(served_ref)
        need(2, 3, 4)
        self_forward_kernel(
            True, span, x_ref, wide_ref, out_weight_ref,
            bias_row(split_ref, places, ("dec_q", None, "dec_v"), half), Rows(shared_ref, (6,)),
            mixed_ref, attended_ref, totals_ref, unit_ref, scale_ref, *rest,
        )
        done(0, 1, 2, 3, 4)
        trade.finish(served_ref)
        fetched_ref[...] = landed_ref[...]
        done(5)

    return call(
        "fetch_and_self_forward", ident, body, [stored, wanted, x, wide, out_weight, shared, split],
        [
            shape(length, 3 * half, dtype=BF16), shape(length, half, dtype=BF16), shape(8, length),
            shape(length, width), shape(length, 1), shape(fetched_rows, width, dtype=BF16),
        ],
        [held(fetched_rows, width // 2, dtype=BF16), held(fetched_rows, width, dtype=BF16)] + Trade.scratch(count)
        + [held(2, length, span), held(half, length, dtype=BF16)] + Swap.scratch(length // ROWS, width),
    )


def decoder_core(
    ident, unit, scale, fetched, cotangent, query_weight, wide, out_weight, up, down, shared, split
):
    length, width = unit.shape
    keys = fetched.shape[0]
    half, hidden_half = out_weight.shape[0], up.shape[1]
    tiles, span = length // ROWS, min(length, 512)
    places = bias_places(half, hidden_half)

    def body(
        need, done, unit_ref, scale_ref, fetched_ref, cotangent_ref, query_weight_ref, wide_ref, out_weight_ref,
        up_ref, down_ref, shared_ref, split_ref,
        states_ref, low_ref, attended_ref, second_low_ref, active_ref,
        feed_low_ref, grad_up_ref, up_bias_ref, sums_after_ref, sums_before_ref,
        cross_low_ref, grad_query_ref, grad_pair_ref, returned_ref, grad_out_ref, cross_sums_ref, vec_sums_ref,
        query_ref, mixed_ref, totals_ref, unit_four_ref, scale_four_ref, states_low_ref, slope_ref,
        unit_five_ref, scale_five_ref, grad_four_ref, inner_ref, score_ref, turned_ref, grad_ref, *swaps,
    ):
        need(0, 1, 2, 4, 5, 6, 9, 10)
        Swap.greet()
        cross_forward_kernel(
            span, unit_ref, fetched_ref, query_weight_ref, wide_ref, out_weight_ref,
            split_ref.at[:, places["crs_q"]], bias_row(split_ref, places, (None, "crs_v"), half),
            Rows(shared_ref, (7, 8, 9)),
            low_ref, query_ref, mixed_ref, attended_ref, totals_ref, unit_four_ref, scale_four_ref,
            score_ref, turned_ref, *swaps[:4],
        )
        done(1, 2)
        need(7, 8)
        feed_forward_kernel(
            length, unit_four_ref, up_ref, down_ref, split_ref.at[:, places["dec_up"]],
            Rows(shared_ref, (10, 11, 12, 13, 14)),
            states_ref, states_low_ref, second_low_ref, active_ref, slope_ref, unit_five_ref, scale_five_ref,
            *swaps[4:8],
        )
        done(0, 3, 4)
        need(3)
        feed_backward_kernel(
            cotangent_ref, unit_five_ref, scale_five_ref, active_ref, slope_ref, up_ref, down_ref,
            unit_four_ref, scale_four_ref, Rows(shared_ref, (13, 10)),
            feed_low_ref, grad_up_ref, up_bias_ref, grad_four_ref, sums_after_ref, sums_before_ref,
            inner_ref, *swaps[8:12],
        )
        done(5, 6, 7, 8, 9)
        cross_backward_kernel(
            grad_four_ref, query_ref, mixed_ref, attended_ref, totals_ref, query_weight_ref, wide_ref,
            out_weight_ref, unit_ref, scale_ref, Rows(shared_ref, (7,)),
            cross_low_ref, grad_query_ref, grad_pair_ref, returned_ref, grad_out_ref, cross_sums_ref, vec_sums_ref,
            grad_ref, turned_ref, *swaps[12:],
        )
        done(*range(10, 17))

    return call(
        "decoder_core", ident, body,
        [unit, scale, fetched, cotangent, query_weight, wide, out_weight, up, down, shared, split],
        [
            shape(length, width), shape(length, width, dtype=BF16), shape(length, half, dtype=BF16),
            shape(length, width, dtype=BF16), shape(length, hidden_half, dtype=BF16),
            shape(length, width, dtype=BF16), shape(length, hidden_half, dtype=BF16), shape(1, hidden_half),
            shape(8, width), shape(8, width),
            shape(length, width, dtype=BF16), shape(length, half, dtype=BF16), shape(keys, 2 * half, dtype=BF16),
            shape(keys, width, dtype=BF16), shape(length, width), shape(1, 3 * half), shape(8, width),
        ],
        [
            held(length, half, dtype=BF16), held(keys, 2 * half, dtype=BF16), held(8, length),
            held(length, width), held(length, 1), held(length, width, dtype=BF16),
            held(length, hidden_half, dtype=BF16), held(length, width), held(length, 1),
            held(length, width), held(length, width), held(2, keys, span), held(half, keys, dtype=BF16),
            held(length, half, dtype=BF16),
        ]
        + Swap.scratch(tiles, width) * 4 + Swap.scratch(keys // ROWS, width),
    )


def decoder_self_backward(ident, grad_pre, mixed, attended, totals, wide, out_weight):
    queries, width = grad_pre.shape
    length, half = mixed.shape[0], out_weight.shape[0]

    def body(need, done, *refs):
        need(*range(6))
        Swap.greet()
        self_backward_kernel(True, *refs)
        done(*range(5))

    return call(
        "decoder_self_backward", ident, body, [grad_pre, mixed, attended, totals, wide, out_weight],
        [
            shape(queries, width, dtype=BF16), shape(queries, half, dtype=BF16), shape(length, 2 * half, dtype=BF16),
            shape(length, width), shape(1, 3 * half),
        ],
        [held(queries, half, dtype=BF16), held(half, length, dtype=BF16)] + Swap.scratch(length // ROWS, width),
    )


def encoder_backward(
    ident, grad, unit_two, scale_two, active, slope, up, down, unit_one, scale_one,
    mixed, attended, totals, wide, out_weight, shared,
):
    queries, width = grad.shape
    length, half, hidden_half = mixed.shape[0], out_weight.shape[0], up.shape[1]

    def body(
        need, done, grad_ref, unit_two_ref, scale_two_ref, active_ref, slope_ref, up_ref, down_ref, unit_one_ref, scale_one_ref,
        mixed_ref, attended_ref, totals_ref, wide_ref, out_weight_ref, shared_ref,
        feed_low_ref, grad_up_ref, up_bias_ref, sums_after_ref, sums_before_ref,
        low_ref, grad_query_ref, grad_pair_ref, grad_x_ref, sums_ref,
        grad_one_ref, inner_ref, grad_out_ref, turned_ref, *swaps,
    ):
        need(*range(9), 14)
        Swap.greet()
        feed_backward_kernel(
            grad_ref, unit_two_ref, scale_two_ref, active_ref, slope_ref, up_ref, down_ref,
            unit_one_ref, scale_one_ref, Rows(shared_ref, (4, 1)),
            feed_low_ref, grad_up_ref, up_bias_ref, grad_one_ref, sums_after_ref, sums_before_ref,
            inner_ref, *swaps[:4],
        )
        done(0, 1, 2, 3, 4)
        need(9, 10, 11, 12, 13)
        self_backward_kernel(
            False, grad_one_ref, mixed_ref, attended_ref, totals_ref, wide_ref, out_weight_ref,
            low_ref, grad_query_ref, grad_pair_ref, grad_x_ref, sums_ref, grad_out_ref, turned_ref, *swaps[4:],
        )
        done(*range(5, 10))

    return call(
        "encoder_backward", ident, body,
        [
            grad, unit_two, scale_two, active, slope, up, down, unit_one, scale_one,
            mixed, attended, totals, wide, out_weight, shared,
        ],
        [
            shape(queries, width, dtype=BF16), shape(queries, hidden_half, dtype=BF16), shape(1, hidden_half),
            shape(8, width), shape(8, width),
            shape(queries, width, dtype=BF16), shape(queries, half, dtype=BF16), shape(length, 2 * half, dtype=BF16),
            shape(length, width), shape(1, 3 * half),
        ],
        [
            held(queries, width), held(queries, width), held(queries, half, dtype=BF16),
            held(half, length, dtype=BF16),
        ]
        + Swap.scratch(queries // ROWS, width) + Swap.scratch(length // ROWS, width),
    )


def adam_vector(grad_value, value, first, second):
    new_first = BETA_ONE * first + (1.0 - BETA_ONE) * grad_value
    new_second = BETA_TWO * second + (1.0 - BETA_TWO) * grad_value * grad_value
    correct_one = 1.0 - BETA_ONE**STEP
    correct_two = 1.0 - BETA_TWO**STEP
    updated = value - VECTOR_RATE * (new_first / correct_one) / (
        jnp.sqrt(new_second / correct_two) + ADAM_EPSILON
    )
    return (new_first, new_second, updated)


def local(
    source_tokens,
    target_tokens,
    target_cotangent,
    retrieved,
    kept_mask,
    owner_slots,
    master,
    first_moment,
    second_moment,
    left_stats,
    right_stats,
    left_basis,
    right_basis,
    shared_vectors,
    shared_first,
    shared_second,
    split_vectors,
    split_first,
    split_second,
):
    tensor_count = lax.axis_size("tensor")
    device_count = lax.axis_size("dp")
    model_width = source_tokens.shape[1]
    tile_size = master.shape[2]
    hidden_width = (split_vectors.shape[1] - 3) * model_width
    half_width = model_width // tensor_count
    hidden_half = hidden_width // tensor_count
    qblocks = retrieved.shape[0]
    per_owner = retrieved.shape[1] // device_count
    me = lax.axis_index("dp")
    vectors = jnp.concatenate([shared_vectors, split_vectors[0]], 0)
    vector_count, vector_width = vectors.shape
    padded = -(-vector_count // 8) * 8
    small = jnp.concatenate(
        [
            jnp.pad(vectors, ((0, padded - vector_count), (0, TILE - vector_width))),
            retrieved.astype(jnp.float32).reshape(-1, TILE),
        ],
        0,
    )
    gathered, smalls = gather_all(master[0].astype(jnp.bfloat16), small, device_count)
    whole = (
        smalls[:, :vector_count, :vector_width]
        .transpose(1, 0, 2)
        .reshape(vector_count, model_width)
        .astype(jnp.bfloat16)
    )
    shared_count = shared_vectors.shape[0]
    shared_whole, split_whole = whole[:shared_count], whole[shared_count:]
    shapes = [s[1:] for s in matrix_list(model_width, hidden_width, tensor_count)]
    names = [s[0] for s in matrix_list(model_width, hidden_width, tensor_count)]
    weights = dict(zip(names, unpack_tiles(gathered, owner_slots, shapes)))
    shared = jnp.pad(shared_whole.astype(F32), ((0, 16 - shared_count), (0, 0)))
    split = split_whole.astype(F32).reshape(1, -1)
    start_row = jnp.argmax(kept_mask)
    turned = jnp.roll(source_tokens, -start_row, 0)

    (enc_mixed, enc_attended, enc_totals, unit_one, scale_one,
     states, stored, hidden_low, enc_active, enc_slope, unit_two, scale_two) = encoder_forward(
        10, turned, weights["enc_qkv"], weights["enc_out"], weights["enc_up"], weights["enc_down"],
        shared, split, KEEP,
    )
    encoder_states = jnp.roll(states, start_row, 0)

    wanted = (
        smalls[:, padded:].reshape(device_count, qblocks, device_count, per_owner)[:, :, me]
        .transpose(1, 0, 2)
        .astype(jnp.int32)
        - KEEP * me
    ).reshape(1, -1)
    matches = (wanted == lax.broadcasted_iota(jnp.int32, (KEEP, 1), 0)).astype(BF16)
    dec_mixed, dec_attended, dec_totals, unit_three, scale_three, fetched = fetch_and_self_forward(
        12, stored, wanted.reshape(-1, 1), target_tokens, weights["dec_qkv"], weights["dec_out"],
        shared, split, hidden_half, device_count,
    )
    (decoder_states, first_low, crs_attended, second_low, dec_active,
     dec_feed_low, dec_grad_up, dec_up_bias, sums_five, sums_four,
     crs_low, crs_grad_query, crs_grad_pair, fetched_low, grad_three, crs_sums, sums_three) = decoder_core(
        13, unit_three, scale_three, fetched, target_cotangent,
        weights["crs_q"], weights["crs_kv"], weights["crs_out"], weights["dec_up"], weights["dec_down"],
        shared, split,
    )
    returned = lax.all_to_all(
        fetched_low.reshape(qblocks, device_count, per_owner, model_width),
        "dp", split_axis=1, concat_axis=1, tiled=True,
    )
    dec_low, dec_grad_query, dec_grad_pair, target_grad, dec_sums = decoder_self_backward(
        17, grad_three, dec_mixed, dec_attended, dec_totals, weights["dec_qkv"], weights["dec_out"]
    )
    stored_grad = jnp.einsum(
        "ka,ab->kb", matches, returned.reshape(-1, model_width), preferred_element_type=F32
    )
    (enc_feed_low, enc_grad_up, enc_up_bias, sums_two, sums_one,
     enc_low, enc_grad_query, enc_grad_pair, grad_turned, enc_sums) = encoder_backward(
        18, stored_grad, unit_two, scale_two, enc_active, enc_slope, weights["enc_up"], weights["enc_down"],
        unit_one, scale_one, enc_mixed, enc_attended, enc_totals, weights["enc_qkv"], weights["enc_out"], shared,
    )
    source_grad = jnp.roll(grad_turned, start_row, 0)

    first_block, total_blocks = {}, 0
    for name, height, breadth in matrix_list(model_width, hidden_width, tensor_count):
        first_block[name] = total_blocks
        total_blocks += height // TILE * (breadth // TILE)
    three = 3 * half_width
    outer = ((0, half_width), (2 * half_width, three))
    everything = ((0, hidden_half),)
    items = [
        (sums, 3 * i, None) for i, sums in enumerate((sums_one, sums_two, sums_three, sums_four, sums_five))
    ]
    at = shared_count * model_width
    for array, pieces in (
        (enc_sums, outer), (enc_up_bias, everything), (dec_sums, outer), (crs_sums, outer), (dec_up_bias, everything)
    ):
        items.append((array, at, pieces))
        at += sum(end - begin for begin, end in pieces)
    (slot_grads,) = weight_grads(
        [
            (first_block["dec_down"], [(dec_active, dec_feed_low)]),
            (first_block["dec_up"], [(second_low, dec_grad_up)]),
            (first_block["crs_out"], [(crs_attended, crs_low)]),
            (first_block["crs_q"], [(first_low, crs_grad_query)]),
            (first_block["crs_kv"], [(fetched, crs_grad_pair)]),
            (first_block["dec_out"], [(dec_attended, dec_low)]),
            (first_block["dec_qkv"], [(target_tokens, dec_grad_query), (target_tokens, dec_grad_pair)]),
        ],
        owner_slots,
        gathered.shape[0],
    )
    slot_grads, vector_grads = weight_grads(
        [
            (first_block["enc_down"], [(enc_active, enc_feed_low)]),
            (first_block["enc_up"], [(hidden_low, enc_grad_up)]),
            (first_block["enc_out"], [(enc_attended, enc_low)]),
            (first_block["enc_qkv"], [(turned, enc_grad_query), (turned, enc_grad_pair)]),
        ],
        owner_slots,
        gathered.shape[0],
        slot_grads,
        (padded, model_width, items),
    )
    slots = master.shape[1]
    owned_slots = me * slots + lax.broadcasted_iota(jnp.int32, (slots, 1), 0)
    used = jnp.any(owned_slots == owner_slots[None, :], 1).astype(jnp.int32)
    results, vector_sums = owner_update(
        used,
        slot_grads,
        vector_grads,
        [
            array[0]
            for array in (
                master, first_moment, second_moment, left_stats, right_stats, left_basis, right_basis
            )
        ],
        device_count,
    )
    vector_owned = lax.dynamic_slice_in_dim(vector_sums, me * vector_width, vector_width, 1)
    shared_owned = vector_owned[:shared_count]
    split_owned = vector_owned[shared_count:vector_count]
    new_master, new_first, new_second, new_left, new_right, new_lbasis, new_rbasis = results
    shared_new_first, shared_new_second, shared_updated = adam_vector(
        shared_owned, shared_vectors, shared_first, shared_second
    )
    split_new_first, split_new_second, split_updated = adam_vector(
        split_owned, split_vectors[0], split_first[0], split_second[0]
    )
    return (
        encoder_states,
        decoder_states,
        source_grad,
        target_grad,
        new_master[None],
        new_first[None],
        new_second[None],
        new_left[None],
        new_right[None],
        new_lbasis[None],
        new_rbasis[None],
        shared_new_first,
        shared_new_second,
        shared_updated,
        split_new_first[None],
        split_new_second[None],
        split_updated[None],
    )


def solution(mesh):
    placed = (
        P("dp", None),
        P("dp", None),
        P("dp", None),
        P("dp", None),
        P("dp"),
        P(),
        P("tensor", "dp", None, None),
        P("tensor", "dp", None, None),
        P("tensor", "dp", None, None),
        P("tensor", "dp", None, None),
        P("tensor", "dp", None, None),
        P("tensor", "dp", None, None),
        P("tensor", "dp", None, None),
        P(None, "dp"),
        P(None, "dp"),
        P(None, "dp"),
        P("tensor", None, "dp"),
        P("tensor", None, "dp"),
        P("tensor", None, "dp"),
    )
    return jax.shard_map(
        local,
        mesh=mesh,
        in_specs=placed,
        out_specs=(
            P("dp", None),
            P("dp", None),
            P("dp", None),
            P("dp", None),
            P("tensor", "dp", None, None),
            P("tensor", "dp", None, None),
            P("tensor", "dp", None, None),
            P("tensor", "dp", None, None),
            P("tensor", "dp", None, None),
            P("tensor", "dp", None, None),
            P("tensor", "dp", None, None),
            P(None, "dp"),
            P(None, "dp"),
            P(None, "dp"),
            P("tensor", None, "dp"),
            P("tensor", None, "dp"),
            P("tensor", None, "dp"),
        ),
        check_vma=False,
    )
```

```python
import functools
from functools import partial

import jax
import jax.numpy as jnp
from jax import lax
from jax.experimental import pallas as pl
from jax.experimental.pallas import tpu as pltpu
from jax.sharding import PartitionSpec as P

HD = 64
KEEP = 512
STEP = 10


BETA_ONE = 0.9
BETA_TWO = 0.95
ADAM_EPSILON = 1e-08
MATRIX_RATE = 0.1
VECTOR_RATE = 0.5
WEIGHT_DECAY = 0.01
NORM_EPSILON = 1e-05
TILE = 128
PANEL = 32
ROWS = 256
KEYS = 256
PAIR = 2 * HD
NN = ((1,), (0,))
NT = ((1,), (1,))
F32 = jnp.float32
BF16 = jnp.bfloat16
MESH = pl.DeviceIdType.MESH
ANY = pl.BlockSpec(memory_space=pl.ANY)


def matrix_list(model_width, hidden_width, tensor_count):
    half_width = model_width // tensor_count
    hidden_half = hidden_width // tensor_count
    return [
        ("enc_qkv", model_width, 3 * half_width),
        ("enc_out", half_width, model_width),
        ("enc_up", model_width, hidden_half),
        ("enc_down", hidden_half, model_width),
        ("dec_qkv", model_width, 3 * half_width),
        ("dec_out", half_width, model_width),
        ("crs_q", model_width, half_width),
        ("crs_kv", model_width, 2 * half_width),
        ("crs_out", half_width, model_width),
        ("dec_up", model_width, hidden_half),
        ("dec_down", hidden_half, model_width),
    ]


def halves(x):
    high = x.astype(BF16)
    return high, (x - high.astype(F32)).astype(BF16)


def mm(a, b, dims=NN):
    ah, al = halves(a)
    bh, bl = halves(b)
    return times(jnp.concatenate([ah, ah, al], 1), jnp.concatenate([bh, bl, bh], dims[1][0]), dims)


def chip_grid(device_count):
    if device_count == 16:
        return 4, 2, 2
    side = round(device_count ** (1 / 3))
    if side**3 == device_count:
        return side, side, side
    return 1, 1, device_count


def place(grid):
    zs, ys, xs = grid
    me = lax.axis_index("dp")
    return me // (ys * xs), lax.rem(me // xs, ys), lax.rem(me, xs)


def peers(grid):
    zs, ys, xs = grid
    z, y, x = place(grid)

    def device(zz, yy, xx):
        return {"dp": (zz * ys + yy) * xs + xx}

    return (
        lambda k: device(lax.rem(z + k, zs), y, x),
        lambda k: device(z, lax.rem(y + k, ys), x),
        lambda k: device(z, y, lax.rem(x + k, xs)),
    )


def greet(grid):
    barrier = pltpu.get_barrier_semaphore()
    count = 0
    for size, peer in zip(grid, peers(grid)):
        for k in range(1, size):
            pl.semaphore_signal(barrier, inc=1, device_id=peer(k), device_id_type=MESH)
            count += 1
    pl.semaphore_wait(barrier, count)


def remote(src, dst, send, recv, device):
    return pltpu.make_async_remote_copy(
        src_ref=src, dst_ref=dst, send_sem=send, recv_sem=recv, device_id=device, device_id_type=MESH
    )


def chunking(slots):
    half = slots // 2
    chunks = min(16, half)
    return half, chunks, half // chunks


def owner_kernel(grid, *refs):
    zs, ys, xs = grid
    used_ref, in_ref, small_ref = refs[:3]
    state_in, state_out, small_out_ref, work_out_ref = refs[3:10], refs[10:17], refs[17], refs[18]
    state, rest = refs[19:26], refs[26:]
    (own0, own1, ra0, ra1, rb0, rb1, rc0, rc1, total, rs_z, rs_y, rs_x, work, load_sem,
     as0, as1, ar0, ar1, bs0, bs1, br0, br1, cs0, cs1, cr0, cr1,
     ssz, ssy, ssx, srz, sry, srx, state_sem) = rest
    own, rec_a, rec_b, rec_c = (own0, own1), (ra0, ra1), (rb0, rb1), (rc0, rc1)
    a_send, a_recv, b_send, b_recv, c_send, c_recv = (as0, as1), (ar0, ar1), (bs0, bs1), (br0, br1), (cs0, cs1), (cr0, cr1)
    rec_s, s_send, s_recv = (rs_z, rs_y, rs_x), (ssz, ssy, ssx), (srz, sry, srx)

    z, y, x = place(grid)
    tos = peers(grid)
    to_z, to_y, to_x = tos
    slots = state[0].shape[0]
    half = slots // 2
    first = ((xs, x, to_x), (ys, y, to_y))
    second = ((ys, y, to_y), (xs, x, to_x))

    def source(g, c, other):
        slot = g * half + c
        return in_ref.at[:, :, other, slot] if g == 0 else in_ref.at[:, other, :, slot]

    def load(g, c):
        return pltpu.make_async_copy(source(g, c, first[g][1]), own[g].at[c], load_sem.at[g, c])

    def send_a(g, c, k):
        count, mine, to = first[g]
        return remote(source(g, c, lax.rem(mine + k, count)), rec_a[g].at[c, k - 1],
                      a_send[g].at[c, k - 1], a_recv[g].at[c, k - 1], to(k))

    def send_b(g, c, k):
        count, mine, to = second[g]
        return remote(own[g].at[c, :, lax.rem(mine + k, count)], rec_b[g].at[c, k - 1],
                      b_send[g].at[c, k - 1], b_recv[g].at[c, k - 1], to(k))

    def send_c(g, c, k):
        return remote(own[g].at[c, lax.rem(z + k, zs), second[g][1]], rec_c[g].at[c, k - 1],
                      c_send[g].at[c, k - 1], c_recv[g].at[c, k - 1], to_z(k))

    def start_a(c):
        for g in range(2):
            for k in range(1, first[g][0]):
                send_a(g, c, k).start()

    def send_s(axis, k):
        return remote(total.at[2 - axis], rec_s[axis].at[k - 1],
                      s_send[axis].at[k - 1], s_recv[axis].at[k - 1], tos[axis](k))

    def small_start(axis):
        for k in range(1, grid[axis]):
            send_s(axis, k).start()

    def small_add(axis):
        value = total[2 - axis]
        for k in range(1, grid[axis]):
            send_s(axis, k).wait_recv()
            value += rec_s[axis][k - 1]
        return value

    def each(count, action):
        def go(c, carry):
            action(c)
            return carry

        lax.fori_loop(0, count, go, 0)

    def load_all(c):
        for g in range(2):
            load(g, c).start()

    each(half, load_all)
    for i in range(7):
        pltpu.make_async_copy(state_in[i], state[i], state_sem.at[0, i]).start()
    total[0] = small_ref[...]
    greet(grid)
    small_start(2)
    start_a(0)
    total[1] = small_add(2)
    small_start(1)
    total[2] = small_add(1)
    small_start(0)
    for i in range(7):
        pltpu.make_async_copy(state_in[i], state[i], state_sem.at[0, i]).wait()

    def step_a(c):
        for g in range(2):
            load(g, c).wait()
            for k in range(1, first[g][0]):
                send_a(g, c, k).wait_recv()

        @pl.when(c + 1 < half)
        def _():
            start_a(c + 1)

        for g in range(2):
            n2 = second[g][0]

            def add(e, carry, g=g, n2=n2):
                a, b = e // n2, lax.rem(e, n2)
                value = own[g][c, a, b].astype(F32)
                for k in range(1, first[g][0]):
                    value += rec_a[g][c, k - 1, a, b].astype(F32)
                own[g][c, a, b] = value.astype(BF16)
                return carry

            lax.fori_loop(0, zs * n2, add, 0)
            for k in range(1, n2):
                send_b(g, c, k).start()

    def step_b(c):
        for g in range(2):
            n2, mine = second[g][0], second[g][1]
            for k in range(1, n2):
                send_b(g, c, k).wait_recv()

            def add(a, carry, g=g, n2=n2, mine=mine):
                value = own[g][c, a, mine].astype(F32)
                for k in range(1, n2):
                    value += rec_b[g][c, k - 1, a].astype(F32)
                own[g][c, a, mine] = value.astype(BF16)
                return carry

            lax.fori_loop(0, zs, add, 0)
            for k in range(1, zs):
                send_c(g, c, k).start()

    def step_c(c):
        batch = lax.rem(c // 4, 2)
        for g in range(2):
            for k in range(1, zs):
                send_c(g, c, k).wait_recv()
        for g in range(2):
            value = own[g][c, z, second[g][1]].astype(F32)
            for k in range(1, zs):
                value += rec_c[g][c, k - 1].astype(F32)
            slot = g * half + c
            value = jnp.where(used_ref[slot] > 0, value, 0.0)
            soap_products(value, slot, state, work, batch, 2 * (4 * g + lax.rem(c, 4)))

    def finish(b):
        batch = lax.rem(b, 2)
        place_bases(work, batch, state[5], state[6], 4 * b)
        emit(b)

    def emit(b):
        for g in range(2):
            span = pl.ds(g * half + 4 * b, 4)
            for i in range(7):
                pltpu.make_async_copy(state[i].at[span], state_out[i].at[span], state_sem.at[1, i]).start()

    def round_of(r, carry):
        for s in range(4):
            t = 4 * r + s

            @pl.when(t < half)
            def _(t=t):
                step_a(t)

            @pl.when((t >= 1) & (t <= half))
            def _(t=t):
                step_b(t - 1)

            @pl.when((t >= 2) & (t < half + 2))
            def _(t=t):
                step_c(t - 2)

            if s >= 1:

                @pl.when((r >= 1) & (r < half // 4))
                def _(s=s):
                    b = r - 1
                    for p in ((0,), (1,), (2, 3))[s - 1]:
                        panel_step(work, lax.rem(b, 2), p)
                    if s == 3:
                        finish(b)

        return carry

    lax.fori_loop(0, half // 4 + 1, round_of, 0)
    emit(half // 4 - 1)
    work_out_ref[...] = work[(half // 4 - 1) % 2]
    small_out_ref[...] = small_add(0)
    for axis in range(3):
        for k in range(1, grid[axis]):
            send_s(axis, k).wait_send()

    def end(c):
        for g in range(2):
            for k in range(1, first[g][0]):
                send_a(g, c, k).wait_send()
            for k in range(1, second[g][0]):
                send_b(g, c, k).wait_send()
            for k in range(1, zs):
                send_c(g, c, k).wait_send()

    each(half, end)
    for i in range(7):
        pltpu.make_async_copy(state[i], state_out[i], state_sem.at[1, i]).wait()


def place_bases(work, batch, left_ref, right_ref, at):
    half = left_ref.shape[0] // 2
    for g in range(2):
        for e in range(4):
            left_ref[g * half + at + e] = work[batch, 2 * (4 * g + e), :, TILE:].T
            right_ref[g * half + at + e] = work[batch, 2 * (4 * g + e) + 1, :, TILE:].T


def last_bases_kernel(work_ref, *refs):
    state_in, state_out, state, work, sems = refs[:7], refs[7:14], refs[14:21], refs[21], refs[22]
    half = state[0].shape[0] // 2

    def copy_in(i):
        return pltpu.make_async_copy(state_in[i], state[i], sems.at[0, i])

    def copy_out(i):
        return pltpu.make_async_copy(state[i], state_out[i], sems.at[1, i])

    for i in range(7):
        copy_in(i).start()
    work[0] = work_ref[...]
    panel_step(work, 0, 0)
    for i in range(7):
        copy_in(i).wait()
        if i < 5:
            copy_out(i).start()
    for p in range(1, TILE // PANEL):
        panel_step(work, 0, p)
    place_bases(work, 0, state[5], state[6], half - 4)
    for i in range(5, 7):
        copy_out(i).start()
    for i in range(7):
        copy_out(i).wait()


def last_bases(work, state):
    whole = state[0].shape
    return pl.pallas_call(
        last_bases_kernel,
        out_shape=[jax.ShapeDtypeStruct(whole, F32)] * 7,
        in_specs=[pl.BlockSpec(memory_space=pltpu.VMEM)] + [ANY] * 7,
        out_specs=[ANY] * 7,
        scratch_shapes=[pltpu.VMEM(whole, F32)] * 7
        + [pltpu.VMEM((1,) + work.shape, F32), pltpu.SemaphoreType.DMA((2, 7))],
        compiler_params=pltpu.CompilerParams(vmem_limit_bytes=56 << 20),
        name="last_bases",
    )(work, *state)


def soap_products(g, i, state, work, batch, at):
    w_ref, m_ref, v_ref, l_ref, r_ref, ql_ref, qr_ref = state
    c1 = 1.0 - BETA_ONE**STEP
    c2 = 1.0 - BETA_TWO**STEP
    ql = ql_ref[i]
    qr = qr_ref[i]
    gt = g.T
    nm = BETA_ONE * m_ref[i] + (1.0 - BETA_ONE) * g
    m_ref[i] = nm
    side = mm(jnp.concatenate([g, nm], 0), qr)
    both = mm(ql.T, jnp.concatenate([side[:TILE], side[TILE:]], 1))
    rotated, rotated_first = both[:, :TILE], both[:, TILE:]
    nv = BETA_TWO * v_ref[i] + (1.0 - BETA_TWO) * rotated * rotated
    v_ref[i] = nv
    normed = rotated_first / c1 / (jnp.sqrt(nv / c2) + ADAM_EPSILON)
    step = mm(mm(ql, normed), qr, NT)
    w = w_ref[i]
    w_ref[i] = w - MATRIX_RATE * step - MATRIX_RATE * WEIGHT_DECAY * w
    for k, (ref, turn, left, right) in enumerate(((l_ref, ql, g, gt), (r_ref, qr, gt, g))):
        stat = BETA_TWO * ref[i] + (1.0 - BETA_TWO) * mm(left, right)
        ref[i] = stat
        a = mm(stat, turn)
        at_turned = a.T
        work[batch, at + k, :, :TILE] = mm(at_turned, a)
        work[batch, at + k, :, TILE:] = at_turned


def panel_step(work, batch, p):
    count = work.shape[1]
    per = TILE // (2 * PANEL)
    r0 = p * PANEL
    rows = count // per * 8
    lane = lax.broadcasted_iota(jnp.int32, (rows, TILE), 1)
    start = lane // (2 * PANEL) * (2 * PANEL)
    row = lax.rem(lax.broadcasted_iota(jnp.int32, (rows, TILE), 0), 8)
    sub = lax.broadcasted_iota(jnp.int32, (count // per, 8, TILE), 1)
    eye = (
        lax.broadcasted_iota(jnp.int32, (PANEL, PANEL), 0) == lax.broadcasted_iota(jnp.int32, (PANEL, PANEL), 1)
    ).astype(F32)
    packs = []
    for q in range(count // per):
        pieces = []
        for k in range(per):
            pieces += [work[batch, q * per + k, r0:r0 + PANEL, r0:r0 + PANEL], eye]
        packs.append(jnp.concatenate(pieces, 1)[None])
    x = jnp.concatenate(packs, 0)
    strips = [x[:, 8 * e:8 * e + 8, :] for e in range(PANEL // 8)]

    def segment(strip, index):
        return jnp.take_along_axis(strip.reshape(-1, TILE), index, axis=1).reshape(strip.shape)

    for j in range(0, PANEL, 2):
        e0, here = j // 8, j % 8
        one = [segment(strip, start + j) for strip in strips[e0:]]
        two = [segment(strip, start + j + 1) for strip in strips[e0:]]
        corner = one[0][:, here:here + 1, :]
        side = one[0][:, here + 1:here + 2, :]
        inverse = 1.0 / corner
        inverse_two = corner * (1.0 / (corner * two[0][:, here + 1:here + 2, :] - side * side))
        shift = side * inverse
        ratio = strips[e0][:, here:here + 1, :] * inverse
        next_off = side * ratio
        ratio_two = (strips[e0][:, here + 1:here + 2, :] - next_off) * inverse_two
        ratio_one = ratio - shift * ratio_two
        for e in range(e0, PANEL // 8):
            change = one[e - e0] * ratio_one + two[e - e0] * ratio_two
            if e == e0:
                change = jnp.where(sub > here + 1, change, jnp.where(sub == here + 1, next_off, 0.0))
            strips[e] = strips[e] - change
    for e in range(PANEL // 8):
        strips[e] = strips[e] * lax.rsqrt(segment(strips[e], start + 8 * e + row))
    x = jnp.concatenate(strips, 1)
    for q in range(count // per):
        for k in range(per):
            i = q * per + k
            inverse = x[q, :, 2 * PANEL * k + PANEL:2 * PANEL * (k + 1)]
            u = mm(inverse, work[batch, i, r0:r0 + PANEL, :])
            work[batch, i, r0:r0 + PANEL, TILE:] = u[:, TILE:]
            if r0 + PANEL < TILE:
                high, low = halves(u)
                left = jnp.concatenate([u[:, :TILE], u[:, :TILE], low[:, :TILE].astype(F32)], 0).T
                work[batch, i, r0 + PANEL:, :] -= times(
                    left[r0 + PANEL:, :].astype(BF16), jnp.concatenate([high, low, high], 0)
                )


def some(shape):
    return tuple(max(1, s) for s in shape)


def owner_update(used, slot_grads, small, state, device_count):
    grid = chip_grid(device_count)
    zs, ys, xs = grid
    slots = slot_grads.shape[0] // device_count
    half = slots // 2
    block = (TILE, TILE)
    dma = pltpu.SemaphoreType.DMA
    firsts, seconds = (xs, ys), (ys, xs)
    whole = (slots,) + block
    scratch = (
        [pltpu.VMEM(whole, F32)] * 7
        + [pltpu.VMEM((half, zs, seconds[g]) + block, BF16) for g in range(2)]
        + [pltpu.VMEM(some((half, firsts[g] - 1, zs, seconds[g])) + block, BF16) for g in range(2)]
        + [pltpu.VMEM(some((half, seconds[g] - 1, zs)) + block, BF16) for g in range(2)]
        + [pltpu.VMEM(some((half, zs - 1)) + block, BF16) for g in range(2)]
        + [pltpu.VMEM((3,) + small.shape, F32)]
        + [pltpu.VMEM((max(1, n - 1),) + small.shape, F32) for n in grid]
        + [pltpu.VMEM((2, 16, TILE, 2 * TILE), F32)]
        + [dma((2, half))]
        + [dma(some((half, firsts[g] - 1))) for g in range(2)] * 2
        + [dma(some((half, seconds[g] - 1))) for g in range(2)] * 2
        + [dma(some((half, zs - 1))) for g in range(2)] * 2
        + [dma((max(1, n - 1),)) for n in grid] * 2
        + [dma((2, 7))]
    )
    results = pl.pallas_call(
        functools.partial(owner_kernel, grid),
        out_shape=[jax.ShapeDtypeStruct(whole, F32)] * 7
        + [jax.ShapeDtypeStruct(small.shape, F32), jax.ShapeDtypeStruct((16, TILE, 2 * TILE), F32)],
        in_specs=[pl.BlockSpec(memory_space=pltpu.SMEM), ANY, pl.BlockSpec(memory_space=pltpu.VMEM)] + [ANY] * 7,
        out_specs=[ANY] * 7 + [pl.BlockSpec(memory_space=pltpu.VMEM)] * 2,
        scratch_shapes=scratch,
        compiler_params=pltpu.CompilerParams(collective_id=1, has_side_effects=True, vmem_limit_bytes=56 << 20),
        name="owner_update",
    )(used, slot_grads.reshape(zs, ys, xs, slots, TILE, TILE), small, *state)
    return last_bases(results[8], results[:7]), results[7]


def ag_kernel(grid, wide_ref, small_ref, out_ref, small_out_ref, own_ref,
              load_sem, z_send, z_recv, b_send0, b_send1, b_recv0, b_recv1, a_send0, a_send1, a_recv0, a_recv1,
              s_load, ssz, ssy, ssx, srz, sry, srx):
    zs, ys, xs = grid
    z, y, x = place(grid)
    tos = peers(grid)
    to_z, to_y, to_x = tos
    slots = own_ref.shape[0]
    half, chunks, size = chunking(slots)
    first = ((xs, to_x), (ys, to_y))
    second = ((ys, to_y), (xs, to_x))
    b_send, b_recv, a_send, a_recv = (b_send0, b_send1), (b_recv0, b_recv1), (a_send0, a_send1), (a_recv0, a_recv1)
    s_send, s_recv = (ssz, ssy, ssx), (srz, sry, srx)

    def span(g, c):
        return pl.ds(g * half + c * size, size)

    def send_z(g, c, k):
        return remote(own_ref.at[span(g, c)], out_ref.at[z, y, x, span(g, c)],
                      z_send.at[g, c, k - 1], z_recv.at[g, c, k - 1], to_z(k))

    def send_b(g, c, k):
        part = out_ref.at[:, y, x, span(g, c)]
        return remote(part, part, b_send[g].at[c, k - 1], b_recv[g].at[c, k - 1], second[g][1](k))

    def send_a(g, c, k):
        part = out_ref.at[:, :, x, span(g, c)] if g == 0 else out_ref.at[:, y, :, span(g, c)]
        return remote(part, part, a_send[g].at[c, k - 1], a_recv[g].at[c, k - 1], first[g][1](k))

    def send_s(axis, k):
        if axis == 0:
            source, target = small_ref, small_out_ref.at[z, y, x]
        else:
            source = target = small_out_ref.at[:, y, x] if axis == 1 else small_out_ref.at[:, :, x]
        return remote(source, target, s_send[axis].at[k - 1], s_recv[axis].at[k - 1], tos[axis](k))

    own_ref[...] = wide_ref[...].astype(BF16)
    keep = pltpu.make_async_copy(own_ref, out_ref.at[z, y, x], load_sem)
    keep_small = pltpu.make_async_copy(small_ref, small_out_ref.at[z, y, x], s_load)
    keep.start()
    keep_small.start()
    greet(grid)

    for k in range(1, grid[0]):
        send_s(0, k).start()
    def start_z(c):
        for g in range(2):
            for k in range(1, zs):
                send_z(g, c, k).start()

    def small_wait(axis):
        for k in range(1, grid[axis]):
            send_s(axis, k).wait_recv()

    def small_start(axis):
        for k in range(1, grid[axis]):
            send_s(axis, k).start()

    start_z(0)
    for t in range(chunks + 1):
        if t < chunks:
            for g in range(2):
                for k in range(1, zs):
                    send_z(g, t, k).wait_recv()
            if t == 0:
                keep.wait()
                keep_small.wait()
                small_wait(0)
                small_start(1)
            if t + 1 < chunks:
                start_z(t + 1)
            for g in range(2):
                for k in range(1, second[g][0]):
                    send_b(g, t, k).start()
        if t >= 1:
            for g in range(2):
                for k in range(1, second[g][0]):
                    send_b(g, t - 1, k).wait_recv()
                for k in range(1, first[g][0]):
                    send_a(g, t - 1, k).start()
        if t == 1:
            small_wait(1)
            small_start(2)
    small_wait(2)
    for c in range(chunks):
        for g in range(2):
            for k in range(1, first[g][0]):
                send_a(g, c, k).wait_recv()
    for axis in range(3):
        for k in range(1, grid[axis]):
            send_s(axis, k).wait_send()
    for c in range(chunks):
        for g in range(2):
            for k in range(1, zs):
                send_z(g, c, k).wait_send()
            for k in range(1, second[g][0]):
                send_b(g, c, k).wait_send()
            for k in range(1, first[g][0]):
                send_a(g, c, k).wait_send()


def gather_all(own, small, device_count):
    grid = chip_grid(device_count)
    zs, ys, xs = grid
    slots = own.shape[0]
    half, chunks, size = chunking(slots)
    dma = pltpu.SemaphoreType.DMA
    firsts, seconds = (xs, ys), (ys, xs)
    scratch = (
        [pltpu.VMEM(own.shape, BF16), dma, dma(some((2, chunks, zs - 1))), dma(some((2, chunks, zs - 1)))]
        + [dma(some((chunks, seconds[g] - 1))) for g in range(2)] * 2
        + [dma(some((chunks, firsts[g] - 1))) for g in range(2)] * 2
        + [dma]
        + [dma((max(1, n - 1),)) for n in grid] * 2
    )
    blocks, smalls = pl.pallas_call(
        functools.partial(ag_kernel, grid),
        out_shape=[jax.ShapeDtypeStruct(grid + own.shape, BF16), jax.ShapeDtypeStruct(grid + small.shape, small.dtype)],
        in_specs=[pl.BlockSpec(memory_space=pltpu.VMEM)] * 2,
        out_specs=[ANY, ANY],
        scratch_shapes=scratch,
        compiler_params=pltpu.CompilerParams(collective_id=2, has_side_effects=True, vmem_limit_bytes=56 << 20),
        name="gather_all",
    )(own, small)
    return blocks.reshape((-1,) + own.shape[1:]), smalls.reshape((-1,) + small.shape)


def unpack_kernel(shapes, slots_ref, packed, *refs):
    count = len(shapes)
    mats, held, sems = refs[:count], refs[count:-1], refs[-1]

    def whole(index):
        return pltpu.make_async_copy(held[index], mats[index], sems.at[1, index])

    offset = 0
    for index, (height, breadth) in enumerate(shapes):
        down, across = height // TILE, breadth // TILE

        def start(i, carry, index=index, offset=offset, across=across):
            for j in range(across):
                tile = held[index].at[pl.ds(pl.multiple_of(i * TILE, TILE), TILE), j * TILE:(j + 1) * TILE]
                slot = packed.at[slots_ref[offset + i * across + j]]
                pltpu.make_async_copy(slot, tile, sems.at[0, index]).start()
            return carry

        lax.fori_loop(0, down, start, 0)
        offset += down * across
    for index in range(count):
        pltpu.make_async_copy(held[index], held[index], sems.at[0, index]).wait()
        whole(index).start()
    for index in range(count):
        whole(index).wait()


def unpack_tiles(packed, slots, shapes):
    return pl.pallas_call(
        functools.partial(unpack_kernel, shapes),
        out_shape=[jax.ShapeDtypeStruct(s, packed.dtype) for s in shapes],
        in_specs=[pl.BlockSpec(memory_space=pltpu.SMEM), ANY],
        out_specs=[ANY] * len(shapes),
        scratch_shapes=[pltpu.VMEM(s, packed.dtype) for s in shapes] + [pltpu.SemaphoreType.DMA((2, len(shapes)))],
        compiler_params=pltpu.CompilerParams(vmem_limit_bytes=56 << 20),
        name="unpack_tiles",
    )(slots, packed)


def weight_grads_kernel(plan, used, vectors, passed, slots_ref, *refs):
    arrays, refs = refs[:used], refs[used:]
    given, refs = refs[:len(vectors)], refs[len(vectors):]
    refs = refs[passed:]
    packed, refs = refs[0], refs[1:]
    if vectors:
        rows_ref, refs = refs[0], refs[1:]
    held, refs = refs[:used], refs[used:]
    turned, refs = refs[0], refs[1:]
    results, sems = refs[:len(plan)], refs[len(plan):]
    load_sem, store_sem = sems

    def load(i):
        return pltpu.make_async_copy(arrays[i], held[i], load_sem.at[i])

    order = []
    for left, tokens, right, *rest in plan:
        for i in (left, right):
            if i not in order:
                order.append(i)
    for i in order:
        load(i).start()
    if vectors:
        width = rows_ref.shape[1]
        rows_ref[...] = jnp.zeros_like(rows_ref)
        for source, (at, pieces) in zip(given, vectors):
            if pieces is None:
                rows_ref[at:at + 3, :] = source[0:3, :]
                continue
            for begin, end in pieces:
                while begin < end:
                    lane = at % width
                    size = min(end - begin, width - lane)
                    rows_ref[at // width:at // width + 1, lane:lane + size] = source[:, begin:begin + size]
                    begin, at = begin + size, at + size
    ready = set()
    last = None
    for index, (left, tokens, right, offset, stride, down, across) in enumerate(plan):
        for i in (left, right):
            if i not in ready:
                ready.add(i)
                load(i).wait()
        height = down * TILE
        if last != (left, tokens):
            for j in range(down):
                turned[j * TILE:(j + 1) * TILE, :tokens] = (
                    held[left][:tokens, j * TILE:(j + 1) * TILE].astype(F32).T.astype(BF16)
                )
            last = (left, tokens)
        result = results[index]
        group = 3 if across % 3 == 0 else 1

        def columns(n, carry, right=right, tokens=tokens, height=height, result=result, offset=offset,
                    stride=stride, down=down, group=group, index=index):
            lanes = pl.ds(pl.multiple_of(n * group * TILE, TILE), group * TILE)
            result[:, lanes] = times(turned[:height, :tokens], held[right][:tokens, lanes]).astype(BF16)

            def send(i, carry):
                for j in range(group):
                    tile = result.at[
                        pl.ds(pl.multiple_of(i * TILE, TILE), TILE),
                        pl.ds(pl.multiple_of((n * group + j) * TILE, TILE), TILE),
                    ]
                    slot = packed.at[slots_ref[offset + i * stride + n * group + j]]
                    pltpu.make_async_copy(tile, slot, store_sem.at[index]).start()
                return carry

            lax.fori_loop(0, down, send, 0)
            return carry

        lax.fori_loop(0, across // group, columns, 0)
    for index in range(len(plan)):
        pltpu.make_async_copy(results[index], results[index], store_sem.at[index]).wait()


def weight_grads(matrices, slots, slot_count, packed=None, vectors=None):
    arrays, plan, results = [], [], []

    def index_of(array):
        for i, other in enumerate(arrays):
            if other is array:
                return i
        arrays.append(array)
        return len(arrays) - 1

    for offset, parts in matrices:
        height = parts[0][0].shape[1]
        stride = sum(right.shape[1] for left, right in parts) // TILE
        for left, right in parts:
            across = right.shape[1] // TILE
            plan.append((index_of(left), right.shape[0], index_of(right), offset, stride, height // TILE, across))
            results.append(pltpu.VMEM((height, right.shape[1]), BF16))
            offset += across
    tall = max(entry[5] for entry in plan) * TILE
    long = max(entry[1] for entry in plan)
    out_shape = [jax.ShapeDtypeStruct((slot_count, TILE, TILE), BF16)]
    given, layout = [], []
    if vectors:
        rows, width, items = vectors
        out_shape.append(jax.ShapeDtypeStruct((rows, width), F32))
        given = [item[0] for item in items]
        layout = [item[1:] for item in items]
    passed = [] if packed is None else [packed]
    return pl.pallas_call(
        functools.partial(weight_grads_kernel, plan, len(arrays), layout, len(passed)),
        out_shape=out_shape,
        in_specs=[pl.BlockSpec(memory_space=pltpu.SMEM)] + [ANY] * len(arrays)
        + [pl.BlockSpec(memory_space=pltpu.VMEM)] * len(given) + [ANY] * len(passed),
        out_specs=[ANY] + [pl.BlockSpec(memory_space=pltpu.VMEM)] * (len(out_shape) - 1),
        scratch_shapes=[pltpu.VMEM(a.shape, a.dtype) for a in arrays] + [pltpu.VMEM((tall, long), BF16)] + results
        + [pltpu.SemaphoreType.DMA((len(arrays),)), pltpu.SemaphoreType.DMA((len(plan),))],
        input_output_aliases={} if packed is None else {1 + len(arrays) + len(given): 0},
        compiler_params=pltpu.CompilerParams(vmem_limit_bytes=56 << 20),
        name="weight_grads",
    )(slots, *arrays, *given, *passed)


VM = pl.BlockSpec(memory_space=pltpu.VMEM)


def times(left, right, dims=NN):
    return lax.dot_general(left, right, (dims, ((), ())), preferred_element_type=F32)


def rows_of(t, size=ROWS):
    return pl.ds(pl.multiple_of(t * size, size), size)


class Swap:
    def __init__(self, out, into, send_sem, recv_sem):
        self.out, self.into, self.send_sem, self.recv_sem = out, into, send_sem, recv_sem

    @staticmethod
    def scratch(tiles, width):
        dma = pltpu.SemaphoreType.DMA((tiles,))
        held = pltpu.VMEM((tiles, ROWS, width), BF16)
        return [held, held, dma, dma]

    @staticmethod
    def greet():
        barrier = pltpu.get_barrier_semaphore()
        other = {"tensor": 1 - lax.axis_index("tensor")}
        pl.semaphore_signal(barrier, inc=1, device_id=other, device_id_type=MESH)
        pl.semaphore_wait(barrier, 1)

    def copy(self, t):
        return pltpu.make_async_remote_copy(
            src_ref=self.out.at[t],
            dst_ref=self.into.at[t],
            send_sem=self.send_sem.at[t],
            recv_sem=self.recv_sem.at[t],
            device_id={"tensor": 1 - lax.axis_index("tensor")},
            device_id_type=MESH,
        )

    def give(self, t, value):
        self.out[t] = value.astype(BF16)
        self.copy(t).start()

    def take(self, t):
        self.copy(t).wait()
        return self.out[t].astype(F32) + self.into[t].astype(F32)


class Rows:
    def __init__(self, ref, rows):
        self.ref, self.rows = ref, rows

    def __getitem__(self, index):
        at = self.rows[index[0].start]
        return self.ref[at:at + 1, :]


def bias_places(half, hidden_half):
    places, at = {}, 0
    for name, length in (
        ("enc_q", half), ("enc_v", half), ("enc_up", hidden_half), ("dec_q", half), ("dec_v", half),
        ("crs_q", half), ("crs_v", half), ("dec_up", hidden_half),
    ):
        places[name] = slice(at, at + length)
        at += length
    return places


def bias_row(split_ref, places, names, half):
    zero = jnp.zeros((1, half), F32)
    return jnp.concatenate([zero if name is None else split_ref[:, places[name]] for name in names], 1)


def standardize(values):
    center = values - jnp.mean(values, -1, keepdims=True)
    scale = lax.rsqrt(jnp.mean(center * center, -1, keepdims=True) + NORM_EPSILON)
    return center * scale, scale


def norm_back(grad, unit, scale, gain):
    inner = grad * gain
    return scale * (
        inner - jnp.mean(inner, -1, keepdims=True) - unit * jnp.mean(inner * unit, -1, keepdims=True)
    )


def add_sums(sums_ref, grad_in, grad_out, unit):
    sums_ref[0:1, :] += jnp.sum(grad_in, 0, keepdims=True)
    sums_ref[1:2, :] += jnp.sum(grad_out * unit, 0, keepdims=True)
    sums_ref[2:3, :] += jnp.sum(grad_out, 0, keepdims=True)


def head_mask(shape):
    return lax.broadcasted_iota(jnp.int32, shape, 1) < HD


def attend(query_ref, key_ref, value_ref, attended_ref, totals_ref, score_ref, turned_ref, causal, span):
    queries, keys = query_ref.shape[0], key_ref.shape[0]
    pairs = query_ref.shape[1] // PAIR
    chunks = keys // KEYS
    for j in range(pairs):
        turned_ref[j * PAIR:(j + 1) * PAIR, :] = (
            value_ref[:, j * PAIR:(j + 1) * PAIR].astype(F32).T.astype(BF16)
        )
    for i in range(queries // span):
        mine = slice(i * span, (i + 1) * span)

        def pair(j, carry, i=i, mine=mine):
            lanes = pl.ds(pl.multiple_of(j * PAIR, PAIR), PAIR)
            query = query_ref[mine, lanes] * jnp.asarray(HD**-0.5, BF16)
            first = head_mask(query.shape)
            parts = []
            for h in range(2):
                masked = jnp.where(first if h == 0 else ~first, query, jnp.zeros_like(query))
                top = jnp.full((1, span), -jnp.inf, F32)
                for c in range(chunks):
                    if causal and c * KEYS >= (i + 1) * span:
                        continue
                    scores = times(key_ref[c * KEYS:(c + 1) * KEYS, lanes], masked, NT)
                    if causal and (c + 1) * KEYS > i * span:
                        key_at = c * KEYS + lax.broadcasted_iota(jnp.int32, scores.shape, 0)
                        query_at = i * span + lax.broadcasted_iota(jnp.int32, scores.shape, 1)
                        scores = jnp.where(key_at <= query_at, scores, -1000000000.0)
                    score_ref[h, c * KEYS:(c + 1) * KEYS, :] = scores
                    top = jnp.maximum(top, jnp.max(scores, 0, keepdims=True))
                total = jnp.zeros((1, span), F32)
                mixed = jnp.zeros((HD, span), F32)
                value_rows = pl.ds(pl.multiple_of(j * PAIR + h * HD, HD), HD)
                for c in range(chunks):
                    if causal and c * KEYS >= (i + 1) * span:
                        continue
                    probs = jnp.exp(score_ref[h, c * KEYS:(c + 1) * KEYS, :] - top)
                    total += jnp.sum(probs, 0, keepdims=True)
                    mixed += times(turned_ref[value_rows, c * KEYS:(c + 1) * KEYS], probs.astype(BF16))
                parts.append(mixed * (1.0 / total))
                totals_ref[pl.ds(2 * j + h, 1), mine] = top + jnp.log(total)
            attended_ref[mine, lanes] = jnp.concatenate(parts, 0).T.astype(BF16)
            return carry

        lax.fori_loop(0, pairs, pair, 0)


def attend_back(
    query_ref, key_ref, value_ref, attended_ref, totals_ref, grad_ref,
    grad_query_ref, grad_key_ref, grad_value_ref, turned_ref, causal,
):
    queries, keys = grad_ref.shape[0], key_ref.shape[0]
    pairs = query_ref.shape[1] // PAIR
    chunks = keys // KEYS
    scale = HD**-0.5
    for j in range(pairs):
        turned_ref[j * PAIR:(j + 1) * PAIR, :] = (
            key_ref[:, j * PAIR:(j + 1) * PAIR].astype(F32).T.astype(BF16)
        )

    def pair(j, carry):
        lanes = pl.ds(pl.multiple_of(j * PAIR, PAIR), PAIR)
        query = query_ref[:queries, lanes] * jnp.asarray(scale, BF16)
        grad = grad_ref[:, lanes]
        first = head_mask(query.shape)
        meet = (grad.astype(F32) * attended_ref[:queries, lanes].astype(F32)).T
        masked, grads, deltas, totals = [], [], [], []
        for h in range(2):
            keep = first if h == 0 else ~first
            masked.append(jnp.where(keep, query, jnp.zeros_like(query)))
            grads.append(jnp.where(keep, grad, jnp.zeros_like(grad)))
            deltas.append(jnp.sum(meet[h * HD:(h + 1) * HD], 0, keepdims=True))
            totals.append(totals_ref[pl.ds(2 * j + h, 1), :queries])
        grad_query = [jnp.zeros((HD, queries), F32) for h in range(2)]
        for c in range(chunks):
            some = slice(c * KEYS, (c + 1) * KEYS)
            low = c * KEYS if causal else 0
            grad_key = grad_value = jnp.zeros((KEYS, PAIR), F32)
            for h in range(2):
                scores = times(key_ref[some, lanes], masked[h][low:], NT)
                if causal:
                    key_at = lax.broadcasted_iota(jnp.int32, scores.shape, 0)
                    query_at = lax.broadcasted_iota(jnp.int32, scores.shape, 1)
                    scores = jnp.where(key_at <= query_at, scores, -1000000000.0)
                probs = jnp.exp(scores - totals[h][:, low:])
                grad_probs = times(value_ref[some, lanes], grads[h][low:], NT)
                grad_scores = (probs * (grad_probs - deltas[h][:, low:])).astype(BF16)
                grad_value += times(probs.astype(BF16), grads[h][low:])
                grad_key += times(grad_scores, masked[h][low:])
                key_rows = pl.ds(pl.multiple_of(j * PAIR + h * HD, HD), HD)
                part = times(turned_ref[key_rows, some], grad_scores)
                if low:
                    part = jnp.concatenate([jnp.zeros((HD, low), F32), part], 1)
                grad_query[h] += part
            grad_key_ref[some, lanes] = grad_key.astype(BF16)
            grad_value_ref[some, lanes] = grad_value.astype(BF16)
        grad_query_ref[:, lanes] = (jnp.concatenate(grad_query, 0) * scale).T.astype(BF16)
        return carry

    lax.fori_loop(0, pairs, pair, 0)


def self_forward_kernel(
    causal, span, x_ref, wide_ref, out_weight_ref, bias_ref, vec_ref,
    mixed_ref, attended_ref, totals_ref, unit_ref, scale_ref,
    score_ref, turned_ref, *swap_refs,
):
    swap = Swap(*swap_refs)
    length, width = x_ref.shape
    half = out_weight_ref.shape[0]
    tiles = length // ROWS
    totals_ref[...] = jnp.zeros_like(totals_ref)

    def mix(t, carry):
        mixed_ref[rows_of(t), :] = (times(x_ref[rows_of(t), :], wide_ref[...]) + bias_ref[...]).astype(BF16)
        return carry

    lax.fori_loop(0, tiles, mix, 0)
    attend(
        mixed_ref.at[:, :half], mixed_ref.at[:, half:2 * half], mixed_ref.at[:, 2 * half:],
        attended_ref, totals_ref, score_ref, turned_ref, causal, span,
    )

    def give(t, carry):
        swap.give(t, times(attended_ref[rows_of(t), :], out_weight_ref[...]))
        return carry

    lax.fori_loop(0, tiles, give, 0)

    def take(t, carry):
        rows = rows_of(t)
        unit, scale = standardize(x_ref[rows, :].astype(F32) + swap.take(t) + vec_ref[0:1, :])
        unit_ref[rows, :] = unit
        scale_ref[rows, :] = scale
        return carry

    lax.fori_loop(0, tiles, take, 0)


def shape(*dims, dtype=F32):
    return jax.ShapeDtypeStruct(dims, dtype)


def params(ident, mib=56):
    return pltpu.CompilerParams(collective_id=ident, has_side_effects=True, vmem_limit_bytes=mib << 20)


def cross_forward_kernel(
    span, unit_ref, fetched_ref, query_weight_ref, wide_ref, out_weight_ref, query_bias_ref, bias_ref, vec_ref,
    low_ref, query_ref, mixed_ref, attended_ref, totals_ref, unit_out_ref, scale_ref,
    score_ref, turned_ref, *swap_refs,
):
    swap = Swap(*swap_refs)
    length, width = unit_ref.shape
    half = out_weight_ref.shape[0]
    tiles = length // ROWS
    totals_ref[...] = jnp.zeros_like(totals_ref)

    def ask(t, carry):
        rows = rows_of(t)
        low = (unit_ref[rows, :] * vec_ref[0:1, :] + vec_ref[1:2, :]).astype(BF16)
        low_ref[rows, :] = low
        query_ref[rows, :] = (times(low, query_weight_ref[...]) + query_bias_ref[...]).astype(BF16)
        return carry

    lax.fori_loop(0, tiles, ask, 0)

    def mix(t, carry):
        mixed_ref[rows_of(t), :] = (
            times(fetched_ref[rows_of(t), :], wide_ref[...]) + bias_ref[...]
        ).astype(BF16)
        return carry

    lax.fori_loop(0, fetched_ref.shape[0] // ROWS, mix, 0)
    attend(
        query_ref, mixed_ref.at[:, :half], mixed_ref.at[:, half:],
        attended_ref, totals_ref, score_ref, turned_ref, False, span,
    )

    def give(t, carry):
        swap.give(t, times(attended_ref[rows_of(t), :], out_weight_ref[...]))
        return carry

    lax.fori_loop(0, tiles, give, 0)

    def take(t, carry):
        rows = rows_of(t)
        hidden = unit_ref[rows, :] * vec_ref[0:1, :] + vec_ref[1:2, :]
        unit, scale = standardize(hidden + swap.take(t) + vec_ref[2:3, :])
        unit_out_ref[rows, :] = unit
        scale_ref[rows, :] = scale
        return carry

    lax.fori_loop(0, tiles, take, 0)


def feed_forward_kernel(
    kept, between, unit_ref, up_ref, down_ref, bias_ref, vec_ref,
    states_ref, states_low_ref, low_ref, active_ref, slope_ref, unit_out_ref, scale_ref, *swap_refs,
):
    swap = Swap(*swap_refs)
    length, width = unit_ref.shape
    hidden_half = up_ref.shape[1]
    tiles, kept_tiles = length // ROWS, kept // ROWS
    step = 512

    def feed(t, carry, keep):
        rows = rows_of(t)
        low = (unit_ref[rows, :] * vec_ref[0:1, :] + vec_ref[1:2, :]).astype(BF16)
        if keep:
            low_ref[rows, :] = low
        total = jnp.zeros((ROWS, width), F32)
        for c in range(0, hidden_half, step):
            upward = times(low, up_ref[:, c:c + step]) + bias_ref[:, c:c + step]
            below = 0.5 * lax.erf(upward * (0.5**0.5)) + 0.5
            active = (upward * below).astype(BF16)
            if keep:
                active_ref[rows, c:c + step] = active
                bell = jnp.exp(-0.5 * upward * upward) * (0.5 / jnp.pi) ** 0.5
                slope_ref[rows, c:c + step] = (below + upward * bell).astype(BF16)
            total += times(active, down_ref[c:c + step, :])
        swap.give(t, total)
        return carry

    def take(t, carry, keep):
        rows = rows_of(t)
        hidden = unit_ref[rows, :] * vec_ref[0:1, :] + vec_ref[1:2, :]
        unit, scale = standardize(hidden + swap.take(t) + vec_ref[2:3, :])
        states = unit * vec_ref[3:4, :] + vec_ref[4:5, :]
        states_ref[rows, :] = states
        if keep:
            states_low_ref[rows, :] = states.astype(BF16)
            unit_out_ref[rows, :] = unit
            scale_ref[rows, :] = scale
        return carry

    lax.fori_loop(0, kept_tiles, functools.partial(feed, keep=True), 0)
    lax.fori_loop(0, kept_tiles, functools.partial(take, keep=True), 0)
    between()
    if kept_tiles < tiles:
        lax.fori_loop(kept_tiles, tiles, functools.partial(feed, keep=False), 0)
        lax.fori_loop(kept_tiles, tiles, functools.partial(take, keep=False), 0)


def feed_backward_kernel(
    grad_ref, unit_after_ref, scale_after_ref, active_ref, slope_ref, up_ref, down_ref,
    unit_before_ref, scale_before_ref, vec_ref,
    low_ref, grad_up_ref, bias_ref, grad_out_ref, sums_after_ref, sums_before_ref,
    held_ref, *swap_refs,
):
    swap = Swap(*swap_refs)
    length, width = grad_ref.shape
    hidden_half = up_ref.shape[1]
    tiles = length // ROWS
    step = 512
    sums_after_ref[...] = jnp.zeros_like(sums_after_ref)
    sums_before_ref[...] = jnp.zeros_like(sums_before_ref)
    bias_ref[...] = jnp.zeros_like(bias_ref)

    def give(t, carry):
        rows = rows_of(t)
        grad = grad_ref[rows, :].astype(F32)
        unit = unit_after_ref[rows, :]
        inner = norm_back(grad, unit, scale_after_ref[rows, :], vec_ref[0:1, :])
        add_sums(sums_after_ref, inner, grad, unit)
        held_ref[rows, :] = inner
        low = inner.astype(BF16)
        low_ref[rows, :] = low
        total = jnp.zeros((ROWS, width), F32)
        for c in range(0, hidden_half, step):
            grad_active = times(low, down_ref[c:c + step, :], NT)
            grad_up = (grad_active * slope_ref[rows, c:c + step].astype(F32)).astype(BF16)
            grad_up_ref[rows, c:c + step] = grad_up
            bias_ref[:, c:c + step] += jnp.sum(grad_up.astype(F32), 0, keepdims=True)
            total += times(grad_up, up_ref[:, c:c + step], NT)
        swap.give(t, total)
        return carry

    lax.fori_loop(0, tiles, give, 0)

    def take(t, carry):
        rows = rows_of(t)
        grad = held_ref[rows, :] + swap.take(t)
        unit = unit_before_ref[rows, :]
        inner = norm_back(grad, unit, scale_before_ref[rows, :], vec_ref[1:2, :])
        add_sums(sums_before_ref, inner, grad, unit)
        grad_out_ref[rows, :] = inner
        return carry

    lax.fori_loop(0, tiles, take, 0)


def spread(grad_pre_ref, out_weight_ref, low_ref, grad_ref):
    def one(t, carry):
        rows = rows_of(t)
        low = grad_pre_ref[rows, :].astype(BF16)
        low_ref[rows, :] = low
        grad_ref[rows, :] = times(low, out_weight_ref[...], NT).astype(BF16)
        return carry

    lax.fori_loop(0, grad_pre_ref.shape[0] // ROWS, one, 0)


def self_backward_kernel(
    causal, grad_pre_ref, mixed_ref, attended_ref, totals_ref, wide_ref, out_weight_ref,
    low_ref, grad_query_ref, grad_pair_ref, grad_x_ref, sums_ref,
    grad_ref, turned_ref, *swap_refs,
):
    swap = Swap(*swap_refs)
    queries, width = grad_pre_ref.shape
    half = out_weight_ref.shape[0]
    length = mixed_ref.shape[0]
    spread(grad_pre_ref, out_weight_ref, low_ref, grad_ref)
    attend_back(
        mixed_ref.at[:, :half], mixed_ref.at[:, half:2 * half], mixed_ref.at[:, 2 * half:],
        attended_ref, totals_ref, grad_ref,
        grad_query_ref, grad_pair_ref.at[:, :half], grad_pair_ref.at[:, half:], turned_ref, causal,
    )
    sums_ref[...] = jnp.zeros_like(sums_ref)
    first = queries // ROWS

    def give(t, carry, asked):
        rows = rows_of(t)
        pair = grad_pair_ref[rows, :]
        sums_ref[:, half:] += jnp.sum(pair.astype(F32), 0, keepdims=True)
        total = times(pair, wide_ref[:, half:], NT)
        if asked:
            query = grad_query_ref[rows, :]
            sums_ref[:, :half] += jnp.sum(query.astype(F32), 0, keepdims=True)
            total += times(query, wide_ref[:, :half], NT)
        swap.give(t, total)
        return carry

    lax.fori_loop(0, first, functools.partial(give, asked=True), 0)
    if first < length // ROWS:
        lax.fori_loop(first, length // ROWS, functools.partial(give, asked=False), 0)

    def take(t, carry, asked):
        rows = rows_of(t)
        total = swap.take(t)
        grad_x_ref[rows, :] = grad_pre_ref[rows, :] + total if asked else total
        return carry

    lax.fori_loop(0, first, functools.partial(take, asked=True), 0)
    if first < length // ROWS:
        lax.fori_loop(first, length // ROWS, functools.partial(take, asked=False), 0)


def cross_backward_kernel(
    between, grad_pre_ref, query_ref, mixed_ref, attended_ref, totals_ref, query_weight_ref, wide_ref, out_weight_ref,
    unit_ref, scale_ref, vec_ref,
    low_ref, grad_query_ref, grad_pair_ref, fetched_ref, grad_out_ref, sums_ref, vec_sums_ref,
    grad_ref, turned_ref, *swap_refs,
):
    near, far = Swap(*swap_refs[:4]), Swap(*swap_refs[4:])
    queries, width = grad_pre_ref.shape
    half = out_weight_ref.shape[0]
    keys = mixed_ref.shape[0]
    spread(grad_pre_ref, out_weight_ref, low_ref, grad_ref)
    attend_back(
        query_ref, mixed_ref.at[:, :half], mixed_ref.at[:, half:],
        attended_ref, totals_ref, grad_ref,
        grad_query_ref, grad_pair_ref.at[:, :half], grad_pair_ref.at[:, half:], turned_ref, False,
    )
    sums_ref[...] = jnp.zeros_like(sums_ref)
    vec_sums_ref[...] = jnp.zeros_like(vec_sums_ref)

    def give_far(t, carry):
        pair = grad_pair_ref[rows_of(t), :]
        sums_ref[:, half:] += jnp.sum(pair.astype(F32), 0, keepdims=True)
        far.give(t, times(pair, wide_ref[...], NT))
        return carry

    lax.fori_loop(0, keys // ROWS, give_far, 0)

    def give_near(t, carry):
        query = grad_query_ref[rows_of(t), :]
        sums_ref[:, :half] += jnp.sum(query.astype(F32), 0, keepdims=True)
        near.give(t, times(query, query_weight_ref[...], NT))
        return carry

    lax.fori_loop(0, queries // ROWS, give_near, 0)

    def take_far(t, carry):
        fetched_ref[rows_of(t), :] = far.take(t).astype(BF16)
        return carry

    lax.fori_loop(0, keys // ROWS, take_far, 0)
    between()

    def take_near(t, carry):
        rows = rows_of(t)
        grad = grad_pre_ref[rows, :] + near.take(t)
        unit = unit_ref[rows, :]
        inner = norm_back(grad, unit, scale_ref[rows, :], vec_ref[0:1, :])
        add_sums(vec_sums_ref, inner, grad, unit)
        grad_out_ref[rows, :] = inner
        return carry

    lax.fori_loop(0, queries // ROWS, take_near, 0)


def held(*dims, dtype=F32):
    return pltpu.VMEM(dims, dtype)


def streams(array):
    rows, width = array.shape
    return rows % 16 == 0 and width % TILE == 0 and rows * width * array.dtype.itemsize >= 1 << 18


def call(name, ident, body, inputs, outputs, scratch, mib=56):
    ins = [i for i, array in enumerate(inputs) if streams(array)]
    outs = [i for i, array in enumerate(outputs) if streams(array)]
    count_in, count_out = len(inputs), len(outputs)

    def kernel(*refs):
        in_refs, out_refs, rest = refs[:count_in], refs[count_in:count_in + count_out], refs[count_in + count_out:]
        near_in, near_out = list(in_refs), list(out_refs)
        for place, ref in zip(ins, rest[:len(ins)]):
            near_in[place] = ref
        rest = rest[len(ins):]
        for place, ref in zip(outs, rest[:len(outs)]):
            near_out[place] = ref
        rest = rest[len(outs):]
        in_sem, out_sem, rest = rest[0], rest[1], rest[2:]

        def load(place):
            return pltpu.make_async_copy(in_refs[place], near_in[place], in_sem.at[place])

        def store(place):
            return pltpu.make_async_copy(near_out[place], out_refs[place], out_sem.at[place])

        def need(*places):
            for place in places:
                if place in ins:
                    load(place).wait()

        def done(*places):
            for place in places:
                if place in outs:
                    store(place).start()

        for place in ins:
            load(place).start()
        body(need, done, *near_in, *near_out, *rest)
        for place in outs:
            store(place).wait()

    return pl.pallas_call(
        kernel,
        out_shape=outputs,
        in_specs=[ANY if i in ins else VM for i in range(count_in)],
        out_specs=[ANY if i in outs else VM for i in range(count_out)],
        scratch_shapes=[pltpu.VMEM(inputs[i].shape, inputs[i].dtype) for i in ins]
        + [pltpu.VMEM(outputs[i].shape, outputs[i].dtype) for i in outs]
        + [pltpu.SemaphoreType.DMA((count_in,)), pltpu.SemaphoreType.DMA((count_out,))]
        + scratch,
        compiler_params=params(ident, mib),
        name=name,
    )(*inputs)


class Trade:
    def __init__(self, count, into, send_sem, recv_sem, give_sem, take_sem):
        self.count, self.into = count, into
        self.send_sem, self.recv_sem, self.give_sem, self.take_sem = send_sem, recv_sem, give_sem, take_sem
        self.me, self.core = lax.axis_index("dp"), lax.axis_index("tensor")
        self.rows, self.half = into.shape[0] // count, into.shape[1] // 2

    @staticmethod
    def scratch(count):
        return [pltpu.SemaphoreType.DMA((count,))] * 4

    def greet(self):
        barrier = pltpu.get_barrier_semaphore()

        def signal(k, carry):
            other = {"dp": lax.rem(self.me + k, self.count)}
            pl.semaphore_signal(barrier, inc=1, device_id=other, device_id_type=MESH)
            return carry

        lax.fori_loop(1, self.count, signal, 0)
        pl.semaphore_signal(barrier, inc=1, device_id={"tensor": 1 - self.core}, device_id_type=MESH)
        pl.semaphore_wait(barrier, self.count)

    def rows_of(self, device):
        return pl.ds(pl.multiple_of(device * self.rows, self.rows), self.rows)

    def mine(self):
        return pl.ds(pl.multiple_of(self.core * self.half, self.half), self.half)

    def lanes_of(self, source):
        return self.mine() if source.shape[1] == self.into.shape[1] else slice(None)

    def send(self, source, k):
        other = lax.rem(self.me + k, self.count)
        return pltpu.make_async_remote_copy(
            src_ref=source.at[self.rows_of(other), self.lanes_of(source)],
            dst_ref=self.into.at[self.rows_of(self.me), self.mine()],
            send_sem=self.send_sem.at[k],
            recv_sem=self.recv_sem.at[k],
            device_id={"dp": other},
            device_id_type=MESH,
        )

    def pass_on(self, k):
        part = self.into.at[self.rows_of(lax.rem(self.me - k + self.count, self.count)), self.mine()]
        return pltpu.make_async_remote_copy(
            src_ref=part,
            dst_ref=part,
            send_sem=self.give_sem.at[k],
            recv_sem=self.take_sem.at[k],
            device_id={"tensor": 1 - self.core},
            device_id_type=MESH,
        )

    def start(self, source):
        def go(k, carry):
            self.send(source, k).start()
            return carry

        lax.fori_loop(1, self.count, go, 0)
        self.into[self.rows_of(self.me), self.mine()] = source[self.rows_of(self.me), self.lanes_of(source)]
        self.pass_on(0).start()

    def finish(self, source):
        def meet(k, carry):
            self.send(source, k).wait_recv()
            self.pass_on(k).start()
            return carry

        lax.fori_loop(1, self.count, meet, 0)

        def end(k, carry):
            self.pass_on(k).wait()
            return carry

        lax.fori_loop(0, self.count, end, 0)

        def sent(k, carry):
            self.send(source, k).wait_send()
            return carry

        lax.fori_loop(1, self.count, sent, 0)


def encoder_and_fetch(
    ident, x, wide, out_weight, up, down, shared, split, kept, wanted, target, dec_wide, dec_out_weight, count
):
    length, width = x.shape
    half, hidden_half = out_weight.shape[0], up.shape[1]
    tiles, span = length // ROWS, min(length, 512)
    target_length = target.shape[0]
    target_span = min(target_length, span)
    fetched_rows = wanted.shape[0]
    places = bias_places(half, hidden_half)

    def body(
        need, done, x_ref, wide_ref, out_weight_ref, up_ref, down_ref, shared_ref, split_ref, wanted_ref,
        target_ref, dec_wide_ref, dec_out_weight_ref, *refs,
    ):
        saved, fed, dec_saved, fetched_ref, rest = refs[:5], refs[5:12], refs[12:17], refs[17], refs[18:]
        served_ref, trade_sems, rest = rest[0], rest[1:5], rest[5:]
        score_ref, turned_ref, rest = rest[0], rest[1], rest[2:]
        trade = Trade(count, fetched_ref, *trade_sems)
        stored_ref = fed[1]
        need(0, 1, 2)
        trade.greet()
        self_forward_kernel(
            False, span, x_ref, wide_ref, out_weight_ref,
            bias_row(split_ref, places, ("enc_q", None, "enc_v"), half), Rows(shared_ref, (0,)),
            *saved, score_ref, turned_ref, *rest[:4],
        )
        done(0, 1, 2, 3, 4)
        need(3, 4, 5, 6, 7)

        def serve(t, carry):
            want = wanted_ref[rows_of(t), :]
            match = want == lax.broadcasted_iota(jnp.int32, (ROWS, kept), 1)
            pick = jnp.where(match, 1.0, 0.0).astype(BF16)
            served_ref[rows_of(t), :] = times(pick, stored_ref[:, trade.mine()]).astype(BF16)
            return carry

        def between():
            lax.fori_loop(0, fetched_rows // ROWS, serve, 0)
            trade.start(served_ref)
            done(6, 7, 8, 9, 10, 11)

        feed_forward_kernel(
            kept, between, saved[3], up_ref, down_ref, split_ref.at[:, places["enc_up"]],
            Rows(shared_ref, (1, 2, 3, 4, 5)), *fed, *rest[4:8],
        )
        done(5)
        need(8, 9, 10)
        self_forward_kernel(
            True, target_span, target_ref, dec_wide_ref, dec_out_weight_ref,
            bias_row(split_ref, places, ("dec_q", None, "dec_v"), half), Rows(shared_ref, (6,)),
            *dec_saved, score_ref.at[:, :, :target_span], turned_ref.at[:, :target_length], *rest[8:],
        )
        done(12, 13, 14, 15, 16)
        trade.finish(served_ref)
        done(17)

    return call(
        "encoder_and_fetch", ident, body,
        [x, wide, out_weight, up, down, shared, split, wanted, target, dec_wide, dec_out_weight],
        [
            shape(length, 3 * half, dtype=BF16), shape(length, half, dtype=BF16), shape(8, length),
            shape(length, width), shape(length, 1),
            shape(length, width), shape(kept, width, dtype=BF16), shape(kept, width, dtype=BF16),
            shape(kept, hidden_half, dtype=BF16), shape(kept, hidden_half, dtype=BF16),
            shape(kept, width), shape(kept, 1),
            shape(target_length, 3 * half, dtype=BF16), shape(target_length, half, dtype=BF16), shape(8, target_length),
            shape(target_length, width), shape(target_length, 1), shape(fetched_rows, width, dtype=BF16),
        ],
        [held(fetched_rows, width // 2, dtype=BF16)] + Trade.scratch(count)
        + [held(2, length, span), held(half, length, dtype=BF16)]
        + Swap.scratch(tiles, width) * 2 + Swap.scratch(target_length // ROWS, width),
    )


def decoder_core(
    ident, unit, scale, fetched, cotangent, query_weight, wide, out_weight, up, down, shared, split,
    mixed, attended, totals, self_wide, self_out_weight, count,
):
    length, width = unit.shape
    keys = fetched.shape[0]
    half, hidden_half = out_weight.shape[0], up.shape[1]
    tiles, span = length // ROWS, min(length, 512)
    places = bias_places(half, hidden_half)

    def body(
        need, done, unit_ref, scale_ref, fetched_ref, cotangent_ref, query_weight_ref, wide_ref, out_weight_ref,
        up_ref, down_ref, shared_ref, split_ref,
        self_mixed_ref, self_attended_ref, self_totals_ref, self_wide_ref, self_out_weight_ref,
        states_ref, low_ref, attended_ref, second_low_ref, active_ref,
        feed_low_ref, grad_up_ref, up_bias_ref, sums_after_ref, sums_before_ref,
        cross_low_ref, grad_query_ref, grad_pair_ref, landed_ref, cross_sums_ref, vec_sums_ref,
        self_low_ref, self_query_ref, self_pair_ref, grad_x_ref, self_sums_ref,
        query_ref, mixed_ref, totals_ref, unit_four_ref, scale_four_ref, slope_ref,
        unit_five_ref, scale_five_ref, grad_four_ref, inner_ref, score_ref, turned_ref, grad_ref, returned_ref, grad_out_ref,
        send_sem, recv_sem, give_sem, take_sem, *swaps,
    ):
        need(0, 1, 2, 4, 5, 6, 9, 10)
        trade = Trade(count, landed_ref, send_sem, recv_sem, give_sem, take_sem)
        trade.greet()
        cross_forward_kernel(
            span, unit_ref, fetched_ref, query_weight_ref, wide_ref, out_weight_ref,
            split_ref.at[:, places["crs_q"]], bias_row(split_ref, places, (None, "crs_v"), half),
            Rows(shared_ref, (7, 8, 9)),
            low_ref, query_ref, mixed_ref, attended_ref, totals_ref, unit_four_ref, scale_four_ref,
            score_ref, turned_ref, *swaps[:4],
        )
        done(1, 2)
        need(7, 8)
        feed_forward_kernel(
            length, lambda: None, unit_four_ref, up_ref, down_ref, split_ref.at[:, places["dec_up"]],
            Rows(shared_ref, (10, 11, 12, 13, 14)),
            states_ref, cross_low_ref, second_low_ref, active_ref, slope_ref, unit_five_ref, scale_five_ref,
            *swaps[4:8],
        )
        done(0, 3, 4)
        need(3)
        feed_backward_kernel(
            cotangent_ref, unit_five_ref, scale_five_ref, active_ref, slope_ref, up_ref, down_ref,
            unit_four_ref, scale_four_ref, Rows(shared_ref, (13, 10)),
            feed_low_ref, grad_up_ref, up_bias_ref, grad_four_ref, sums_after_ref, sums_before_ref,
            inner_ref, *swaps[8:12],
        )
        done(5, 6, 7, 8, 9)
        cross_backward_kernel(
            lambda: trade.start(returned_ref), grad_four_ref, query_ref, mixed_ref, attended_ref, totals_ref, query_weight_ref, wide_ref,
            out_weight_ref, unit_ref, scale_ref, Rows(shared_ref, (7,)),
            cross_low_ref, grad_query_ref, grad_pair_ref, returned_ref, grad_out_ref, cross_sums_ref, vec_sums_ref,
            grad_ref, turned_ref, *swaps[12:20],
        )
        done(10, 11, 12, 14, 15)
        need(11, 12, 13, 14, 15)
        self_backward_kernel(
            True, grad_out_ref, self_mixed_ref, self_attended_ref, self_totals_ref, self_wide_ref, self_out_weight_ref,
            self_low_ref, self_query_ref, self_pair_ref, grad_x_ref, self_sums_ref,
            grad_ref, turned_ref.at[:, :length], *swaps[20:],
        )
        done(16, 17, 18, 19, 20)
        trade.finish(returned_ref)
        done(13)

    return call(
        "decoder_core", ident, body,
        [
            unit, scale, fetched, cotangent, query_weight, wide, out_weight, up, down, shared, split,
            mixed, attended, totals, self_wide, self_out_weight,
        ],
        [
            shape(length, width), shape(length, width, dtype=BF16), shape(length, half, dtype=BF16),
            shape(length, width, dtype=BF16), shape(length, hidden_half, dtype=BF16),
            shape(length, width, dtype=BF16), shape(length, hidden_half, dtype=BF16), shape(1, hidden_half),
            shape(8, width), shape(8, width),
            shape(length, width, dtype=BF16), shape(length, half, dtype=BF16), shape(keys, 2 * half, dtype=BF16),
            shape(keys, width, dtype=BF16), shape(1, 3 * half), shape(8, width),
            shape(length, width, dtype=BF16), shape(length, half, dtype=BF16), shape(length, 2 * half, dtype=BF16),
            shape(length, width), shape(1, 3 * half),
        ],
        [
            held(length, half, dtype=BF16), held(keys, 2 * half, dtype=BF16), held(8, length),
            held(length, width), held(length, 1),
            held(length, hidden_half, dtype=BF16), held(length, width), held(length, 1),
            held(length, width), held(length, width), held(2, keys, span), held(half, keys, dtype=BF16),
            held(length, half, dtype=BF16), held(keys, width, dtype=BF16), held(length, width),
        ]
        + Trade.scratch(count)
        + Swap.scratch(tiles, width) * 4 + Swap.scratch(keys // ROWS, width) + Swap.scratch(tiles, width),
        60,
    )


def encoder_backward(
    ident, returned, wanted, unit_two, scale_two, active, slope, up, down, unit_one, scale_one,
    mixed, attended, totals, wide, out_weight, shared,
):
    queries, width = unit_two.shape
    length, half, hidden_half = mixed.shape[0], out_weight.shape[0], up.shape[1]

    def body(
        need, done, returned_ref, wanted_ref, unit_two_ref, scale_two_ref, active_ref, slope_ref, up_ref, down_ref, unit_one_ref, scale_one_ref,
        mixed_ref, attended_ref, totals_ref, wide_ref, out_weight_ref, shared_ref,
        feed_low_ref, grad_up_ref, up_bias_ref, sums_after_ref, sums_before_ref,
        low_ref, grad_query_ref, grad_pair_ref, grad_x_ref, sums_ref,
        grad_ref, grad_one_ref, inner_ref, grad_out_ref, turned_ref, *swaps,
    ):
        need(0, 1)

        def collect(t, carry):
            place = t * ROWS + lax.broadcasted_iota(jnp.int32, (ROWS, returned_ref.shape[0]), 0)
            match = jnp.where(wanted_ref[...] == place, 1.0, 0.0).astype(BF16)
            grad_ref[rows_of(t), :] = times(match, returned_ref[...])
            return carry

        lax.fori_loop(0, queries // ROWS, collect, 0)
        need(*range(2, 10), 15)
        Swap.greet()
        feed_backward_kernel(
            grad_ref, unit_two_ref, scale_two_ref, active_ref, slope_ref, up_ref, down_ref,
            unit_one_ref, scale_one_ref, Rows(shared_ref, (4, 1)),
            feed_low_ref, grad_up_ref, up_bias_ref, grad_one_ref, sums_after_ref, sums_before_ref,
            inner_ref, *swaps[:4],
        )
        done(0, 1, 2, 3, 4)
        need(10, 11, 12, 13, 14)
        self_backward_kernel(
            False, grad_one_ref, mixed_ref, attended_ref, totals_ref, wide_ref, out_weight_ref,
            low_ref, grad_query_ref, grad_pair_ref, grad_x_ref, sums_ref, grad_out_ref, turned_ref, *swaps[4:],
        )
        done(*range(5, 10))

    return call(
        "encoder_backward", ident, body,
        [
            returned, wanted, unit_two, scale_two, active, slope, up, down, unit_one, scale_one,
            mixed, attended, totals, wide, out_weight, shared,
        ],
        [
            shape(queries, width, dtype=BF16), shape(queries, hidden_half, dtype=BF16), shape(1, hidden_half),
            shape(8, width), shape(8, width),
            shape(queries, width, dtype=BF16), shape(queries, half, dtype=BF16), shape(length, 2 * half, dtype=BF16),
            shape(length, width), shape(1, 3 * half),
        ],
        [
            held(queries, width), held(queries, width), held(queries, width), held(queries, half, dtype=BF16),
            held(half, length, dtype=BF16),
        ]
        + Swap.scratch(queries // ROWS, width) + Swap.scratch(length // ROWS, width),
    )


def adam_vector(grad_value, value, first, second):
    new_first = BETA_ONE * first + (1.0 - BETA_ONE) * grad_value
    new_second = BETA_TWO * second + (1.0 - BETA_TWO) * grad_value * grad_value
    correct_one = 1.0 - BETA_ONE**STEP
    correct_two = 1.0 - BETA_TWO**STEP
    updated = value - VECTOR_RATE * (new_first / correct_one) / (
        jnp.sqrt(new_second / correct_two) + ADAM_EPSILON
    )
    return (new_first, new_second, updated)


def local(
    source_tokens,
    target_tokens,
    target_cotangent,
    retrieved,
    kept_mask,
    owner_slots,
    master,
    first_moment,
    second_moment,
    left_stats,
    right_stats,
    left_basis,
    right_basis,
    shared_vectors,
    shared_first,
    shared_second,
    split_vectors,
    split_first,
    split_second,
):
    tensor_count = lax.axis_size("tensor")
    device_count = lax.axis_size("dp")
    model_width = source_tokens.shape[1]
    tile_size = master.shape[2]
    hidden_width = (split_vectors.shape[1] - 3) * model_width
    half_width = model_width // tensor_count
    hidden_half = hidden_width // tensor_count
    qblocks = retrieved.shape[0]
    per_owner = retrieved.shape[1] // device_count
    me = lax.axis_index("dp")
    vectors = jnp.concatenate([shared_vectors, split_vectors[0]], 0)
    vector_count, vector_width = vectors.shape
    padded = -(-vector_count // 8) * 8
    small = jnp.concatenate(
        [
            jnp.pad(vectors, ((0, padded - vector_count), (0, TILE - vector_width))),
            retrieved.astype(jnp.float32).reshape(-1, TILE),
        ],
        0,
    )
    gathered, smalls = gather_all(master[0], small, device_count)
    whole = (
        smalls[:, :vector_count, :vector_width]
        .transpose(1, 0, 2)
        .reshape(vector_count, model_width)
        .astype(jnp.bfloat16)
    )
    shared_count = shared_vectors.shape[0]
    shared_whole, split_whole = whole[:shared_count], whole[shared_count:]
    shapes = [s[1:] for s in matrix_list(model_width, hidden_width, tensor_count)]
    names = [s[0] for s in matrix_list(model_width, hidden_width, tensor_count)]
    weights = dict(zip(names, unpack_tiles(gathered, owner_slots, shapes)))
    shared = jnp.pad(shared_whole.astype(F32), ((0, 16 - shared_count), (0, 0)))
    split = split_whole.astype(F32).reshape(1, -1)
    start_row = jnp.argmax(kept_mask)
    turned = jnp.roll(source_tokens, -start_row, 0)


    wanted = (
        smalls[:, padded:].reshape(device_count, qblocks, device_count, per_owner)[:, :, me]
        .transpose(1, 0, 2)
        .astype(jnp.int32)
        - KEEP * me
    ).reshape(1, -1)
    (enc_mixed, enc_attended, enc_totals, unit_one, scale_one,
     states, _, hidden_low, enc_active, enc_slope, unit_two, scale_two,
     dec_mixed, dec_attended, dec_totals, unit_three, scale_three, fetched) = encoder_and_fetch(
        10, turned, weights["enc_qkv"], weights["enc_out"], weights["enc_up"], weights["enc_down"],
        shared, split, KEEP, wanted.reshape(-1, 1), target_tokens, weights["dec_qkv"], weights["dec_out"], device_count,
    )
    encoder_states = jnp.roll(states, start_row, 0)
    (decoder_states, first_low, crs_attended, second_low, dec_active,
     dec_feed_low, dec_grad_up, dec_up_bias, sums_five, sums_four,
     crs_low, crs_grad_query, crs_grad_pair, returned, crs_sums, sums_three,
     dec_low, dec_grad_query, dec_grad_pair, target_grad, dec_sums) = decoder_core(
        13, unit_three, scale_three, fetched, target_cotangent,
        weights["crs_q"], weights["crs_kv"], weights["crs_out"], weights["dec_up"], weights["dec_down"],
        shared, split, dec_mixed, dec_attended, dec_totals, weights["dec_qkv"], weights["dec_out"], device_count,
    )
    (enc_feed_low, enc_grad_up, enc_up_bias, sums_two, sums_one,
     enc_low, enc_grad_query, enc_grad_pair, grad_turned, enc_sums) = encoder_backward(
        18, returned, wanted, unit_two, scale_two, enc_active, enc_slope, weights["enc_up"], weights["enc_down"],
        unit_one, scale_one, enc_mixed, enc_attended, enc_totals, weights["enc_qkv"], weights["enc_out"], shared,
    )
    source_grad = jnp.roll(grad_turned, start_row, 0)

    first_block, total_blocks = {}, 0
    for name, height, breadth in matrix_list(model_width, hidden_width, tensor_count):
        first_block[name] = total_blocks
        total_blocks += height // TILE * (breadth // TILE)
    three = 3 * half_width
    outer = ((0, half_width), (2 * half_width, three))
    everything = ((0, hidden_half),)
    items = [
        (sums, 3 * i, None) for i, sums in enumerate((sums_one, sums_two, sums_three, sums_four, sums_five))
    ]
    at = shared_count * model_width
    for array, pieces in (
        (enc_sums, outer), (enc_up_bias, everything), (dec_sums, outer), (crs_sums, outer), (dec_up_bias, everything)
    ):
        items.append((array, at, pieces))
        at += sum(end - begin for begin, end in pieces)
    (slot_grads,) = weight_grads(
        [
            (first_block["dec_down"], [(dec_active, dec_feed_low)]),
            (first_block["dec_up"], [(second_low, dec_grad_up)]),
            (first_block["crs_out"], [(crs_attended, crs_low)]),
            (first_block["crs_q"], [(first_low, crs_grad_query)]),
            (first_block["crs_kv"], [(fetched, crs_grad_pair)]),
            (first_block["dec_out"], [(dec_attended, dec_low)]),
            (first_block["dec_qkv"], [(target_tokens, dec_grad_query), (target_tokens, dec_grad_pair)]),
        ],
        owner_slots,
        gathered.shape[0],
    )
    slot_grads, vector_grads = weight_grads(
        [
            (first_block["enc_down"], [(enc_active, enc_feed_low)]),
            (first_block["enc_up"], [(hidden_low, enc_grad_up)]),
            (first_block["enc_out"], [(enc_attended, enc_low)]),
            (first_block["enc_qkv"], [(turned, enc_grad_query), (turned, enc_grad_pair)]),
        ],
        owner_slots,
        gathered.shape[0],
        slot_grads,
        (padded, model_width, items),
    )
    slots = master.shape[1]
    owned_slots = me * slots + lax.broadcasted_iota(jnp.int32, (slots, 1), 0)
    used = jnp.any(owned_slots == owner_slots[None, :], 1).astype(jnp.int32)
    results, vector_sums = owner_update(
        used,
        slot_grads,
        vector_grads,
        [
            array[0]
            for array in (
                master, first_moment, second_moment, left_stats, right_stats, left_basis, right_basis
            )
        ],
        device_count,
    )
    vector_owned = lax.dynamic_slice_in_dim(vector_sums, me * vector_width, vector_width, 1)
    shared_owned = vector_owned[:shared_count]
    split_owned = vector_owned[shared_count:vector_count]
    new_master, new_first, new_second, new_left, new_right, new_lbasis, new_rbasis = results
    shared_new_first, shared_new_second, shared_updated = adam_vector(
        shared_owned, shared_vectors, shared_first, shared_second
    )
    split_new_first, split_new_second, split_updated = adam_vector(
        split_owned, split_vectors[0], split_first[0], split_second[0]
    )
    return (
        encoder_states,
        decoder_states,
        source_grad,
        target_grad,
        new_master[None],
        new_first[None],
        new_second[None],
        new_left[None],
        new_right[None],
        new_lbasis[None],
        new_rbasis[None],
        shared_new_first,
        shared_new_second,
        shared_updated,
        split_new_first[None],
        split_new_second[None],
        split_updated[None],
    )


def solution(mesh):
    placed = (
        P("dp", None),
        P("dp", None),
        P("dp", None),
        P("dp", None),
        P("dp"),
        P(),
        P("tensor", "dp", None, None),
        P("tensor", "dp", None, None),
        P("tensor", "dp", None, None),
        P("tensor", "dp", None, None),
        P("tensor", "dp", None, None),
        P("tensor", "dp", None, None),
        P("tensor", "dp", None, None),
        P(None, "dp"),
        P(None, "dp"),
        P(None, "dp"),
        P("tensor", None, "dp"),
        P("tensor", None, "dp"),
        P("tensor", None, "dp"),
    )
    return jax.shard_map(
        local,
        mesh=mesh,
        in_specs=placed,
        out_specs=(
            P("dp", None),
            P("dp", None),
            P("dp", None),
            P("dp", None),
            P("tensor", "dp", None, None),
            P("tensor", "dp", None, None),
            P("tensor", "dp", None, None),
            P("tensor", "dp", None, None),
            P("tensor", "dp", None, None),
            P("tensor", "dp", None, None),
            P("tensor", "dp", None, None),
            P(None, "dp"),
            P(None, "dp"),
            P(None, "dp"),
            P("tensor", None, "dp"),
            P("tensor", None, "dp"),
            P("tensor", None, "dp"),
        ),
        check_vma=False,
    )
```

```python
import functools
from functools import partial

import jax
import jax.numpy as jnp
from jax import lax
from jax.experimental import pallas as pl
from jax.experimental.pallas import tpu as pltpu
from jax.sharding import PartitionSpec as P

HD = 64
KEEP = 512
STEP = 10


BETA_ONE = 0.9
BETA_TWO = 0.95
ADAM_EPSILON = 1e-08
MATRIX_RATE = 0.1
VECTOR_RATE = 0.5
WEIGHT_DECAY = 0.01
NORM_EPSILON = 1e-05
TILE = 128
PANEL = 32
ROWS = 256
KEYS = 256
PAIR = 2 * HD
NN = ((1,), (0,))
NT = ((1,), (1,))
F32 = jnp.float32
BF16 = jnp.bfloat16
MESH = pl.DeviceIdType.MESH
ANY = pl.BlockSpec(memory_space=pl.ANY)


def matrix_list(model_width, hidden_width, tensor_count):
    half_width = model_width // tensor_count
    hidden_half = hidden_width // tensor_count
    return [
        ("enc_qkv", model_width, 3 * half_width),
        ("enc_out", half_width, model_width),
        ("enc_up", model_width, hidden_half),
        ("enc_down", hidden_half, model_width),
        ("dec_qkv", model_width, 3 * half_width),
        ("dec_out", half_width, model_width),
        ("crs_q", model_width, half_width),
        ("crs_kv", model_width, 2 * half_width),
        ("crs_out", half_width, model_width),
        ("dec_up", model_width, hidden_half),
        ("dec_down", hidden_half, model_width),
    ]


def halves(x):
    high = x.astype(BF16)
    return high, (x - high.astype(F32)).astype(BF16)


def mm(a, b, dims=NN):
    ah, al = halves(a)
    bh, bl = halves(b)
    return times(jnp.concatenate([ah, ah, al], 1), jnp.concatenate([bh, bl, bh], dims[1][0]), dims)


def chip_grid(device_count):
    if device_count == 16:
        return 4, 2, 2
    side = round(device_count ** (1 / 3))
    if side**3 == device_count:
        return side, side, side
    return 1, 1, device_count


def place(grid):
    zs, ys, xs = grid
    me = lax.axis_index("dp")
    return me // (ys * xs), lax.rem(me // xs, ys), lax.rem(me, xs)


def peers(grid):
    zs, ys, xs = grid
    z, y, x = place(grid)

    def device(zz, yy, xx):
        return {"dp": (zz * ys + yy) * xs + xx}

    return (
        lambda k: device(lax.rem(z + k, zs), y, x),
        lambda k: device(z, lax.rem(y + k, ys), x),
        lambda k: device(z, y, lax.rem(x + k, xs)),
    )


def greet(grid):
    barrier = pltpu.get_barrier_semaphore()
    count = 0
    for size, peer in zip(grid, peers(grid)):
        for k in range(1, size):
            pl.semaphore_signal(barrier, inc=1, device_id=peer(k), device_id_type=MESH)
            count += 1
    pl.semaphore_wait(barrier, count)


def remote(src, dst, send, recv, device):
    return pltpu.make_async_remote_copy(
        src_ref=src, dst_ref=dst, send_sem=send, recv_sem=recv, device_id=device, device_id_type=MESH
    )


def chunking(slots):
    half = slots // 2
    chunks = min(16, half)
    return half, chunks, half // chunks


def owner_kernel(grid, *refs):
    zs, ys, xs = grid
    used_ref, in_ref, small_ref = refs[:3]
    state_in, state_out, small_out_ref, work_out_ref = refs[3:10], refs[10:17], refs[17], refs[18]
    state, rest = refs[19:26], refs[26:]
    (own0, own1, ra0, ra1, rb0, rb1, rc0, rc1, total, rs_z, rs_y, rs_x, work, load_sem,
     as0, as1, ar0, ar1, bs0, bs1, br0, br1, cs0, cs1, cr0, cr1,
     ssz, ssy, ssx, srz, sry, srx, state_sem) = rest
    own, rec_a, rec_b, rec_c = (own0, own1), (ra0, ra1), (rb0, rb1), (rc0, rc1)
    a_send, a_recv, b_send, b_recv, c_send, c_recv = (as0, as1), (ar0, ar1), (bs0, bs1), (br0, br1), (cs0, cs1), (cr0, cr1)
    rec_s, s_send, s_recv = (rs_z, rs_y, rs_x), (ssz, ssy, ssx), (srz, sry, srx)

    z, y, x = place(grid)
    tos = peers(grid)
    to_z, to_y, to_x = tos
    slots = state[0].shape[0]
    half = slots // 2
    first = ((xs, x, to_x), (ys, y, to_y))
    second = ((ys, y, to_y), (xs, x, to_x))

    def source(g, c, other):
        slot = g * half + c
        return in_ref.at[:, :, other, slot] if g == 0 else in_ref.at[:, other, :, slot]

    def load(g, c):
        return pltpu.make_async_copy(source(g, c, first[g][1]), own[g].at[c], load_sem.at[g, c])

    def send_a(g, c, k):
        count, mine, to = first[g]
        return remote(source(g, c, lax.rem(mine + k, count)), rec_a[g].at[c, k - 1],
                      a_send[g].at[c, k - 1], a_recv[g].at[c, k - 1], to(k))

    def send_b(g, c, k):
        count, mine, to = second[g]
        return remote(own[g].at[c, :, lax.rem(mine + k, count)], rec_b[g].at[c, k - 1],
                      b_send[g].at[c, k - 1], b_recv[g].at[c, k - 1], to(k))

    def send_c(g, c, k):
        return remote(own[g].at[c, lax.rem(z + k, zs), second[g][1]], rec_c[g].at[c, k - 1],
                      c_send[g].at[c, k - 1], c_recv[g].at[c, k - 1], to_z(k))

    def start_a(c):
        for g in range(2):
            for k in range(1, first[g][0]):
                send_a(g, c, k).start()

    def send_s(axis, k):
        return remote(total.at[2 - axis], rec_s[axis].at[k - 1],
                      s_send[axis].at[k - 1], s_recv[axis].at[k - 1], tos[axis](k))

    def small_start(axis):
        for k in range(1, grid[axis]):
            send_s(axis, k).start()

    def small_add(axis):
        value = total[2 - axis]
        for k in range(1, grid[axis]):
            send_s(axis, k).wait_recv()
            value += rec_s[axis][k - 1]
        return value

    def each(count, action):
        def go(c, carry):
            action(c)
            return carry

        lax.fori_loop(0, count, go, 0)

    def load_all(c):
        for g in range(2):
            load(g, c).start()

    each(half, load_all)
    for i in range(7):
        pltpu.make_async_copy(state_in[i], state[i], state_sem.at[0, i]).start()
    total[0] = small_ref[...]
    greet(grid)
    small_start(2)
    start_a(0)
    total[1] = small_add(2)
    small_start(1)
    total[2] = small_add(1)
    small_start(0)
    for i in range(7):
        pltpu.make_async_copy(state_in[i], state[i], state_sem.at[0, i]).wait()

    def step_a(c):
        for g in range(2):
            load(g, c).wait()
            for k in range(1, first[g][0]):
                send_a(g, c, k).wait_recv()

        @pl.when(c + 1 < half)
        def _():
            start_a(c + 1)

        for g in range(2):
            n2 = second[g][0]

            def add(e, carry, g=g, n2=n2):
                a, b = e // n2, lax.rem(e, n2)
                value = own[g][c, a, b].astype(F32)
                for k in range(1, first[g][0]):
                    value += rec_a[g][c, k - 1, a, b].astype(F32)
                own[g][c, a, b] = value.astype(BF16)
                return carry

            lax.fori_loop(0, zs * n2, add, 0)
            for k in range(1, n2):
                send_b(g, c, k).start()

    def step_b(c):
        for g in range(2):
            n2, mine = second[g][0], second[g][1]
            for k in range(1, n2):
                send_b(g, c, k).wait_recv()

            def add(a, carry, g=g, n2=n2, mine=mine):
                value = own[g][c, a, mine].astype(F32)
                for k in range(1, n2):
                    value += rec_b[g][c, k - 1, a].astype(F32)
                own[g][c, a, mine] = value.astype(BF16)
                return carry

            lax.fori_loop(0, zs, add, 0)
            for k in range(1, zs):
                send_c(g, c, k).start()

    def step_c(c):
        batch = lax.rem(c // 4, 2)
        for g in range(2):
            for k in range(1, zs):
                send_c(g, c, k).wait_recv()
        for g in range(2):
            value = own[g][c, z, second[g][1]].astype(F32)
            for k in range(1, zs):
                value += rec_c[g][c, k - 1].astype(F32)
            slot = g * half + c
            value = jnp.where(used_ref[slot] > 0, value, 0.0)
            soap_products(value, slot, state, work, batch, 2 * (4 * g + lax.rem(c, 4)))

    def finish(b):
        batch = lax.rem(b, 2)
        place_bases(work, batch, state[5], state[6], 4 * b)
        emit(b)

    def emit(b):
        for g in range(2):
            span = pl.ds(g * half + 4 * b, 4)
            for i in range(7):
                pltpu.make_async_copy(state[i].at[span], state_out[i].at[span], state_sem.at[1, i]).start()

    def round_of(r, carry):
        for s in range(4):
            t = 4 * r + s

            @pl.when(t < half)
            def _(t=t):
                step_a(t)

            @pl.when((t >= 1) & (t <= half))
            def _(t=t):
                step_b(t - 1)

            @pl.when((t >= 2) & (t < half + 2))
            def _(t=t):
                step_c(t - 2)

            if s >= 1:

                @pl.when((r >= 1) & (r < half // 4))
                def _(s=s):
                    panel_step(work, lax.rem(r - 1, 2), s - 1)

            else:

                @pl.when((r >= 2) & (r <= half // 4))
                def _():
                    panel_step(work, lax.rem(r - 2, 2), TILE // PANEL - 1)
                    finish(r - 2)

        return carry

    lax.fori_loop(0, half // 4 + 1, round_of, 0)
    emit(half // 4 - 1)
    work_out_ref[...] = work[(half // 4 - 1) % 2]
    small_out_ref[...] = small_add(0)
    for axis in range(3):
        for k in range(1, grid[axis]):
            send_s(axis, k).wait_send()

    def end(c):
        for g in range(2):
            for k in range(1, first[g][0]):
                send_a(g, c, k).wait_send()
            for k in range(1, second[g][0]):
                send_b(g, c, k).wait_send()
            for k in range(1, zs):
                send_c(g, c, k).wait_send()

    each(half, end)
    for i in range(7):
        pltpu.make_async_copy(state[i], state_out[i], state_sem.at[1, i]).wait()


def place_bases(work, batch, left_ref, right_ref, at):
    half = left_ref.shape[0] // 2
    for g in range(2):
        for e in range(4):
            left_ref[g * half + at + e] = work[batch, 2 * (4 * g + e), :, TILE:].T
            right_ref[g * half + at + e] = work[batch, 2 * (4 * g + e) + 1, :, TILE:].T


def last_bases_kernel(work_ref, *refs):
    state_in, state_out, state, work, sems = refs[:7], refs[7:14], refs[14:21], refs[21], refs[22]
    half = state[0].shape[0] // 2

    def copy_in(i):
        return pltpu.make_async_copy(state_in[i], state[i], sems.at[0, i])

    def copy_out(i):
        return pltpu.make_async_copy(state[i], state_out[i], sems.at[1, i])

    for i in range(7):
        copy_in(i).start()
    work[0] = work_ref[...]
    panel_step(work, 0, 0)
    for i in range(7):
        copy_in(i).wait()
        if i < 5:
            copy_out(i).start()
    for p in range(1, TILE // PANEL):
        panel_step(work, 0, p)
    place_bases(work, 0, state[5], state[6], half - 4)
    for i in range(5, 7):
        copy_out(i).start()
    for i in range(7):
        copy_out(i).wait()


def last_bases(work, state):
    whole = state[0].shape
    return pl.pallas_call(
        last_bases_kernel,
        out_shape=[jax.ShapeDtypeStruct(whole, F32)] * 7,
        in_specs=[pl.BlockSpec(memory_space=pltpu.VMEM)] + [ANY] * 7,
        out_specs=[ANY] * 7,
        scratch_shapes=[pltpu.VMEM(whole, F32)] * 7
        + [pltpu.VMEM((1,) + work.shape, F32), pltpu.SemaphoreType.DMA((2, 7))],
        compiler_params=pltpu.CompilerParams(vmem_limit_bytes=56 << 20),
        name="last_bases",
    )(work, *state)


def soap_products(g, i, state, work, batch, at):
    w_ref, m_ref, v_ref, l_ref, r_ref, ql_ref, qr_ref = state
    c1 = 1.0 - BETA_ONE**STEP
    c2 = 1.0 - BETA_TWO**STEP
    ql = ql_ref[i]
    qr = qr_ref[i]
    gt = g.T
    nm = BETA_ONE * m_ref[i] + (1.0 - BETA_ONE) * g
    m_ref[i] = nm
    side = mm(jnp.concatenate([g, nm], 0), qr)
    both = mm(ql.T, jnp.concatenate([side[:TILE], side[TILE:]], 1))
    rotated, rotated_first = both[:, :TILE], both[:, TILE:]
    nv = BETA_TWO * v_ref[i] + (1.0 - BETA_TWO) * rotated * rotated
    v_ref[i] = nv
    normed = rotated_first / c1 / (jnp.sqrt(nv / c2) + ADAM_EPSILON)
    step = mm(mm(ql, normed), qr, NT)
    w = w_ref[i]
    w_ref[i] = w - MATRIX_RATE * step - MATRIX_RATE * WEIGHT_DECAY * w
    for k, (ref, turn, left, right) in enumerate(((l_ref, ql, g, gt), (r_ref, qr, gt, g))):
        stat = BETA_TWO * ref[i] + (1.0 - BETA_TWO) * mm(left, right)
        ref[i] = stat
        a = mm(stat, turn)
        at_turned = a.T
        work[batch, at + k, :, :TILE] = mm(at_turned, a)
        work[batch, at + k, :, TILE:] = at_turned


def panel_step(work, batch, p):
    count = work.shape[1]
    per = TILE // (2 * PANEL)
    r0 = p * PANEL
    rows = count // per * 8
    lane = lax.broadcasted_iota(jnp.int32, (rows, TILE), 1)
    start = lane // (2 * PANEL) * (2 * PANEL)
    row = lax.rem(lax.broadcasted_iota(jnp.int32, (rows, TILE), 0), 8)
    sub = lax.broadcasted_iota(jnp.int32, (count // per, 8, TILE), 1)
    eye = (
        lax.broadcasted_iota(jnp.int32, (PANEL, PANEL), 0) == lax.broadcasted_iota(jnp.int32, (PANEL, PANEL), 1)
    ).astype(F32)
    packs = []
    for q in range(count // per):
        pieces = []
        for k in range(per):
            pieces += [work[batch, q * per + k, r0:r0 + PANEL, r0:r0 + PANEL], eye]
        packs.append(jnp.concatenate(pieces, 1)[None])
    x = jnp.concatenate(packs, 0)
    strips = [x[:, 8 * e:8 * e + 8, :] for e in range(PANEL // 8)]

    def segment(strip, index):
        return jnp.take_along_axis(strip.reshape(-1, TILE), index, axis=1).reshape(strip.shape)

    for j in range(0, PANEL, 2):
        e0, here = j // 8, j % 8
        one = [segment(strip, start + j) for strip in strips[e0:]]
        two = [segment(strip, start + j + 1) for strip in strips[e0:]]
        corner = one[0][:, here:here + 1, :]
        side = one[0][:, here + 1:here + 2, :]
        inverse = 1.0 / corner
        inverse_two = corner * (1.0 / (corner * two[0][:, here + 1:here + 2, :] - side * side))
        shift = side * inverse
        ratio = strips[e0][:, here:here + 1, :] * inverse
        next_off = side * ratio
        ratio_two = (strips[e0][:, here + 1:here + 2, :] - next_off) * inverse_two
        ratio_one = ratio - shift * ratio_two
        for e in range(e0, PANEL // 8):
            change = one[e - e0] * ratio_one + two[e - e0] * ratio_two
            if e == e0:
                change = jnp.where(sub > here + 1, change, jnp.where(sub == here + 1, next_off, 0.0))
            strips[e] = strips[e] - change
    for e in range(PANEL // 8):
        strips[e] = strips[e] * lax.rsqrt(segment(strips[e], start + 8 * e + row))
    x = jnp.concatenate(strips, 1)
    for q in range(count // per):
        for k in range(per):
            i = q * per + k
            inverse = x[q, :, 2 * PANEL * k + PANEL:2 * PANEL * (k + 1)]
            u = mm(inverse, work[batch, i, r0:r0 + PANEL, :])
            work[batch, i, r0:r0 + PANEL, TILE:] = u[:, TILE:]
            if r0 + PANEL < TILE:
                high, low = halves(u)
                left = jnp.concatenate([u[:, :TILE], u[:, :TILE], low[:, :TILE].astype(F32)], 0).T
                work[batch, i, r0 + PANEL:, :] -= times(
                    left[r0 + PANEL:, :].astype(BF16), jnp.concatenate([high, low, high], 0)
                )


def some(shape):
    return tuple(max(1, s) for s in shape)


def owner_update(used, slot_grads, small, state, device_count):
    grid = chip_grid(device_count)
    zs, ys, xs = grid
    slots = slot_grads.shape[0] // device_count
    half = slots // 2
    block = (TILE, TILE)
    dma = pltpu.SemaphoreType.DMA
    firsts, seconds = (xs, ys), (ys, xs)
    whole = (slots,) + block
    scratch = (
        [pltpu.VMEM(whole, F32)] * 7
        + [pltpu.VMEM((half, zs, seconds[g]) + block, BF16) for g in range(2)]
        + [pltpu.VMEM(some((half, firsts[g] - 1, zs, seconds[g])) + block, BF16) for g in range(2)]
        + [pltpu.VMEM(some((half, seconds[g] - 1, zs)) + block, BF16) for g in range(2)]
        + [pltpu.VMEM(some((half, zs - 1)) + block, BF16) for g in range(2)]
        + [pltpu.VMEM((3,) + small.shape, F32)]
        + [pltpu.VMEM((max(1, n - 1),) + small.shape, F32) for n in grid]
        + [pltpu.VMEM((2, 16, TILE, 2 * TILE), F32)]
        + [dma((2, half))]
        + [dma(some((half, firsts[g] - 1))) for g in range(2)] * 2
        + [dma(some((half, seconds[g] - 1))) for g in range(2)] * 2
        + [dma(some((half, zs - 1))) for g in range(2)] * 2
        + [dma((max(1, n - 1),)) for n in grid] * 2
        + [dma((2, 7))]
    )
    results = pl.pallas_call(
        functools.partial(owner_kernel, grid),
        out_shape=[jax.ShapeDtypeStruct(whole, F32)] * 7
        + [jax.ShapeDtypeStruct(small.shape, F32), jax.ShapeDtypeStruct((16, TILE, 2 * TILE), F32)],
        in_specs=[pl.BlockSpec(memory_space=pltpu.SMEM), ANY, pl.BlockSpec(memory_space=pltpu.VMEM)] + [ANY] * 7,
        out_specs=[ANY] * 7 + [pl.BlockSpec(memory_space=pltpu.VMEM)] * 2,
        scratch_shapes=scratch,
        compiler_params=pltpu.CompilerParams(collective_id=1, has_side_effects=True, vmem_limit_bytes=56 << 20),
        name="owner_update",
    )(used, slot_grads.reshape(zs, ys, xs, slots, TILE, TILE), small, *state)
    return last_bases(results[8], results[:7]), results[7]


def ag_kernel(grid, wide_ref, small_ref, out_ref, small_out_ref, own_ref,
              load_sem, z_send, z_recv, b_send0, b_send1, b_recv0, b_recv1, a_send0, a_send1, a_recv0, a_recv1,
              s_load, ssz, ssy, ssx, srz, sry, srx):
    zs, ys, xs = grid
    z, y, x = place(grid)
    tos = peers(grid)
    to_z, to_y, to_x = tos
    slots = own_ref.shape[0]
    half, chunks, size = chunking(slots)
    first = ((xs, to_x), (ys, to_y))
    second = ((ys, to_y), (xs, to_x))
    b_send, b_recv, a_send, a_recv = (b_send0, b_send1), (b_recv0, b_recv1), (a_send0, a_send1), (a_recv0, a_recv1)
    s_send, s_recv = (ssz, ssy, ssx), (srz, sry, srx)

    def span(g, c):
        return pl.ds(g * half + c * size, size)

    def send_z(g, c, k):
        return remote(own_ref.at[span(g, c)], out_ref.at[z, y, x, span(g, c)],
                      z_send.at[g, c, k - 1], z_recv.at[g, c, k - 1], to_z(k))

    def send_b(g, c, k):
        part = out_ref.at[:, y, x, span(g, c)]
        return remote(part, part, b_send[g].at[c, k - 1], b_recv[g].at[c, k - 1], second[g][1](k))

    def send_a(g, c, k):
        part = out_ref.at[:, :, x, span(g, c)] if g == 0 else out_ref.at[:, y, :, span(g, c)]
        return remote(part, part, a_send[g].at[c, k - 1], a_recv[g].at[c, k - 1], first[g][1](k))

    def send_s(axis, k):
        if axis == 0:
            source, target = small_ref, small_out_ref.at[z, y, x]
        else:
            source = target = small_out_ref.at[:, y, x] if axis == 1 else small_out_ref.at[:, :, x]
        return remote(source, target, s_send[axis].at[k - 1], s_recv[axis].at[k - 1], tos[axis](k))

    own_ref[...] = wide_ref[...].astype(BF16)
    keep = pltpu.make_async_copy(own_ref, out_ref.at[z, y, x], load_sem)
    keep_small = pltpu.make_async_copy(small_ref, small_out_ref.at[z, y, x], s_load)
    keep.start()
    keep_small.start()
    greet(grid)

    for k in range(1, grid[0]):
        send_s(0, k).start()
    def start_z(c):
        for g in range(2):
            for k in range(1, zs):
                send_z(g, c, k).start()

    def small_wait(axis):
        for k in range(1, grid[axis]):
            send_s(axis, k).wait_recv()

    def small_start(axis):
        for k in range(1, grid[axis]):
            send_s(axis, k).start()

    start_z(0)
    for t in range(chunks + 1):
        if t < chunks:
            for g in range(2):
                for k in range(1, zs):
                    send_z(g, t, k).wait_recv()
            if t == 0:
                keep.wait()
                keep_small.wait()
                small_wait(0)
                small_start(1)
            if t + 1 < chunks:
                start_z(t + 1)
            for g in range(2):
                for k in range(1, second[g][0]):
                    send_b(g, t, k).start()
        if t >= 1:
            for g in range(2):
                for k in range(1, second[g][0]):
                    send_b(g, t - 1, k).wait_recv()
                for k in range(1, first[g][0]):
                    send_a(g, t - 1, k).start()
        if t == 1:
            small_wait(1)
            small_start(2)
    small_wait(2)
    for c in range(chunks):
        for g in range(2):
            for k in range(1, first[g][0]):
                send_a(g, c, k).wait_recv()
    for axis in range(3):
        for k in range(1, grid[axis]):
            send_s(axis, k).wait_send()
    for c in range(chunks):
        for g in range(2):
            for k in range(1, zs):
                send_z(g, c, k).wait_send()
            for k in range(1, second[g][0]):
                send_b(g, c, k).wait_send()
            for k in range(1, first[g][0]):
                send_a(g, c, k).wait_send()


def gather_all(own, small, device_count):
    grid = chip_grid(device_count)
    zs, ys, xs = grid
    slots = own.shape[0]
    half, chunks, size = chunking(slots)
    dma = pltpu.SemaphoreType.DMA
    firsts, seconds = (xs, ys), (ys, xs)
    scratch = (
        [pltpu.VMEM(own.shape, BF16), dma, dma(some((2, chunks, zs - 1))), dma(some((2, chunks, zs - 1)))]
        + [dma(some((chunks, seconds[g] - 1))) for g in range(2)] * 2
        + [dma(some((chunks, firsts[g] - 1))) for g in range(2)] * 2
        + [dma]
        + [dma((max(1, n - 1),)) for n in grid] * 2
    )
    blocks, smalls = pl.pallas_call(
        functools.partial(ag_kernel, grid),
        out_shape=[jax.ShapeDtypeStruct(grid + own.shape, BF16), jax.ShapeDtypeStruct(grid + small.shape, small.dtype)],
        in_specs=[pl.BlockSpec(memory_space=pltpu.VMEM)] * 2,
        out_specs=[ANY, ANY],
        scratch_shapes=scratch,
        compiler_params=pltpu.CompilerParams(collective_id=2, has_side_effects=True, vmem_limit_bytes=56 << 20),
        name="gather_all",
    )(own, small)
    return blocks.reshape((-1,) + own.shape[1:]), smalls.reshape((-1,) + small.shape)


def unpack_and_attend(packed, slots, shapes, x, split, places, half):
    length, width = x.shape
    span, count = min(length, 512), len(shapes)

    def kernel(slots_ref, split_ref, packed_ref, x_ref, *refs):
        mats, mixed_out, attended_out, totals_ref = refs[:count], refs[count], refs[count + 1], refs[count + 2]
        near, rest = refs[count + 3:2 * count + 3], refs[2 * count + 3:]
        x_near, mixed_ref, attended_ref, score_ref, turned_ref, sems, own_sems = rest

        def whole(index):
            return pltpu.make_async_copy(near[index], mats[index], sems.at[1, index])

        load_x = pltpu.make_async_copy(x_ref, x_near, own_sems.at[0])
        load_x.start()
        offset = 0
        for index, (height, breadth) in enumerate(shapes):
            down, across = height // TILE, breadth // TILE

            def start(i, carry, index=index, offset=offset, across=across):
                for j in range(across):
                    tile = near[index].at[pl.ds(pl.multiple_of(i * TILE, TILE), TILE), j * TILE:(j + 1) * TILE]
                    slot = packed_ref.at[slots_ref[offset + i * across + j]]
                    pltpu.make_async_copy(slot, tile, sems.at[0, index]).start()
                return carry

            lax.fori_loop(0, down, start, 0)
            offset += down * across

        def landed(index):
            pltpu.make_async_copy(near[index], near[index], sems.at[0, index]).wait()
            whole(index).start()

        load_x.wait()
        landed(0)
        mix(x_near, near[0], bias_row(split_ref, places, ("enc_q", None, "enc_v"), half), mixed_ref)
        keep_mixed = pltpu.make_async_copy(mixed_ref, mixed_out, own_sems.at[1])
        keep_mixed.start()
        for index in range(1, count):
            landed(index)
        totals_ref[...] = jnp.zeros_like(totals_ref)
        attend(
            mixed_ref.at[:, :half], mixed_ref.at[:, half:2 * half], mixed_ref.at[:, 2 * half:],
            attended_ref, totals_ref, score_ref, turned_ref, False, span,
        )
        keep_attended = pltpu.make_async_copy(attended_ref, attended_out, own_sems.at[2])
        keep_attended.start()
        for index in range(count):
            whole(index).wait()
        keep_mixed.wait()
        keep_attended.wait()

    results = pl.pallas_call(
        kernel,
        out_shape=[jax.ShapeDtypeStruct(s, BF16) for s in shapes]
        + [shape(length, 3 * half, dtype=BF16), shape(length, half, dtype=BF16), shape(8, length)],
        in_specs=[pl.BlockSpec(memory_space=pltpu.SMEM), VM, ANY, ANY],
        out_specs=[ANY] * (count + 2) + [VM],
        scratch_shapes=[held(*s, dtype=BF16) for s in shapes]
        + [
            held(length, width, dtype=BF16), held(length, 3 * half, dtype=BF16), held(length, half, dtype=BF16),
            held(2, length, span), held(half, length, dtype=BF16),
            pltpu.SemaphoreType.DMA((2, count)), pltpu.SemaphoreType.DMA((3,)),
        ],
        compiler_params=pltpu.CompilerParams(vmem_limit_bytes=56 << 20),
        name="unpack_and_attend",
    )(slots, split, packed, x)
    return results[:count], results[count:]


def weight_grads_kernel(plan, used, vectors, passed, slots_ref, *refs):
    arrays, refs = refs[:used], refs[used:]
    given, refs = refs[:len(vectors)], refs[len(vectors):]
    refs = refs[passed:]
    packed, refs = refs[0], refs[1:]
    if vectors:
        rows_ref, refs = refs[0], refs[1:]
    held, refs = refs[:used], refs[used:]
    turned, refs = refs[0], refs[1:]
    results, sems = refs[:len(plan)], refs[len(plan):]
    load_sem, store_sem = sems

    def load(i):
        return pltpu.make_async_copy(arrays[i], held[i], load_sem.at[i])

    order = []
    for left, tokens, right, *rest in plan:
        for i in (left, right):
            if i not in order:
                order.append(i)
    for i in order:
        load(i).start()
    if vectors:
        width = rows_ref.shape[1]
        rows_ref[...] = jnp.zeros_like(rows_ref)
        for source, (at, pieces) in zip(given, vectors):
            if pieces is None:
                rows_ref[at:at + 3, :] = source[0:3, :]
                continue
            for begin, end in pieces:
                while begin < end:
                    lane = at % width
                    size = min(end - begin, width - lane)
                    rows_ref[at // width:at // width + 1, lane:lane + size] = source[:, begin:begin + size]
                    begin, at = begin + size, at + size
    ready = set()
    last = None
    for index, (left, tokens, right, offset, stride, down, across) in enumerate(plan):
        for i in (left, right):
            if i not in ready:
                ready.add(i)
                load(i).wait()
        height = down * TILE
        if last != (left, tokens):
            for j in range(down):
                turned[j * TILE:(j + 1) * TILE, :tokens] = (
                    held[left][:tokens, j * TILE:(j + 1) * TILE].astype(F32).T.astype(BF16)
                )
            last = (left, tokens)
        result = results[index]
        group = 3 if across % 3 == 0 else 1

        def columns(n, carry, right=right, tokens=tokens, height=height, result=result, offset=offset,
                    stride=stride, down=down, group=group, index=index):
            lanes = pl.ds(pl.multiple_of(n * group * TILE, TILE), group * TILE)
            result[:, lanes] = times(turned[:height, :tokens], held[right][:tokens, lanes]).astype(BF16)

            def send(i, carry):
                for j in range(group):
                    tile = result.at[
                        pl.ds(pl.multiple_of(i * TILE, TILE), TILE),
                        pl.ds(pl.multiple_of((n * group + j) * TILE, TILE), TILE),
                    ]
                    slot = packed.at[slots_ref[offset + i * stride + n * group + j]]
                    pltpu.make_async_copy(tile, slot, store_sem.at[index]).start()
                return carry

            lax.fori_loop(0, down, send, 0)
            return carry

        lax.fori_loop(0, across // group, columns, 0)
    for index in range(len(plan)):
        pltpu.make_async_copy(results[index], results[index], store_sem.at[index]).wait()


def weight_grads(matrices, slots, slot_count, packed=None, vectors=None):
    arrays, plan, results = [], [], []

    def index_of(array):
        for i, other in enumerate(arrays):
            if other is array:
                return i
        arrays.append(array)
        return len(arrays) - 1

    for offset, parts in matrices:
        height = parts[0][0].shape[1]
        stride = sum(right.shape[1] for left, right in parts) // TILE
        for left, right in parts:
            across = right.shape[1] // TILE
            plan.append((index_of(left), right.shape[0], index_of(right), offset, stride, height // TILE, across))
            results.append(pltpu.VMEM((height, right.shape[1]), BF16))
            offset += across
    tall = max(entry[5] for entry in plan) * TILE
    long = max(entry[1] for entry in plan)
    out_shape = [jax.ShapeDtypeStruct((slot_count, TILE, TILE), BF16)]
    given, layout = [], []
    if vectors:
        rows, width, items = vectors
        out_shape.append(jax.ShapeDtypeStruct((rows, width), F32))
        given = [item[0] for item in items]
        layout = [item[1:] for item in items]
    passed = [] if packed is None else [packed]
    return pl.pallas_call(
        functools.partial(weight_grads_kernel, plan, len(arrays), layout, len(passed)),
        out_shape=out_shape,
        in_specs=[pl.BlockSpec(memory_space=pltpu.SMEM)] + [ANY] * len(arrays)
        + [pl.BlockSpec(memory_space=pltpu.VMEM)] * len(given) + [ANY] * len(passed),
        out_specs=[ANY] + [pl.BlockSpec(memory_space=pltpu.VMEM)] * (len(out_shape) - 1),
        scratch_shapes=[pltpu.VMEM(a.shape, a.dtype) for a in arrays] + [pltpu.VMEM((tall, long), BF16)] + results
        + [pltpu.SemaphoreType.DMA((len(arrays),)), pltpu.SemaphoreType.DMA((len(plan),))],
        input_output_aliases={} if packed is None else {1 + len(arrays) + len(given): 0},
        compiler_params=pltpu.CompilerParams(vmem_limit_bytes=56 << 20),
        name="weight_grads",
    )(slots, *arrays, *given, *passed)


VM = pl.BlockSpec(memory_space=pltpu.VMEM)


def times(left, right, dims=NN):
    return lax.dot_general(left, right, (dims, ((), ())), preferred_element_type=F32)


def rows_of(t, size=ROWS):
    return pl.ds(pl.multiple_of(t * size, size), size)


class Swap:
    def __init__(self, out, into, send_sem, recv_sem):
        self.out, self.into, self.send_sem, self.recv_sem = out, into, send_sem, recv_sem

    @staticmethod
    def scratch(tiles, width):
        dma = pltpu.SemaphoreType.DMA((tiles,))
        held = pltpu.VMEM((tiles, ROWS, width), BF16)
        return [held, held, dma, dma]

    @staticmethod
    def greet():
        barrier = pltpu.get_barrier_semaphore()
        other = {"tensor": 1 - lax.axis_index("tensor")}
        pl.semaphore_signal(barrier, inc=1, device_id=other, device_id_type=MESH)
        pl.semaphore_wait(barrier, 1)

    def copy(self, t):
        return pltpu.make_async_remote_copy(
            src_ref=self.out.at[t],
            dst_ref=self.into.at[t],
            send_sem=self.send_sem.at[t],
            recv_sem=self.recv_sem.at[t],
            device_id={"tensor": 1 - lax.axis_index("tensor")},
            device_id_type=MESH,
        )

    def give(self, t, value):
        self.out[t] = value.astype(BF16)
        self.copy(t).start()

    def take(self, t):
        self.copy(t).wait()
        return self.out[t].astype(F32) + self.into[t].astype(F32)


class Rows:
    def __init__(self, ref, rows):
        self.ref, self.rows = ref, rows

    def __getitem__(self, index):
        at = self.rows[index[0].start]
        return self.ref[at:at + 1, :]


def bias_places(half, hidden_half):
    places, at = {}, 0
    for name, length in (
        ("enc_q", half), ("enc_v", half), ("enc_up", hidden_half), ("dec_q", half), ("dec_v", half),
        ("crs_q", half), ("crs_v", half), ("dec_up", hidden_half),
    ):
        places[name] = slice(at, at + length)
        at += length
    return places


def bias_row(split_ref, places, names, half):
    zero = jnp.zeros((1, half), F32)
    return jnp.concatenate([zero if name is None else split_ref[:, places[name]] for name in names], 1)


def standardize(values):
    center = values - jnp.mean(values, -1, keepdims=True)
    scale = lax.rsqrt(jnp.mean(center * center, -1, keepdims=True) + NORM_EPSILON)
    return center * scale, scale


def norm_back(grad, unit, scale, gain):
    inner = grad * gain
    return scale * (
        inner - jnp.mean(inner, -1, keepdims=True) - unit * jnp.mean(inner * unit, -1, keepdims=True)
    )


def add_sums(sums_ref, grad_in, grad_out, unit):
    sums_ref[0:1, :] += jnp.sum(grad_in, 0, keepdims=True)
    sums_ref[1:2, :] += jnp.sum(grad_out * unit, 0, keepdims=True)
    sums_ref[2:3, :] += jnp.sum(grad_out, 0, keepdims=True)


def head_mask(shape):
    return lax.broadcasted_iota(jnp.int32, shape, 1) < HD


def attend(query_ref, key_ref, value_ref, attended_ref, totals_ref, score_ref, turned_ref, causal, span):
    queries, keys = query_ref.shape[0], key_ref.shape[0]
    pairs = query_ref.shape[1] // PAIR
    chunks = keys // KEYS
    for j in range(pairs):
        turned_ref[j * PAIR:(j + 1) * PAIR, :] = (
            value_ref[:, j * PAIR:(j + 1) * PAIR].astype(F32).T.astype(BF16)
        )
    for i in range(queries // span):
        mine = slice(i * span, (i + 1) * span)

        def pair(j, carry, i=i, mine=mine):
            lanes = pl.ds(pl.multiple_of(j * PAIR, PAIR), PAIR)
            query = query_ref[mine, lanes] * jnp.asarray(HD**-0.5, BF16)
            first = head_mask(query.shape)
            parts = []
            for h in range(2):
                masked = jnp.where(first if h == 0 else ~first, query, jnp.zeros_like(query))
                top = jnp.full((1, span), -jnp.inf, F32)
                for c in range(chunks):
                    if causal and c * KEYS >= (i + 1) * span:
                        continue
                    scores = times(key_ref[c * KEYS:(c + 1) * KEYS, lanes], masked, NT)
                    if causal and (c + 1) * KEYS > i * span:
                        key_at = c * KEYS + lax.broadcasted_iota(jnp.int32, scores.shape, 0)
                        query_at = i * span + lax.broadcasted_iota(jnp.int32, scores.shape, 1)
                        scores = jnp.where(key_at <= query_at, scores, -1000000000.0)
                    score_ref[h, c * KEYS:(c + 1) * KEYS, :] = scores
                    top = jnp.maximum(top, jnp.max(scores, 0, keepdims=True))
                total = jnp.zeros((1, span), F32)
                mixed = jnp.zeros((HD, span), F32)
                value_rows = pl.ds(pl.multiple_of(j * PAIR + h * HD, HD), HD)
                for c in range(chunks):
                    if causal and c * KEYS >= (i + 1) * span:
                        continue
                    probs = jnp.exp(score_ref[h, c * KEYS:(c + 1) * KEYS, :] - top)
                    total += jnp.sum(probs, 0, keepdims=True)
                    mixed += times(turned_ref[value_rows, c * KEYS:(c + 1) * KEYS], probs.astype(BF16))
                parts.append(mixed * (1.0 / total))
                totals_ref[pl.ds(2 * j + h, 1), mine] = top + jnp.log(total)
            attended_ref[mine, lanes] = jnp.concatenate(parts, 0).T.astype(BF16)
            return carry

        lax.fori_loop(0, pairs, pair, 0)


def attend_back(
    query_ref, key_ref, value_ref, attended_ref, totals_ref, grad_ref,
    grad_query_ref, grad_key_ref, grad_value_ref, turned_ref, causal,
):
    queries, keys = grad_ref.shape[0], key_ref.shape[0]
    pairs = query_ref.shape[1] // PAIR
    chunks = keys // KEYS
    scale = HD**-0.5
    for j in range(pairs):
        turned_ref[j * PAIR:(j + 1) * PAIR, :] = (
            key_ref[:, j * PAIR:(j + 1) * PAIR].astype(F32).T.astype(BF16)
        )

    def pair(j, carry):
        lanes = pl.ds(pl.multiple_of(j * PAIR, PAIR), PAIR)
        query = query_ref[:queries, lanes] * jnp.asarray(scale, BF16)
        grad = grad_ref[:, lanes]
        first = head_mask(query.shape)
        meet = (grad.astype(F32) * attended_ref[:queries, lanes].astype(F32)).T
        masked, grads, deltas, totals = [], [], [], []
        for h in range(2):
            keep = first if h == 0 else ~first
            masked.append(jnp.where(keep, query, jnp.zeros_like(query)))
            grads.append(jnp.where(keep, grad, jnp.zeros_like(grad)))
            deltas.append(jnp.sum(meet[h * HD:(h + 1) * HD], 0, keepdims=True))
            totals.append(totals_ref[pl.ds(2 * j + h, 1), :queries])
        grad_query = [jnp.zeros((HD, queries), F32) for h in range(2)]
        for c in range(chunks):
            some = slice(c * KEYS, (c + 1) * KEYS)
            low = c * KEYS if causal else 0
            grad_key = grad_value = jnp.zeros((KEYS, PAIR), F32)
            for h in range(2):
                scores = times(key_ref[some, lanes], masked[h][low:], NT)
                if causal:
                    key_at = lax.broadcasted_iota(jnp.int32, scores.shape, 0)
                    query_at = lax.broadcasted_iota(jnp.int32, scores.shape, 1)
                    scores = jnp.where(key_at <= query_at, scores, -1000000000.0)
                probs = jnp.exp(scores - totals[h][:, low:])
                grad_probs = times(value_ref[some, lanes], grads[h][low:], NT)
                grad_scores = (probs * (grad_probs - deltas[h][:, low:])).astype(BF16)
                grad_value += times(probs.astype(BF16), grads[h][low:])
                grad_key += times(grad_scores, masked[h][low:])
                key_rows = pl.ds(pl.multiple_of(j * PAIR + h * HD, HD), HD)
                part = times(turned_ref[key_rows, some], grad_scores)
                if low:
                    part = jnp.concatenate([jnp.zeros((HD, low), F32), part], 1)
                grad_query[h] += part
            grad_key_ref[some, lanes] = grad_key.astype(BF16)
            grad_value_ref[some, lanes] = grad_value.astype(BF16)
        grad_query_ref[:, lanes] = (jnp.concatenate(grad_query, 0) * scale).T.astype(BF16)
        return carry

    lax.fori_loop(0, pairs, pair, 0)


def mix(x_ref, wide_ref, bias, mixed_ref):
    def one(t, carry):
        mixed_ref[rows_of(t), :] = (times(x_ref[rows_of(t), :], wide_ref[...]) + bias).astype(BF16)
        return carry

    lax.fori_loop(0, x_ref.shape[0] // ROWS, one, 0)


def close_branch(x_ref, attended_ref, out_weight_ref, vec_ref, unit_ref, scale_ref, *swap_refs):
    swap = Swap(*swap_refs)
    tiles = x_ref.shape[0] // ROWS

    def give(t, carry):
        swap.give(t, times(attended_ref[rows_of(t), :], out_weight_ref[...]))
        return carry

    lax.fori_loop(0, tiles, give, 0)

    def take(t, carry):
        rows = rows_of(t)
        unit, scale = standardize(x_ref[rows, :].astype(F32) + swap.take(t) + vec_ref[0:1, :])
        unit_ref[rows, :] = unit
        scale_ref[rows, :] = scale
        return carry

    lax.fori_loop(0, tiles, take, 0)


def self_forward_kernel(
    causal, span, x_ref, wide_ref, out_weight_ref, bias, vec_ref,
    mixed_ref, attended_ref, totals_ref, unit_ref, scale_ref,
    score_ref, turned_ref, *swap_refs,
):
    half = out_weight_ref.shape[0]
    totals_ref[...] = jnp.zeros_like(totals_ref)
    mix(x_ref, wide_ref, bias, mixed_ref)
    attend(
        mixed_ref.at[:, :half], mixed_ref.at[:, half:2 * half], mixed_ref.at[:, 2 * half:],
        attended_ref, totals_ref, score_ref, turned_ref, causal, span,
    )
    close_branch(x_ref, attended_ref, out_weight_ref, vec_ref, unit_ref, scale_ref, *swap_refs)


def shape(*dims, dtype=F32):
    return jax.ShapeDtypeStruct(dims, dtype)


def params(ident, mib=56):
    return pltpu.CompilerParams(collective_id=ident, has_side_effects=True, vmem_limit_bytes=mib << 20)


def cross_forward_kernel(
    span, unit_ref, fetched_ref, query_weight_ref, wide_ref, out_weight_ref, query_bias_ref, bias_ref, vec_ref,
    low_ref, query_ref, mixed_ref, attended_ref, totals_ref, unit_out_ref, scale_ref,
    score_ref, turned_ref, *swap_refs,
):
    swap = Swap(*swap_refs)
    length, width = unit_ref.shape
    half = out_weight_ref.shape[0]
    tiles = length // ROWS
    totals_ref[...] = jnp.zeros_like(totals_ref)

    def ask(t, carry):
        rows = rows_of(t)
        low = (unit_ref[rows, :] * vec_ref[0:1, :] + vec_ref[1:2, :]).astype(BF16)
        low_ref[rows, :] = low
        query_ref[rows, :] = (times(low, query_weight_ref[...]) + query_bias_ref[...]).astype(BF16)
        return carry

    lax.fori_loop(0, tiles, ask, 0)

    def mix(t, carry):
        mixed_ref[rows_of(t), :] = (
            times(fetched_ref[rows_of(t), :], wide_ref[...]) + bias_ref[...]
        ).astype(BF16)
        return carry

    lax.fori_loop(0, fetched_ref.shape[0] // ROWS, mix, 0)
    attend(
        query_ref, mixed_ref.at[:, :half], mixed_ref.at[:, half:],
        attended_ref, totals_ref, score_ref, turned_ref, False, span,
    )

    def give(t, carry):
        swap.give(t, times(attended_ref[rows_of(t), :], out_weight_ref[...]))
        return carry

    lax.fori_loop(0, tiles, give, 0)

    def take(t, carry):
        rows = rows_of(t)
        hidden = unit_ref[rows, :] * vec_ref[0:1, :] + vec_ref[1:2, :]
        unit, scale = standardize(hidden + swap.take(t) + vec_ref[2:3, :])
        unit_out_ref[rows, :] = unit
        scale_ref[rows, :] = scale
        return carry

    lax.fori_loop(0, tiles, take, 0)


def feed_forward_kernel(
    kept, between, unit_ref, up_ref, down_ref, bias_ref, vec_ref,
    states_ref, states_low_ref, low_ref, active_ref, slope_ref, unit_out_ref, scale_ref, *swap_refs,
):
    swap = Swap(*swap_refs)
    length, width = unit_ref.shape
    hidden_half = up_ref.shape[1]
    tiles, kept_tiles = length // ROWS, kept // ROWS
    step = 512

    def feed(t, carry, keep):
        rows = rows_of(t)
        low = (unit_ref[rows, :] * vec_ref[0:1, :] + vec_ref[1:2, :]).astype(BF16)
        if keep:
            low_ref[rows, :] = low
        total = jnp.zeros((ROWS, width), F32)
        for c in range(0, hidden_half, step):
            upward = times(low, up_ref[:, c:c + step]) + bias_ref[:, c:c + step]
            below = 0.5 * lax.erf(upward * (0.5**0.5)) + 0.5
            active = (upward * below).astype(BF16)
            if keep:
                active_ref[rows, c:c + step] = active
                bell = jnp.exp(-0.5 * upward * upward) * (0.5 / jnp.pi) ** 0.5
                slope_ref[rows, c:c + step] = (below + upward * bell).astype(BF16)
            total += times(active, down_ref[c:c + step, :])
        swap.give(t, total)
        return carry

    def take(t, carry, keep):
        rows = rows_of(t)
        hidden = unit_ref[rows, :] * vec_ref[0:1, :] + vec_ref[1:2, :]
        unit, scale = standardize(hidden + swap.take(t) + vec_ref[2:3, :])
        states = unit * vec_ref[3:4, :] + vec_ref[4:5, :]
        states_ref[rows, :] = states
        if keep:
            states_low_ref[rows, :] = states.astype(BF16)
            unit_out_ref[rows, :] = unit
            scale_ref[rows, :] = scale
        return carry

    lax.fori_loop(0, kept_tiles, functools.partial(feed, keep=True), 0)
    lax.fori_loop(0, kept_tiles, functools.partial(take, keep=True), 0)
    between()
    if kept_tiles < tiles:
        lax.fori_loop(kept_tiles, tiles, functools.partial(feed, keep=False), 0)
        lax.fori_loop(kept_tiles, tiles, functools.partial(take, keep=False), 0)


def feed_backward_kernel(
    grad_ref, unit_after_ref, scale_after_ref, active_ref, slope_ref, up_ref, down_ref,
    unit_before_ref, scale_before_ref, vec_ref,
    low_ref, grad_up_ref, bias_ref, grad_out_ref, sums_after_ref, sums_before_ref,
    held_ref, *swap_refs,
):
    swap = Swap(*swap_refs)
    length, width = grad_ref.shape
    hidden_half = up_ref.shape[1]
    tiles = length // ROWS
    step = 512
    sums_after_ref[...] = jnp.zeros_like(sums_after_ref)
    sums_before_ref[...] = jnp.zeros_like(sums_before_ref)
    bias_ref[...] = jnp.zeros_like(bias_ref)

    def give(t, carry):
        rows = rows_of(t)
        grad = grad_ref[rows, :].astype(F32)
        unit = unit_after_ref[rows, :]
        inner = norm_back(grad, unit, scale_after_ref[rows, :], vec_ref[0:1, :])
        add_sums(sums_after_ref, inner, grad, unit)
        held_ref[rows, :] = inner
        low = inner.astype(BF16)
        low_ref[rows, :] = low
        total = jnp.zeros((ROWS, width), F32)
        for c in range(0, hidden_half, step):
            grad_active = times(low, down_ref[c:c + step, :], NT)
            grad_up = (grad_active * slope_ref[rows, c:c + step].astype(F32)).astype(BF16)
            grad_up_ref[rows, c:c + step] = grad_up
            bias_ref[:, c:c + step] += jnp.sum(grad_up.astype(F32), 0, keepdims=True)
            total += times(grad_up, up_ref[:, c:c + step], NT)
        swap.give(t, total)
        return carry

    lax.fori_loop(0, tiles, give, 0)

    def take(t, carry):
        rows = rows_of(t)
        grad = held_ref[rows, :] + swap.take(t)
        unit = unit_before_ref[rows, :]
        inner = norm_back(grad, unit, scale_before_ref[rows, :], vec_ref[1:2, :])
        add_sums(sums_before_ref, inner, grad, unit)
        grad_out_ref[rows, :] = inner
        return carry

    lax.fori_loop(0, tiles, take, 0)


def spread(grad_pre_ref, out_weight_ref, low_ref, grad_ref):
    def one(t, carry):
        rows = rows_of(t)
        low = grad_pre_ref[rows, :].astype(BF16)
        low_ref[rows, :] = low
        grad_ref[rows, :] = times(low, out_weight_ref[...], NT).astype(BF16)
        return carry

    lax.fori_loop(0, grad_pre_ref.shape[0] // ROWS, one, 0)


def self_backward_kernel(
    causal, grad_pre_ref, mixed_ref, attended_ref, totals_ref, wide_ref, out_weight_ref,
    low_ref, grad_query_ref, grad_pair_ref, grad_x_ref, sums_ref,
    grad_ref, turned_ref, *swap_refs,
):
    swap = Swap(*swap_refs)
    queries, width = grad_pre_ref.shape
    half = out_weight_ref.shape[0]
    length = mixed_ref.shape[0]
    spread(grad_pre_ref, out_weight_ref, low_ref, grad_ref)
    attend_back(
        mixed_ref.at[:, :half], mixed_ref.at[:, half:2 * half], mixed_ref.at[:, 2 * half:],
        attended_ref, totals_ref, grad_ref,
        grad_query_ref, grad_pair_ref.at[:, :half], grad_pair_ref.at[:, half:], turned_ref, causal,
    )
    sums_ref[...] = jnp.zeros_like(sums_ref)
    first = queries // ROWS

    def give(t, carry, asked):
        rows = rows_of(t)
        pair = grad_pair_ref[rows, :]
        sums_ref[:, half:] += jnp.sum(pair.astype(F32), 0, keepdims=True)
        total = times(pair, wide_ref[:, half:], NT)
        if asked:
            query = grad_query_ref[rows, :]
            sums_ref[:, :half] += jnp.sum(query.astype(F32), 0, keepdims=True)
            total += times(query, wide_ref[:, :half], NT)
        swap.give(t, total)
        return carry

    lax.fori_loop(0, first, functools.partial(give, asked=True), 0)
    if first < length // ROWS:
        lax.fori_loop(first, length // ROWS, functools.partial(give, asked=False), 0)

    def take(t, carry, asked):
        rows = rows_of(t)
        total = swap.take(t)
        grad_x_ref[rows, :] = grad_pre_ref[rows, :] + total if asked else total
        return carry

    lax.fori_loop(0, first, functools.partial(take, asked=True), 0)
    if first < length // ROWS:
        lax.fori_loop(first, length // ROWS, functools.partial(take, asked=False), 0)


def cross_backward_kernel(
    between, grad_pre_ref, query_ref, mixed_ref, attended_ref, totals_ref, query_weight_ref, wide_ref, out_weight_ref,
    unit_ref, scale_ref, vec_ref,
    low_ref, grad_query_ref, grad_pair_ref, fetched_ref, grad_out_ref, sums_ref, vec_sums_ref,
    grad_ref, turned_ref, *swap_refs,
):
    near, far = Swap(*swap_refs[:4]), Swap(*swap_refs[4:])
    queries, width = grad_pre_ref.shape
    half = out_weight_ref.shape[0]
    keys = mixed_ref.shape[0]
    spread(grad_pre_ref, out_weight_ref, low_ref, grad_ref)
    attend_back(
        query_ref, mixed_ref.at[:, :half], mixed_ref.at[:, half:],
        attended_ref, totals_ref, grad_ref,
        grad_query_ref, grad_pair_ref.at[:, :half], grad_pair_ref.at[:, half:], turned_ref, False,
    )
    sums_ref[...] = jnp.zeros_like(sums_ref)
    vec_sums_ref[...] = jnp.zeros_like(vec_sums_ref)

    def give_far(t, carry):
        pair = grad_pair_ref[rows_of(t), :]
        sums_ref[:, half:] += jnp.sum(pair.astype(F32), 0, keepdims=True)
        far.give(t, times(pair, wide_ref[...], NT))
        return carry

    lax.fori_loop(0, keys // ROWS, give_far, 0)

    def give_near(t, carry):
        query = grad_query_ref[rows_of(t), :]
        sums_ref[:, :half] += jnp.sum(query.astype(F32), 0, keepdims=True)
        near.give(t, times(query, query_weight_ref[...], NT))
        return carry

    lax.fori_loop(0, queries // ROWS, give_near, 0)

    def take_far(t, carry):
        fetched_ref[rows_of(t), :] = far.take(t).astype(BF16)
        return carry

    lax.fori_loop(0, keys // ROWS, take_far, 0)
    between()

    def take_near(t, carry):
        rows = rows_of(t)
        grad = grad_pre_ref[rows, :] + near.take(t)
        unit = unit_ref[rows, :]
        inner = norm_back(grad, unit, scale_ref[rows, :], vec_ref[0:1, :])
        add_sums(vec_sums_ref, inner, grad, unit)
        grad_out_ref[rows, :] = inner
        return carry

    lax.fori_loop(0, queries // ROWS, take_near, 0)


def held(*dims, dtype=F32):
    return pltpu.VMEM(dims, dtype)


def streams(array):
    rows, width = array.shape
    return rows % 16 == 0 and width % TILE == 0 and rows * width * array.dtype.itemsize >= 1 << 18


def call(name, ident, body, inputs, outputs, scratch, mib=56):
    ins = [i for i, array in enumerate(inputs) if streams(array)]
    outs = [i for i, array in enumerate(outputs) if streams(array)]
    count_in, count_out = len(inputs), len(outputs)

    def kernel(*refs):
        in_refs, out_refs, rest = refs[:count_in], refs[count_in:count_in + count_out], refs[count_in + count_out:]
        near_in, near_out = list(in_refs), list(out_refs)
        for place, ref in zip(ins, rest[:len(ins)]):
            near_in[place] = ref
        rest = rest[len(ins):]
        for place, ref in zip(outs, rest[:len(outs)]):
            near_out[place] = ref
        rest = rest[len(outs):]
        in_sem, out_sem, rest = rest[0], rest[1], rest[2:]

        def load(place):
            return pltpu.make_async_copy(in_refs[place], near_in[place], in_sem.at[place])

        def store(place):
            return pltpu.make_async_copy(near_out[place], out_refs[place], out_sem.at[place])

        def need(*places):
            for place in places:
                if place in ins:
                    load(place).wait()

        def done(*places):
            for place in places:
                if place in outs:
                    store(place).start()

        for place in ins:
            load(place).start()
        body(need, done, *near_in, *near_out, *rest)
        for place in outs:
            store(place).wait()

    return pl.pallas_call(
        kernel,
        out_shape=outputs,
        in_specs=[ANY if i in ins else VM for i in range(count_in)],
        out_specs=[ANY if i in outs else VM for i in range(count_out)],
        scratch_shapes=[pltpu.VMEM(inputs[i].shape, inputs[i].dtype) for i in ins]
        + [pltpu.VMEM(outputs[i].shape, outputs[i].dtype) for i in outs]
        + [pltpu.SemaphoreType.DMA((count_in,)), pltpu.SemaphoreType.DMA((count_out,))]
        + scratch,
        compiler_params=params(ident, mib),
        name=name,
    )(*inputs)


class Trade:
    def __init__(self, count, into, send_sem, recv_sem, give_sem, take_sem):
        self.count, self.into = count, into
        self.send_sem, self.recv_sem, self.give_sem, self.take_sem = send_sem, recv_sem, give_sem, take_sem
        self.me, self.core = lax.axis_index("dp"), lax.axis_index("tensor")
        self.rows, self.half = into.shape[0] // count, into.shape[1] // 2

    @staticmethod
    def scratch(count):
        return [pltpu.SemaphoreType.DMA((count,))] * 4

    def greet(self):
        barrier = pltpu.get_barrier_semaphore()

        def signal(k, carry):
            other = {"dp": lax.rem(self.me + k, self.count)}
            pl.semaphore_signal(barrier, inc=1, device_id=other, device_id_type=MESH)
            return carry

        lax.fori_loop(1, self.count, signal, 0)
        pl.semaphore_signal(barrier, inc=1, device_id={"tensor": 1 - self.core}, device_id_type=MESH)
        pl.semaphore_wait(barrier, self.count)

    def rows_of(self, device):
        return pl.ds(pl.multiple_of(device * self.rows, self.rows), self.rows)

    def mine(self):
        return pl.ds(pl.multiple_of(self.core * self.half, self.half), self.half)

    def lanes_of(self, source):
        return self.mine() if source.shape[1] == self.into.shape[1] else slice(None)

    def send(self, source, k):
        other = lax.rem(self.me + k, self.count)
        return pltpu.make_async_remote_copy(
            src_ref=source.at[self.rows_of(other), self.lanes_of(source)],
            dst_ref=self.into.at[self.rows_of(self.me), self.mine()],
            send_sem=self.send_sem.at[k],
            recv_sem=self.recv_sem.at[k],
            device_id={"dp": other},
            device_id_type=MESH,
        )

    def pass_on(self, k):
        part = self.into.at[self.rows_of(lax.rem(self.me - k + self.count, self.count)), self.mine()]
        return pltpu.make_async_remote_copy(
            src_ref=part,
            dst_ref=part,
            send_sem=self.give_sem.at[k],
            recv_sem=self.take_sem.at[k],
            device_id={"tensor": 1 - self.core},
            device_id_type=MESH,
        )

    def start(self, source):
        def go(k, carry):
            self.send(source, k).start()
            return carry

        lax.fori_loop(1, self.count, go, 0)
        self.into[self.rows_of(self.me), self.mine()] = source[self.rows_of(self.me), self.lanes_of(source)]
        self.pass_on(0).start()

    def finish(self, source):
        def meet(k, carry):
            self.send(source, k).wait_recv()
            self.pass_on(k).start()
            return carry

        lax.fori_loop(1, self.count, meet, 0)

        def end(k, carry):
            self.pass_on(k).wait()
            return carry

        lax.fori_loop(0, self.count, end, 0)

        def sent(k, carry):
            self.send(source, k).wait_send()
            return carry

        lax.fori_loop(1, self.count, sent, 0)


def encoder_and_fetch(
    ident, x, attended, out_weight, up, down, shared, split, kept, wanted, target, dec_wide, dec_out_weight, count
):
    length, width = x.shape
    half, hidden_half = out_weight.shape[0], up.shape[1]
    tiles, target_length = length // ROWS, target.shape[0]
    span = min(target_length, 512)
    fetched_rows = wanted.shape[0]
    places = bias_places(half, hidden_half)

    def body(
        need, done, x_ref, attended_ref, out_weight_ref, up_ref, down_ref, shared_ref, split_ref, wanted_ref,
        target_ref, dec_wide_ref, dec_out_weight_ref, *refs,
    ):
        saved, fed, dec_saved, fetched_ref, rest = refs[:2], refs[2:9], refs[9:14], refs[14], refs[15:]
        served_ref, trade_sems, rest = rest[0], rest[1:5], rest[5:]
        score_ref, turned_ref, rest = rest[0], rest[1], rest[2:]
        trade = Trade(count, fetched_ref, *trade_sems)
        stored_ref = fed[1]
        need(0, 1, 2)
        trade.greet()
        close_branch(x_ref, attended_ref, out_weight_ref, Rows(shared_ref, (0,)), *saved, *rest[:4])
        done(0, 1)
        need(3, 4, 5, 6, 7)

        def serve(t, carry):
            want = wanted_ref[rows_of(t), :]
            match = want == lax.broadcasted_iota(jnp.int32, (ROWS, kept), 1)
            pick = jnp.where(match, 1.0, 0.0).astype(BF16)
            served_ref[rows_of(t), :] = times(pick, stored_ref[:, trade.mine()]).astype(BF16)
            return carry

        def between():
            lax.fori_loop(0, fetched_rows // ROWS, serve, 0)
            trade.start(served_ref)
            done(3, 4, 5, 6, 7, 8)

        feed_forward_kernel(
            kept, between, saved[0], up_ref, down_ref, split_ref.at[:, places["enc_up"]],
            Rows(shared_ref, (1, 2, 3, 4, 5)), *fed, *rest[4:8],
        )
        done(2)
        need(8, 9, 10)
        self_forward_kernel(
            True, span, target_ref, dec_wide_ref, dec_out_weight_ref,
            bias_row(split_ref, places, ("dec_q", None, "dec_v"), half), Rows(shared_ref, (6,)),
            *dec_saved, score_ref, turned_ref, *rest[8:],
        )
        done(9, 10, 11, 12, 13)
        trade.finish(served_ref)
        done(14)

    return call(
        "encoder_and_fetch", ident, body,
        [x, attended, out_weight, up, down, shared, split, wanted, target, dec_wide, dec_out_weight],
        [
            shape(length, width), shape(length, 1),
            shape(length, width), shape(kept, width, dtype=BF16), shape(kept, width, dtype=BF16),
            shape(kept, hidden_half, dtype=BF16), shape(kept, hidden_half, dtype=BF16),
            shape(kept, width), shape(kept, 1),
            shape(target_length, 3 * half, dtype=BF16), shape(target_length, half, dtype=BF16), shape(8, target_length),
            shape(target_length, width), shape(target_length, 1), shape(fetched_rows, width, dtype=BF16),
        ],
        [held(fetched_rows, width // 2, dtype=BF16)] + Trade.scratch(count)
        + [held(2, target_length, span), held(half, target_length, dtype=BF16)]
        + Swap.scratch(tiles, width) * 2 + Swap.scratch(target_length // ROWS, width),
    )


def decoder_core(
    ident, unit, scale, fetched, cotangent, query_weight, wide, out_weight, up, down, shared, split,
    mixed, attended, totals, self_wide, self_out_weight, count,
):
    length, width = unit.shape
    keys = fetched.shape[0]
    half, hidden_half = out_weight.shape[0], up.shape[1]
    tiles, span = length // ROWS, min(length, 512)
    places = bias_places(half, hidden_half)

    def body(
        need, done, unit_ref, scale_ref, fetched_ref, cotangent_ref, query_weight_ref, wide_ref, out_weight_ref,
        up_ref, down_ref, shared_ref, split_ref,
        self_mixed_ref, self_attended_ref, self_totals_ref, self_wide_ref, self_out_weight_ref,
        states_ref, low_ref, attended_ref, second_low_ref, active_ref,
        feed_low_ref, grad_up_ref, up_bias_ref, sums_after_ref, sums_before_ref,
        cross_low_ref, grad_query_ref, grad_pair_ref, landed_ref, cross_sums_ref, vec_sums_ref,
        self_low_ref, self_query_ref, self_pair_ref, grad_x_ref, self_sums_ref,
        query_ref, mixed_ref, totals_ref, unit_four_ref, scale_four_ref, slope_ref,
        unit_five_ref, scale_five_ref, grad_four_ref, inner_ref, score_ref, turned_ref, grad_ref, returned_ref, grad_out_ref,
        send_sem, recv_sem, give_sem, take_sem, *swaps,
    ):
        need(0, 1, 2, 4, 5, 6, 9, 10)
        trade = Trade(count, landed_ref, send_sem, recv_sem, give_sem, take_sem)
        trade.greet()
        cross_forward_kernel(
            span, unit_ref, fetched_ref, query_weight_ref, wide_ref, out_weight_ref,
            split_ref.at[:, places["crs_q"]], bias_row(split_ref, places, (None, "crs_v"), half),
            Rows(shared_ref, (7, 8, 9)),
            low_ref, query_ref, mixed_ref, attended_ref, totals_ref, unit_four_ref, scale_four_ref,
            score_ref, turned_ref, *swaps[:4],
        )
        done(1, 2)
        need(7, 8)
        feed_forward_kernel(
            length, lambda: None, unit_four_ref, up_ref, down_ref, split_ref.at[:, places["dec_up"]],
            Rows(shared_ref, (10, 11, 12, 13, 14)),
            states_ref, cross_low_ref, second_low_ref, active_ref, slope_ref, unit_five_ref, scale_five_ref,
            *swaps[4:8],
        )
        done(0, 3, 4)
        need(3)
        feed_backward_kernel(
            cotangent_ref, unit_five_ref, scale_five_ref, active_ref, slope_ref, up_ref, down_ref,
            unit_four_ref, scale_four_ref, Rows(shared_ref, (13, 10)),
            feed_low_ref, grad_up_ref, up_bias_ref, grad_four_ref, sums_after_ref, sums_before_ref,
            inner_ref, *swaps[8:12],
        )
        done(5, 6, 7, 8, 9)
        cross_backward_kernel(
            lambda: trade.start(returned_ref), grad_four_ref, query_ref, mixed_ref, attended_ref, totals_ref, query_weight_ref, wide_ref,
            out_weight_ref, unit_ref, scale_ref, Rows(shared_ref, (7,)),
            cross_low_ref, grad_query_ref, grad_pair_ref, returned_ref, grad_out_ref, cross_sums_ref, vec_sums_ref,
            grad_ref, turned_ref, *swaps[12:20],
        )
        done(10, 11, 12, 14, 15)
        need(11, 12, 13, 14, 15)
        self_backward_kernel(
            True, grad_out_ref, self_mixed_ref, self_attended_ref, self_totals_ref, self_wide_ref, self_out_weight_ref,
            self_low_ref, self_query_ref, self_pair_ref, grad_x_ref, self_sums_ref,
            grad_ref, turned_ref.at[:, :length], *swaps[20:],
        )
        done(16, 17, 18, 19, 20)
        trade.finish(returned_ref)
        done(13)

    return call(
        "decoder_core", ident, body,
        [
            unit, scale, fetched, cotangent, query_weight, wide, out_weight, up, down, shared, split,
            mixed, attended, totals, self_wide, self_out_weight,
        ],
        [
            shape(length, width), shape(length, width, dtype=BF16), shape(length, half, dtype=BF16),
            shape(length, width, dtype=BF16), shape(length, hidden_half, dtype=BF16),
            shape(length, width, dtype=BF16), shape(length, hidden_half, dtype=BF16), shape(1, hidden_half),
            shape(8, width), shape(8, width),
            shape(length, width, dtype=BF16), shape(length, half, dtype=BF16), shape(keys, 2 * half, dtype=BF16),
            shape(keys, width, dtype=BF16), shape(1, 3 * half), shape(8, width),
            shape(length, width, dtype=BF16), shape(length, half, dtype=BF16), shape(length, 2 * half, dtype=BF16),
            shape(length, width), shape(1, 3 * half),
        ],
        [
            held(length, half, dtype=BF16), held(keys, 2 * half, dtype=BF16), held(8, length),
            held(length, width), held(length, 1),
            held(length, hidden_half, dtype=BF16), held(length, width), held(length, 1),
            held(length, width), held(length, width), held(2, keys, span), held(half, keys, dtype=BF16),
            held(length, half, dtype=BF16), held(keys, width, dtype=BF16), held(length, width),
        ]
        + Trade.scratch(count)
        + Swap.scratch(tiles, width) * 4 + Swap.scratch(keys // ROWS, width) + Swap.scratch(tiles, width),
        60,
    )


def encoder_backward(
    ident, returned, wanted, unit_two, scale_two, active, slope, up, down, unit_one, scale_one,
    mixed, attended, totals, wide, out_weight, shared,
):
    queries, width = unit_two.shape
    length, half, hidden_half = mixed.shape[0], out_weight.shape[0], up.shape[1]

    def body(
        need, done, returned_ref, wanted_ref, unit_two_ref, scale_two_ref, active_ref, slope_ref, up_ref, down_ref, unit_one_ref, scale_one_ref,
        mixed_ref, attended_ref, totals_ref, wide_ref, out_weight_ref, shared_ref,
        feed_low_ref, grad_up_ref, up_bias_ref, sums_after_ref, sums_before_ref,
        low_ref, grad_query_ref, grad_pair_ref, grad_x_ref, sums_ref,
        grad_ref, grad_one_ref, inner_ref, grad_out_ref, turned_ref, *swaps,
    ):
        need(0, 1)

        def collect(t, carry):
            place = t * ROWS + lax.broadcasted_iota(jnp.int32, (ROWS, returned_ref.shape[0]), 0)
            match = jnp.where(wanted_ref[...] == place, 1.0, 0.0).astype(BF16)
            grad_ref[rows_of(t), :] = times(match, returned_ref[...])
            return carry

        lax.fori_loop(0, queries // ROWS, collect, 0)
        need(*range(2, 10), 15)
        Swap.greet()
        feed_backward_kernel(
            grad_ref, unit_two_ref, scale_two_ref, active_ref, slope_ref, up_ref, down_ref,
            unit_one_ref, scale_one_ref, Rows(shared_ref, (4, 1)),
            feed_low_ref, grad_up_ref, up_bias_ref, grad_one_ref, sums_after_ref, sums_before_ref,
            inner_ref, *swaps[:4],
        )
        done(0, 1, 2, 3, 4)
        need(10, 11, 12, 13, 14)
        self_backward_kernel(
            False, grad_one_ref, mixed_ref, attended_ref, totals_ref, wide_ref, out_weight_ref,
            low_ref, grad_query_ref, grad_pair_ref, grad_x_ref, sums_ref, grad_out_ref, turned_ref, *swaps[4:],
        )
        done(*range(5, 10))

    return call(
        "encoder_backward", ident, body,
        [
            returned, wanted, unit_two, scale_two, active, slope, up, down, unit_one, scale_one,
            mixed, attended, totals, wide, out_weight, shared,
        ],
        [
            shape(queries, width, dtype=BF16), shape(queries, hidden_half, dtype=BF16), shape(1, hidden_half),
            shape(8, width), shape(8, width),
            shape(queries, width, dtype=BF16), shape(queries, half, dtype=BF16), shape(length, 2 * half, dtype=BF16),
            shape(length, width), shape(1, 3 * half),
        ],
        [
            held(queries, width), held(queries, width), held(queries, width), held(queries, half, dtype=BF16),
            held(half, length, dtype=BF16),
        ]
        + Swap.scratch(queries // ROWS, width) + Swap.scratch(length // ROWS, width),
    )


def adam_vector(grad_value, value, first, second):
    new_first = BETA_ONE * first + (1.0 - BETA_ONE) * grad_value
    new_second = BETA_TWO * second + (1.0 - BETA_TWO) * grad_value * grad_value
    correct_one = 1.0 - BETA_ONE**STEP
    correct_two = 1.0 - BETA_TWO**STEP
    updated = value - VECTOR_RATE * (new_first / correct_one) / (
        jnp.sqrt(new_second / correct_two) + ADAM_EPSILON
    )
    return (new_first, new_second, updated)


def local(
    source_tokens,
    target_tokens,
    target_cotangent,
    retrieved,
    kept_mask,
    owner_slots,
    master,
    first_moment,
    second_moment,
    left_stats,
    right_stats,
    left_basis,
    right_basis,
    shared_vectors,
    shared_first,
    shared_second,
    split_vectors,
    split_first,
    split_second,
):
    tensor_count = lax.axis_size("tensor")
    device_count = lax.axis_size("dp")
    model_width = source_tokens.shape[1]
    tile_size = master.shape[2]
    hidden_width = (split_vectors.shape[1] - 3) * model_width
    half_width = model_width // tensor_count
    hidden_half = hidden_width // tensor_count
    qblocks = retrieved.shape[0]
    per_owner = retrieved.shape[1] // device_count
    me = lax.axis_index("dp")
    vectors = jnp.concatenate([shared_vectors, split_vectors[0]], 0)
    vector_count, vector_width = vectors.shape
    padded = -(-vector_count // 8) * 8
    small = jnp.concatenate(
        [
            jnp.pad(vectors, ((0, padded - vector_count), (0, TILE - vector_width))),
            retrieved.astype(jnp.float32).reshape(-1, TILE),
        ],
        0,
    )
    gathered, smalls = gather_all(master[0], small, device_count)
    whole = (
        smalls[:, :vector_count, :vector_width]
        .transpose(1, 0, 2)
        .reshape(vector_count, model_width)
        .astype(jnp.bfloat16)
    )
    shared_count = shared_vectors.shape[0]
    shared_whole, split_whole = whole[:shared_count], whole[shared_count:]
    shapes = [s[1:] for s in matrix_list(model_width, hidden_width, tensor_count)]
    names = [s[0] for s in matrix_list(model_width, hidden_width, tensor_count)]
    shared = jnp.pad(shared_whole.astype(F32), ((0, 16 - shared_count), (0, 0)))
    split = split_whole.astype(F32).reshape(1, -1)
    start_row = jnp.argmax(kept_mask)
    turned = jnp.roll(source_tokens, -start_row, 0)


    wanted = (
        smalls[:, padded:].reshape(device_count, qblocks, device_count, per_owner)[:, :, me]
        .transpose(1, 0, 2)
        .astype(jnp.int32)
        - KEEP * me
    ).reshape(1, -1)
    matrices, (enc_mixed, enc_attended, enc_totals) = unpack_and_attend(
        gathered, owner_slots, shapes, turned, split, bias_places(half_width, hidden_half), half_width
    )
    weights = dict(zip(names, matrices))
    (unit_one, scale_one,
     states, _, hidden_low, enc_active, enc_slope, unit_two, scale_two,
     dec_mixed, dec_attended, dec_totals, unit_three, scale_three, fetched) = encoder_and_fetch(
        10, turned, enc_attended, weights["enc_out"], weights["enc_up"], weights["enc_down"],
        shared, split, KEEP, wanted.reshape(-1, 1), target_tokens, weights["dec_qkv"], weights["dec_out"], device_count,
    )
    encoder_states = jnp.roll(states, start_row, 0)
    (decoder_states, first_low, crs_attended, second_low, dec_active,
     dec_feed_low, dec_grad_up, dec_up_bias, sums_five, sums_four,
     crs_low, crs_grad_query, crs_grad_pair, returned, crs_sums, sums_three,
     dec_low, dec_grad_query, dec_grad_pair, target_grad, dec_sums) = decoder_core(
        13, unit_three, scale_three, fetched, target_cotangent,
        weights["crs_q"], weights["crs_kv"], weights["crs_out"], weights["dec_up"], weights["dec_down"],
        shared, split, dec_mixed, dec_attended, dec_totals, weights["dec_qkv"], weights["dec_out"], device_count,
    )
    (enc_feed_low, enc_grad_up, enc_up_bias, sums_two, sums_one,
     enc_low, enc_grad_query, enc_grad_pair, grad_turned, enc_sums) = encoder_backward(
        18, returned, wanted, unit_two, scale_two, enc_active, enc_slope, weights["enc_up"], weights["enc_down"],
        unit_one, scale_one, enc_mixed, enc_attended, enc_totals, weights["enc_qkv"], weights["enc_out"], shared,
    )
    source_grad = jnp.roll(grad_turned, start_row, 0)

    first_block, total_blocks = {}, 0
    for name, height, breadth in matrix_list(model_width, hidden_width, tensor_count):
        first_block[name] = total_blocks
        total_blocks += height // TILE * (breadth // TILE)
    three = 3 * half_width
    outer = ((0, half_width), (2 * half_width, three))
    everything = ((0, hidden_half),)
    items = [
        (sums, 3 * i, None) for i, sums in enumerate((sums_one, sums_two, sums_three, sums_four, sums_five))
    ]
    at = shared_count * model_width
    for array, pieces in (
        (enc_sums, outer), (enc_up_bias, everything), (dec_sums, outer), (crs_sums, outer), (dec_up_bias, everything)
    ):
        items.append((array, at, pieces))
        at += sum(end - begin for begin, end in pieces)
    (slot_grads,) = weight_grads(
        [
            (first_block["dec_down"], [(dec_active, dec_feed_low)]),
            (first_block["dec_up"], [(second_low, dec_grad_up)]),
            (first_block["crs_out"], [(crs_attended, crs_low)]),
            (first_block["crs_q"], [(first_low, crs_grad_query)]),
            (first_block["crs_kv"], [(fetched, crs_grad_pair)]),
            (first_block["dec_out"], [(dec_attended, dec_low)]),
            (first_block["dec_qkv"], [(target_tokens, dec_grad_query), (target_tokens, dec_grad_pair)]),
        ],
        owner_slots,
        gathered.shape[0],
    )
    slot_grads, vector_grads = weight_grads(
        [
            (first_block["enc_down"], [(enc_active, enc_feed_low)]),
            (first_block["enc_up"], [(hidden_low, enc_grad_up)]),
            (first_block["enc_out"], [(enc_attended, enc_low)]),
            (first_block["enc_qkv"], [(turned, enc_grad_query), (turned, enc_grad_pair)]),
        ],
        owner_slots,
        gathered.shape[0],
        slot_grads,
        (padded, model_width, items),
    )
    slots = master.shape[1]
    owned_slots = me * slots + lax.broadcasted_iota(jnp.int32, (slots, 1), 0)
    used = jnp.any(owned_slots == owner_slots[None, :], 1).astype(jnp.int32)
    results, vector_sums = owner_update(
        used,
        slot_grads,
        vector_grads,
        [
            array[0]
            for array in (
                master, first_moment, second_moment, left_stats, right_stats, left_basis, right_basis
            )
        ],
        device_count,
    )
    vector_owned = lax.dynamic_slice_in_dim(vector_sums, me * vector_width, vector_width, 1)
    shared_owned = vector_owned[:shared_count]
    split_owned = vector_owned[shared_count:vector_count]
    new_master, new_first, new_second, new_left, new_right, new_lbasis, new_rbasis = results
    shared_new_first, shared_new_second, shared_updated = adam_vector(
        shared_owned, shared_vectors, shared_first, shared_second
    )
    split_new_first, split_new_second, split_updated = adam_vector(
        split_owned, split_vectors[0], split_first[0], split_second[0]
    )
    return (
        encoder_states,
        decoder_states,
        source_grad,
        target_grad,
        new_master[None],
        new_first[None],
        new_second[None],
        new_left[None],
        new_right[None],
        new_lbasis[None],
        new_rbasis[None],
        shared_new_first,
        shared_new_second,
        shared_updated,
        split_new_first[None],
        split_new_second[None],
        split_updated[None],
    )


def solution(mesh):
    placed = (
        P("dp", None),
        P("dp", None),
        P("dp", None),
        P("dp", None),
        P("dp"),
        P(),
        P("tensor", "dp", None, None),
        P("tensor", "dp", None, None),
        P("tensor", "dp", None, None),
        P("tensor", "dp", None, None),
        P("tensor", "dp", None, None),
        P("tensor", "dp", None, None),
        P("tensor", "dp", None, None),
        P(None, "dp"),
        P(None, "dp"),
        P(None, "dp"),
        P("tensor", None, "dp"),
        P("tensor", None, "dp"),
        P("tensor", None, "dp"),
    )
    return jax.shard_map(
        local,
        mesh=mesh,
        in_specs=placed,
        out_specs=(
            P("dp", None),
            P("dp", None),
            P("dp", None),
            P("dp", None),
            P("tensor", "dp", None, None),
            P("tensor", "dp", None, None),
            P("tensor", "dp", None, None),
            P("tensor", "dp", None, None),
            P("tensor", "dp", None, None),
            P("tensor", "dp", None, None),
            P("tensor", "dp", None, None),
            P(None, "dp"),
            P(None, "dp"),
            P(None, "dp"),
            P("tensor", None, "dp"),
            P("tensor", None, "dp"),
            P("tensor", None, "dp"),
        ),
        check_vma=False,
    )
```

```python
import functools
from functools import partial

import jax
import jax.numpy as jnp
from jax import lax
from jax.experimental import pallas as pl
from jax.experimental.pallas import tpu as pltpu
from jax.sharding import PartitionSpec as P

HD = 64
KEEP = 512
STEP = 10


BETA_ONE = 0.9
BETA_TWO = 0.95
ADAM_EPSILON = 1e-08
MATRIX_RATE = 0.1
VECTOR_RATE = 0.5
WEIGHT_DECAY = 0.01
NORM_EPSILON = 1e-05
TILE = 128
PANEL = 32
ROWS = 256
KEYS = 256
PAIR = 2 * HD
NN = ((1,), (0,))
NT = ((1,), (1,))
F32 = jnp.float32
BF16 = jnp.bfloat16
MESH = pl.DeviceIdType.MESH
ANY = pl.BlockSpec(memory_space=pl.ANY)


def matrix_list(model_width, hidden_width, tensor_count):
    half_width = model_width // tensor_count
    hidden_half = hidden_width // tensor_count
    return [
        ("enc_qkv", model_width, 3 * half_width),
        ("enc_out", half_width, model_width),
        ("enc_up", model_width, hidden_half),
        ("enc_down", hidden_half, model_width),
        ("dec_qkv", model_width, 3 * half_width),
        ("dec_out", half_width, model_width),
        ("crs_q", model_width, half_width),
        ("crs_kv", model_width, 2 * half_width),
        ("crs_out", half_width, model_width),
        ("dec_up", model_width, hidden_half),
        ("dec_down", hidden_half, model_width),
    ]


def halves(x):
    high = x.astype(BF16)
    return high, (x - high.astype(F32)).astype(BF16)


def mm(a, b, dims=NN):
    ah, al = halves(a)
    bh, bl = halves(b)
    return times(jnp.concatenate([ah, ah, al], 1), jnp.concatenate([bh, bl, bh], dims[1][0]), dims)


def chip_grid(device_count):
    if device_count == 16:
        return 4, 2, 2
    side = round(device_count ** (1 / 3))
    if side**3 == device_count:
        return side, side, side
    return 1, 1, device_count


def place(grid):
    zs, ys, xs = grid
    me = lax.axis_index("dp")
    return me // (ys * xs), lax.rem(me // xs, ys), lax.rem(me, xs)


def peers(grid):
    zs, ys, xs = grid
    z, y, x = place(grid)

    def device(zz, yy, xx):
        return {"dp": (zz * ys + yy) * xs + xx}

    return (
        lambda k: device(lax.rem(z + k, zs), y, x),
        lambda k: device(z, lax.rem(y + k, ys), x),
        lambda k: device(z, y, lax.rem(x + k, xs)),
    )


def greet(grid):
    barrier = pltpu.get_barrier_semaphore()
    count = 0
    for size, peer in zip(grid, peers(grid)):
        for k in range(1, size):
            pl.semaphore_signal(barrier, inc=1, device_id=peer(k), device_id_type=MESH)
            count += 1
    pl.semaphore_wait(barrier, count)


def remote(src, dst, send, recv, device):
    return pltpu.make_async_remote_copy(
        src_ref=src, dst_ref=dst, send_sem=send, recv_sem=recv, device_id=device, device_id_type=MESH
    )


def chunking(slots):
    half = slots // 2
    chunks = min(16, half)
    return half, chunks, half // chunks


def owner_kernel(grid, *refs):
    zs, ys, xs = grid
    used_ref, in_ref, small_ref = refs[:3]
    state_in, state_out, small_out_ref, work_out_ref = refs[3:10], refs[10:17], refs[17], refs[18]
    state, rest = refs[19:26], refs[26:]
    (own0, own1, ra0, ra1, rb0, rb1, rc0, rc1, total, rs_z, rs_y, rs_x, work, load_sem,
     as0, as1, ar0, ar1, bs0, bs1, br0, br1, cs0, cs1, cr0, cr1,
     ssz, ssy, ssx, srz, sry, srx, state_sem) = rest
    own, rec_a, rec_b, rec_c = (own0, own1), (ra0, ra1), (rb0, rb1), (rc0, rc1)
    a_send, a_recv, b_send, b_recv, c_send, c_recv = (as0, as1), (ar0, ar1), (bs0, bs1), (br0, br1), (cs0, cs1), (cr0, cr1)
    rec_s, s_send, s_recv = (rs_z, rs_y, rs_x), (ssz, ssy, ssx), (srz, sry, srx)

    z, y, x = place(grid)
    tos = peers(grid)
    to_z, to_y, to_x = tos
    slots = state[0].shape[0]
    half = slots // 2
    first = ((xs, x, to_x), (ys, y, to_y))
    second = ((ys, y, to_y), (xs, x, to_x))

    def source(g, c, other):
        slot = g * half + c
        return in_ref.at[:, :, other, slot] if g == 0 else in_ref.at[:, other, :, slot]

    def load(g, c):
        return pltpu.make_async_copy(source(g, c, first[g][1]), own[g].at[c], load_sem.at[g, c])

    def send_a(g, c, k):
        count, mine, to = first[g]
        return remote(source(g, c, lax.rem(mine + k, count)), rec_a[g].at[c, k - 1],
                      a_send[g].at[c, k - 1], a_recv[g].at[c, k - 1], to(k))

    def send_b(g, c, k):
        count, mine, to = second[g]
        return remote(own[g].at[c, :, lax.rem(mine + k, count)], rec_b[g].at[c, k - 1],
                      b_send[g].at[c, k - 1], b_recv[g].at[c, k - 1], to(k))

    def send_c(g, c, k):
        return remote(own[g].at[c, lax.rem(z + k, zs), second[g][1]], rec_c[g].at[c, k - 1],
                      c_send[g].at[c, k - 1], c_recv[g].at[c, k - 1], to_z(k))

    def start_a(c):
        for g in range(2):
            for k in range(1, first[g][0]):
                send_a(g, c, k).start()

    def send_s(axis, k):
        return remote(total.at[2 - axis], rec_s[axis].at[k - 1],
                      s_send[axis].at[k - 1], s_recv[axis].at[k - 1], tos[axis](k))

    def small_start(axis):
        for k in range(1, grid[axis]):
            send_s(axis, k).start()

    def small_add(axis):
        value = total[2 - axis]
        for k in range(1, grid[axis]):
            send_s(axis, k).wait_recv()
            value += rec_s[axis][k - 1]
        return value

    def each(count, action):
        def go(c, carry):
            action(c)
            return carry

        lax.fori_loop(0, count, go, 0)

    def load_all(c):
        for g in range(2):
            load(g, c).start()

    each(half, load_all)
    for i in range(7):
        pltpu.make_async_copy(state_in[i], state[i], state_sem.at[0, i]).start()
    total[0] = small_ref[...]
    greet(grid)
    small_start(2)
    start_a(0)
    total[1] = small_add(2)
    small_start(1)
    total[2] = small_add(1)
    small_start(0)
    for i in range(7):
        pltpu.make_async_copy(state_in[i], state[i], state_sem.at[0, i]).wait()

    def step_a(c):
        for g in range(2):
            load(g, c).wait()
            for k in range(1, first[g][0]):
                send_a(g, c, k).wait_recv()

        @pl.when(c + 1 < half)
        def _():
            start_a(c + 1)

        for g in range(2):
            n2 = second[g][0]

            def add(e, carry, g=g, n2=n2):
                a, b = e // n2, lax.rem(e, n2)
                value = own[g][c, a, b].astype(F32)
                for k in range(1, first[g][0]):
                    value += rec_a[g][c, k - 1, a, b].astype(F32)
                own[g][c, a, b] = value.astype(BF16)
                return carry

            lax.fori_loop(0, zs * n2, add, 0)
            for k in range(1, n2):
                send_b(g, c, k).start()

    def step_b(c):
        for g in range(2):
            n2, mine = second[g][0], second[g][1]
            for k in range(1, n2):
                send_b(g, c, k).wait_recv()

            def add(a, carry, g=g, n2=n2, mine=mine):
                value = own[g][c, a, mine].astype(F32)
                for k in range(1, n2):
                    value += rec_b[g][c, k - 1, a].astype(F32)
                own[g][c, a, mine] = value.astype(BF16)
                return carry

            lax.fori_loop(0, zs, add, 0)
            for k in range(1, zs):
                send_c(g, c, k).start()

    def step_c(c):
        batch = lax.rem(c // 4, 2)
        for g in range(2):
            for k in range(1, zs):
                send_c(g, c, k).wait_recv()
        for g in range(2):
            value = own[g][c, z, second[g][1]].astype(F32)
            for k in range(1, zs):
                value += rec_c[g][c, k - 1].astype(F32)
            slot = g * half + c
            value = jnp.where(used_ref[slot] > 0, value, 0.0)
            soap_products(value, slot, state, work, batch, 2 * (4 * g + lax.rem(c, 4)))

    def finish(b):
        batch = lax.rem(b, 2)
        place_bases(work, batch, state[5], state[6], 4 * b)
        emit(b)

    def emit(b):
        for g in range(2):
            span = pl.ds(g * half + 4 * b, 4)
            for i in range(7):
                pltpu.make_async_copy(state[i].at[span], state_out[i].at[span], state_sem.at[1, i]).start()

    def round_of(r, carry):
        for s in range(4):
            t = 4 * r + s

            @pl.when(t < half)
            def _(t=t):
                step_a(t)

            @pl.when((t >= 1) & (t <= half))
            def _(t=t):
                step_b(t - 1)

            @pl.when((t >= 2) & (t < half + 2))
            def _(t=t):
                step_c(t - 2)

            if s >= 1:

                @pl.when((r >= 1) & (r < half // 4))
                def _(s=s):
                    panel_step(work, lax.rem(r - 1, 2), s - 1)

            else:

                @pl.when((r >= 2) & (r <= half // 4))
                def _():
                    panel_step(work, lax.rem(r - 2, 2), TILE // PANEL - 1)
                    finish(r - 2)

        return carry

    lax.fori_loop(0, half // 4 + 1, round_of, 0)
    emit(half // 4 - 1)
    work_out_ref[...] = work[(half // 4 - 1) % 2]
    small_out_ref[...] = small_add(0)
    for axis in range(3):
        for k in range(1, grid[axis]):
            send_s(axis, k).wait_send()

    def end(c):
        for g in range(2):
            for k in range(1, first[g][0]):
                send_a(g, c, k).wait_send()
            for k in range(1, second[g][0]):
                send_b(g, c, k).wait_send()
            for k in range(1, zs):
                send_c(g, c, k).wait_send()

    each(half, end)
    for i in range(7):
        pltpu.make_async_copy(state[i], state_out[i], state_sem.at[1, i]).wait()


def place_bases(work, batch, left_ref, right_ref, at):
    half = left_ref.shape[0] // 2
    for g in range(2):
        for e in range(4):
            left_ref[g * half + at + e] = work[batch, 2 * (4 * g + e), :, TILE:].T
            right_ref[g * half + at + e] = work[batch, 2 * (4 * g + e) + 1, :, TILE:].T


def last_bases_kernel(work_ref, *refs):
    state_in, state_out, state, work, sems = refs[:7], refs[7:14], refs[14:21], refs[21], refs[22]
    half = state[0].shape[0] // 2

    def copy_in(i):
        return pltpu.make_async_copy(state_in[i], state[i], sems.at[0, i])

    def copy_out(i):
        return pltpu.make_async_copy(state[i], state_out[i], sems.at[1, i])

    for i in range(7):
        copy_in(i).start()
    work[0] = work_ref[...]
    panel_step(work, 0, 0)
    for i in range(7):
        copy_in(i).wait()
        if i < 5:
            copy_out(i).start()
    for p in range(1, TILE // PANEL):
        panel_step(work, 0, p)
    place_bases(work, 0, state[5], state[6], half - 4)
    for i in range(5, 7):
        copy_out(i).start()
    for i in range(7):
        copy_out(i).wait()


def last_bases(work, state):
    whole = state[0].shape
    return pl.pallas_call(
        last_bases_kernel,
        out_shape=[jax.ShapeDtypeStruct(whole, F32)] * 7,
        in_specs=[pl.BlockSpec(memory_space=pltpu.VMEM)] + [ANY] * 7,
        out_specs=[ANY] * 7,
        scratch_shapes=[pltpu.VMEM(whole, F32)] * 7
        + [pltpu.VMEM((1,) + work.shape, F32), pltpu.SemaphoreType.DMA((2, 7))],
        compiler_params=pltpu.CompilerParams(vmem_limit_bytes=56 << 20),
        name="last_bases",
    )(work, *state)


def soap_products(g, i, state, work, batch, at):
    w_ref, m_ref, v_ref, l_ref, r_ref, ql_ref, qr_ref = state
    c1 = 1.0 - BETA_ONE**STEP
    c2 = 1.0 - BETA_TWO**STEP
    ql = ql_ref[i]
    qr = qr_ref[i]
    gt = g.T
    nm = BETA_ONE * m_ref[i] + (1.0 - BETA_ONE) * g
    m_ref[i] = nm
    side = mm(jnp.concatenate([g, nm], 0), qr)
    both = mm(ql.T, jnp.concatenate([side[:TILE], side[TILE:]], 1))
    rotated, rotated_first = both[:, :TILE], both[:, TILE:]
    nv = BETA_TWO * v_ref[i] + (1.0 - BETA_TWO) * rotated * rotated
    v_ref[i] = nv
    normed = rotated_first / c1 / (jnp.sqrt(nv / c2) + ADAM_EPSILON)
    step = mm(mm(ql, normed), qr, NT)
    w = w_ref[i]
    w_ref[i] = w - MATRIX_RATE * step - MATRIX_RATE * WEIGHT_DECAY * w
    for k, (ref, turn, left, right) in enumerate(((l_ref, ql, g, gt), (r_ref, qr, gt, g))):
        stat = BETA_TWO * ref[i] + (1.0 - BETA_TWO) * mm(left, right)
        ref[i] = stat
        a = mm(stat, turn)
        at_turned = a.T
        work[batch, at + k, :, :TILE] = mm(at_turned, a)
        work[batch, at + k, :, TILE:] = at_turned


def panel_step(work, batch, p):
    count = work.shape[1]
    per = TILE // (2 * PANEL)
    r0 = p * PANEL
    rows = count // per * 8
    lane = lax.broadcasted_iota(jnp.int32, (rows, TILE), 1)
    start = lane // (2 * PANEL) * (2 * PANEL)
    row = lax.rem(lax.broadcasted_iota(jnp.int32, (rows, TILE), 0), 8)
    sub = lax.broadcasted_iota(jnp.int32, (count // per, 8, TILE), 1)
    eye = (
        lax.broadcasted_iota(jnp.int32, (PANEL, PANEL), 0) == lax.broadcasted_iota(jnp.int32, (PANEL, PANEL), 1)
    ).astype(F32)
    packs = []
    for q in range(count // per):
        pieces = []
        for k in range(per):
            pieces += [work[batch, q * per + k, r0:r0 + PANEL, r0:r0 + PANEL], eye]
        packs.append(jnp.concatenate(pieces, 1)[None])
    x = jnp.concatenate(packs, 0)
    strips = [x[:, 8 * e:8 * e + 8, :] for e in range(PANEL // 8)]

    def segment(strip, index):
        return jnp.take_along_axis(strip.reshape(-1, TILE), index, axis=1).reshape(strip.shape)

    for j in range(0, PANEL, 2):
        e0, here = j // 8, j % 8
        one = [segment(strip, start + j) for strip in strips[e0:]]
        two = [segment(strip, start + j + 1) for strip in strips[e0:]]
        corner = one[0][:, here:here + 1, :]
        side = one[0][:, here + 1:here + 2, :]
        inverse = 1.0 / corner
        inverse_two = corner * (1.0 / (corner * two[0][:, here + 1:here + 2, :] - side * side))
        shift = side * inverse
        ratio = strips[e0][:, here:here + 1, :] * inverse
        next_off = side * ratio
        ratio_two = (strips[e0][:, here + 1:here + 2, :] - next_off) * inverse_two
        ratio_one = ratio - shift * ratio_two
        for e in range(e0, PANEL // 8):
            change = one[e - e0] * ratio_one + two[e - e0] * ratio_two
            if e == e0:
                change = jnp.where(sub > here + 1, change, jnp.where(sub == here + 1, next_off, 0.0))
            strips[e] = strips[e] - change
    for e in range(PANEL // 8):
        strips[e] = strips[e] * lax.rsqrt(segment(strips[e], start + 8 * e + row))
    x = jnp.concatenate(strips, 1)
    for q in range(count // per):
        for k in range(per):
            i = q * per + k
            inverse = x[q, :, 2 * PANEL * k + PANEL:2 * PANEL * (k + 1)]
            u = mm(inverse, work[batch, i, r0:r0 + PANEL, :])
            work[batch, i, r0:r0 + PANEL, TILE:] = u[:, TILE:]
            if r0 + PANEL < TILE:
                high, low = halves(u)
                left = jnp.concatenate([u[:, :TILE], u[:, :TILE], low[:, :TILE].astype(F32)], 0).T
                work[batch, i, r0 + PANEL:, :] -= times(
                    left[r0 + PANEL:, :].astype(BF16), jnp.concatenate([high, low, high], 0)
                )


def some(shape):
    return tuple(max(1, s) for s in shape)


def owner_update(used, slot_grads, small, state, device_count):
    grid = chip_grid(device_count)
    zs, ys, xs = grid
    slots = slot_grads.shape[0] // device_count
    half = slots // 2
    block = (TILE, TILE)
    dma = pltpu.SemaphoreType.DMA
    firsts, seconds = (xs, ys), (ys, xs)
    whole = (slots,) + block
    scratch = (
        [pltpu.VMEM(whole, F32)] * 7
        + [pltpu.VMEM((half, zs, seconds[g]) + block, BF16) for g in range(2)]
        + [pltpu.VMEM(some((half, firsts[g] - 1, zs, seconds[g])) + block, BF16) for g in range(2)]
        + [pltpu.VMEM(some((half, seconds[g] - 1, zs)) + block, BF16) for g in range(2)]
        + [pltpu.VMEM(some((half, zs - 1)) + block, BF16) for g in range(2)]
        + [pltpu.VMEM((3,) + small.shape, F32)]
        + [pltpu.VMEM((max(1, n - 1),) + small.shape, F32) for n in grid]
        + [pltpu.VMEM((2, 16, TILE, 2 * TILE), F32)]
        + [dma((2, half))]
        + [dma(some((half, firsts[g] - 1))) for g in range(2)] * 2
        + [dma(some((half, seconds[g] - 1))) for g in range(2)] * 2
        + [dma(some((half, zs - 1))) for g in range(2)] * 2
        + [dma((max(1, n - 1),)) for n in grid] * 2
        + [dma((2, 7))]
    )
    results = pl.pallas_call(
        functools.partial(owner_kernel, grid),
        out_shape=[jax.ShapeDtypeStruct(whole, F32)] * 7
        + [jax.ShapeDtypeStruct(small.shape, F32), jax.ShapeDtypeStruct((16, TILE, 2 * TILE), F32)],
        in_specs=[pl.BlockSpec(memory_space=pltpu.SMEM), ANY, pl.BlockSpec(memory_space=pltpu.VMEM)] + [ANY] * 7,
        out_specs=[ANY] * 7 + [pl.BlockSpec(memory_space=pltpu.VMEM)] * 2,
        scratch_shapes=scratch,
        compiler_params=pltpu.CompilerParams(collective_id=1, has_side_effects=True, vmem_limit_bytes=56 << 20),
        name="owner_update",
    )(used, slot_grads.reshape(zs, ys, xs, slots, TILE, TILE), small, *state)
    return last_bases(results[8], results[:7]), results[7]


def ag_kernel(grid, wide_ref, small_ref, out_ref, small_out_ref, own_ref,
              load_sem, z_send, z_recv, b_send0, b_send1, b_recv0, b_recv1, a_send0, a_send1, a_recv0, a_recv1,
              s_load, ssz, ssy, ssx, srz, sry, srx):
    zs, ys, xs = grid
    z, y, x = place(grid)
    tos = peers(grid)
    to_z, to_y, to_x = tos
    slots = own_ref.shape[0]
    half, chunks, size = chunking(slots)
    first = ((xs, to_x), (ys, to_y))
    second = ((ys, to_y), (xs, to_x))
    b_send, b_recv, a_send, a_recv = (b_send0, b_send1), (b_recv0, b_recv1), (a_send0, a_send1), (a_recv0, a_recv1)
    s_send, s_recv = (ssz, ssy, ssx), (srz, sry, srx)

    def span(g, c):
        return pl.ds(g * half + c * size, size)

    def send_z(g, c, k):
        return remote(own_ref.at[span(g, c)], out_ref.at[z, y, x, span(g, c)],
                      z_send.at[g, c, k - 1], z_recv.at[g, c, k - 1], to_z(k))

    def send_b(g, c, k):
        part = out_ref.at[:, y, x, span(g, c)]
        return remote(part, part, b_send[g].at[c, k - 1], b_recv[g].at[c, k - 1], second[g][1](k))

    def send_a(g, c, k):
        part = out_ref.at[:, :, x, span(g, c)] if g == 0 else out_ref.at[:, y, :, span(g, c)]
        return remote(part, part, a_send[g].at[c, k - 1], a_recv[g].at[c, k - 1], first[g][1](k))

    def send_s(axis, k):
        if axis == 0:
            source, target = small_ref, small_out_ref.at[z, y, x]
        else:
            source = target = small_out_ref.at[:, y, x] if axis == 1 else small_out_ref.at[:, :, x]
        return remote(source, target, s_send[axis].at[k - 1], s_recv[axis].at[k - 1], tos[axis](k))

    own_ref[...] = wide_ref[...].astype(BF16)
    keep = pltpu.make_async_copy(own_ref, out_ref.at[z, y, x], load_sem)
    keep_small = pltpu.make_async_copy(small_ref, small_out_ref.at[z, y, x], s_load)
    keep.start()
    keep_small.start()
    greet(grid)

    for k in range(1, grid[0]):
        send_s(0, k).start()
    def start_z(c):
        for g in range(2):
            for k in range(1, zs):
                send_z(g, c, k).start()

    def small_wait(axis):
        for k in range(1, grid[axis]):
            send_s(axis, k).wait_recv()

    def small_start(axis):
        for k in range(1, grid[axis]):
            send_s(axis, k).start()

    start_z(0)
    for t in range(chunks + 1):
        if t < chunks:
            for g in range(2):
                for k in range(1, zs):
                    send_z(g, t, k).wait_recv()
            if t == 0:
                keep.wait()
                keep_small.wait()
                small_wait(0)
                small_start(1)
            if t + 1 < chunks:
                start_z(t + 1)
            for g in range(2):
                for k in range(1, second[g][0]):
                    send_b(g, t, k).start()
        if t >= 1:
            for g in range(2):
                for k in range(1, second[g][0]):
                    send_b(g, t - 1, k).wait_recv()
                for k in range(1, first[g][0]):
                    send_a(g, t - 1, k).start()
        if t == 1:
            small_wait(1)
            small_start(2)
    small_wait(2)
    for c in range(chunks):
        for g in range(2):
            for k in range(1, first[g][0]):
                send_a(g, c, k).wait_recv()
    for axis in range(3):
        for k in range(1, grid[axis]):
            send_s(axis, k).wait_send()
    for c in range(chunks):
        for g in range(2):
            for k in range(1, zs):
                send_z(g, c, k).wait_send()
            for k in range(1, second[g][0]):
                send_b(g, c, k).wait_send()
            for k in range(1, first[g][0]):
                send_a(g, c, k).wait_send()


def gather_all(own, small, device_count):
    grid = chip_grid(device_count)
    zs, ys, xs = grid
    slots = own.shape[0]
    half, chunks, size = chunking(slots)
    dma = pltpu.SemaphoreType.DMA
    firsts, seconds = (xs, ys), (ys, xs)
    scratch = (
        [pltpu.VMEM(own.shape, BF16), dma, dma(some((2, chunks, zs - 1))), dma(some((2, chunks, zs - 1)))]
        + [dma(some((chunks, seconds[g] - 1))) for g in range(2)] * 2
        + [dma(some((chunks, firsts[g] - 1))) for g in range(2)] * 2
        + [dma]
        + [dma((max(1, n - 1),)) for n in grid] * 2
    )
    blocks, smalls = pl.pallas_call(
        functools.partial(ag_kernel, grid),
        out_shape=[jax.ShapeDtypeStruct(grid + own.shape, BF16), jax.ShapeDtypeStruct(grid + small.shape, small.dtype)],
        in_specs=[pl.BlockSpec(memory_space=pltpu.VMEM)] * 2,
        out_specs=[ANY, ANY],
        scratch_shapes=scratch,
        compiler_params=pltpu.CompilerParams(collective_id=2, has_side_effects=True, vmem_limit_bytes=56 << 20),
        name="gather_all",
    )(own, small)
    return blocks.reshape((-1,) + own.shape[1:]), smalls.reshape((-1,) + small.shape)


def unpack_and_attend(packed, slots, shapes, x, split, places, half):
    length, width = x.shape
    span, count = min(length, 512), len(shapes)

    def kernel(slots_ref, split_ref, packed_ref, x_ref, *refs):
        mats, mixed_out, attended_out, totals_ref = refs[:count], refs[count], refs[count + 1], refs[count + 2]
        near, rest = refs[count + 3:2 * count + 3], refs[2 * count + 3:]
        x_near, mixed_ref, attended_ref, score_ref, turned_ref, sems, own_sems = rest

        def whole(index):
            return pltpu.make_async_copy(near[index], mats[index], sems.at[1, index])

        load_x = pltpu.make_async_copy(x_ref, x_near, own_sems.at[0])
        load_x.start()
        offsets = [0]
        for height, breadth in shapes:
            offsets.append(offsets[-1] + height // TILE * (breadth // TILE))

        def start(index):
            height, breadth = shapes[index]
            across = breadth // TILE
            for i in range(height // TILE):
                for j in range(across):
                    tile = near[index].at[i * TILE:(i + 1) * TILE, j * TILE:(j + 1) * TILE]
                    slot = packed_ref.at[slots_ref[offsets[index] + i * across + j]]
                    pltpu.make_async_copy(slot, tile, sems.at[0, index]).start()

        start(0)

        def landed(index):
            pltpu.make_async_copy(near[index], near[index], sems.at[0, index]).wait()
            whole(index).start()

        load_x.wait()
        landed(0)
        mix(x_near, near[0], bias_row(split_ref, places, ("enc_q", None, "enc_v"), half), mixed_ref)
        keep_mixed = pltpu.make_async_copy(mixed_ref, mixed_out, own_sems.at[1])
        keep_mixed.start()

        def beside(part, parts):
            lead = parts // 2
            share = -(-(count - 1) // lead)
            place = part if part < lead else part - lead
            for index in range(1 + place * share, min(count, 1 + (place + 1) * share)):
                if part < lead:
                    start(index)
                elif part < 2 * lead:
                    landed(index)

        totals_ref[...] = jnp.zeros_like(totals_ref)
        attend(
            mixed_ref.at[:, :half], mixed_ref.at[:, half:2 * half], mixed_ref.at[:, 2 * half:],
            attended_ref, totals_ref, score_ref, turned_ref, False, span, beside,
        )
        keep_attended = pltpu.make_async_copy(attended_ref, attended_out, own_sems.at[2])
        keep_attended.start()
        for index in range(count):
            whole(index).wait()
        keep_mixed.wait()
        keep_attended.wait()

    results = pl.pallas_call(
        kernel,
        out_shape=[jax.ShapeDtypeStruct(s, BF16) for s in shapes]
        + [shape(length, 3 * half, dtype=BF16), shape(length, half, dtype=BF16), shape(8, length)],
        in_specs=[pl.BlockSpec(memory_space=pltpu.SMEM), VM, ANY, ANY],
        out_specs=[ANY] * (count + 2) + [VM],
        scratch_shapes=[held(*s, dtype=BF16) for s in shapes]
        + [
            held(length, width, dtype=BF16), held(length, 3 * half, dtype=BF16), held(length, half, dtype=BF16),
            held(2, length, span), held(half, length, dtype=BF16),
            pltpu.SemaphoreType.DMA((2, count)), pltpu.SemaphoreType.DMA((3,)),
        ],
        compiler_params=pltpu.CompilerParams(vmem_limit_bytes=56 << 20),
        name="unpack_and_attend",
    )(slots, split, packed, x)
    return results[:count], results[count:]


def weight_grads_kernel(plan, used, vectors, passed, slots_ref, *refs):
    arrays, refs = refs[:used], refs[used:]
    given, refs = refs[:len(vectors)], refs[len(vectors):]
    refs = refs[passed:]
    packed, refs = refs[0], refs[1:]
    if vectors:
        rows_ref, refs = refs[0], refs[1:]
    held, refs = refs[:used], refs[used:]
    turned, refs = refs[0], refs[1:]
    results, sems = refs[:len(plan)], refs[len(plan):]
    load_sem, store_sem = sems

    def load(i):
        return pltpu.make_async_copy(arrays[i], held[i], load_sem.at[i])

    order = []
    for left, tokens, right, *rest in plan:
        for i in (left, right):
            if i not in order:
                order.append(i)
    for i in order:
        load(i).start()
    if vectors:
        width = rows_ref.shape[1]
        rows_ref[...] = jnp.zeros_like(rows_ref)
        for source, (at, pieces) in zip(given, vectors):
            if pieces is None:
                rows_ref[at:at + 3, :] = source[0:3, :]
                continue
            for begin, end in pieces:
                while begin < end:
                    lane = at % width
                    size = min(end - begin, width - lane)
                    rows_ref[at // width:at // width + 1, lane:lane + size] = source[:, begin:begin + size]
                    begin, at = begin + size, at + size
    ready = set()
    last = None
    ready_columns = []

    def send(result, index, offset, stride, down, group, n):
        for i in range(down):
            for j in range(n * group, (n + 1) * group):
                tile = result.at[i * TILE:(i + 1) * TILE, j * TILE:(j + 1) * TILE]
                slot = packed.at[slots_ref[offset + i * stride + j]]
                pltpu.make_async_copy(tile, slot, store_sem.at[index]).start()

    for index, (left, tokens, right, offset, stride, down, across) in enumerate(plan):
        for i in (left, right):
            if i not in ready:
                ready.add(i)
                load(i).wait()
        height = down * TILE
        if last != (left, tokens):
            for j in range(down):
                turned[j * TILE:(j + 1) * TILE, :tokens] = (
                    held[left][:tokens, j * TILE:(j + 1) * TILE].astype(F32).T.astype(BF16)
                )
            last = (left, tokens)
        result = results[index]
        group = 3 if across % 3 == 0 else 1

        for n in range(across // group):
            lanes = slice(n * group * TILE, (n + 1) * group * TILE)
            result[:, lanes] = times(turned[:height, :tokens], held[right][:tokens, lanes]).astype(BF16)
            ready_columns.append((result, index, offset, stride, down, group, n))
            if len(ready_columns) > 1:
                send(*ready_columns.pop(0))
    for columns in ready_columns:
        send(*columns)
    for index in range(len(plan)):
        pltpu.make_async_copy(results[index], results[index], store_sem.at[index]).wait()


def weight_grads(matrices, slots, slot_count, packed=None, vectors=None):
    arrays, plan, results = [], [], []

    def index_of(array):
        for i, other in enumerate(arrays):
            if other is array:
                return i
        arrays.append(array)
        return len(arrays) - 1

    for offset, parts in matrices:
        height = parts[0][0].shape[1]
        stride = sum(right.shape[1] for left, right in parts) // TILE
        for left, right in parts:
            across = right.shape[1] // TILE
            plan.append((index_of(left), right.shape[0], index_of(right), offset, stride, height // TILE, across))
            results.append(pltpu.VMEM((height, right.shape[1]), BF16))
            offset += across
    tall = max(entry[5] for entry in plan) * TILE
    long = max(entry[1] for entry in plan)
    out_shape = [jax.ShapeDtypeStruct((slot_count, TILE, TILE), BF16)]
    given, layout = [], []
    if vectors:
        rows, width, items = vectors
        out_shape.append(jax.ShapeDtypeStruct((rows, width), F32))
        given = [item[0] for item in items]
        layout = [item[1:] for item in items]
    passed = [] if packed is None else [packed]
    return pl.pallas_call(
        functools.partial(weight_grads_kernel, plan, len(arrays), layout, len(passed)),
        out_shape=out_shape,
        in_specs=[pl.BlockSpec(memory_space=pltpu.SMEM)] + [ANY] * len(arrays)
        + [pl.BlockSpec(memory_space=pltpu.VMEM)] * len(given) + [ANY] * len(passed),
        out_specs=[ANY] + [pl.BlockSpec(memory_space=pltpu.VMEM)] * (len(out_shape) - 1),
        scratch_shapes=[pltpu.VMEM(a.shape, a.dtype) for a in arrays] + [pltpu.VMEM((tall, long), BF16)] + results
        + [pltpu.SemaphoreType.DMA((len(arrays),)), pltpu.SemaphoreType.DMA((len(plan),))],
        input_output_aliases={} if packed is None else {1 + len(arrays) + len(given): 0},
        compiler_params=pltpu.CompilerParams(vmem_limit_bytes=56 << 20),
        name="weight_grads",
    )(slots, *arrays, *given, *passed)


VM = pl.BlockSpec(memory_space=pltpu.VMEM)


def times(left, right, dims=NN):
    return lax.dot_general(left, right, (dims, ((), ())), preferred_element_type=F32)


def rows_of(t, size=ROWS):
    return pl.ds(pl.multiple_of(t * size, size), size)


class Swap:
    def __init__(self, out, into, send_sem, recv_sem):
        self.out, self.into, self.send_sem, self.recv_sem = out, into, send_sem, recv_sem

    @staticmethod
    def scratch(tiles, width):
        dma = pltpu.SemaphoreType.DMA((tiles,))
        held = pltpu.VMEM((tiles, ROWS, width), BF16)
        return [held, held, dma, dma]

    @staticmethod
    def greet():
        barrier = pltpu.get_barrier_semaphore()
        other = {"tensor": 1 - lax.axis_index("tensor")}
        pl.semaphore_signal(barrier, inc=1, device_id=other, device_id_type=MESH)
        pl.semaphore_wait(barrier, 1)

    def copy(self, t):
        return pltpu.make_async_remote_copy(
            src_ref=self.out.at[t],
            dst_ref=self.into.at[t],
            send_sem=self.send_sem.at[t],
            recv_sem=self.recv_sem.at[t],
            device_id={"tensor": 1 - lax.axis_index("tensor")},
            device_id_type=MESH,
        )

    def give(self, t, value):
        self.out[t] = value.astype(BF16)
        self.copy(t).start()

    def take(self, t):
        self.copy(t).wait()
        return self.out[t].astype(F32) + self.into[t].astype(F32)


class Rows:
    def __init__(self, ref, rows):
        self.ref, self.rows = ref, rows

    def __getitem__(self, index):
        at = self.rows[index[0].start]
        return self.ref[at:at + 1, :]


def bias_places(half, hidden_half):
    places, at = {}, 0
    for name, length in (
        ("enc_q", half), ("enc_v", half), ("enc_up", hidden_half), ("dec_q", half), ("dec_v", half),
        ("crs_q", half), ("crs_v", half), ("dec_up", hidden_half),
    ):
        places[name] = slice(at, at + length)
        at += length
    return places


def bias_row(split_ref, places, names, half):
    zero = jnp.zeros((1, half), F32)
    return jnp.concatenate([zero if name is None else split_ref[:, places[name]] for name in names], 1)


def standardize(values):
    center = values - jnp.mean(values, -1, keepdims=True)
    scale = lax.rsqrt(jnp.mean(center * center, -1, keepdims=True) + NORM_EPSILON)
    return center * scale, scale


def norm_back(grad, unit, scale, gain):
    inner = grad * gain
    return scale * (
        inner - jnp.mean(inner, -1, keepdims=True) - unit * jnp.mean(inner * unit, -1, keepdims=True)
    )


def add_sums(sums_ref, grad_in, grad_out, unit):
    sums_ref[0:1, :] += jnp.sum(grad_in, 0, keepdims=True)
    sums_ref[1:2, :] += jnp.sum(grad_out * unit, 0, keepdims=True)
    sums_ref[2:3, :] += jnp.sum(grad_out, 0, keepdims=True)


def head_mask(shape):
    return lax.broadcasted_iota(jnp.int32, shape, 1) < HD


def attend(query_ref, key_ref, value_ref, attended_ref, totals_ref, score_ref, turned_ref, causal, span, beside=None):
    queries, keys = query_ref.shape[0], key_ref.shape[0]
    pairs = query_ref.shape[1] // PAIR
    chunks = keys // KEYS
    for j in range(pairs):
        turned_ref[j * PAIR:(j + 1) * PAIR, :] = (
            value_ref[:, j * PAIR:(j + 1) * PAIR].astype(F32).T.astype(BF16)
        )
    for i in range(queries // span):
        mine = slice(i * span, (i + 1) * span)

        def pair(j, carry, i=i, mine=mine):
            lanes = pl.ds(j * PAIR if isinstance(j, int) else pl.multiple_of(j * PAIR, PAIR), PAIR)
            query = query_ref[mine, lanes] * jnp.asarray(HD**-0.5, BF16)
            first = head_mask(query.shape)
            parts = []
            for h in range(2):
                masked = jnp.where(first if h == 0 else ~first, query, jnp.zeros_like(query))
                top = jnp.full((1, span), -jnp.inf, F32)
                for c in range(chunks):
                    if causal and c * KEYS >= (i + 1) * span:
                        continue
                    scores = times(key_ref[c * KEYS:(c + 1) * KEYS, lanes], masked, NT)
                    if causal and (c + 1) * KEYS > i * span:
                        key_at = c * KEYS + lax.broadcasted_iota(jnp.int32, scores.shape, 0)
                        query_at = i * span + lax.broadcasted_iota(jnp.int32, scores.shape, 1)
                        scores = jnp.where(key_at <= query_at, scores, -1000000000.0)
                    score_ref[h, c * KEYS:(c + 1) * KEYS, :] = scores
                    top = jnp.maximum(top, jnp.max(scores, 0, keepdims=True))
                total = jnp.zeros((1, span), F32)
                mixed = jnp.zeros((HD, span), F32)
                value_rows = pl.ds(j * PAIR + h * HD if isinstance(j, int) else pl.multiple_of(j * PAIR + h * HD, HD), HD)
                for c in range(chunks):
                    if causal and c * KEYS >= (i + 1) * span:
                        continue
                    probs = jnp.exp(score_ref[h, c * KEYS:(c + 1) * KEYS, :] - top)
                    total += jnp.sum(probs, 0, keepdims=True)
                    mixed += times(turned_ref[value_rows, c * KEYS:(c + 1) * KEYS], probs.astype(BF16))
                parts.append(mixed * (1.0 / total))
                totals_ref[pl.ds(2 * j + h, 1), mine] = top + jnp.log(total)
            attended_ref[mine, lanes] = jnp.concatenate(parts, 0).T.astype(BF16)
            return carry

        if beside is None:
            lax.fori_loop(0, pairs, pair, 0)
        else:
            for j in range(pairs):
                beside(i * pairs + j, queries // span * pairs)
                pair(j, 0)


def attend_back(
    query_ref, key_ref, value_ref, attended_ref, totals_ref, grad_ref,
    grad_query_ref, grad_key_ref, grad_value_ref, turned_ref, causal,
):
    queries, keys = grad_ref.shape[0], key_ref.shape[0]
    pairs = query_ref.shape[1] // PAIR
    chunks = keys // KEYS
    scale = HD**-0.5
    for j in range(pairs):
        turned_ref[j * PAIR:(j + 1) * PAIR, :] = (
            key_ref[:, j * PAIR:(j + 1) * PAIR].astype(F32).T.astype(BF16)
        )

    def pair(j, carry):
        lanes = pl.ds(pl.multiple_of(j * PAIR, PAIR), PAIR)
        query = query_ref[:queries, lanes] * jnp.asarray(scale, BF16)
        grad = grad_ref[:, lanes]
        first = head_mask(query.shape)
        meet = (grad.astype(F32) * attended_ref[:queries, lanes].astype(F32)).T
        masked, grads, deltas, totals = [], [], [], []
        for h in range(2):
            keep = first if h == 0 else ~first
            masked.append(jnp.where(keep, query, jnp.zeros_like(query)))
            grads.append(jnp.where(keep, grad, jnp.zeros_like(grad)))
            deltas.append(jnp.sum(meet[h * HD:(h + 1) * HD], 0, keepdims=True))
            totals.append(totals_ref[pl.ds(2 * j + h, 1), :queries])
        grad_query = [jnp.zeros((HD, queries), F32) for h in range(2)]
        for c in range(chunks):
            some = slice(c * KEYS, (c + 1) * KEYS)
            low = c * KEYS if causal else 0
            grad_key = grad_value = jnp.zeros((KEYS, PAIR), F32)
            for h in range(2):
                scores = times(key_ref[some, lanes], masked[h][low:], NT)
                if causal:
                    key_at = lax.broadcasted_iota(jnp.int32, scores.shape, 0)
                    query_at = lax.broadcasted_iota(jnp.int32, scores.shape, 1)
                    scores = jnp.where(key_at <= query_at, scores, -1000000000.0)
                probs = jnp.exp(scores - totals[h][:, low:])
                grad_probs = times(value_ref[some, lanes], grads[h][low:], NT)
                grad_scores = (probs * (grad_probs - deltas[h][:, low:])).astype(BF16)
                grad_value += times(probs.astype(BF16), grads[h][low:])
                grad_key += times(grad_scores, masked[h][low:])
                key_rows = pl.ds(pl.multiple_of(j * PAIR + h * HD, HD), HD)
                part = times(turned_ref[key_rows, some], grad_scores)
                if low:
                    part = jnp.concatenate([jnp.zeros((HD, low), F32), part], 1)
                grad_query[h] += part
            grad_key_ref[some, lanes] = grad_key.astype(BF16)
            grad_value_ref[some, lanes] = grad_value.astype(BF16)
        grad_query_ref[:, lanes] = (jnp.concatenate(grad_query, 0) * scale).T.astype(BF16)
        return carry

    lax.fori_loop(0, pairs, pair, 0)


def mix(x_ref, wide_ref, bias, mixed_ref):
    def one(t, carry):
        mixed_ref[rows_of(t), :] = (times(x_ref[rows_of(t), :], wide_ref[...]) + bias).astype(BF16)
        return carry

    lax.fori_loop(0, x_ref.shape[0] // ROWS, one, 0)


def close_branch(x_ref, attended_ref, out_weight_ref, vec_ref, unit_ref, scale_ref, *swap_refs):
    swap = Swap(*swap_refs)
    tiles = x_ref.shape[0] // ROWS

    def give(t, carry):
        swap.give(t, times(attended_ref[rows_of(t), :], out_weight_ref[...]))
        return carry

    lax.fori_loop(0, tiles, give, 0)

    def take(t, carry):
        rows = rows_of(t)
        unit, scale = standardize(x_ref[rows, :].astype(F32) + swap.take(t) + vec_ref[0:1, :])
        unit_ref[rows, :] = unit
        scale_ref[rows, :] = scale
        return carry

    lax.fori_loop(0, tiles, take, 0)


def self_forward_kernel(
    causal, span, x_ref, wide_ref, out_weight_ref, bias, vec_ref,
    mixed_ref, attended_ref, totals_ref, unit_ref, scale_ref,
    score_ref, turned_ref, *swap_refs,
):
    half = out_weight_ref.shape[0]
    totals_ref[...] = jnp.zeros_like(totals_ref)
    mix(x_ref, wide_ref, bias, mixed_ref)
    attend(
        mixed_ref.at[:, :half], mixed_ref.at[:, half:2 * half], mixed_ref.at[:, 2 * half:],
        attended_ref, totals_ref, score_ref, turned_ref, causal, span,
    )
    close_branch(x_ref, attended_ref, out_weight_ref, vec_ref, unit_ref, scale_ref, *swap_refs)


def shape(*dims, dtype=F32):
    return jax.ShapeDtypeStruct(dims, dtype)


def params(ident, mib=56):
    return pltpu.CompilerParams(collective_id=ident, has_side_effects=True, vmem_limit_bytes=mib << 20)


def cross_forward_kernel(
    span, unit_ref, fetched_ref, query_weight_ref, wide_ref, out_weight_ref, query_bias_ref, bias_ref, vec_ref,
    low_ref, query_ref, mixed_ref, attended_ref, totals_ref, unit_out_ref, scale_ref,
    score_ref, turned_ref, *swap_refs,
):
    swap = Swap(*swap_refs)
    length, width = unit_ref.shape
    half = out_weight_ref.shape[0]
    tiles = length // ROWS
    totals_ref[...] = jnp.zeros_like(totals_ref)

    def ask(t, carry):
        rows = rows_of(t)
        low = (unit_ref[rows, :] * vec_ref[0:1, :] + vec_ref[1:2, :]).astype(BF16)
        low_ref[rows, :] = low
        query_ref[rows, :] = (times(low, query_weight_ref[...]) + query_bias_ref[...]).astype(BF16)
        return carry

    lax.fori_loop(0, tiles, ask, 0)

    def mix(t, carry):
        mixed_ref[rows_of(t), :] = (
            times(fetched_ref[rows_of(t), :], wide_ref[...]) + bias_ref[...]
        ).astype(BF16)
        return carry

    lax.fori_loop(0, fetched_ref.shape[0] // ROWS, mix, 0)
    attend(
        query_ref, mixed_ref.at[:, :half], mixed_ref.at[:, half:],
        attended_ref, totals_ref, score_ref, turned_ref, False, span,
    )

    def give(t, carry):
        swap.give(t, times(attended_ref[rows_of(t), :], out_weight_ref[...]))
        return carry

    lax.fori_loop(0, tiles, give, 0)

    def take(t, carry):
        rows = rows_of(t)
        hidden = unit_ref[rows, :] * vec_ref[0:1, :] + vec_ref[1:2, :]
        unit, scale = standardize(hidden + swap.take(t) + vec_ref[2:3, :])
        unit_out_ref[rows, :] = unit
        scale_ref[rows, :] = scale
        return carry

    lax.fori_loop(0, tiles, take, 0)


def feed_forward_kernel(
    kept, between, unit_ref, up_ref, down_ref, bias_ref, vec_ref,
    states_ref, states_low_ref, low_ref, active_ref, slope_ref, unit_out_ref, scale_ref, *swap_refs,
):
    swap = Swap(*swap_refs)
    length, width = unit_ref.shape
    hidden_half = up_ref.shape[1]
    tiles, kept_tiles = length // ROWS, kept // ROWS
    step = 512

    def feed(t, carry, keep):
        rows = rows_of(t)
        low = (unit_ref[rows, :] * vec_ref[0:1, :] + vec_ref[1:2, :]).astype(BF16)
        if keep:
            low_ref[rows, :] = low
        total = jnp.zeros((ROWS, width), F32)
        for c in range(0, hidden_half, step):
            upward = times(low, up_ref[:, c:c + step]) + bias_ref[:, c:c + step]
            below = 0.5 * lax.erf(upward * (0.5**0.5)) + 0.5
            active = (upward * below).astype(BF16)
            if keep:
                active_ref[rows, c:c + step] = active
                bell = jnp.exp(-0.5 * upward * upward) * (0.5 / jnp.pi) ** 0.5
                slope_ref[rows, c:c + step] = (below + upward * bell).astype(BF16)
            total += times(active, down_ref[c:c + step, :])
        swap.give(t, total)
        return carry

    def take(t, carry, keep):
        rows = rows_of(t)
        hidden = unit_ref[rows, :] * vec_ref[0:1, :] + vec_ref[1:2, :]
        unit, scale = standardize(hidden + swap.take(t) + vec_ref[2:3, :])
        states = unit * vec_ref[3:4, :] + vec_ref[4:5, :]
        states_ref[rows, :] = states
        if keep:
            states_low_ref[rows, :] = states.astype(BF16)
            unit_out_ref[rows, :] = unit
            scale_ref[rows, :] = scale
        return carry

    lax.fori_loop(0, kept_tiles, functools.partial(feed, keep=True), 0)
    lax.fori_loop(0, kept_tiles, functools.partial(take, keep=True), 0)
    between()
    if kept_tiles < tiles:
        lax.fori_loop(kept_tiles, tiles, functools.partial(feed, keep=False), 0)
        lax.fori_loop(kept_tiles, tiles, functools.partial(take, keep=False), 0)


def feed_backward_kernel(
    grad_ref, unit_after_ref, scale_after_ref, active_ref, slope_ref, up_ref, down_ref,
    unit_before_ref, scale_before_ref, vec_ref,
    low_ref, grad_up_ref, bias_ref, grad_out_ref, sums_after_ref, sums_before_ref,
    held_ref, *swap_refs,
):
    swap = Swap(*swap_refs)
    length, width = grad_ref.shape
    hidden_half = up_ref.shape[1]
    tiles = length // ROWS
    step = 512
    sums_after_ref[...] = jnp.zeros_like(sums_after_ref)
    sums_before_ref[...] = jnp.zeros_like(sums_before_ref)
    bias_ref[...] = jnp.zeros_like(bias_ref)

    def give(t, carry):
        rows = rows_of(t)
        grad = grad_ref[rows, :].astype(F32)
        unit = unit_after_ref[rows, :]
        inner = norm_back(grad, unit, scale_after_ref[rows, :], vec_ref[0:1, :])
        add_sums(sums_after_ref, inner, grad, unit)
        held_ref[rows, :] = inner
        low = inner.astype(BF16)
        low_ref[rows, :] = low
        total = jnp.zeros((ROWS, width), F32)
        for c in range(0, hidden_half, step):
            grad_active = times(low, down_ref[c:c + step, :], NT)
            grad_up = (grad_active * slope_ref[rows, c:c + step].astype(F32)).astype(BF16)
            grad_up_ref[rows, c:c + step] = grad_up
            bias_ref[:, c:c + step] += jnp.sum(grad_up.astype(F32), 0, keepdims=True)
            total += times(grad_up, up_ref[:, c:c + step], NT)
        swap.give(t, total)
        return carry

    lax.fori_loop(0, tiles, give, 0)

    def take(t, carry):
        rows = rows_of(t)
        grad = held_ref[rows, :] + swap.take(t)
        unit = unit_before_ref[rows, :]
        inner = norm_back(grad, unit, scale_before_ref[rows, :], vec_ref[1:2, :])
        add_sums(sums_before_ref, inner, grad, unit)
        grad_out_ref[rows, :] = inner
        return carry

    lax.fori_loop(0, tiles, take, 0)


def spread(grad_pre_ref, out_weight_ref, low_ref, grad_ref):
    def one(t, carry):
        rows = rows_of(t)
        low = grad_pre_ref[rows, :].astype(BF16)
        low_ref[rows, :] = low
        grad_ref[rows, :] = times(low, out_weight_ref[...], NT).astype(BF16)
        return carry

    lax.fori_loop(0, grad_pre_ref.shape[0] // ROWS, one, 0)


def self_backward_kernel(
    causal, grad_pre_ref, mixed_ref, attended_ref, totals_ref, wide_ref, out_weight_ref,
    low_ref, grad_query_ref, grad_pair_ref, grad_x_ref, sums_ref,
    grad_ref, turned_ref, *swap_refs,
):
    swap = Swap(*swap_refs)
    queries, width = grad_pre_ref.shape
    half = out_weight_ref.shape[0]
    length = mixed_ref.shape[0]
    spread(grad_pre_ref, out_weight_ref, low_ref, grad_ref)
    attend_back(
        mixed_ref.at[:, :half], mixed_ref.at[:, half:2 * half], mixed_ref.at[:, 2 * half:],
        attended_ref, totals_ref, grad_ref,
        grad_query_ref, grad_pair_ref.at[:, :half], grad_pair_ref.at[:, half:], turned_ref, causal,
    )
    sums_ref[...] = jnp.zeros_like(sums_ref)
    first = queries // ROWS

    def give(t, carry, asked):
        rows = rows_of(t)
        pair = grad_pair_ref[rows, :]
        sums_ref[:, half:] += jnp.sum(pair.astype(F32), 0, keepdims=True)
        total = times(pair, wide_ref[:, half:], NT)
        if asked:
            query = grad_query_ref[rows, :]
            sums_ref[:, :half] += jnp.sum(query.astype(F32), 0, keepdims=True)
            total += times(query, wide_ref[:, :half], NT)
        swap.give(t, total)
        return carry

    lax.fori_loop(0, first, functools.partial(give, asked=True), 0)
    if first < length // ROWS:
        lax.fori_loop(first, length // ROWS, functools.partial(give, asked=False), 0)

    def take(t, carry, asked):
        rows = rows_of(t)
        total = swap.take(t)
        grad_x_ref[rows, :] = grad_pre_ref[rows, :] + total if asked else total
        return carry

    lax.fori_loop(0, first, functools.partial(take, asked=True), 0)
    if first < length // ROWS:
        lax.fori_loop(first, length // ROWS, functools.partial(take, asked=False), 0)


def cross_backward_kernel(
    between, grad_pre_ref, query_ref, mixed_ref, attended_ref, totals_ref, query_weight_ref, wide_ref, out_weight_ref,
    unit_ref, scale_ref, vec_ref,
    low_ref, grad_query_ref, grad_pair_ref, fetched_ref, grad_out_ref, sums_ref, vec_sums_ref,
    grad_ref, turned_ref, *swap_refs,
):
    near, far = Swap(*swap_refs[:4]), Swap(*swap_refs[4:])
    queries, width = grad_pre_ref.shape
    half = out_weight_ref.shape[0]
    keys = mixed_ref.shape[0]
    spread(grad_pre_ref, out_weight_ref, low_ref, grad_ref)
    attend_back(
        query_ref, mixed_ref.at[:, :half], mixed_ref.at[:, half:],
        attended_ref, totals_ref, grad_ref,
        grad_query_ref, grad_pair_ref.at[:, :half], grad_pair_ref.at[:, half:], turned_ref, False,
    )
    sums_ref[...] = jnp.zeros_like(sums_ref)
    vec_sums_ref[...] = jnp.zeros_like(vec_sums_ref)

    def give_far(t, carry):
        pair = grad_pair_ref[rows_of(t), :]
        sums_ref[:, half:] += jnp.sum(pair.astype(F32), 0, keepdims=True)
        far.give(t, times(pair, wide_ref[...], NT))
        return carry

    lax.fori_loop(0, keys // ROWS, give_far, 0)

    def give_near(t, carry):
        query = grad_query_ref[rows_of(t), :]
        sums_ref[:, :half] += jnp.sum(query.astype(F32), 0, keepdims=True)
        near.give(t, times(query, query_weight_ref[...], NT))
        return carry

    lax.fori_loop(0, queries // ROWS, give_near, 0)

    def take_far(t, carry):
        fetched_ref[rows_of(t), :] = far.take(t).astype(BF16)
        return carry

    lax.fori_loop(0, keys // ROWS, take_far, 0)
    between()

    def take_near(t, carry):
        rows = rows_of(t)
        grad = grad_pre_ref[rows, :] + near.take(t)
        unit = unit_ref[rows, :]
        inner = norm_back(grad, unit, scale_ref[rows, :], vec_ref[0:1, :])
        add_sums(vec_sums_ref, inner, grad, unit)
        grad_out_ref[rows, :] = inner
        return carry

    lax.fori_loop(0, queries // ROWS, take_near, 0)


def held(*dims, dtype=F32):
    return pltpu.VMEM(dims, dtype)


def streams(array):
    rows, width = array.shape
    return rows % 16 == 0 and width % TILE == 0 and rows * width * array.dtype.itemsize >= 1 << 18


def call(name, ident, body, inputs, outputs, scratch, mib=56):
    ins = [i for i, array in enumerate(inputs) if streams(array)]
    outs = [i for i, array in enumerate(outputs) if streams(array)]
    count_in, count_out = len(inputs), len(outputs)

    def kernel(*refs):
        in_refs, out_refs, rest = refs[:count_in], refs[count_in:count_in + count_out], refs[count_in + count_out:]
        near_in, near_out = list(in_refs), list(out_refs)
        for place, ref in zip(ins, rest[:len(ins)]):
            near_in[place] = ref
        rest = rest[len(ins):]
        for place, ref in zip(outs, rest[:len(outs)]):
            near_out[place] = ref
        rest = rest[len(outs):]
        in_sem, out_sem, rest = rest[0], rest[1], rest[2:]

        def load(place):
            return pltpu.make_async_copy(in_refs[place], near_in[place], in_sem.at[place])

        def store(place):
            return pltpu.make_async_copy(near_out[place], out_refs[place], out_sem.at[place])

        def need(*places):
            for place in places:
                if place in ins:
                    load(place).wait()

        def done(*places):
            for place in places:
                if place in outs:
                    store(place).start()

        for place in ins:
            load(place).start()
        body(need, done, *near_in, *near_out, *rest)
        for place in outs:
            store(place).wait()

    return pl.pallas_call(
        kernel,
        out_shape=outputs,
        in_specs=[ANY if i in ins else VM for i in range(count_in)],
        out_specs=[ANY if i in outs else VM for i in range(count_out)],
        scratch_shapes=[pltpu.VMEM(inputs[i].shape, inputs[i].dtype) for i in ins]
        + [pltpu.VMEM(outputs[i].shape, outputs[i].dtype) for i in outs]
        + [pltpu.SemaphoreType.DMA((count_in,)), pltpu.SemaphoreType.DMA((count_out,))]
        + scratch,
        compiler_params=params(ident, mib),
        name=name,
    )(*inputs)


class Trade:
    def __init__(self, count, into, send_sem, recv_sem, give_sem, take_sem):
        self.count, self.into = count, into
        self.send_sem, self.recv_sem, self.give_sem, self.take_sem = send_sem, recv_sem, give_sem, take_sem
        self.me, self.core = lax.axis_index("dp"), lax.axis_index("tensor")
        self.rows, self.half = into.shape[0] // count, into.shape[1] // 2

    @staticmethod
    def scratch(count):
        return [pltpu.SemaphoreType.DMA((count,))] * 4

    def greet(self):
        barrier = pltpu.get_barrier_semaphore()

        def signal(k, carry):
            other = {"dp": lax.rem(self.me + k, self.count)}
            pl.semaphore_signal(barrier, inc=1, device_id=other, device_id_type=MESH)
            return carry

        lax.fori_loop(1, self.count, signal, 0)
        pl.semaphore_signal(barrier, inc=1, device_id={"tensor": 1 - self.core}, device_id_type=MESH)
        pl.semaphore_wait(barrier, self.count)

    def rows_of(self, device):
        return pl.ds(pl.multiple_of(device * self.rows, self.rows), self.rows)

    def mine(self):
        return pl.ds(pl.multiple_of(self.core * self.half, self.half), self.half)

    def lanes_of(self, source):
        return self.mine() if source.shape[1] == self.into.shape[1] else slice(None)

    def send(self, source, k):
        other = lax.rem(self.me + k, self.count)
        return pltpu.make_async_remote_copy(
            src_ref=source.at[self.rows_of(other), self.lanes_of(source)],
            dst_ref=self.into.at[self.rows_of(self.me), self.mine()],
            send_sem=self.send_sem.at[k],
            recv_sem=self.recv_sem.at[k],
            device_id={"dp": other},
            device_id_type=MESH,
        )

    def pass_on(self, k):
        part = self.into.at[self.rows_of(lax.rem(self.me - k + self.count, self.count)), self.mine()]
        return pltpu.make_async_remote_copy(
            src_ref=part,
            dst_ref=part,
            send_sem=self.give_sem.at[k],
            recv_sem=self.take_sem.at[k],
            device_id={"tensor": 1 - self.core},
            device_id_type=MESH,
        )

    def start(self, source):
        def go(k, carry):
            self.send(source, k).start()
            return carry

        lax.fori_loop(1, self.count, go, 0)
        self.into[self.rows_of(self.me), self.mine()] = source[self.rows_of(self.me), self.lanes_of(source)]
        self.pass_on(0).start()

    def finish(self, source):
        def meet(k, carry):
            self.send(source, k).wait_recv()
            self.pass_on(k).start()
            return carry

        lax.fori_loop(1, self.count, meet, 0)

        def end(k, carry):
            self.pass_on(k).wait()
            return carry

        lax.fori_loop(0, self.count, end, 0)

        def sent(k, carry):
            self.send(source, k).wait_send()
            return carry

        lax.fori_loop(1, self.count, sent, 0)


def encoder_and_fetch(
    ident, x, attended, out_weight, up, down, shared, split, kept, wanted, target, dec_wide, dec_out_weight, count
):
    length, width = x.shape
    half, hidden_half = out_weight.shape[0], up.shape[1]
    tiles, target_length = length // ROWS, target.shape[0]
    span = min(target_length, 512)
    fetched_rows = wanted.shape[0]
    places = bias_places(half, hidden_half)

    def body(
        need, done, x_ref, attended_ref, out_weight_ref, up_ref, down_ref, shared_ref, split_ref, wanted_ref,
        target_ref, dec_wide_ref, dec_out_weight_ref, *refs,
    ):
        saved, fed, dec_saved, fetched_ref, rest = refs[:2], refs[2:9], refs[9:14], refs[14], refs[15:]
        served_ref, trade_sems, rest = rest[0], rest[1:5], rest[5:]
        score_ref, turned_ref, rest = rest[0], rest[1], rest[2:]
        trade = Trade(count, fetched_ref, *trade_sems)
        stored_ref = fed[1]
        need(0, 1, 2)
        trade.greet()
        close_branch(x_ref, attended_ref, out_weight_ref, Rows(shared_ref, (0,)), *saved, *rest[:4])
        done(0, 1)
        need(3, 4, 5, 6, 7)

        def serve(t, carry):
            want = wanted_ref[rows_of(t), :]
            match = want == lax.broadcasted_iota(jnp.int32, (ROWS, kept), 1)
            pick = jnp.where(match, 1.0, 0.0).astype(BF16)
            served_ref[rows_of(t), :] = times(pick, stored_ref[:, trade.mine()]).astype(BF16)
            return carry

        def between():
            lax.fori_loop(0, fetched_rows // ROWS, serve, 0)
            trade.start(served_ref)
            done(3, 4, 5, 6, 7, 8)

        feed_forward_kernel(
            kept, between, saved[0], up_ref, down_ref, split_ref.at[:, places["enc_up"]],
            Rows(shared_ref, (1, 2, 3, 4, 5)), *fed, *rest[4:8],
        )
        done(2)
        need(8, 9, 10)
        self_forward_kernel(
            True, span, target_ref, dec_wide_ref, dec_out_weight_ref,
            bias_row(split_ref, places, ("dec_q", None, "dec_v"), half), Rows(shared_ref, (6,)),
            *dec_saved, score_ref, turned_ref, *rest[8:],
        )
        done(9, 10, 11, 12, 13)
        trade.finish(served_ref)
        done(14)

    return call(
        "encoder_and_fetch", ident, body,
        [x, attended, out_weight, up, down, shared, split, wanted, target, dec_wide, dec_out_weight],
        [
            shape(length, width), shape(length, 1),
            shape(length, width), shape(kept, width, dtype=BF16), shape(kept, width, dtype=BF16),
            shape(kept, hidden_half, dtype=BF16), shape(kept, hidden_half, dtype=BF16),
            shape(kept, width), shape(kept, 1),
            shape(target_length, 3 * half, dtype=BF16), shape(target_length, half, dtype=BF16), shape(8, target_length),
            shape(target_length, width), shape(target_length, 1), shape(fetched_rows, width, dtype=BF16),
        ],
        [held(fetched_rows, width // 2, dtype=BF16)] + Trade.scratch(count)
        + [held(2, target_length, span), held(half, target_length, dtype=BF16)]
        + Swap.scratch(tiles, width) * 2 + Swap.scratch(target_length // ROWS, width),
    )


def decoder_core(
    ident, unit, scale, fetched, cotangent, query_weight, wide, out_weight, up, down, shared, split,
    mixed, attended, totals, self_wide, self_out_weight, count,
):
    length, width = unit.shape
    keys = fetched.shape[0]
    half, hidden_half = out_weight.shape[0], up.shape[1]
    tiles, span = length // ROWS, min(length, 512)
    places = bias_places(half, hidden_half)

    def body(
        need, done, unit_ref, scale_ref, fetched_ref, cotangent_ref, query_weight_ref, wide_ref, out_weight_ref,
        up_ref, down_ref, shared_ref, split_ref,
        self_mixed_ref, self_attended_ref, self_totals_ref, self_wide_ref, self_out_weight_ref,
        states_ref, low_ref, attended_ref, second_low_ref, active_ref,
        feed_low_ref, grad_up_ref, up_bias_ref, sums_after_ref, sums_before_ref,
        cross_low_ref, grad_query_ref, grad_pair_ref, landed_ref, cross_sums_ref, vec_sums_ref,
        self_low_ref, self_query_ref, self_pair_ref, grad_x_ref, self_sums_ref,
        query_ref, mixed_ref, totals_ref, unit_four_ref, scale_four_ref, slope_ref,
        unit_five_ref, scale_five_ref, grad_four_ref, inner_ref, score_ref, turned_ref, grad_ref, returned_ref, grad_out_ref,
        send_sem, recv_sem, give_sem, take_sem, *swaps,
    ):
        need(0, 1, 2, 4, 5, 6, 9, 10)
        trade = Trade(count, landed_ref, send_sem, recv_sem, give_sem, take_sem)
        trade.greet()
        cross_forward_kernel(
            span, unit_ref, fetched_ref, query_weight_ref, wide_ref, out_weight_ref,
            split_ref.at[:, places["crs_q"]], bias_row(split_ref, places, (None, "crs_v"), half),
            Rows(shared_ref, (7, 8, 9)),
            low_ref, query_ref, mixed_ref, attended_ref, totals_ref, unit_four_ref, scale_four_ref,
            score_ref, turned_ref, *swaps[:4],
        )
        done(1, 2)
        need(7, 8)
        feed_forward_kernel(
            length, lambda: None, unit_four_ref, up_ref, down_ref, split_ref.at[:, places["dec_up"]],
            Rows(shared_ref, (10, 11, 12, 13, 14)),
            states_ref, cross_low_ref, second_low_ref, active_ref, slope_ref, unit_five_ref, scale_five_ref,
            *swaps[4:8],
        )
        done(0, 3, 4)
        need(3)
        feed_backward_kernel(
            cotangent_ref, unit_five_ref, scale_five_ref, active_ref, slope_ref, up_ref, down_ref,
            unit_four_ref, scale_four_ref, Rows(shared_ref, (13, 10)),
            feed_low_ref, grad_up_ref, up_bias_ref, grad_four_ref, sums_after_ref, sums_before_ref,
            inner_ref, *swaps[8:12],
        )
        done(5, 6, 7, 8, 9)
        cross_backward_kernel(
            lambda: trade.start(returned_ref), grad_four_ref, query_ref, mixed_ref, attended_ref, totals_ref, query_weight_ref, wide_ref,
            out_weight_ref, unit_ref, scale_ref, Rows(shared_ref, (7,)),
            cross_low_ref, grad_query_ref, grad_pair_ref, returned_ref, grad_out_ref, cross_sums_ref, vec_sums_ref,
            grad_ref, turned_ref, *swaps[12:20],
        )
        done(10, 11, 12, 14, 15)
        need(11, 12, 13, 14, 15)
        self_backward_kernel(
            True, grad_out_ref, self_mixed_ref, self_attended_ref, self_totals_ref, self_wide_ref, self_out_weight_ref,
            self_low_ref, self_query_ref, self_pair_ref, grad_x_ref, self_sums_ref,
            grad_ref, turned_ref.at[:, :length], *swaps[20:],
        )
        done(16, 17, 18, 19, 20)
        trade.finish(returned_ref)
        done(13)

    return call(
        "decoder_core", ident, body,
        [
            unit, scale, fetched, cotangent, query_weight, wide, out_weight, up, down, shared, split,
            mixed, attended, totals, self_wide, self_out_weight,
        ],
        [
            shape(length, width), shape(length, width, dtype=BF16), shape(length, half, dtype=BF16),
            shape(length, width, dtype=BF16), shape(length, hidden_half, dtype=BF16),
            shape(length, width, dtype=BF16), shape(length, hidden_half, dtype=BF16), shape(1, hidden_half),
            shape(8, width), shape(8, width),
            shape(length, width, dtype=BF16), shape(length, half, dtype=BF16), shape(keys, 2 * half, dtype=BF16),
            shape(keys, width, dtype=BF16), shape(1, 3 * half), shape(8, width),
            shape(length, width, dtype=BF16), shape(length, half, dtype=BF16), shape(length, 2 * half, dtype=BF16),
            shape(length, width), shape(1, 3 * half),
        ],
        [
            held(length, half, dtype=BF16), held(keys, 2 * half, dtype=BF16), held(8, length),
            held(length, width), held(length, 1),
            held(length, hidden_half, dtype=BF16), held(length, width), held(length, 1),
            held(length, width), held(length, width), held(2, keys, span), held(half, keys, dtype=BF16),
            held(length, half, dtype=BF16), held(keys, width, dtype=BF16), held(length, width),
        ]
        + Trade.scratch(count)
        + Swap.scratch(tiles, width) * 4 + Swap.scratch(keys // ROWS, width) + Swap.scratch(tiles, width),
        60,
    )


def encoder_backward(
    ident, returned, wanted, unit_two, scale_two, active, slope, up, down, unit_one, scale_one,
    mixed, attended, totals, wide, out_weight, shared,
):
    queries, width = unit_two.shape
    length, half, hidden_half = mixed.shape[0], out_weight.shape[0], up.shape[1]

    def body(
        need, done, returned_ref, wanted_ref, unit_two_ref, scale_two_ref, active_ref, slope_ref, up_ref, down_ref, unit_one_ref, scale_one_ref,
        mixed_ref, attended_ref, totals_ref, wide_ref, out_weight_ref, shared_ref,
        feed_low_ref, grad_up_ref, up_bias_ref, sums_after_ref, sums_before_ref,
        low_ref, grad_query_ref, grad_pair_ref, grad_x_ref, sums_ref,
        grad_ref, grad_one_ref, inner_ref, grad_out_ref, turned_ref, *swaps,
    ):
        need(0, 1)

        def collect(t, carry):
            place = t * ROWS + lax.broadcasted_iota(jnp.int32, (ROWS, returned_ref.shape[0]), 0)
            match = jnp.where(wanted_ref[...] == place, 1.0, 0.0).astype(BF16)
            grad_ref[rows_of(t), :] = times(match, returned_ref[...])
            return carry

        lax.fori_loop(0, queries // ROWS, collect, 0)
        need(*range(2, 10), 15)
        Swap.greet()
        feed_backward_kernel(
            grad_ref, unit_two_ref, scale_two_ref, active_ref, slope_ref, up_ref, down_ref,
            unit_one_ref, scale_one_ref, Rows(shared_ref, (4, 1)),
            feed_low_ref, grad_up_ref, up_bias_ref, grad_one_ref, sums_after_ref, sums_before_ref,
            inner_ref, *swaps[:4],
        )
        done(0, 1, 2, 3, 4)
        need(10, 11, 12, 13, 14)
        self_backward_kernel(
            False, grad_one_ref, mixed_ref, attended_ref, totals_ref, wide_ref, out_weight_ref,
            low_ref, grad_query_ref, grad_pair_ref, grad_x_ref, sums_ref, grad_out_ref, turned_ref, *swaps[4:],
        )
        done(*range(5, 10))

    return call(
        "encoder_backward", ident, body,
        [
            returned, wanted, unit_two, scale_two, active, slope, up, down, unit_one, scale_one,
            mixed, attended, totals, wide, out_weight, shared,
        ],
        [
            shape(queries, width, dtype=BF16), shape(queries, hidden_half, dtype=BF16), shape(1, hidden_half),
            shape(8, width), shape(8, width),
            shape(queries, width, dtype=BF16), shape(queries, half, dtype=BF16), shape(length, 2 * half, dtype=BF16),
            shape(length, width), shape(1, 3 * half),
        ],
        [
            held(queries, width), held(queries, width), held(queries, width), held(queries, half, dtype=BF16),
            held(half, length, dtype=BF16),
        ]
        + Swap.scratch(queries // ROWS, width) + Swap.scratch(length // ROWS, width),
    )


def adam_vector(grad_value, value, first, second):
    new_first = BETA_ONE * first + (1.0 - BETA_ONE) * grad_value
    new_second = BETA_TWO * second + (1.0 - BETA_TWO) * grad_value * grad_value
    correct_one = 1.0 - BETA_ONE**STEP
    correct_two = 1.0 - BETA_TWO**STEP
    updated = value - VECTOR_RATE * (new_first / correct_one) / (
        jnp.sqrt(new_second / correct_two) + ADAM_EPSILON
    )
    return (new_first, new_second, updated)


def local(
    source_tokens,
    target_tokens,
    target_cotangent,
    retrieved,
    kept_mask,
    owner_slots,
    master,
    first_moment,
    second_moment,
    left_stats,
    right_stats,
    left_basis,
    right_basis,
    shared_vectors,
    shared_first,
    shared_second,
    split_vectors,
    split_first,
    split_second,
):
    tensor_count = lax.axis_size("tensor")
    device_count = lax.axis_size("dp")
    model_width = source_tokens.shape[1]
    tile_size = master.shape[2]
    hidden_width = (split_vectors.shape[1] - 3) * model_width
    half_width = model_width // tensor_count
    hidden_half = hidden_width // tensor_count
    qblocks = retrieved.shape[0]
    per_owner = retrieved.shape[1] // device_count
    me = lax.axis_index("dp")
    vectors = jnp.concatenate([shared_vectors, split_vectors[0]], 0)
    vector_count, vector_width = vectors.shape
    padded = -(-vector_count // 8) * 8
    small = jnp.concatenate(
        [
            jnp.pad(vectors, ((0, padded - vector_count), (0, TILE - vector_width))),
            retrieved.astype(jnp.float32).reshape(-1, TILE),
        ],
        0,
    )
    gathered, smalls = gather_all(master[0], small, device_count)
    whole = (
        smalls[:, :vector_count, :vector_width]
        .transpose(1, 0, 2)
        .reshape(vector_count, model_width)
        .astype(jnp.bfloat16)
    )
    shared_count = shared_vectors.shape[0]
    shared_whole, split_whole = whole[:shared_count], whole[shared_count:]
    shapes = [s[1:] for s in matrix_list(model_width, hidden_width, tensor_count)]
    names = [s[0] for s in matrix_list(model_width, hidden_width, tensor_count)]
    shared = jnp.pad(shared_whole.astype(F32), ((0, 16 - shared_count), (0, 0)))
    split = split_whole.astype(F32).reshape(1, -1)
    start_row = jnp.argmax(kept_mask)
    turned = jnp.roll(source_tokens, -start_row, 0)


    wanted = (
        smalls[:, padded:].reshape(device_count, qblocks, device_count, per_owner)[:, :, me]
        .transpose(1, 0, 2)
        .astype(jnp.int32)
        - KEEP * me
    ).reshape(1, -1)
    matrices, (enc_mixed, enc_attended, enc_totals) = unpack_and_attend(
        gathered, owner_slots, shapes, turned, split, bias_places(half_width, hidden_half), half_width
    )
    weights = dict(zip(names, matrices))
    (unit_one, scale_one,
     states, _, hidden_low, enc_active, enc_slope, unit_two, scale_two,
     dec_mixed, dec_attended, dec_totals, unit_three, scale_three, fetched) = encoder_and_fetch(
        10, turned, enc_attended, weights["enc_out"], weights["enc_up"], weights["enc_down"],
        shared, split, KEEP, wanted.reshape(-1, 1), target_tokens, weights["dec_qkv"], weights["dec_out"], device_count,
    )
    encoder_states = jnp.roll(states, start_row, 0)
    (decoder_states, first_low, crs_attended, second_low, dec_active,
     dec_feed_low, dec_grad_up, dec_up_bias, sums_five, sums_four,
     crs_low, crs_grad_query, crs_grad_pair, returned, crs_sums, sums_three,
     dec_low, dec_grad_query, dec_grad_pair, target_grad, dec_sums) = decoder_core(
        13, unit_three, scale_three, fetched, target_cotangent,
        weights["crs_q"], weights["crs_kv"], weights["crs_out"], weights["dec_up"], weights["dec_down"],
        shared, split, dec_mixed, dec_attended, dec_totals, weights["dec_qkv"], weights["dec_out"], device_count,
    )
    (enc_feed_low, enc_grad_up, enc_up_bias, sums_two, sums_one,
     enc_low, enc_grad_query, enc_grad_pair, grad_turned, enc_sums) = encoder_backward(
        18, returned, wanted, unit_two, scale_two, enc_active, enc_slope, weights["enc_up"], weights["enc_down"],
        unit_one, scale_one, enc_mixed, enc_attended, enc_totals, weights["enc_qkv"], weights["enc_out"], shared,
    )
    source_grad = jnp.roll(grad_turned, start_row, 0)

    first_block, total_blocks = {}, 0
    for name, height, breadth in matrix_list(model_width, hidden_width, tensor_count):
        first_block[name] = total_blocks
        total_blocks += height // TILE * (breadth // TILE)
    three = 3 * half_width
    outer = ((0, half_width), (2 * half_width, three))
    everything = ((0, hidden_half),)
    items = [
        (sums, 3 * i, None) for i, sums in enumerate((sums_one, sums_two, sums_three, sums_four, sums_five))
    ]
    at = shared_count * model_width
    for array, pieces in (
        (enc_sums, outer), (enc_up_bias, everything), (dec_sums, outer), (crs_sums, outer), (dec_up_bias, everything)
    ):
        items.append((array, at, pieces))
        at += sum(end - begin for begin, end in pieces)
    (slot_grads,) = weight_grads(
        [
            (first_block["dec_down"], [(dec_active, dec_feed_low)]),
            (first_block["dec_up"], [(second_low, dec_grad_up)]),
            (first_block["crs_out"], [(crs_attended, crs_low)]),
            (first_block["crs_q"], [(first_low, crs_grad_query)]),
            (first_block["crs_kv"], [(fetched, crs_grad_pair)]),
            (first_block["dec_out"], [(dec_attended, dec_low)]),
            (first_block["dec_qkv"], [(target_tokens, dec_grad_query), (target_tokens, dec_grad_pair)]),
        ],
        owner_slots,
        gathered.shape[0],
    )
    slot_grads, vector_grads = weight_grads(
        [
            (first_block["enc_down"], [(enc_active, enc_feed_low)]),
            (first_block["enc_up"], [(hidden_low, enc_grad_up)]),
            (first_block["enc_out"], [(enc_attended, enc_low)]),
            (first_block["enc_qkv"], [(turned, enc_grad_query), (turned, enc_grad_pair)]),
        ],
        owner_slots,
        gathered.shape[0],
        slot_grads,
        (padded, model_width, items),
    )
    slots = master.shape[1]
    owned_slots = me * slots + lax.broadcasted_iota(jnp.int32, (slots, 1), 0)
    used = jnp.any(owned_slots == owner_slots[None, :], 1).astype(jnp.int32)
    results, vector_sums = owner_update(
        used,
        slot_grads,
        vector_grads,
        [
            array[0]
            for array in (
                master, first_moment, second_moment, left_stats, right_stats, left_basis, right_basis
            )
        ],
        device_count,
    )
    vector_owned = lax.dynamic_slice_in_dim(vector_sums, me * vector_width, vector_width, 1)
    shared_owned = vector_owned[:shared_count]
    split_owned = vector_owned[shared_count:vector_count]
    new_master, new_first, new_second, new_left, new_right, new_lbasis, new_rbasis = results
    shared_new_first, shared_new_second, shared_updated = adam_vector(
        shared_owned, shared_vectors, shared_first, shared_second
    )
    split_new_first, split_new_second, split_updated = adam_vector(
        split_owned, split_vectors[0], split_first[0], split_second[0]
    )
    return (
        encoder_states,
        decoder_states,
        source_grad,
        target_grad,
        new_master[None],
        new_first[None],
        new_second[None],
        new_left[None],
        new_right[None],
        new_lbasis[None],
        new_rbasis[None],
        shared_new_first,
        shared_new_second,
        shared_updated,
        split_new_first[None],
        split_new_second[None],
        split_updated[None],
    )


def solution(mesh):
    placed = (
        P("dp", None),
        P("dp", None),
        P("dp", None),
        P("dp", None),
        P("dp"),
        P(),
        P("tensor", "dp", None, None),
        P("tensor", "dp", None, None),
        P("tensor", "dp", None, None),
        P("tensor", "dp", None, None),
        P("tensor", "dp", None, None),
        P("tensor", "dp", None, None),
        P("tensor", "dp", None, None),
        P(None, "dp"),
        P(None, "dp"),
        P(None, "dp"),
        P("tensor", None, "dp"),
        P("tensor", None, "dp"),
        P("tensor", None, "dp"),
    )
    return jax.shard_map(
        local,
        mesh=mesh,
        in_specs=placed,
        out_specs=(
            P("dp", None),
            P("dp", None),
            P("dp", None),
            P("dp", None),
            P("tensor", "dp", None, None),
            P("tensor", "dp", None, None),
            P("tensor", "dp", None, None),
            P("tensor", "dp", None, None),
            P("tensor", "dp", None, None),
            P("tensor", "dp", None, None),
            P("tensor", "dp", None, None),
            P(None, "dp"),
            P(None, "dp"),
            P(None, "dp"),
            P("tensor", None, "dp"),
            P("tensor", None, "dp"),
            P("tensor", None, "dp"),
        ),
        check_vma=False,
    )
```

```python
import functools
from functools import partial

import jax
import jax.numpy as jnp
from jax import lax
from jax.experimental import pallas as pl
from jax.experimental.pallas import tpu as pltpu
from jax.sharding import PartitionSpec as P

HD = 64
KEEP = 512
STEP = 10


BETA_ONE = 0.9
BETA_TWO = 0.95
ADAM_EPSILON = 1e-08
MATRIX_RATE = 0.1
VECTOR_RATE = 0.5
WEIGHT_DECAY = 0.01
NORM_EPSILON = 1e-05
TILE = 128
PANEL = 32
ROWS = 256
KEYS = 256
PAIR = 2 * HD
NN = ((1,), (0,))
NT = ((1,), (1,))
F32 = jnp.float32
BF16 = jnp.bfloat16
MESH = pl.DeviceIdType.MESH
ANY = pl.BlockSpec(memory_space=pl.ANY)


def matrix_list(model_width, hidden_width, tensor_count):
    half_width = model_width // tensor_count
    hidden_half = hidden_width // tensor_count
    return [
        ("enc_qkv", model_width, 3 * half_width),
        ("enc_out", half_width, model_width),
        ("enc_up", model_width, hidden_half),
        ("enc_down", hidden_half, model_width),
        ("dec_qkv", model_width, 3 * half_width),
        ("dec_out", half_width, model_width),
        ("crs_q", model_width, half_width),
        ("crs_kv", model_width, 2 * half_width),
        ("crs_out", half_width, model_width),
        ("dec_up", model_width, hidden_half),
        ("dec_down", hidden_half, model_width),
    ]


def halves(x):
    high = x.astype(BF16)
    return high, (x - high.astype(F32)).astype(BF16)


def mm(a, b, dims=NN):
    ah, al = halves(a)
    bh, bl = halves(b)
    return times(jnp.concatenate([ah, ah, al], 1), jnp.concatenate([bh, bl, bh], dims[1][0]), dims)


def chip_grid(device_count):
    if device_count == 16:
        return 4, 2, 2
    side = round(device_count ** (1 / 3))
    if side**3 == device_count:
        return side, side, side
    return 1, 1, device_count


def place(grid):
    zs, ys, xs = grid
    me = lax.axis_index("dp")
    return me // (ys * xs), lax.rem(me // xs, ys), lax.rem(me, xs)


def peers(grid):
    zs, ys, xs = grid
    z, y, x = place(grid)

    def device(zz, yy, xx):
        return {"dp": (zz * ys + yy) * xs + xx}

    return (
        lambda k: device(lax.rem(z + k, zs), y, x),
        lambda k: device(z, lax.rem(y + k, ys), x),
        lambda k: device(z, y, lax.rem(x + k, xs)),
    )


def greet(grid):
    barrier = pltpu.get_barrier_semaphore()
    count = 0
    for size, peer in zip(grid, peers(grid)):
        for k in range(1, size):
            pl.semaphore_signal(barrier, inc=1, device_id=peer(k), device_id_type=MESH)
            count += 1
    pl.semaphore_wait(barrier, count)


def remote(src, dst, send, recv, device):
    return pltpu.make_async_remote_copy(
        src_ref=src, dst_ref=dst, send_sem=send, recv_sem=recv, device_id=device, device_id_type=MESH
    )


def chunking(slots):
    half = slots // 2
    chunks = min(16, half)
    return half, chunks, half // chunks


def owner_kernel(grid, *refs):
    zs, ys, xs = grid
    used_ref, in_ref, small_ref = refs[:3]
    state_in, state_out, small_out_ref, work_out_ref = refs[3:10], refs[10:17], refs[17], refs[18]
    state, rest = refs[19:26], refs[26:]
    (own0, own1, ra0, ra1, rb0, rb1, rc0, rc1, total, rs_z, rs_y, rs_x, work, load_sem,
     as0, as1, ar0, ar1, bs0, bs1, br0, br1, cs0, cs1, cr0, cr1,
     ssz, ssy, ssx, srz, sry, srx, state_sem) = rest
    own, rec_a, rec_b, rec_c = (own0, own1), (ra0, ra1), (rb0, rb1), (rc0, rc1)
    a_send, a_recv, b_send, b_recv, c_send, c_recv = (as0, as1), (ar0, ar1), (bs0, bs1), (br0, br1), (cs0, cs1), (cr0, cr1)
    rec_s, s_send, s_recv = (rs_z, rs_y, rs_x), (ssz, ssy, ssx), (srz, sry, srx)

    z, y, x = place(grid)
    tos = peers(grid)
    to_z, to_y, to_x = tos
    slots = state[0].shape[0]
    half = slots // 2
    first = ((xs, x, to_x), (ys, y, to_y))
    second = ((ys, y, to_y), (xs, x, to_x))

    def source(g, c, other):
        slot = g * half + c
        return in_ref.at[:, :, other, slot] if g == 0 else in_ref.at[:, other, :, slot]

    def load(g, c):
        return pltpu.make_async_copy(source(g, c, first[g][1]), own[g].at[c], load_sem.at[g, c])

    def send_a(g, c, k):
        count, mine, to = first[g]
        return remote(source(g, c, lax.rem(mine + k, count)), rec_a[g].at[c, k - 1],
                      a_send[g].at[c, k - 1], a_recv[g].at[c, k - 1], to(k))

    def send_b(g, c, k):
        count, mine, to = second[g]
        return remote(own[g].at[c, :, lax.rem(mine + k, count)], rec_b[g].at[c, k - 1],
                      b_send[g].at[c, k - 1], b_recv[g].at[c, k - 1], to(k))

    def send_c(g, c, k):
        return remote(own[g].at[c, lax.rem(z + k, zs), second[g][1]], rec_c[g].at[c, k - 1],
                      c_send[g].at[c, k - 1], c_recv[g].at[c, k - 1], to_z(k))

    def start_a(c):
        for g in range(2):
            for k in range(1, first[g][0]):
                send_a(g, c, k).start()

    def send_s(axis, k):
        return remote(total.at[2 - axis], rec_s[axis].at[k - 1],
                      s_send[axis].at[k - 1], s_recv[axis].at[k - 1], tos[axis](k))

    def small_start(axis):
        for k in range(1, grid[axis]):
            send_s(axis, k).start()

    def small_add(axis):
        value = total[2 - axis]
        for k in range(1, grid[axis]):
            send_s(axis, k).wait_recv()
            value += rec_s[axis][k - 1]
        return value

    def each(count, action):
        def go(c, carry):
            action(c)
            return carry

        lax.fori_loop(0, count, go, 0)

    def load_all(c):
        for g in range(2):
            load(g, c).start()

    each(half, load_all)
    for i in range(7):
        pltpu.make_async_copy(state_in[i], state[i], state_sem.at[0, i]).start()
    total[0] = small_ref[...]
    greet(grid)
    small_start(2)
    start_a(0)
    total[1] = small_add(2)
    small_start(1)
    total[2] = small_add(1)
    small_start(0)
    for i in range(7):
        pltpu.make_async_copy(state_in[i], state[i], state_sem.at[0, i]).wait()

    def step_a(c):
        for g in range(2):
            load(g, c).wait()
            for k in range(1, first[g][0]):
                send_a(g, c, k).wait_recv()

        @pl.when(c + 1 < half)
        def _():
            start_a(c + 1)

        for g in range(2):
            n2 = second[g][0]

            def add(e, carry, g=g, n2=n2):
                a, b = e // n2, lax.rem(e, n2)
                value = own[g][c, a, b].astype(F32)
                for k in range(1, first[g][0]):
                    value += rec_a[g][c, k - 1, a, b].astype(F32)
                own[g][c, a, b] = value.astype(BF16)
                return carry

            lax.fori_loop(0, zs * n2, add, 0)
            for k in range(1, n2):
                send_b(g, c, k).start()

    def step_b(c):
        for g in range(2):
            n2, mine = second[g][0], second[g][1]
            for k in range(1, n2):
                send_b(g, c, k).wait_recv()

            def add(a, carry, g=g, n2=n2, mine=mine):
                value = own[g][c, a, mine].astype(F32)
                for k in range(1, n2):
                    value += rec_b[g][c, k - 1, a].astype(F32)
                own[g][c, a, mine] = value.astype(BF16)
                return carry

            lax.fori_loop(0, zs, add, 0)
            for k in range(1, zs):
                send_c(g, c, k).start()

    def step_c(c):
        batch = lax.rem(c // 4, 2)
        for g in range(2):
            for k in range(1, zs):
                send_c(g, c, k).wait_recv()
        for g in range(2):
            value = own[g][c, z, second[g][1]].astype(F32)
            for k in range(1, zs):
                value += rec_c[g][c, k - 1].astype(F32)
            slot = g * half + c
            value = jnp.where(used_ref[slot] > 0, value, 0.0)
            soap_products(value, slot, state, work, batch, 2 * (4 * g + lax.rem(c, 4)))

    def finish(b):
        batch = lax.rem(b, 2)
        place_bases(work, batch, state[5], state[6], 4 * b)
        emit(b)

    def emit(b):
        for g in range(2):
            span = pl.ds(g * half + 4 * b, 4)
            for i in range(7):
                pltpu.make_async_copy(state[i].at[span], state_out[i].at[span], state_sem.at[1, i]).start()

    def round_of(r, carry):
        for s in range(4):
            t = 4 * r + s

            @pl.when(t < half)
            def _(t=t):
                step_a(t)

            @pl.when((t >= 1) & (t <= half))
            def _(t=t):
                step_b(t - 1)

            @pl.when((t >= 2) & (t < half + 2))
            def _(t=t):
                step_c(t - 2)

            if s >= 1:

                @pl.when((r >= 1) & (r < half // 4))
                def _(s=s):
                    panel_step(work, lax.rem(r - 1, 2), s - 1)

            else:

                @pl.when((r >= 2) & (r <= half // 4))
                def _():
                    panel_step(work, lax.rem(r - 2, 2), TILE // PANEL - 1)
                    finish(r - 2)

        return carry

    lax.fori_loop(0, half // 4 + 1, round_of, 0)
    emit(half // 4 - 1)
    work_out_ref[...] = work[(half // 4 - 1) % 2]
    small_out_ref[...] = small_add(0)
    for axis in range(3):
        for k in range(1, grid[axis]):
            send_s(axis, k).wait_send()

    def end(c):
        for g in range(2):
            for k in range(1, first[g][0]):
                send_a(g, c, k).wait_send()
            for k in range(1, second[g][0]):
                send_b(g, c, k).wait_send()
            for k in range(1, zs):
                send_c(g, c, k).wait_send()

    each(half, end)
    for i in range(7):
        pltpu.make_async_copy(state[i], state_out[i], state_sem.at[1, i]).wait()


def place_bases(work, batch, left_ref, right_ref, at):
    half = left_ref.shape[0] // 2
    for g in range(2):
        for e in range(4):
            left_ref[g * half + at + e] = work[batch, 2 * (4 * g + e), :, TILE:].T
            right_ref[g * half + at + e] = work[batch, 2 * (4 * g + e) + 1, :, TILE:].T


def last_bases_kernel(work_ref, *refs):
    state_in, state_out, state, work, sems = refs[:7], refs[7:14], refs[14:21], refs[21], refs[22]
    half = state[0].shape[0] // 2

    def copy_in(i):
        return pltpu.make_async_copy(state_in[i], state[i], sems.at[0, i])

    def copy_out(i):
        return pltpu.make_async_copy(state[i], state_out[i], sems.at[1, i])

    for i in range(7):
        copy_in(i).start()
    work[0] = work_ref[...]
    panel_step(work, 0, 0)
    for i in range(7):
        copy_in(i).wait()
        if i < 5:
            copy_out(i).start()
    for p in range(1, TILE // PANEL):
        panel_step(work, 0, p)
    place_bases(work, 0, state[5], state[6], half - 4)
    for i in range(5, 7):
        copy_out(i).start()
    for i in range(7):
        copy_out(i).wait()


def last_bases(work, state):
    whole = state[0].shape
    return pl.pallas_call(
        last_bases_kernel,
        out_shape=[jax.ShapeDtypeStruct(whole, F32)] * 7,
        in_specs=[pl.BlockSpec(memory_space=pltpu.VMEM)] + [ANY] * 7,
        out_specs=[ANY] * 7,
        scratch_shapes=[pltpu.VMEM(whole, F32)] * 7
        + [pltpu.VMEM((1,) + work.shape, F32), pltpu.SemaphoreType.DMA((2, 7))],
        compiler_params=pltpu.CompilerParams(vmem_limit_bytes=56 << 20),
        name="last_bases",
    )(work, *state)


def soap_products(g, i, state, work, batch, at):
    w_ref, m_ref, v_ref, l_ref, r_ref, ql_ref, qr_ref = state
    c1 = 1.0 - BETA_ONE**STEP
    c2 = 1.0 - BETA_TWO**STEP
    ql = ql_ref[i]
    qr = qr_ref[i]
    gt = g.T
    nm = BETA_ONE * m_ref[i] + (1.0 - BETA_ONE) * g
    m_ref[i] = nm
    side = mm(jnp.concatenate([g, nm], 0), qr)
    both = mm(ql.T, jnp.concatenate([side[:TILE], side[TILE:]], 1))
    rotated, rotated_first = both[:, :TILE], both[:, TILE:]
    nv = BETA_TWO * v_ref[i] + (1.0 - BETA_TWO) * rotated * rotated
    v_ref[i] = nv
    normed = rotated_first / c1 / (jnp.sqrt(nv / c2) + ADAM_EPSILON)
    step = mm(mm(ql, normed), qr, NT)
    w = w_ref[i]
    w_ref[i] = w - MATRIX_RATE * step - MATRIX_RATE * WEIGHT_DECAY * w
    for k, (ref, turn, left, right) in enumerate(((l_ref, ql, g, gt), (r_ref, qr, gt, g))):
        stat = BETA_TWO * ref[i] + (1.0 - BETA_TWO) * mm(left, right)
        ref[i] = stat
        a = mm(stat, turn)
        at_turned = a.T
        work[batch, at + k, :, :TILE] = mm(at_turned, a)
        work[batch, at + k, :, TILE:] = at_turned


def panel_step(work, batch, p):
    count = work.shape[1]
    per = TILE // (2 * PANEL)
    r0 = p * PANEL
    rows = count // per * 8
    lane = lax.broadcasted_iota(jnp.int32, (rows, TILE), 1)
    start = lane // (2 * PANEL) * (2 * PANEL)
    row = lax.rem(lax.broadcasted_iota(jnp.int32, (rows, TILE), 0), 8)
    sub = lax.broadcasted_iota(jnp.int32, (count // per, 8, TILE), 1)
    eye = (
        lax.broadcasted_iota(jnp.int32, (PANEL, PANEL), 0) == lax.broadcasted_iota(jnp.int32, (PANEL, PANEL), 1)
    ).astype(F32)
    packs = []
    for q in range(count // per):
        pieces = []
        for k in range(per):
            pieces += [work[batch, q * per + k, r0:r0 + PANEL, r0:r0 + PANEL], eye]
        packs.append(jnp.concatenate(pieces, 1)[None])
    x = jnp.concatenate(packs, 0)
    strips = [x[:, 8 * e:8 * e + 8, :] for e in range(PANEL // 8)]

    def segment(strip, index):
        return jnp.take_along_axis(strip.reshape(-1, TILE), index, axis=1).reshape(strip.shape)

    for j in range(0, PANEL, 2):
        e0, here = j // 8, j % 8
        one = [segment(strip, start + j) for strip in strips[e0:]]
        two = [segment(strip, start + j + 1) for strip in strips[e0:]]
        corner = one[0][:, here:here + 1, :]
        side = one[0][:, here + 1:here + 2, :]
        inverse = 1.0 / corner
        inverse_two = corner * (1.0 / (corner * two[0][:, here + 1:here + 2, :] - side * side))
        shift = side * inverse
        ratio = strips[e0][:, here:here + 1, :] * inverse
        next_off = side * ratio
        ratio_two = (strips[e0][:, here + 1:here + 2, :] - next_off) * inverse_two
        ratio_one = ratio - shift * ratio_two
        for e in range(e0, PANEL // 8):
            change = one[e - e0] * ratio_one + two[e - e0] * ratio_two
            if e == e0:
                change = jnp.where(sub > here + 1, change, jnp.where(sub == here + 1, next_off, 0.0))
            strips[e] = strips[e] - change
    for e in range(PANEL // 8):
        strips[e] = strips[e] * lax.rsqrt(segment(strips[e], start + 8 * e + row))
    x = jnp.concatenate(strips, 1)
    for q in range(count // per):
        for k in range(per):
            i = q * per + k
            inverse = x[q, :, 2 * PANEL * k + PANEL:2 * PANEL * (k + 1)]
            u = mm(inverse, work[batch, i, r0:r0 + PANEL, :])
            work[batch, i, r0:r0 + PANEL, TILE:] = u[:, TILE:]
            if r0 + PANEL < TILE:
                high, low = halves(u)
                left = jnp.concatenate([u[:, :TILE], u[:, :TILE], low[:, :TILE].astype(F32)], 0).T
                work[batch, i, r0 + PANEL:, :] -= times(
                    left[r0 + PANEL:, :].astype(BF16), jnp.concatenate([high, low, high], 0)
                )


def some(shape):
    return tuple(max(1, s) for s in shape)


def owner_update(used, slot_grads, small, state, device_count):
    grid = chip_grid(device_count)
    zs, ys, xs = grid
    slots = slot_grads.shape[0] // device_count
    half = slots // 2
    block = (TILE, TILE)
    dma = pltpu.SemaphoreType.DMA
    firsts, seconds = (xs, ys), (ys, xs)
    whole = (slots,) + block
    scratch = (
        [pltpu.VMEM(whole, F32)] * 7
        + [pltpu.VMEM((half, zs, seconds[g]) + block, BF16) for g in range(2)]
        + [pltpu.VMEM(some((half, firsts[g] - 1, zs, seconds[g])) + block, BF16) for g in range(2)]
        + [pltpu.VMEM(some((half, seconds[g] - 1, zs)) + block, BF16) for g in range(2)]
        + [pltpu.VMEM(some((half, zs - 1)) + block, BF16) for g in range(2)]
        + [pltpu.VMEM((3,) + small.shape, F32)]
        + [pltpu.VMEM((max(1, n - 1),) + small.shape, F32) for n in grid]
        + [pltpu.VMEM((2, 16, TILE, 2 * TILE), F32)]
        + [dma((2, half))]
        + [dma(some((half, firsts[g] - 1))) for g in range(2)] * 2
        + [dma(some((half, seconds[g] - 1))) for g in range(2)] * 2
        + [dma(some((half, zs - 1))) for g in range(2)] * 2
        + [dma((max(1, n - 1),)) for n in grid] * 2
        + [dma((2, 7))]
    )
    results = pl.pallas_call(
        functools.partial(owner_kernel, grid),
        out_shape=[jax.ShapeDtypeStruct(whole, F32)] * 7
        + [jax.ShapeDtypeStruct(small.shape, F32), jax.ShapeDtypeStruct((16, TILE, 2 * TILE), F32)],
        in_specs=[pl.BlockSpec(memory_space=pltpu.SMEM), ANY, pl.BlockSpec(memory_space=pltpu.VMEM)] + [ANY] * 7,
        out_specs=[ANY] * 7 + [pl.BlockSpec(memory_space=pltpu.VMEM)] * 2,
        scratch_shapes=scratch,
        compiler_params=pltpu.CompilerParams(collective_id=1, has_side_effects=True, vmem_limit_bytes=56 << 20),
        name="owner_update",
    )(used, slot_grads.reshape(zs, ys, xs, slots, TILE, TILE), small, *state)
    return last_bases(results[8], results[:7]), results[7]


def ag_kernel(grid, wide_ref, small_ref, out_ref, small_out_ref, own_ref,
              load_sem, z_send, z_recv, b_send0, b_send1, b_recv0, b_recv1, a_send0, a_send1, a_recv0, a_recv1,
              s_load, ssz, ssy, ssx, srz, sry, srx):
    zs, ys, xs = grid
    z, y, x = place(grid)
    tos = peers(grid)
    to_z, to_y, to_x = tos
    slots = own_ref.shape[0]
    half, chunks, size = chunking(slots)
    first = ((xs, to_x), (ys, to_y))
    second = ((ys, to_y), (xs, to_x))
    b_send, b_recv, a_send, a_recv = (b_send0, b_send1), (b_recv0, b_recv1), (a_send0, a_send1), (a_recv0, a_recv1)
    s_send, s_recv = (ssz, ssy, ssx), (srz, sry, srx)

    def span(g, c):
        return pl.ds(g * half + c * size, size)

    def send_z(g, c, k):
        return remote(own_ref.at[span(g, c)], out_ref.at[z, y, x, span(g, c)],
                      z_send.at[g, c, k - 1], z_recv.at[g, c, k - 1], to_z(k))

    def send_b(g, c, k):
        part = out_ref.at[:, y, x, span(g, c)]
        return remote(part, part, b_send[g].at[c, k - 1], b_recv[g].at[c, k - 1], second[g][1](k))

    def send_a(g, c, k):
        part = out_ref.at[:, :, x, span(g, c)] if g == 0 else out_ref.at[:, y, :, span(g, c)]
        return remote(part, part, a_send[g].at[c, k - 1], a_recv[g].at[c, k - 1], first[g][1](k))

    def send_s(axis, k):
        if axis == 0:
            source, target = small_ref, small_out_ref.at[z, y, x]
        else:
            source = target = small_out_ref.at[:, y, x] if axis == 1 else small_out_ref.at[:, :, x]
        return remote(source, target, s_send[axis].at[k - 1], s_recv[axis].at[k - 1], tos[axis](k))

    own_ref[...] = wide_ref[...].astype(BF16)
    keep = pltpu.make_async_copy(own_ref, out_ref.at[z, y, x], load_sem)
    keep_small = pltpu.make_async_copy(small_ref, small_out_ref.at[z, y, x], s_load)
    keep.start()
    keep_small.start()
    greet(grid)

    for k in range(1, grid[0]):
        send_s(0, k).start()
    def start_z(c):
        for g in range(2):
            for k in range(1, zs):
                send_z(g, c, k).start()

    def small_wait(axis):
        for k in range(1, grid[axis]):
            send_s(axis, k).wait_recv()

    def small_start(axis):
        for k in range(1, grid[axis]):
            send_s(axis, k).start()

    start_z(0)
    for t in range(chunks + 1):
        if t < chunks:
            for g in range(2):
                for k in range(1, zs):
                    send_z(g, t, k).wait_recv()
            if t == 0:
                keep.wait()
                keep_small.wait()
                small_wait(0)
                small_start(1)
            if t + 1 < chunks:
                start_z(t + 1)
            for g in range(2):
                for k in range(1, second[g][0]):
                    send_b(g, t, k).start()
        if t >= 1:
            for g in range(2):
                for k in range(1, second[g][0]):
                    send_b(g, t - 1, k).wait_recv()
                for k in range(1, first[g][0]):
                    send_a(g, t - 1, k).start()
        if t == 1:
            small_wait(1)
            small_start(2)
    small_wait(2)
    for c in range(chunks):
        for g in range(2):
            for k in range(1, first[g][0]):
                send_a(g, c, k).wait_recv()
    for axis in range(3):
        for k in range(1, grid[axis]):
            send_s(axis, k).wait_send()
    for c in range(chunks):
        for g in range(2):
            for k in range(1, zs):
                send_z(g, c, k).wait_send()
            for k in range(1, second[g][0]):
                send_b(g, c, k).wait_send()
            for k in range(1, first[g][0]):
                send_a(g, c, k).wait_send()


def gather_all(own, small, device_count):
    grid = chip_grid(device_count)
    zs, ys, xs = grid
    slots = own.shape[0]
    half, chunks, size = chunking(slots)
    dma = pltpu.SemaphoreType.DMA
    firsts, seconds = (xs, ys), (ys, xs)
    scratch = (
        [pltpu.VMEM(own.shape, BF16), dma, dma(some((2, chunks, zs - 1))), dma(some((2, chunks, zs - 1)))]
        + [dma(some((chunks, seconds[g] - 1))) for g in range(2)] * 2
        + [dma(some((chunks, firsts[g] - 1))) for g in range(2)] * 2
        + [dma]
        + [dma((max(1, n - 1),)) for n in grid] * 2
    )
    blocks, smalls = pl.pallas_call(
        functools.partial(ag_kernel, grid),
        out_shape=[jax.ShapeDtypeStruct(grid + own.shape, BF16), jax.ShapeDtypeStruct(grid + small.shape, small.dtype)],
        in_specs=[pl.BlockSpec(memory_space=pltpu.VMEM)] * 2,
        out_specs=[ANY, ANY],
        scratch_shapes=scratch,
        compiler_params=pltpu.CompilerParams(collective_id=2, has_side_effects=True, vmem_limit_bytes=56 << 20),
        name="gather_all",
    )(own, small)
    return blocks.reshape((-1,) + own.shape[1:]), smalls.reshape((-1,) + small.shape)


def unpack_and_attend(packed, slots, shapes, x, split, places, half):
    length, width = x.shape
    span, count = min(length, 512), len(shapes)

    def kernel(slots_ref, split_ref, packed_ref, x_ref, *refs):
        mats, mixed_out, attended_out, totals_ref = refs[:count], refs[count], refs[count + 1], refs[count + 2]
        near, rest = refs[count + 3:2 * count + 3], refs[2 * count + 3:]
        x_near, mixed_ref, attended_ref, score_ref, turned_ref, sems, own_sems = rest

        def whole(index):
            return pltpu.make_async_copy(near[index], mats[index], sems.at[1, index])

        load_x = pltpu.make_async_copy(x_ref, x_near, own_sems.at[0])
        load_x.start()
        offsets = [0]
        for height, breadth in shapes:
            offsets.append(offsets[-1] + height // TILE * (breadth // TILE))

        def start(index):
            height, breadth = shapes[index]
            across = breadth // TILE
            for i in range(height // TILE):
                for j in range(across):
                    tile = near[index].at[i * TILE:(i + 1) * TILE, j * TILE:(j + 1) * TILE]
                    slot = packed_ref.at[slots_ref[offsets[index] + i * across + j]]
                    pltpu.make_async_copy(slot, tile, sems.at[0, index]).start()

        start(0)

        def landed(index):
            pltpu.make_async_copy(near[index], near[index], sems.at[0, index]).wait()
            whole(index).start()

        load_x.wait()
        landed(0)
        mix(x_near, near[0], bias_row(split_ref, places, ("enc_q", None, "enc_v"), half), mixed_ref)
        keep_mixed = pltpu.make_async_copy(mixed_ref, mixed_out, own_sems.at[1])
        keep_mixed.start()

        def beside(part, parts):
            lead = parts // 2
            share = -(-(count - 1) // lead)
            place = part if part < lead else part - lead
            for index in range(1 + place * share, min(count, 1 + (place + 1) * share)):
                if part < lead:
                    start(index)
                elif part < 2 * lead:
                    landed(index)

        totals_ref[...] = jnp.zeros_like(totals_ref)
        attend(
            mixed_ref.at[:, :half], mixed_ref.at[:, half:2 * half], mixed_ref.at[:, 2 * half:],
            attended_ref, totals_ref, score_ref, turned_ref, False, span, beside,
        )
        keep_attended = pltpu.make_async_copy(attended_ref, attended_out, own_sems.at[2])
        keep_attended.start()
        for index in range(count):
            whole(index).wait()
        keep_mixed.wait()
        keep_attended.wait()

    results = pl.pallas_call(
        kernel,
        out_shape=[jax.ShapeDtypeStruct(s, BF16) for s in shapes]
        + [shape(length, 3 * half, dtype=BF16), shape(length, half, dtype=BF16), shape(8, length)],
        in_specs=[pl.BlockSpec(memory_space=pltpu.SMEM), VM, ANY, ANY],
        out_specs=[ANY] * (count + 2) + [VM],
        scratch_shapes=[held(*s, dtype=BF16) for s in shapes]
        + [
            held(length, width, dtype=BF16), held(length, 3 * half, dtype=BF16), held(length, half, dtype=BF16),
            held(2, length, span), held(half, length, dtype=BF16),
            pltpu.SemaphoreType.DMA((2, count)), pltpu.SemaphoreType.DMA((3,)),
        ],
        compiler_params=pltpu.CompilerParams(vmem_limit_bytes=56 << 20),
        name="unpack_and_attend",
    )(slots, split, packed, x)
    return results[:count], results[count:]


def weight_grads_kernel(plan, used, vectors, passed, slots_ref, *refs):
    arrays, refs = refs[:used], refs[used:]
    given, refs = refs[:len(vectors)], refs[len(vectors):]
    refs = refs[passed:]
    packed, refs = refs[0], refs[1:]
    if vectors:
        rows_ref, refs = refs[0], refs[1:]
    held, refs = refs[:used], refs[used:]
    turned, refs = refs[0], refs[1:]
    results, sems = refs[:len(plan)], refs[len(plan):]
    load_sem, store_sem = sems

    def load(i):
        return pltpu.make_async_copy(arrays[i], held[i], load_sem.at[i])

    order = []
    for left, tokens, right, *rest in plan:
        for i in (left, right):
            if i not in order:
                order.append(i)
    for i in order:
        load(i).start()
    if vectors:
        width = rows_ref.shape[1]
        rows_ref[...] = jnp.zeros_like(rows_ref)
        for source, (at, pieces) in zip(given, vectors):
            if pieces is None:
                rows_ref[at:at + 3, :] = source[0:3, :]
                continue
            for begin, end in pieces:
                while begin < end:
                    lane = at % width
                    size = min(end - begin, width - lane)
                    rows_ref[at // width:at // width + 1, lane:lane + size] = source[:, begin:begin + size]
                    begin, at = begin + size, at + size
    ready = set()
    last = None
    ready_columns = []

    def send(result, index, offset, stride, down, group, n):
        for i in range(down):
            for j in range(n * group, (n + 1) * group):
                tile = result.at[i * TILE:(i + 1) * TILE, j * TILE:(j + 1) * TILE]
                slot = packed.at[slots_ref[offset + i * stride + j]]
                pltpu.make_async_copy(tile, slot, store_sem.at[index]).start()

    for index, (left, tokens, right, offset, stride, down, across) in enumerate(plan):
        for i in (left, right):
            if i not in ready:
                ready.add(i)
                load(i).wait()
        height = down * TILE
        if last != (left, tokens):
            for j in range(down):
                turned[j * TILE:(j + 1) * TILE, :tokens] = (
                    held[left][:tokens, j * TILE:(j + 1) * TILE].astype(F32).T.astype(BF16)
                )
            last = (left, tokens)
        result = results[index]
        group = 3 if across % 3 == 0 else 1

        for n in range(across // group):
            lanes = slice(n * group * TILE, (n + 1) * group * TILE)
            result[:, lanes] = times(turned[:height, :tokens], held[right][:tokens, lanes]).astype(BF16)
            ready_columns.append((result, index, offset, stride, down, group, n))
            if len(ready_columns) > 1:
                send(*ready_columns.pop(0))
    for columns in ready_columns:
        send(*columns)
    for index in range(len(plan)):
        pltpu.make_async_copy(results[index], results[index], store_sem.at[index]).wait()


def weight_grads(matrices, slots, slot_count, packed=None, vectors=None):
    arrays, plan, results = [], [], []

    def index_of(array):
        for i, other in enumerate(arrays):
            if other is array:
                return i
        arrays.append(array)
        return len(arrays) - 1

    for offset, parts in matrices:
        height = parts[0][0].shape[1]
        stride = sum(right.shape[1] for left, right in parts) // TILE
        for left, right in parts:
            across = right.shape[1] // TILE
            plan.append((index_of(left), right.shape[0], index_of(right), offset, stride, height // TILE, across))
            results.append(pltpu.VMEM((height, right.shape[1]), BF16))
            offset += across
    tall = max(entry[5] for entry in plan) * TILE
    long = max(entry[1] for entry in plan)
    out_shape = [jax.ShapeDtypeStruct((slot_count, TILE, TILE), BF16)]
    given, layout = [], []
    if vectors:
        rows, width, items = vectors
        out_shape.append(jax.ShapeDtypeStruct((rows, width), F32))
        given = [item[0] for item in items]
        layout = [item[1:] for item in items]
    passed = [] if packed is None else [packed]
    return pl.pallas_call(
        functools.partial(weight_grads_kernel, plan, len(arrays), layout, len(passed)),
        out_shape=out_shape,
        in_specs=[pl.BlockSpec(memory_space=pltpu.SMEM)] + [ANY] * len(arrays)
        + [pl.BlockSpec(memory_space=pltpu.VMEM)] * len(given) + [ANY] * len(passed),
        out_specs=[ANY] + [pl.BlockSpec(memory_space=pltpu.VMEM)] * (len(out_shape) - 1),
        scratch_shapes=[pltpu.VMEM(a.shape, a.dtype) for a in arrays] + [pltpu.VMEM((tall, long), BF16)] + results
        + [pltpu.SemaphoreType.DMA((len(arrays),)), pltpu.SemaphoreType.DMA((len(plan),))],
        input_output_aliases={} if packed is None else {1 + len(arrays) + len(given): 0},
        compiler_params=pltpu.CompilerParams(vmem_limit_bytes=56 << 20),
        name="weight_grads",
    )(slots, *arrays, *given, *passed)


VM = pl.BlockSpec(memory_space=pltpu.VMEM)


def times(left, right, dims=NN):
    return lax.dot_general(left, right, (dims, ((), ())), preferred_element_type=F32)


def rows_of(t, size=ROWS):
    return pl.ds(pl.multiple_of(t * size, size), size)


class Swap:
    def __init__(self, out, into, send_sem, recv_sem):
        self.out, self.into, self.send_sem, self.recv_sem = out, into, send_sem, recv_sem

    @staticmethod
    def scratch(tiles, width):
        dma = pltpu.SemaphoreType.DMA((tiles,))
        held = pltpu.VMEM((tiles, ROWS, width), BF16)
        return [held, held, dma, dma]

    @staticmethod
    def greet():
        barrier = pltpu.get_barrier_semaphore()
        other = {"tensor": 1 - lax.axis_index("tensor")}
        pl.semaphore_signal(barrier, inc=1, device_id=other, device_id_type=MESH)
        pl.semaphore_wait(barrier, 1)

    def copy(self, t):
        return pltpu.make_async_remote_copy(
            src_ref=self.out.at[t],
            dst_ref=self.into.at[t],
            send_sem=self.send_sem.at[t],
            recv_sem=self.recv_sem.at[t],
            device_id={"tensor": 1 - lax.axis_index("tensor")},
            device_id_type=MESH,
        )

    def give(self, t, value):
        self.out[t] = value.astype(BF16)
        self.copy(t).start()

    def take(self, t):
        self.copy(t).wait()
        return self.out[t].astype(F32) + self.into[t].astype(F32)


class Rows:
    def __init__(self, ref, rows):
        self.ref, self.rows = ref, rows

    def __getitem__(self, index):
        at = self.rows[index[0].start]
        return self.ref[at:at + 1, :]


def bias_places(half, hidden_half):
    places, at = {}, 0
    for name, length in (
        ("enc_q", half), ("enc_v", half), ("enc_up", hidden_half), ("dec_q", half), ("dec_v", half),
        ("crs_q", half), ("crs_v", half), ("dec_up", hidden_half),
    ):
        places[name] = slice(at, at + length)
        at += length
    return places


def bias_row(split_ref, places, names, half):
    zero = jnp.zeros((1, half), F32)
    return jnp.concatenate([zero if name is None else split_ref[:, places[name]] for name in names], 1)


def standardize(values):
    center = values - jnp.mean(values, -1, keepdims=True)
    scale = lax.rsqrt(jnp.mean(center * center, -1, keepdims=True) + NORM_EPSILON)
    return center * scale, scale


def norm_back(grad, unit, scale, gain):
    inner = grad * gain
    return scale * (
        inner - jnp.mean(inner, -1, keepdims=True) - unit * jnp.mean(inner * unit, -1, keepdims=True)
    )


def add_sums(sums_ref, grad_in, grad_out, unit):
    sums_ref[0:1, :] += jnp.sum(grad_in, 0, keepdims=True)
    sums_ref[1:2, :] += jnp.sum(grad_out * unit, 0, keepdims=True)
    sums_ref[2:3, :] += jnp.sum(grad_out, 0, keepdims=True)


def head_mask(shape):
    return lax.broadcasted_iota(jnp.int32, shape, 1) < HD


def attend(query_ref, key_ref, value_ref, attended_ref, totals_ref, score_ref, turned_ref, causal, span, beside=None):
    queries, keys = query_ref.shape[0], key_ref.shape[0]
    pairs = query_ref.shape[1] // PAIR
    chunks = keys // KEYS
    for j in range(pairs):
        turned_ref[j * PAIR:(j + 1) * PAIR, :] = (
            value_ref[:, j * PAIR:(j + 1) * PAIR].astype(F32).T.astype(BF16)
        )
    for i in range(queries // span):
        mine = slice(i * span, (i + 1) * span)

        def pair(j, carry, i=i, mine=mine):
            lanes = pl.ds(j * PAIR if isinstance(j, int) else pl.multiple_of(j * PAIR, PAIR), PAIR)
            query = query_ref[mine, lanes] * jnp.asarray(HD**-0.5, BF16)
            first = head_mask(query.shape)
            parts = []
            for h in range(2):
                masked = jnp.where(first if h == 0 else ~first, query, jnp.zeros_like(query))
                top = jnp.full((1, span), -jnp.inf, F32)
                for c in range(chunks):
                    if causal and c * KEYS >= (i + 1) * span:
                        continue
                    scores = times(key_ref[c * KEYS:(c + 1) * KEYS, lanes], masked, NT)
                    if causal and (c + 1) * KEYS > i * span:
                        key_at = c * KEYS + lax.broadcasted_iota(jnp.int32, scores.shape, 0)
                        query_at = i * span + lax.broadcasted_iota(jnp.int32, scores.shape, 1)
                        scores = jnp.where(key_at <= query_at, scores, -1000000000.0)
                    score_ref[h, c * KEYS:(c + 1) * KEYS, :] = scores
                    top = jnp.maximum(top, jnp.max(scores, 0, keepdims=True))
                total = jnp.zeros((1, span), F32)
                mixed = jnp.zeros((HD, span), F32)
                value_rows = pl.ds(j * PAIR + h * HD if isinstance(j, int) else pl.multiple_of(j * PAIR + h * HD, HD), HD)
                for c in range(chunks):
                    if causal and c * KEYS >= (i + 1) * span:
                        continue
                    probs = jnp.exp(score_ref[h, c * KEYS:(c + 1) * KEYS, :] - top)
                    total += jnp.sum(probs, 0, keepdims=True)
                    mixed += times(turned_ref[value_rows, c * KEYS:(c + 1) * KEYS], probs.astype(BF16))
                parts.append(mixed * (1.0 / total))
                totals_ref[pl.ds(2 * j + h, 1), mine] = top + jnp.log(total)
            attended_ref[mine, lanes] = jnp.concatenate(parts, 0).T.astype(BF16)
            return carry

        if beside is None:
            lax.fori_loop(0, pairs, pair, 0)
        else:
            for j in range(pairs):
                beside(i * pairs + j, queries // span * pairs)
                pair(j, 0)


def attend_back(
    query_ref, key_ref, value_ref, attended_ref, totals_ref, grad_ref,
    grad_query_ref, grad_key_ref, grad_value_ref, turned_ref, causal,
):
    queries, keys = grad_ref.shape[0], key_ref.shape[0]
    pairs = query_ref.shape[1] // PAIR
    chunks = keys // KEYS
    scale = HD**-0.5
    for j in range(pairs):
        turned_ref[j * PAIR:(j + 1) * PAIR, :] = (
            key_ref[:, j * PAIR:(j + 1) * PAIR].astype(F32).T.astype(BF16)
        )

    def pair(j, carry):
        lanes = pl.ds(pl.multiple_of(j * PAIR, PAIR), PAIR)
        query = query_ref[:queries, lanes] * jnp.asarray(scale, BF16)
        grad = grad_ref[:, lanes]
        first = head_mask(query.shape)
        meet = (grad.astype(F32) * attended_ref[:queries, lanes].astype(F32)).T
        masked, grads, deltas, totals = [], [], [], []
        for h in range(2):
            keep = first if h == 0 else ~first
            masked.append(jnp.where(keep, query, jnp.zeros_like(query)))
            grads.append(jnp.where(keep, grad, jnp.zeros_like(grad)))
            deltas.append(jnp.sum(meet[h * HD:(h + 1) * HD], 0, keepdims=True))
            totals.append(totals_ref[pl.ds(2 * j + h, 1), :queries])
        grad_query = [jnp.zeros((HD, queries), F32) for h in range(2)]
        for c in range(chunks):
            some = slice(c * KEYS, (c + 1) * KEYS)
            low = c * KEYS if causal else 0
            grad_key = grad_value = jnp.zeros((KEYS, PAIR), F32)
            for h in range(2):
                scores = times(key_ref[some, lanes], masked[h][low:], NT)
                if causal:
                    key_at = lax.broadcasted_iota(jnp.int32, scores.shape, 0)
                    query_at = lax.broadcasted_iota(jnp.int32, scores.shape, 1)
                    scores = jnp.where(key_at <= query_at, scores, -1000000000.0)
                probs = jnp.exp(scores - totals[h][:, low:])
                grad_probs = times(value_ref[some, lanes], grads[h][low:], NT)
                grad_scores = (probs * (grad_probs - deltas[h][:, low:])).astype(BF16)
                grad_value += times(probs.astype(BF16), grads[h][low:])
                grad_key += times(grad_scores, masked[h][low:])
                key_rows = pl.ds(pl.multiple_of(j * PAIR + h * HD, HD), HD)
                part = times(turned_ref[key_rows, some], grad_scores)
                if low:
                    part = jnp.concatenate([jnp.zeros((HD, low), F32), part], 1)
                grad_query[h] += part
            grad_key_ref[some, lanes] = grad_key.astype(BF16)
            grad_value_ref[some, lanes] = grad_value.astype(BF16)
        grad_query_ref[:, lanes] = (jnp.concatenate(grad_query, 0) * scale).T.astype(BF16)
        return carry

    lax.fori_loop(0, pairs, pair, 0, unroll=True)


def mix(x_ref, wide_ref, bias, mixed_ref):
    def one(t, carry):
        mixed_ref[rows_of(t), :] = (times(x_ref[rows_of(t), :], wide_ref[...]) + bias).astype(BF16)
        return carry

    lax.fori_loop(0, x_ref.shape[0] // ROWS, one, 0)


def close_branch(x_ref, attended_ref, out_weight_ref, vec_ref, unit_ref, scale_ref, *swap_refs):
    swap = Swap(*swap_refs)
    tiles = x_ref.shape[0] // ROWS

    def give(t, carry):
        swap.give(t, times(attended_ref[rows_of(t), :], out_weight_ref[...]))
        return carry

    lax.fori_loop(0, tiles, give, 0)

    def take(t, carry):
        rows = rows_of(t)
        unit, scale = standardize(x_ref[rows, :].astype(F32) + swap.take(t) + vec_ref[0:1, :])
        unit_ref[rows, :] = unit
        scale_ref[rows, :] = scale
        return carry

    lax.fori_loop(0, tiles, take, 0)


def self_forward_kernel(
    causal, span, x_ref, wide_ref, out_weight_ref, bias, vec_ref,
    mixed_ref, attended_ref, totals_ref, unit_ref, scale_ref,
    score_ref, turned_ref, *swap_refs,
):
    half = out_weight_ref.shape[0]
    totals_ref[...] = jnp.zeros_like(totals_ref)
    mix(x_ref, wide_ref, bias, mixed_ref)
    attend(
        mixed_ref.at[:, :half], mixed_ref.at[:, half:2 * half], mixed_ref.at[:, 2 * half:],
        attended_ref, totals_ref, score_ref, turned_ref, causal, span,
    )
    close_branch(x_ref, attended_ref, out_weight_ref, vec_ref, unit_ref, scale_ref, *swap_refs)


def shape(*dims, dtype=F32):
    return jax.ShapeDtypeStruct(dims, dtype)


def params(ident, mib=56):
    return pltpu.CompilerParams(collective_id=ident, has_side_effects=True, vmem_limit_bytes=mib << 20)


def cross_forward_kernel(
    span, unit_ref, fetched_ref, query_weight_ref, wide_ref, out_weight_ref, query_bias_ref, bias_ref, vec_ref,
    low_ref, query_ref, mixed_ref, attended_ref, totals_ref, unit_out_ref, scale_ref,
    score_ref, turned_ref, *swap_refs,
):
    swap = Swap(*swap_refs)
    length, width = unit_ref.shape
    half = out_weight_ref.shape[0]
    tiles = length // ROWS
    totals_ref[...] = jnp.zeros_like(totals_ref)

    def ask(t, carry):
        rows = rows_of(t)
        low = (unit_ref[rows, :] * vec_ref[0:1, :] + vec_ref[1:2, :]).astype(BF16)
        low_ref[rows, :] = low
        query_ref[rows, :] = (times(low, query_weight_ref[...]) + query_bias_ref[...]).astype(BF16)
        return carry

    lax.fori_loop(0, tiles, ask, 0)

    def mix(t, carry):
        mixed_ref[rows_of(t), :] = (
            times(fetched_ref[rows_of(t), :], wide_ref[...]) + bias_ref[...]
        ).astype(BF16)
        return carry

    lax.fori_loop(0, fetched_ref.shape[0] // ROWS, mix, 0)
    attend(
        query_ref, mixed_ref.at[:, :half], mixed_ref.at[:, half:],
        attended_ref, totals_ref, score_ref, turned_ref, False, span,
    )

    def give(t, carry):
        swap.give(t, times(attended_ref[rows_of(t), :], out_weight_ref[...]))
        return carry

    lax.fori_loop(0, tiles, give, 0)

    def take(t, carry):
        rows = rows_of(t)
        hidden = unit_ref[rows, :] * vec_ref[0:1, :] + vec_ref[1:2, :]
        unit, scale = standardize(hidden + swap.take(t) + vec_ref[2:3, :])
        unit_out_ref[rows, :] = unit
        scale_ref[rows, :] = scale
        return carry

    lax.fori_loop(0, tiles, take, 0)


def feed_forward_kernel(
    kept, between, unit_ref, up_ref, down_ref, bias_ref, vec_ref,
    states_ref, states_low_ref, low_ref, active_ref, slope_ref, unit_out_ref, scale_ref, *swap_refs,
):
    swap = Swap(*swap_refs)
    length, width = unit_ref.shape
    hidden_half = up_ref.shape[1]
    tiles, kept_tiles = length // ROWS, kept // ROWS
    step = 512

    def feed(t, carry, keep):
        rows = rows_of(t)
        low = (unit_ref[rows, :] * vec_ref[0:1, :] + vec_ref[1:2, :]).astype(BF16)
        if keep:
            low_ref[rows, :] = low
        total = jnp.zeros((ROWS, width), F32)
        for c in range(0, hidden_half, step):
            upward = times(low, up_ref[:, c:c + step]) + bias_ref[:, c:c + step]
            below = 0.5 * lax.erf(upward * (0.5**0.5)) + 0.5
            active = (upward * below).astype(BF16)
            if keep:
                active_ref[rows, c:c + step] = active
                bell = jnp.exp(-0.5 * upward * upward) * (0.5 / jnp.pi) ** 0.5
                slope_ref[rows, c:c + step] = (below + upward * bell).astype(BF16)
            total += times(active, down_ref[c:c + step, :])
        swap.give(t, total)
        return carry

    def take(t, carry, keep):
        rows = rows_of(t)
        hidden = unit_ref[rows, :] * vec_ref[0:1, :] + vec_ref[1:2, :]
        unit, scale = standardize(hidden + swap.take(t) + vec_ref[2:3, :])
        states = unit * vec_ref[3:4, :] + vec_ref[4:5, :]
        states_ref[rows, :] = states
        if keep:
            states_low_ref[rows, :] = states.astype(BF16)
            unit_out_ref[rows, :] = unit
            scale_ref[rows, :] = scale
        return carry

    lax.fori_loop(0, kept_tiles, functools.partial(feed, keep=True), 0)
    lax.fori_loop(0, kept_tiles, functools.partial(take, keep=True), 0)
    between()
    if kept_tiles < tiles:
        lax.fori_loop(kept_tiles, tiles, functools.partial(feed, keep=False), 0)
        lax.fori_loop(kept_tiles, tiles, functools.partial(take, keep=False), 0)


def feed_backward_kernel(
    grad_ref, unit_after_ref, scale_after_ref, active_ref, slope_ref, up_ref, down_ref,
    unit_before_ref, scale_before_ref, vec_ref,
    low_ref, grad_up_ref, bias_ref, grad_out_ref, sums_after_ref, sums_before_ref,
    held_ref, *swap_refs,
):
    swap = Swap(*swap_refs)
    length, width = grad_ref.shape
    hidden_half = up_ref.shape[1]
    tiles = length // ROWS
    step = 512
    sums_after_ref[...] = jnp.zeros_like(sums_after_ref)
    sums_before_ref[...] = jnp.zeros_like(sums_before_ref)
    bias_ref[...] = jnp.zeros_like(bias_ref)

    def give(t, carry):
        rows = rows_of(t)
        grad = grad_ref[rows, :].astype(F32)
        unit = unit_after_ref[rows, :]
        inner = norm_back(grad, unit, scale_after_ref[rows, :], vec_ref[0:1, :])
        add_sums(sums_after_ref, inner, grad, unit)
        held_ref[rows, :] = inner
        low = inner.astype(BF16)
        low_ref[rows, :] = low
        total = jnp.zeros((ROWS, width), F32)
        for c in range(0, hidden_half, step):
            grad_active = times(low, down_ref[c:c + step, :], NT)
            grad_up = (grad_active * slope_ref[rows, c:c + step].astype(F32)).astype(BF16)
            grad_up_ref[rows, c:c + step] = grad_up
            bias_ref[:, c:c + step] += jnp.sum(grad_up.astype(F32), 0, keepdims=True)
            total += times(grad_up, up_ref[:, c:c + step], NT)
        swap.give(t, total)
        return carry

    lax.fori_loop(0, tiles, give, 0)

    def take(t, carry):
        rows = rows_of(t)
        grad = held_ref[rows, :] + swap.take(t)
        unit = unit_before_ref[rows, :]
        inner = norm_back(grad, unit, scale_before_ref[rows, :], vec_ref[1:2, :])
        add_sums(sums_before_ref, inner, grad, unit)
        grad_out_ref[rows, :] = inner
        return carry

    lax.fori_loop(0, tiles, take, 0)


def spread(grad_pre_ref, out_weight_ref, low_ref, grad_ref):
    def one(t, carry):
        rows = rows_of(t)
        low = grad_pre_ref[rows, :].astype(BF16)
        low_ref[rows, :] = low
        grad_ref[rows, :] = times(low, out_weight_ref[...], NT).astype(BF16)
        return carry

    lax.fori_loop(0, grad_pre_ref.shape[0] // ROWS, one, 0)


def self_backward_kernel(
    causal, grad_pre_ref, mixed_ref, attended_ref, totals_ref, wide_ref, out_weight_ref,
    low_ref, grad_query_ref, grad_pair_ref, grad_x_ref, sums_ref,
    grad_ref, turned_ref, *swap_refs,
):
    swap = Swap(*swap_refs)
    queries, width = grad_pre_ref.shape
    half = out_weight_ref.shape[0]
    length = mixed_ref.shape[0]
    spread(grad_pre_ref, out_weight_ref, low_ref, grad_ref)
    attend_back(
        mixed_ref.at[:, :half], mixed_ref.at[:, half:2 * half], mixed_ref.at[:, 2 * half:],
        attended_ref, totals_ref, grad_ref,
        grad_query_ref, grad_pair_ref.at[:, :half], grad_pair_ref.at[:, half:], turned_ref, causal,
    )
    sums_ref[...] = jnp.zeros_like(sums_ref)
    first = queries // ROWS

    def give(t, carry, asked):
        rows = rows_of(t)
        pair = grad_pair_ref[rows, :]
        sums_ref[:, half:] += jnp.sum(pair.astype(F32), 0, keepdims=True)
        total = times(pair, wide_ref[:, half:], NT)
        if asked:
            query = grad_query_ref[rows, :]
            sums_ref[:, :half] += jnp.sum(query.astype(F32), 0, keepdims=True)
            total += times(query, wide_ref[:, :half], NT)
        swap.give(t, total)
        return carry

    lax.fori_loop(0, first, functools.partial(give, asked=True), 0)
    if first < length // ROWS:
        lax.fori_loop(first, length // ROWS, functools.partial(give, asked=False), 0)

    def take(t, carry, asked):
        rows = rows_of(t)
        total = swap.take(t)
        grad_x_ref[rows, :] = grad_pre_ref[rows, :] + total if asked else total
        return carry

    lax.fori_loop(0, first, functools.partial(take, asked=True), 0)
    if first < length // ROWS:
        lax.fori_loop(first, length // ROWS, functools.partial(take, asked=False), 0)


def cross_backward_kernel(
    between, grad_pre_ref, query_ref, mixed_ref, attended_ref, totals_ref, query_weight_ref, wide_ref, out_weight_ref,
    unit_ref, scale_ref, vec_ref,
    low_ref, grad_query_ref, grad_pair_ref, fetched_ref, grad_out_ref, sums_ref, vec_sums_ref,
    grad_ref, turned_ref, *swap_refs,
):
    near, far = Swap(*swap_refs[:4]), Swap(*swap_refs[4:])
    queries, width = grad_pre_ref.shape
    half = out_weight_ref.shape[0]
    keys = mixed_ref.shape[0]
    spread(grad_pre_ref, out_weight_ref, low_ref, grad_ref)
    attend_back(
        query_ref, mixed_ref.at[:, :half], mixed_ref.at[:, half:],
        attended_ref, totals_ref, grad_ref,
        grad_query_ref, grad_pair_ref.at[:, :half], grad_pair_ref.at[:, half:], turned_ref, False,
    )
    sums_ref[...] = jnp.zeros_like(sums_ref)
    vec_sums_ref[...] = jnp.zeros_like(vec_sums_ref)

    def give_far(t, carry):
        pair = grad_pair_ref[rows_of(t), :]
        sums_ref[:, half:] += jnp.sum(pair.astype(F32), 0, keepdims=True)
        far.give(t, times(pair, wide_ref[...], NT))
        return carry

    lax.fori_loop(0, keys // ROWS, give_far, 0)

    def give_near(t, carry):
        query = grad_query_ref[rows_of(t), :]
        sums_ref[:, :half] += jnp.sum(query.astype(F32), 0, keepdims=True)
        near.give(t, times(query, query_weight_ref[...], NT))
        return carry

    lax.fori_loop(0, queries // ROWS, give_near, 0)

    def take_far(t, carry):
        fetched_ref[rows_of(t), :] = far.take(t).astype(BF16)
        return carry

    lax.fori_loop(0, keys // ROWS, take_far, 0)
    between()

    def take_near(t, carry):
        rows = rows_of(t)
        grad = grad_pre_ref[rows, :] + near.take(t)
        unit = unit_ref[rows, :]
        inner = norm_back(grad, unit, scale_ref[rows, :], vec_ref[0:1, :])
        add_sums(vec_sums_ref, inner, grad, unit)
        grad_out_ref[rows, :] = inner
        return carry

    lax.fori_loop(0, queries // ROWS, take_near, 0)


def held(*dims, dtype=F32):
    return pltpu.VMEM(dims, dtype)


def streams(array):
    rows, width = array.shape
    return rows % 16 == 0 and width % TILE == 0 and rows * width * array.dtype.itemsize >= 1 << 18


def call(name, ident, body, inputs, outputs, scratch, mib=56):
    ins = [i for i, array in enumerate(inputs) if streams(array)]
    outs = [i for i, array in enumerate(outputs) if streams(array)]
    count_in, count_out = len(inputs), len(outputs)

    def kernel(*refs):
        in_refs, out_refs, rest = refs[:count_in], refs[count_in:count_in + count_out], refs[count_in + count_out:]
        near_in, near_out = list(in_refs), list(out_refs)
        for place, ref in zip(ins, rest[:len(ins)]):
            near_in[place] = ref
        rest = rest[len(ins):]
        for place, ref in zip(outs, rest[:len(outs)]):
            near_out[place] = ref
        rest = rest[len(outs):]
        in_sem, out_sem, rest = rest[0], rest[1], rest[2:]

        def load(place):
            return pltpu.make_async_copy(in_refs[place], near_in[place], in_sem.at[place])

        def store(place):
            return pltpu.make_async_copy(near_out[place], out_refs[place], out_sem.at[place])

        def need(*places):
            for place in places:
                if place in ins:
                    load(place).wait()

        def done(*places):
            for place in places:
                if place in outs:
                    store(place).start()

        for place in ins:
            load(place).start()
        body(need, done, *near_in, *near_out, *rest)
        for place in outs:
            store(place).wait()

    return pl.pallas_call(
        kernel,
        out_shape=outputs,
        in_specs=[ANY if i in ins else VM for i in range(count_in)],
        out_specs=[ANY if i in outs else VM for i in range(count_out)],
        scratch_shapes=[pltpu.VMEM(inputs[i].shape, inputs[i].dtype) for i in ins]
        + [pltpu.VMEM(outputs[i].shape, outputs[i].dtype) for i in outs]
        + [pltpu.SemaphoreType.DMA((count_in,)), pltpu.SemaphoreType.DMA((count_out,))]
        + scratch,
        compiler_params=params(ident, mib),
        name=name,
    )(*inputs)


class Trade:
    def __init__(self, count, into, send_sem, recv_sem, give_sem, take_sem):
        self.count, self.into = count, into
        self.send_sem, self.recv_sem, self.give_sem, self.take_sem = send_sem, recv_sem, give_sem, take_sem
        self.me, self.core = lax.axis_index("dp"), lax.axis_index("tensor")
        self.rows, self.half = into.shape[0] // count, into.shape[1] // 2

    @staticmethod
    def scratch(count):
        return [pltpu.SemaphoreType.DMA((count,))] * 4

    def greet(self):
        barrier = pltpu.get_barrier_semaphore()

        def signal(k, carry):
            other = {"dp": lax.rem(self.me + k, self.count)}
            pl.semaphore_signal(barrier, inc=1, device_id=other, device_id_type=MESH)
            return carry

        lax.fori_loop(1, self.count, signal, 0)
        pl.semaphore_signal(barrier, inc=1, device_id={"tensor": 1 - self.core}, device_id_type=MESH)
        pl.semaphore_wait(barrier, self.count)

    def rows_of(self, device):
        return pl.ds(pl.multiple_of(device * self.rows, self.rows), self.rows)

    def mine(self):
        return pl.ds(pl.multiple_of(self.core * self.half, self.half), self.half)

    def lanes_of(self, source):
        return self.mine() if source.shape[1] == self.into.shape[1] else slice(None)

    def send(self, source, k):
        other = lax.rem(self.me + k, self.count)
        return pltpu.make_async_remote_copy(
            src_ref=source.at[self.rows_of(other), self.lanes_of(source)],
            dst_ref=self.into.at[self.rows_of(self.me), self.mine()],
            send_sem=self.send_sem.at[k],
            recv_sem=self.recv_sem.at[k],
            device_id={"dp": other},
            device_id_type=MESH,
        )

    def pass_on(self, k):
        part = self.into.at[self.rows_of(lax.rem(self.me - k + self.count, self.count)), self.mine()]
        return pltpu.make_async_remote_copy(
            src_ref=part,
            dst_ref=part,
            send_sem=self.give_sem.at[k],
            recv_sem=self.take_sem.at[k],
            device_id={"tensor": 1 - self.core},
            device_id_type=MESH,
        )

    def start(self, source):
        def go(k, carry):
            self.send(source, k).start()
            return carry

        lax.fori_loop(1, self.count, go, 0)
        self.into[self.rows_of(self.me), self.mine()] = source[self.rows_of(self.me), self.lanes_of(source)]
        self.pass_on(0).start()

    def finish(self, source):
        def meet(k, carry):
            self.send(source, k).wait_recv()
            self.pass_on(k).start()
            return carry

        lax.fori_loop(1, self.count, meet, 0)

        def end(k, carry):
            self.pass_on(k).wait()
            return carry

        lax.fori_loop(0, self.count, end, 0)

        def sent(k, carry):
            self.send(source, k).wait_send()
            return carry

        lax.fori_loop(1, self.count, sent, 0)


def encoder_and_fetch(
    ident, x, attended, out_weight, up, down, shared, split, kept, wanted, target, dec_wide, dec_out_weight, count
):
    length, width = x.shape
    half, hidden_half = out_weight.shape[0], up.shape[1]
    tiles, target_length = length // ROWS, target.shape[0]
    span = min(target_length, 512)
    fetched_rows = wanted.shape[0]
    places = bias_places(half, hidden_half)

    def body(
        need, done, x_ref, attended_ref, out_weight_ref, up_ref, down_ref, shared_ref, split_ref, wanted_ref,
        target_ref, dec_wide_ref, dec_out_weight_ref, *refs,
    ):
        saved, fed, dec_saved, fetched_ref, rest = refs[:2], refs[2:9], refs[9:14], refs[14], refs[15:]
        served_ref, trade_sems, rest = rest[0], rest[1:5], rest[5:]
        score_ref, turned_ref, rest = rest[0], rest[1], rest[2:]
        trade = Trade(count, fetched_ref, *trade_sems)
        stored_ref = fed[1]
        need(0, 1, 2)
        trade.greet()
        close_branch(x_ref, attended_ref, out_weight_ref, Rows(shared_ref, (0,)), *saved, *rest[:4])
        done(0, 1)
        need(3, 4, 5, 6, 7)

        def serve(t, carry):
            want = wanted_ref[rows_of(t), :]
            match = want == lax.broadcasted_iota(jnp.int32, (ROWS, kept), 1)
            pick = jnp.where(match, 1.0, 0.0).astype(BF16)
            served_ref[rows_of(t), :] = times(pick, stored_ref[:, trade.mine()]).astype(BF16)
            return carry

        def between():
            lax.fori_loop(0, fetched_rows // ROWS, serve, 0)
            trade.start(served_ref)
            done(3, 4, 5, 6, 7, 8)

        feed_forward_kernel(
            kept, between, saved[0], up_ref, down_ref, split_ref.at[:, places["enc_up"]],
            Rows(shared_ref, (1, 2, 3, 4, 5)), *fed, *rest[4:8],
        )
        done(2)
        need(8, 9, 10)
        self_forward_kernel(
            True, span, target_ref, dec_wide_ref, dec_out_weight_ref,
            bias_row(split_ref, places, ("dec_q", None, "dec_v"), half), Rows(shared_ref, (6,)),
            *dec_saved, score_ref, turned_ref, *rest[8:],
        )
        done(9, 10, 11, 12, 13)
        trade.finish(served_ref)
        done(14)

    return call(
        "encoder_and_fetch", ident, body,
        [x, attended, out_weight, up, down, shared, split, wanted, target, dec_wide, dec_out_weight],
        [
            shape(length, width), shape(length, 1),
            shape(length, width), shape(kept, width, dtype=BF16), shape(kept, width, dtype=BF16),
            shape(kept, hidden_half, dtype=BF16), shape(kept, hidden_half, dtype=BF16),
            shape(kept, width), shape(kept, 1),
            shape(target_length, 3 * half, dtype=BF16), shape(target_length, half, dtype=BF16), shape(8, target_length),
            shape(target_length, width), shape(target_length, 1), shape(fetched_rows, width, dtype=BF16),
        ],
        [held(fetched_rows, width // 2, dtype=BF16)] + Trade.scratch(count)
        + [held(2, target_length, span), held(half, target_length, dtype=BF16)]
        + Swap.scratch(tiles, width) * 2 + Swap.scratch(target_length // ROWS, width),
    )


def decoder_core(
    ident, unit, scale, fetched, cotangent, query_weight, wide, out_weight, up, down, shared, split,
    mixed, attended, totals, self_wide, self_out_weight, count,
):
    length, width = unit.shape
    keys = fetched.shape[0]
    half, hidden_half = out_weight.shape[0], up.shape[1]
    tiles, span = length // ROWS, min(length, 512)
    places = bias_places(half, hidden_half)

    def body(
        need, done, unit_ref, scale_ref, fetched_ref, cotangent_ref, query_weight_ref, wide_ref, out_weight_ref,
        up_ref, down_ref, shared_ref, split_ref,
        self_mixed_ref, self_attended_ref, self_totals_ref, self_wide_ref, self_out_weight_ref,
        states_ref, low_ref, attended_ref, second_low_ref, active_ref,
        feed_low_ref, grad_up_ref, up_bias_ref, sums_after_ref, sums_before_ref,
        cross_low_ref, grad_query_ref, grad_pair_ref, landed_ref, cross_sums_ref, vec_sums_ref,
        self_low_ref, self_query_ref, self_pair_ref, grad_x_ref, self_sums_ref,
        query_ref, mixed_ref, totals_ref, unit_four_ref, scale_four_ref, slope_ref,
        unit_five_ref, scale_five_ref, grad_four_ref, inner_ref, score_ref, turned_ref, grad_ref, returned_ref, grad_out_ref,
        send_sem, recv_sem, give_sem, take_sem, *swaps,
    ):
        need(0, 1, 2, 4, 5, 6, 9, 10)
        trade = Trade(count, landed_ref, send_sem, recv_sem, give_sem, take_sem)
        trade.greet()
        cross_forward_kernel(
            span, unit_ref, fetched_ref, query_weight_ref, wide_ref, out_weight_ref,
            split_ref.at[:, places["crs_q"]], bias_row(split_ref, places, (None, "crs_v"), half),
            Rows(shared_ref, (7, 8, 9)),
            low_ref, query_ref, mixed_ref, attended_ref, totals_ref, unit_four_ref, scale_four_ref,
            score_ref, turned_ref, *swaps[:4],
        )
        done(1, 2)
        need(7, 8)
        feed_forward_kernel(
            length, lambda: None, unit_four_ref, up_ref, down_ref, split_ref.at[:, places["dec_up"]],
            Rows(shared_ref, (10, 11, 12, 13, 14)),
            states_ref, cross_low_ref, second_low_ref, active_ref, slope_ref, unit_five_ref, scale_five_ref,
            *swaps[4:8],
        )
        done(0, 3, 4)
        need(3)
        feed_backward_kernel(
            cotangent_ref, unit_five_ref, scale_five_ref, active_ref, slope_ref, up_ref, down_ref,
            unit_four_ref, scale_four_ref, Rows(shared_ref, (13, 10)),
            feed_low_ref, grad_up_ref, up_bias_ref, grad_four_ref, sums_after_ref, sums_before_ref,
            inner_ref, *swaps[8:12],
        )
        done(5, 6, 7, 8, 9)
        cross_backward_kernel(
            lambda: trade.start(returned_ref), grad_four_ref, query_ref, mixed_ref, attended_ref, totals_ref, query_weight_ref, wide_ref,
            out_weight_ref, unit_ref, scale_ref, Rows(shared_ref, (7,)),
            cross_low_ref, grad_query_ref, grad_pair_ref, returned_ref, grad_out_ref, cross_sums_ref, vec_sums_ref,
            grad_ref, turned_ref, *swaps[12:20],
        )
        done(10, 11, 12, 14, 15)
        need(11, 12, 13, 14, 15)
        self_backward_kernel(
            True, grad_out_ref, self_mixed_ref, self_attended_ref, self_totals_ref, self_wide_ref, self_out_weight_ref,
            self_low_ref, self_query_ref, self_pair_ref, grad_x_ref, self_sums_ref,
            grad_ref, turned_ref.at[:, :length], *swaps[20:],
        )
        done(16, 17, 18, 19, 20)
        trade.finish(returned_ref)
        done(13)

    return call(
        "decoder_core", ident, body,
        [
            unit, scale, fetched, cotangent, query_weight, wide, out_weight, up, down, shared, split,
            mixed, attended, totals, self_wide, self_out_weight,
        ],
        [
            shape(length, width), shape(length, width, dtype=BF16), shape(length, half, dtype=BF16),
            shape(length, width, dtype=BF16), shape(length, hidden_half, dtype=BF16),
            shape(length, width, dtype=BF16), shape(length, hidden_half, dtype=BF16), shape(1, hidden_half),
            shape(8, width), shape(8, width),
            shape(length, width, dtype=BF16), shape(length, half, dtype=BF16), shape(keys, 2 * half, dtype=BF16),
            shape(keys, width, dtype=BF16), shape(1, 3 * half), shape(8, width),
            shape(length, width, dtype=BF16), shape(length, half, dtype=BF16), shape(length, 2 * half, dtype=BF16),
            shape(length, width), shape(1, 3 * half),
        ],
        [
            held(length, half, dtype=BF16), held(keys, 2 * half, dtype=BF16), held(8, length),
            held(length, width), held(length, 1),
            held(length, hidden_half, dtype=BF16), held(length, width), held(length, 1),
            held(length, width), held(length, width), held(2, keys, span), held(half, keys, dtype=BF16),
            held(length, half, dtype=BF16), held(keys, width, dtype=BF16), held(length, width),
        ]
        + Trade.scratch(count)
        + Swap.scratch(tiles, width) * 4 + Swap.scratch(keys // ROWS, width) + Swap.scratch(tiles, width),
        60,
    )


def encoder_backward(
    ident, returned, wanted, unit_two, scale_two, active, slope, up, down, unit_one, scale_one,
    mixed, attended, totals, wide, out_weight, shared,
):
    queries, width = unit_two.shape
    length, half, hidden_half = mixed.shape[0], out_weight.shape[0], up.shape[1]

    def body(
        need, done, returned_ref, wanted_ref, unit_two_ref, scale_two_ref, active_ref, slope_ref, up_ref, down_ref, unit_one_ref, scale_one_ref,
        mixed_ref, attended_ref, totals_ref, wide_ref, out_weight_ref, shared_ref,
        feed_low_ref, grad_up_ref, up_bias_ref, sums_after_ref, sums_before_ref,
        low_ref, grad_query_ref, grad_pair_ref, grad_x_ref, sums_ref,
        grad_ref, grad_one_ref, inner_ref, grad_out_ref, turned_ref, *swaps,
    ):
        need(0, 1)

        def collect(t, carry):
            place = t * ROWS + lax.broadcasted_iota(jnp.int32, (ROWS, returned_ref.shape[0]), 0)
            match = jnp.where(wanted_ref[...] == place, 1.0, 0.0).astype(BF16)
            grad_ref[rows_of(t), :] = times(match, returned_ref[...])
            return carry

        lax.fori_loop(0, queries // ROWS, collect, 0)
        need(*range(2, 10), 15)
        Swap.greet()
        feed_backward_kernel(
            grad_ref, unit_two_ref, scale_two_ref, active_ref, slope_ref, up_ref, down_ref,
            unit_one_ref, scale_one_ref, Rows(shared_ref, (4, 1)),
            feed_low_ref, grad_up_ref, up_bias_ref, grad_one_ref, sums_after_ref, sums_before_ref,
            inner_ref, *swaps[:4],
        )
        done(0, 1, 2, 3, 4)
        need(10, 11, 12, 13, 14)
        self_backward_kernel(
            False, grad_one_ref, mixed_ref, attended_ref, totals_ref, wide_ref, out_weight_ref,
            low_ref, grad_query_ref, grad_pair_ref, grad_x_ref, sums_ref, grad_out_ref, turned_ref, *swaps[4:],
        )
        done(*range(5, 10))

    return call(
        "encoder_backward", ident, body,
        [
            returned, wanted, unit_two, scale_two, active, slope, up, down, unit_one, scale_one,
            mixed, attended, totals, wide, out_weight, shared,
        ],
        [
            shape(queries, width, dtype=BF16), shape(queries, hidden_half, dtype=BF16), shape(1, hidden_half),
            shape(8, width), shape(8, width),
            shape(queries, width, dtype=BF16), shape(queries, half, dtype=BF16), shape(length, 2 * half, dtype=BF16),
            shape(length, width), shape(1, 3 * half),
        ],
        [
            held(queries, width), held(queries, width), held(queries, width), held(queries, half, dtype=BF16),
            held(half, length, dtype=BF16),
        ]
        + Swap.scratch(queries // ROWS, width) + Swap.scratch(length // ROWS, width),
    )


def adam_vector(grad_value, value, first, second):
    new_first = BETA_ONE * first + (1.0 - BETA_ONE) * grad_value
    new_second = BETA_TWO * second + (1.0 - BETA_TWO) * grad_value * grad_value
    correct_one = 1.0 - BETA_ONE**STEP
    correct_two = 1.0 - BETA_TWO**STEP
    updated = value - VECTOR_RATE * (new_first / correct_one) / (
        jnp.sqrt(new_second / correct_two) + ADAM_EPSILON
    )
    return (new_first, new_second, updated)


def local(
    source_tokens,
    target_tokens,
    target_cotangent,
    retrieved,
    kept_mask,
    owner_slots,
    master,
    first_moment,
    second_moment,
    left_stats,
    right_stats,
    left_basis,
    right_basis,
    shared_vectors,
    shared_first,
    shared_second,
    split_vectors,
    split_first,
    split_second,
):
    tensor_count = lax.axis_size("tensor")
    device_count = lax.axis_size("dp")
    model_width = source_tokens.shape[1]
    tile_size = master.shape[2]
    hidden_width = (split_vectors.shape[1] - 3) * model_width
    half_width = model_width // tensor_count
    hidden_half = hidden_width // tensor_count
    qblocks = retrieved.shape[0]
    per_owner = retrieved.shape[1] // device_count
    me = lax.axis_index("dp")
    vectors = jnp.concatenate([shared_vectors, split_vectors[0]], 0)
    vector_count, vector_width = vectors.shape
    padded = -(-vector_count // 8) * 8
    small = jnp.concatenate(
        [
            jnp.pad(vectors, ((0, padded - vector_count), (0, TILE - vector_width))),
            retrieved.astype(jnp.float32).reshape(-1, TILE),
        ],
        0,
    )
    gathered, smalls = gather_all(master[0], small, device_count)
    whole = (
        smalls[:, :vector_count, :vector_width]
        .transpose(1, 0, 2)
        .reshape(vector_count, model_width)
        .astype(jnp.bfloat16)
    )
    shared_count = shared_vectors.shape[0]
    shared_whole, split_whole = whole[:shared_count], whole[shared_count:]
    shapes = [s[1:] for s in matrix_list(model_width, hidden_width, tensor_count)]
    names = [s[0] for s in matrix_list(model_width, hidden_width, tensor_count)]
    shared = jnp.pad(shared_whole.astype(F32), ((0, 16 - shared_count), (0, 0)))
    split = split_whole.astype(F32).reshape(1, -1)
    start_row = jnp.argmax(kept_mask)
    turned = jnp.roll(source_tokens, -start_row, 0)


    wanted = (
        smalls[:, padded:].reshape(device_count, qblocks, device_count, per_owner)[:, :, me]
        .transpose(1, 0, 2)
        .astype(jnp.int32)
        - KEEP * me
    ).reshape(1, -1)
    matrices, (enc_mixed, enc_attended, enc_totals) = unpack_and_attend(
        gathered, owner_slots, shapes, turned, split, bias_places(half_width, hidden_half), half_width
    )
    weights = dict(zip(names, matrices))
    (unit_one, scale_one,
     states, _, hidden_low, enc_active, enc_slope, unit_two, scale_two,
     dec_mixed, dec_attended, dec_totals, unit_three, scale_three, fetched) = encoder_and_fetch(
        10, turned, enc_attended, weights["enc_out"], weights["enc_up"], weights["enc_down"],
        shared, split, KEEP, wanted.reshape(-1, 1), target_tokens, weights["dec_qkv"], weights["dec_out"], device_count,
    )
    encoder_states = jnp.roll(states, start_row, 0)
    (decoder_states, first_low, crs_attended, second_low, dec_active,
     dec_feed_low, dec_grad_up, dec_up_bias, sums_five, sums_four,
     crs_low, crs_grad_query, crs_grad_pair, returned, crs_sums, sums_three,
     dec_low, dec_grad_query, dec_grad_pair, target_grad, dec_sums) = decoder_core(
        13, unit_three, scale_three, fetched, target_cotangent,
        weights["crs_q"], weights["crs_kv"], weights["crs_out"], weights["dec_up"], weights["dec_down"],
        shared, split, dec_mixed, dec_attended, dec_totals, weights["dec_qkv"], weights["dec_out"], device_count,
    )
    (enc_feed_low, enc_grad_up, enc_up_bias, sums_two, sums_one,
     enc_low, enc_grad_query, enc_grad_pair, grad_turned, enc_sums) = encoder_backward(
        18, returned, wanted, unit_two, scale_two, enc_active, enc_slope, weights["enc_up"], weights["enc_down"],
        unit_one, scale_one, enc_mixed, enc_attended, enc_totals, weights["enc_qkv"], weights["enc_out"], shared,
    )
    source_grad = jnp.roll(grad_turned, start_row, 0)

    first_block, total_blocks = {}, 0
    for name, height, breadth in matrix_list(model_width, hidden_width, tensor_count):
        first_block[name] = total_blocks
        total_blocks += height // TILE * (breadth // TILE)
    three = 3 * half_width
    outer = ((0, half_width), (2 * half_width, three))
    everything = ((0, hidden_half),)
    items = [
        (sums, 3 * i, None) for i, sums in enumerate((sums_one, sums_two, sums_three, sums_four, sums_five))
    ]
    at = shared_count * model_width
    for array, pieces in (
        (enc_sums, outer), (enc_up_bias, everything), (dec_sums, outer), (crs_sums, outer), (dec_up_bias, everything)
    ):
        items.append((array, at, pieces))
        at += sum(end - begin for begin, end in pieces)
    (slot_grads,) = weight_grads(
        [
            (first_block["dec_down"], [(dec_active, dec_feed_low)]),
            (first_block["dec_up"], [(second_low, dec_grad_up)]),
            (first_block["crs_out"], [(crs_attended, crs_low)]),
            (first_block["crs_q"], [(first_low, crs_grad_query)]),
            (first_block["crs_kv"], [(fetched, crs_grad_pair)]),
            (first_block["dec_out"], [(dec_attended, dec_low)]),
            (first_block["dec_qkv"], [(target_tokens, dec_grad_query), (target_tokens, dec_grad_pair)]),
        ],
        owner_slots,
        gathered.shape[0],
    )
    slot_grads, vector_grads = weight_grads(
        [
            (first_block["enc_down"], [(enc_active, enc_feed_low)]),
            (first_block["enc_up"], [(hidden_low, enc_grad_up)]),
            (first_block["enc_out"], [(enc_attended, enc_low)]),
            (first_block["enc_qkv"], [(turned, enc_grad_query), (turned, enc_grad_pair)]),
        ],
        owner_slots,
        gathered.shape[0],
        slot_grads,
        (padded, model_width, items),
    )
    slots = master.shape[1]
    owned_slots = me * slots + lax.broadcasted_iota(jnp.int32, (slots, 1), 0)
    used = jnp.any(owned_slots == owner_slots[None, :], 1).astype(jnp.int32)
    results, vector_sums = owner_update(
        used,
        slot_grads,
        vector_grads,
        [
            array[0]
            for array in (
                master, first_moment, second_moment, left_stats, right_stats, left_basis, right_basis
            )
        ],
        device_count,
    )
    vector_owned = lax.dynamic_slice_in_dim(vector_sums, me * vector_width, vector_width, 1)
    shared_owned = vector_owned[:shared_count]
    split_owned = vector_owned[shared_count:vector_count]
    new_master, new_first, new_second, new_left, new_right, new_lbasis, new_rbasis = results
    shared_new_first, shared_new_second, shared_updated = adam_vector(
        shared_owned, shared_vectors, shared_first, shared_second
    )
    split_new_first, split_new_second, split_updated = adam_vector(
        split_owned, split_vectors[0], split_first[0], split_second[0]
    )
    return (
        encoder_states,
        decoder_states,
        source_grad,
        target_grad,
        new_master[None],
        new_first[None],
        new_second[None],
        new_left[None],
        new_right[None],
        new_lbasis[None],
        new_rbasis[None],
        shared_new_first,
        shared_new_second,
        shared_updated,
        split_new_first[None],
        split_new_second[None],
        split_updated[None],
    )


def solution(mesh):
    placed = (
        P("dp", None),
        P("dp", None),
        P("dp", None),
        P("dp", None),
        P("dp"),
        P(),
        P("tensor", "dp", None, None),
        P("tensor", "dp", None, None),
        P("tensor", "dp", None, None),
        P("tensor", "dp", None, None),
        P("tensor", "dp", None, None),
        P("tensor", "dp", None, None),
        P("tensor", "dp", None, None),
        P(None, "dp"),
        P(None, "dp"),
        P(None, "dp"),
        P("tensor", None, "dp"),
        P("tensor", None, "dp"),
        P("tensor", None, "dp"),
    )
    return jax.shard_map(
        local,
        mesh=mesh,
        in_specs=placed,
        out_specs=(
            P("dp", None),
            P("dp", None),
            P("dp", None),
            P("dp", None),
            P("tensor", "dp", None, None),
            P("tensor", "dp", None, None),
            P("tensor", "dp", None, None),
            P("tensor", "dp", None, None),
            P("tensor", "dp", None, None),
            P("tensor", "dp", None, None),
            P("tensor", "dp", None, None),
            P(None, "dp"),
            P(None, "dp"),
            P(None, "dp"),
            P("tensor", None, "dp"),
            P("tensor", None, "dp"),
            P("tensor", None, "dp"),
        ),
        check_vma=False,
    )
```
